32 devices in a mesh: seq: 16 (over z, y, x), head: 2 (over core).
Axes of the slice: x: 2, y: 2, z: 4, core: 2. Of those that a mesh axis runs over, the one named last changes fastest.
Arguments:
- tokens: bfloat16 [2, 2, 4096, 768], P(None, None, 'seq', 'head'), may hold values from -6 to 6
- doc_starts: int32 [2, 2, 4096], P(None, None, 'seq'), may hold values from 0 to 1, as said below
- norm_gain: float32 [768], replicated, may hold values from 0.5 to 1.5
- input_gate_features: bfloat16 [768, 2, 1536], P('seq', None, 'head'), may hold values from -0.21875 to 0.21875
- input_state_weight: bfloat16 [768, 256], P('seq'), may hold values from -0.21875 to 0.21875
- input_step_weight: bfloat16 [768, 24], P('seq', 'head'), may hold values from -0.21875 to 0.21875
- conv_taps_x: float32 [4, 1536], P(None, 'head'), may hold values from -3 to 3
- conv_bias_x: float32 [1536], P('head'), may hold values from -1.8 to 1.8
- conv_taps_bc: float32 [4, 256], replicated, may hold values from -3 to 3
- conv_bias_bc: float32 [256], replicated, may hold values from -1.8 to 1.8
- step_bias: float32 [24], P('head'), may hold values from -1 to 1
- decay_log: float32 [24], P('head')
- skip_gain: float32 [24], P('head'), may hold values from 0.5 to 1.5
- inner_gain: float32 [1536], P('head'), may hold values from 0.5 to 1.5
- output_projection: bfloat16 [1536, 768], P('head', 'seq'), may hold values from -0.15625 to 0.15625
- out_grad: bfloat16 [2, 2, 4096, 768], P(None, None, 'seq', 'head'), may hold values from -6 to 6
Outputs:
- mixed: bfloat16 [2, 2, 4096, 768], P(None, None, 'seq', 'head')
- tokens_grad: float32 [2, 2, 4096, 768], P(None, None, 'seq', 'head')
- norm_gain_grad: float32 [768], replicated
- in_gate_x_grad: float32 [768, 2, 1536], P('seq', None, 'head')
- in_states_grad: float32 [768, 256], P('seq')
- in_steps_grad: float32 [768, 24], P('seq', 'head')
- conv_taps_x_grad: float32 [4, 1536], P(None, 'head')
- conv_bias_x_grad: float32 [1536], P('head')
- conv_taps_bc_grad: float32 [4, 256], replicated
- conv_bias_bc_grad: float32 [256], replicated
- step_bias_grad: float32 [24], P('head')
- decay_log_grad: float32 [24], P('head')
- skip_gain_grad: float32 [24], P('head')
- inner_gain_grad: float32 [1536], P('head')
- out_proj_grad: float32 [1536, 768], P('head', 'seq')
The draws below stay inside these ranges and needn't reach their ends.
Inputs may be any that keep to these rules, and one draw needn't show every extreme that they name: `doc_starts`: every sequence begins with a 1. In each micro-batch one of the 2 sequences, drawn from the seed, is a single document; the others hold documents of max(2, 25) to max(2, 25) + max(2, 256 - max(2, 25)) positions, the last one of a sequence possibly shorter.
All inputs are finite; a program needn't handle non-finite values.
Results may differ from the reference program's by a relative error of at most 0.019.
The reference program's roundings to bfloat16 on the way count: a program that leaves them out, or rounds other values in their place, can miss the bound.
Values may be sent and summed in bfloat16 or wider, within the bound.
A program may use at most 448 MiB of HBM per device.

```python
import jax
import jax.numpy as jnp
from jax import lax

D = 768
HEADS = 24
HEAD_DIM = 64
NSTATE = 128
CONV = 4
BLOCK = 256
SEQS = 2
MICRO = 2
INNER = 1536
SEQLEN = 4096


def draw_doc_starts(key, part):
    key = jax.random.fold_in(key, 11)
    shortest = max(2, SEQLEN // 160)
    longest = shortest + max(2, SEQLEN // 16 - shortest)
    count = SEQLEN // shortest + 2
    gaps = jax.random.randint(key, (MICRO, SEQS, count), shortest, longest + 1)
    ends = jnp.cumsum(gaps, axis=-1)
    begins = jnp.concatenate([jnp.zeros((MICRO, SEQS, 1), jnp.int32), ends[..., :-1]], axis=-1)
    begins = jnp.minimum(begins, SEQLEN)
    micro_index = jnp.broadcast_to(jnp.arange(MICRO)[:, None, None], begins.shape)
    seq_index = jnp.broadcast_to(jnp.arange(SEQS)[None, :, None], begins.shape)
    marks = jnp.zeros((MICRO, SEQS, SEQLEN + 1), jnp.int32).at[micro_index, seq_index, begins].set(1)
    hits = marks[..., :SEQLEN]
    whole = jax.random.randint(jax.random.fold_in(key, 1), (MICRO, 1), 0, SEQS)
    single = jnp.arange(SEQS)[None, :] == whole
    first = (jnp.arange(SEQLEN) == 0).astype(jnp.int32)
    flags = jnp.where(single[..., None], first[None, None, :], hits)
    return flags.astype(jnp.int32)


def draw_decay_log(key, part):
    key = jax.random.fold_in(key, 23)
    quick = jax.random.permutation(key, HEADS) < HEADS // 2
    spot = jax.random.uniform(jax.random.fold_in(key, 1), (HEADS,), jnp.float32)
    slow = jnp.log(0.2 / SEQLEN) + spot * jnp.log(5.0)
    fast = jnp.log(0.02) + spot * jnp.log(2.5)
    return jnp.where(quick, fast, slow).astype(jnp.float32)


def block_levels(key, extent, cuts, low, high):
    loudness = 1.0
    for position, blocks in cuts:
        draws = jax.random.uniform(jax.random.fold_in(jax.random.fold_in(key, 6), position), (blocks,), jnp.float32, low / len(cuts), high / len(cuts))
        loudness = loudness * jnp.repeat(jnp.exp(draws), extent[position] // blocks).reshape((-1,) + (1,) * (len(extent) - 1 - position))
    return loudness


def normal_values(rng, dims, deviation, most, cuts=(), held_as=jnp.bfloat16):
    level = block_levels(rng, dims, cuts, -0.22, 0.18) if cuts else 1.0
    values = jax.random.normal(rng, dims, jnp.float32) * deviation * level
    return jnp.minimum(jnp.maximum(values, -most), most).astype(held_as)


def setup_inputs(seed: int = 0) -> dict:
    streams_of = jax.random.split(jax.random.key(seed), 17)
    tokens = normal_values(streams_of[0], (MICRO, SEQS, SEQLEN, D), 1.0, 6.0, ((2, 16), (3, 2)))
    doc_starts = draw_doc_starts(jax.random.fold_in(streams_of[16], 71), 0)
    norm_gain = jnp.clip(1.0 + 0.1 * jax.random.normal(streams_of[2], (D,), jnp.float32), 0.5, 1.5)
    input_gate_features = normal_values(streams_of[3], (D, 2, INNER), D ** -0.5, 0.21875, ((0, 16), (2, 2)))
    input_state_weight = normal_values(streams_of[4], (D, 2 * NSTATE), D ** -0.5, 0.21875, ((0, 16),))
    input_step_weight = normal_values(streams_of[5], (D, HEADS), D ** -0.5, 0.21875, ((0, 16), (1, 2)))
    conv_taps_x = normal_values(streams_of[6], (CONV, INNER), CONV ** -0.5, 3.0, ((1, 2),), jnp.float32)
    conv_bias_x = normal_values(streams_of[7], (INNER,), 0.3, 1.8, ((0, 2),), jnp.float32)
    conv_taps_bc = normal_values(streams_of[8], (CONV, 2 * NSTATE), CONV ** -0.5, 3.0, (), jnp.float32)
    conv_bias_bc = normal_values(streams_of[9], (2 * NSTATE,), 0.3, 1.8, (), jnp.float32)
    step_bias = jnp.clip(jax.random.uniform(streams_of[10], (HEADS,), jnp.float32, -1.0, 1.0) * block_levels(streams_of[10], (HEADS,), ((0, 2),), -0.4, 0.0), -1.0, 1.0)
    decay_log = draw_decay_log(jax.random.fold_in(streams_of[16], 71), 0)
    skip_gain = jnp.clip(0.5 + 1.0 * jax.random.uniform(streams_of[12], (HEADS,), jnp.float32) ** block_levels(streams_of[12], (HEADS,), ((0, 2),), -0.2, 0.2), 0.5, 1.5)
    inner_gain = jnp.clip(1.0 + 0.1 * jax.random.normal(streams_of[13], (INNER,), jnp.float32), 0.5, 1.5)
    output_projection = normal_values(streams_of[14], (INNER, D), INNER ** -0.5, 0.15625, ((0, 2), (1, 16)))
    out_grad = normal_values(streams_of[15], (MICRO, SEQS, SEQLEN, D), 1.0, 6.0, ((2, 16), (3, 2)))
    return {"tokens": tokens, "doc_starts": doc_starts, "norm_gain": norm_gain, "input_gate_features": input_gate_features, "input_state_weight": input_state_weight, "input_step_weight": input_step_weight, "conv_taps_x": conv_taps_x, "conv_bias_x": conv_bias_x, "conv_taps_bc": conv_taps_bc, "conv_bias_bc": conv_bias_bc, "step_bias": step_bias, "decay_log": decay_log, "skip_gain": skip_gain, "inner_gain": inner_gain, "output_projection": output_projection, "out_grad": out_grad}


EPSILON = 1e-05
EXACT_MATMUL = lax.Precision.HIGHEST

@jax.custom_vjp
def reduced_precision(v):
    return lax.optimization_barrier(v.astype(jnp.bfloat16)).astype(jnp.float32)

@jax.custom_vjp
def reduced_precision_backward(v):
    return v

def low_keep(v):
    return (reduced_precision(v), None)

def low_pass(kept, grad):
    return (grad,)

def back_keep(v):
    return (v, None)

def back_low(kept, grad):
    return (reduced_precision(grad),)
reduced_precision.defvjp(low_keep, low_pass)
reduced_precision_backward.defvjp(back_keep, back_low)

def swish(inputs):
    return inputs * jax.nn.sigmoid(inputs)

def block_step(decay_rate, hstate, pieces):
    values, in_state, out_state, step_size, doc_number, entry_number = pieces
    log_decay = jnp.cumsum(step_size * decay_rate, axis=1)
    length = doc_number.shape[1]
    places = jnp.arange(length)
    causal = places[:, None] >= places[None, :]
    allowed = causal[None] & (doc_number[:, :, None] == doc_number[:, None, :])
    allowed_h = allowed[..., None]
    spread = log_decay[:, :, None, :] - log_decay[:, None, :, :]
    decay_mat = jnp.where(allowed_h, jnp.exp(jnp.where(allowed_h, spread, 0.0)), 0.0)
    scores = jnp.einsum('sin,sjn->sij', out_state, in_state, precision=EXACT_MATMUL)
    mixing = scores[..., None] * decay_mat * step_size[:, None, :, :]
    inside = jnp.einsum('sijh,sjhp->sihp', mixing, values, precision=EXACT_MATMUL)
    entry_decay = jnp.exp(log_decay) * (doc_number == entry_number[:, None])[..., None]
    carried = jnp.einsum('sin,shpn->sihp', out_state, hstate, precision=EXACT_MATMUL) * entry_decay[..., None]
    tail_weight = jnp.exp(log_decay[:, -1:, :] - log_decay) * (doc_number == doc_number[:, -1:])[..., None] * step_size
    new_state = entry_decay[:, -1, :, None, None] * hstate + jnp.einsum('sjh,sjhp,sjn->shpn', tail_weight, values, in_state, precision=EXACT_MATMUL)
    return (new_state, inside + carried)

def to_blocks(source):
    shaped = source.reshape((source.shape[0], source.shape[1] // BLOCK, BLOCK) + source.shape[2:])
    return jnp.moveaxis(shaped, 1, 0)

def run_blocks(values, in_state, out_state, step_size, decay_rate, doc_number, entry_number, hstate):
    stepper = jax.checkpoint(block_step)

    def advance(current, pieces):
        return stepper(decay_rate, current, pieces)
    pieces = (to_blocks(values), to_blocks(in_state), to_blocks(out_state), to_blocks(step_size), to_blocks(doc_number), jnp.moveaxis(entry_number, 1, 0))
    last_state, outputs = lax.scan(advance, hstate, pieces)
    merged = jnp.moveaxis(outputs, 0, 1)
    return (merged.reshape(values.shape), last_state)

def block_entry_numbers(doc_number):
    shifted = jnp.concatenate([jnp.zeros_like(doc_number[:, :1]), doc_number[:, :-1]], axis=1)
    return shifted[:, ::BLOCK]

def causal_conv(inputs, taps, offset):
    width = taps.shape[0]
    length = inputs.shape[1]
    padded = jnp.pad(inputs, ((0, 0), (width - 1, 0), (0, 0)))
    total = offset + taps[0] * padded[:, 0:length]
    for tap_index in range(1, width):
        total = total + taps[tap_index] * padded[:, tap_index:tap_index + length]
    return total

def mixer(tokens, doc_flags, norm_gain, input_gate_features, input_state_weight, input_step_weight, conv_taps_x, conv_bias_x, conv_taps_bc, conv_bias_bc, step_bias, decay_log, skip_gain, inner_gain, output_projection):
    seq_count = tokens.shape[0]
    length = tokens.shape[1]
    row_scale = lax.rsqrt(lax.optimization_barrier(jnp.mean(tokens * tokens, axis=-1, keepdims=True)) + EPSILON)
    normalized_rows = reduced_precision(tokens * row_scale * norm_gain)
    gate_projected = reduced_precision_backward(jnp.einsum('zxw,wt->zxt', normalized_rows, input_gate_features[:, 0], precision=EXACT_MATMUL))
    feature_projected = reduced_precision_backward(reduced_precision(jnp.einsum('zxw,wt->zxt', normalized_rows, input_gate_features[:, 1], precision=EXACT_MATMUL)))
    state_projected = reduced_precision(jnp.einsum('zxw,wt->zxt', normalized_rows, input_state_weight, precision=EXACT_MATMUL))
    step_projected = jnp.einsum('zxw,wt->zxt', normalized_rows, input_step_weight, precision=EXACT_MATMUL)
    values = reduced_precision(swish(causal_conv(feature_projected, conv_taps_x, conv_bias_x)))
    states = reduced_precision(swish(causal_conv(state_projected, conv_taps_bc, conv_bias_bc)))
    step_size = jax.nn.softplus(step_projected + step_bias)
    decay_rate = -jnp.exp(decay_log)
    doc_number = jnp.cumsum(doc_flags, axis=1).astype(jnp.int32)
    head_values = values.reshape(seq_count, length, HEADS, HEAD_DIM)
    start_state = jnp.zeros((seq_count, HEADS, HEAD_DIM, NSTATE), jnp.float32)
    scanned, last_state = run_blocks(head_values, states[..., :NSTATE], states[..., NSTATE:], step_size, decay_rate, doc_number, block_entry_numbers(doc_number), start_state)
    mixed_heads = scanned + skip_gain[:, None] * head_values
    gated_out = mixed_heads.reshape(seq_count, length, INNER) * swish(gate_projected)
    inner_scale = lax.rsqrt(lax.optimization_barrier(jnp.mean(gated_out * gated_out, axis=-1, keepdims=True)) + EPSILON)
    gated_normalized = reduced_precision(gated_out * inner_scale * inner_gain)
    return tokens + jnp.einsum('amz,ze->ame', gated_normalized, output_projection, precision=EXACT_MATMUL)

def reference(tokens, doc_starts, norm_gain, input_gate_features, input_state_weight, input_step_weight, conv_taps_x, conv_bias_x, conv_taps_bc, conv_bias_bc, step_bias, decay_log, skip_gain, inner_gain, output_projection, out_grad):
    params = tuple((weight_arg.astype(jnp.float32) for weight_arg in (norm_gain, input_gate_features, input_state_weight, input_step_weight, conv_taps_x, conv_bias_x, conv_taps_bc, conv_bias_bc, step_bias, decay_log, skip_gain, inner_gain, output_projection)))
    grads = tuple((jnp.zeros_like(weight_arg) for weight_arg in params))
    outputs = []
    input_grads = []
    for micro_index in range(MICRO):
        flags = doc_starts[micro_index]

        def layer(inputs, *weights):
            return mixer(inputs, flags, *weights)
        result, backward = jax.vjp(layer, tokens[micro_index].astype(jnp.float32), *params)
        cotangents = backward(out_grad[micro_index].astype(jnp.float32))
        outputs.append(result.astype(jnp.bfloat16))
        input_grads.append(cotangents[0])
        grads = jax.tree.map(jnp.add, grads, tuple(cotangents[1:]))
    return (jnp.stack(outputs), jnp.stack(input_grads), grads[0], grads[1], grads[2], grads[3], grads[4], grads[5], grads[6], grads[7], grads[8], grads[9], grads[10], grads[11], grads[12])
```

```python
import functools

import jax
import jax.numpy as jnp
from jax import lax
from jax.experimental import pallas as pl
from jax.experimental.pallas import tpu as pltpu
from jax.sharding import PartitionSpec as P

F32 = jnp.float32
BF16 = jnp.bfloat16
EPSILON = 1e-05
MASKED = -1e30
HALO = 16
EDGE = 8
HEAD_ROWS = 16
LANES = 128
MESH = pl.DeviceIdType.MESH
NN = ((1,), (0,))
NT = ((1,), (1,))
TN = ((0,), (0,))
VMEM_LIMIT = 60 * 2**20

GAIN, INNER_GAIN, SKIP, BIAS, STEP_BIAS, RATE, TAPS = 0, 1, 2, 3, 4, 5, 6


def dot(a, b, dims=NN):
    return lax.dot_general(a, b, (dims, ((), ())), preferred_element_type=F32)


def split2(v):
    high = v.astype(BF16)
    return high, (v - high.astype(F32)).astype(BF16)


def split3(v):
    high = v.astype(BF16)
    rest = v - high.astype(F32)
    middle = rest.astype(BF16)
    return high, middle, (rest - middle.astype(F32)).astype(BF16)


def sigmoid(v):
    return 1.0 / (1.0 + jnp.exp(-v))


def softplus(v):
    return jnp.maximum(v, 0.0) + jnp.log1p(jnp.exp(-jnp.abs(v)))


def head_spread(inner, size):
    rows = lax.broadcasted_iota(jnp.int32, (LANES, inner), 0)
    columns = lax.broadcasted_iota(jnp.int32, (LANES, inner), 1)
    return jnp.where(rows == columns // size, 1.0, 0.0).astype(BF16)


def expand(per_head, spread):
    high, low = split2(per_head)
    return dot(high, spread) + dot(low, spread)


def head_sums(wide, spread):
    high, low = split2(wide)
    return dot(high, spread, NT) + dot(low, spread, NT)


def triangle(length, upper=False):
    rows = lax.broadcasted_iota(jnp.int32, (length, length), 0)
    columns = lax.broadcasted_iota(jnp.int32, (length, length), 1)
    kept = rows <= columns if upper else rows >= columns
    return kept, jnp.where(kept, 1.0, 0.0).astype(BF16)


def running_sum(ones, v):
    a, b, c = split3(v)
    return dot(ones, a) + dot(ones, b) + dot(ones, c)


def doc_numbers(doc, ones):
    flags = doc.astype(BF16)
    return dot(ones, flags, NT)[:, :1], dot(flags, ones, NT)[:1]


def call(kernel, grid, in_specs, out_specs, out_shape, scratch=(), name=None, flops=10**9):
    return pl.pallas_call(
        kernel,
        grid=grid,
        in_specs=in_specs,
        out_specs=out_specs,
        out_shape=out_shape,
        scratch_shapes=list(scratch),
        compiler_params=pltpu.CompilerParams(
            vmem_limit_bytes=VMEM_LIMIT, dimension_semantics=("arbitrary",) * len(grid)
        ),
        cost_estimate=pl.CostEstimate(flops=flops, bytes_accessed=10**7, transcendentals=0),
        name=name,
    )


def whole(array):
    rank = len(array.shape)
    return pl.BlockSpec(array.shape, lambda i: (0,) * rank)


def per_seq(array):
    rank = len(array.shape)
    return pl.BlockSpec((1,) + tuple(array.shape[1:]), lambda i: (i,) + (0,) * (rank - 1))


def shape(dims, dtype):
    return jax.ShapeDtypeStruct(tuple(dims), dtype)


def forward_kernel(
    sizes, tok, halo, doc, prm, w, normed_o, gate_o, xs_o, pre_o, act_o, scan_o, state_o, aux_o,
    dec_o, ext,
):
    length, inner, nstate, size, taps = sizes
    channels = inner + 2 * nstate
    first = lax.axis_index("seq") == 0
    edge = jnp.where(first, 0.0, halo[0].astype(F32))
    x = jnp.concatenate([edge, tok[0].astype(F32)], axis=0)
    scale = lax.rsqrt(jnp.mean(x * x, axis=-1, keepdims=True) + EPSILON)
    normed = (x * scale * prm[GAIN : GAIN + 1, : x.shape[1]]).astype(BF16)
    normed_o[0] = normed[HALO:]
    gate_o[0] = dot(normed[HALO:], w[:, :inner])
    xs = dot(normed, w[:, inner : inner + channels]).astype(BF16)
    xs_o[0] = xs
    ext[...] = xs.astype(F32)
    pre = prm[BIAS : BIAS + 1, :channels]
    for k in range(taps):
        start = HALO - taps + 1 + k
        pre = pre + prm[TAPS + k : TAPS + k + 1, :channels] * ext[start : start + length]
    pre_o[0] = pre
    act = (pre * sigmoid(pre)).astype(BF16)
    act_o[0] = act
    step_pre = (
        dot(normed[HALO:], w[:, inner + channels :]) + prm[STEP_BIAS : STEP_BIAS + 1, :LANES]
    )
    step = softplus(step_pre)
    kept, ones = triangle(length)
    log_decay = running_sum(ones, step * prm[RATE : RATE + 1, :LANES])
    doc_col, doc_row = doc_numbers(doc[0], ones)
    entry = jnp.where(doc_col == 0.0, jnp.exp(log_decay), 0.0)
    last = log_decay[length - 1 :]
    tail = jnp.where(doc_col == doc_col[length - 1 :], jnp.exp(last - log_decay), 0.0)
    aux_o[0, :, 0:LANES] = log_decay
    aux_o[0, :, LANES : 2 * LANES] = step
    aux_o[0, :, 2 * LANES : 3 * LANES] = step_pre
    aux_o[0, :, 3 * LANES : 4 * LANES] = entry
    aux_o[0, :, 4 * LANES :] = tail
    spread = head_spread(inner, size)
    values = act[:, :inner].astype(F32)
    inputs = values * expand(step, spread)
    low_inputs = inputs.astype(BF16)
    in_state = act[:, inner : inner + nstate]
    out_state = act[:, inner + nstate :]
    state_o[0] = dot((inputs * expand(tail, spread)).astype(BF16), in_state, TN).astype(BF16)
    scores = dot(out_state, in_state, NT)
    closed = jnp.where(kept & (doc_col == doc_row), 0.0, MASKED)
    log_rows = log_decay.T
    whole_decay = jnp.where(doc_row[:, length - 1 :] == 0.0, jnp.exp(log_rows[:HEAD_ROWS, length - 1 :]), 0.0)
    dec_o[0] = jnp.broadcast_to(whole_decay, (HEAD_ROWS, LANES))
    left = lax.broadcasted_iota(jnp.int32, (length, LANES), 1) < size
    for pair in range(inner // LANES):
        columns = slice(pair * LANES, (pair + 1) * LANES)
        part = low_inputs[:, columns]
        total = None
        for side in range(2):
            h = 2 * pair + side
            decay = jnp.exp(log_decay[:, h : h + 1] - log_rows[h : h + 1] + closed)
            own = jnp.where(left if side == 0 else ~left, part, jnp.zeros_like(part))
            term = dot((scores * decay).astype(BF16), own)
            total = term if total is None else total + term
        scan_o[0, :, columns] = total


def gate_kernel(sizes, scan, act, aux, gate, hin, g, prm, wout, full_o, gn_o, sums_o):
    length, inner, nstate, size, taps = sizes
    spread = head_spread(inner, size)
    values = act[0, :, :inner].astype(F32)
    out_state = act[0, :, inner + nstate :]
    scanned = scan[0] + dot(out_state, hin[0], NT) * expand(aux[0, :, 3 * LANES : 4 * LANES], spread)
    full_o[0] = scanned
    mixed = scanned + prm[SKIP : SKIP + 1, :inner] * values
    gated = mixed * (gate[0] * sigmoid(gate[0]))
    grad_norm = dot(g[0], wout[...])
    gn_o[0] = grad_norm
    squares = jnp.sum(gated * gated, axis=-1, keepdims=True)
    cross = jnp.sum(
        grad_norm * prm[INNER_GAIN : INNER_GAIN + 1, :inner] * gated, axis=-1, keepdims=True
    )
    lane = lax.broadcasted_iota(jnp.int32, (length, LANES), 1)
    sums_o[0] = jnp.where(lane == 0, squares, jnp.where(lane == 1, cross, 0.0))


def output_kernel(
    sizes, total_inner, full, act, aux, gate, gn, sums, sums_in, g, normed, prm, wout,
    keep_o, send_o, dy_o, ggate_o, prior_o, small_o, dout_o, dgate_o, acc_out, acc_gate, wide,
):
    length, inner, nstate, size, taps = sizes
    at = pl.program_id(0)
    spread = head_spread(inner, size)
    values = act[0, :, :inner].astype(F32)
    out_state = act[0, :, inner + nstate :]
    mixed = full[0] + prm[SKIP : SKIP + 1, :inner] * values
    z = gate[0]
    sig = sigmoid(z)
    swish = z * sig
    gated = mixed * swish
    both = sums[0] + sums_in[0]
    inner_scale = lax.rsqrt(both[:, 0:1] / total_inner + EPSILON)
    gain = prm[INNER_GAIN : INNER_GAIN + 1, :inner]
    unit = gated * inner_scale
    normal = (unit * gain).astype(BF16)
    wide[...] = dot(normal, wout[...], NT)
    half = wide.shape[1] // 2
    core = lax.axis_index("head")
    keep_o[0] = wide[:, pl.ds(pl.multiple_of(core * half, LANES), half)]
    send_o[0] = wide[:, pl.ds(pl.multiple_of((1 - core) * half, LANES), half)].astype(BF16)
    grad_norm = gn[0]
    grad_inner = jnp.sum(grad_norm * unit, axis=0, keepdims=True)
    grad_gated = inner_scale * (grad_norm * gain) - unit * (
        inner_scale * inner_scale * (both[:, 1:2] / total_inner)
    )
    dy = grad_gated * swish
    low_dy = dy.astype(BF16)
    dy_o[0] = low_dy
    ggate = (grad_gated * mixed * (sig * (1.0 + z * (1.0 - sig)))).astype(BF16)
    ggate_o[0] = ggate
    grad_skip = jnp.sum(dy * values, axis=0, keepdims=True)
    entry = expand(aux[0, :, 3 * LANES : 4 * LANES], spread)
    prior_o[0] = dot((dy * entry).astype(BF16), out_state, TN).astype(BF16)
    rows = jnp.concatenate([grad_inner, grad_skip, jnp.zeros((6, inner), F32)], axis=0)
    term_out = dot(g[0], normal, TN)
    term_gate = dot(normed[0], ggate, TN)

    @pl.when(at == 0)
    def _():
        small_o[...] = rows
        acc_out[...] = term_out
        acc_gate[...] = term_gate

    @pl.when(at > 0)
    def _():
        small_o[...] += rows
        acc_out[...] += term_out
        acc_gate[...] += term_gate

    @pl.when(at == pl.num_programs(0) - 1)
    def _():
        dout_o[...] = acc_out[...].astype(BF16)
        dgate_o[...] = acc_gate[...].astype(BF16)


def backward_kernel(
    sizes, full, act, aux, dy, hin, later, state, doc, pre, prm,
    gcx_o, own_o, send_o, gpre_o, small_o, edge_o, slope_o, dcb,
):
    length, inner, nstate, size, taps = sizes
    at = pl.program_id(0)
    core = lax.axis_index("head")
    spread = head_spread(inner, size)
    log_decay = aux[0, :, 0:LANES]
    step = aux[0, :, LANES : 2 * LANES]
    step_pre = aux[0, :, 2 * LANES : 3 * LANES]
    entry = aux[0, :, 3 * LANES : 4 * LANES]
    tail = aux[0, :, 4 * LANES :]
    values = act[0, :, :inner].astype(F32)
    in_state = act[0, :, inner : inner + nstate]
    out_state = act[0, :, inner + nstate :]
    low_dy = dy[0]
    wide_dy = low_dy.astype(F32)
    step_wide = expand(step, spread)
    tail_wide = expand(tail, spread)
    entry_wide = expand(entry, spread)
    inputs = values * step_wide
    low_inputs = inputs.astype(BF16)
    kept, ones = triangle(length)
    upper, ones_upper = triangle(length, True)
    doc_col, doc_row = doc_numbers(doc[0], ones)
    closed = jnp.where(upper & (doc_col == doc_row), 0.0, MASKED)
    scores = dot(in_state, out_state, NT)
    log_rows = log_decay.T
    left = lax.broadcasted_iota(jnp.int32, (length, LANES), 1) < size
    grad_inputs = tail_wide * dot(in_state, later[0], NT)
    parts = []
    for pair in range(inner // LANES):
        columns = slice(pair * LANES, (pair + 1) * LANES)
        pair_dy = low_dy[:, columns]
        pair_in = low_inputs[:, columns]
        total = grad_inputs[:, columns]
        for side in range(2):
            h = 2 * pair + side
            chosen = left if side == 0 else ~left
            own_dy = jnp.where(chosen, pair_dy, jnp.zeros_like(pair_dy))
            decay = jnp.exp(log_rows[h : h + 1] - log_decay[:, h : h + 1] + closed)
            total = total + dot((scores * decay).astype(BF16), own_dy)
            grad_decay = dot(pair_in, own_dy, NT) * decay
            if h == 0:
                dcb[...] = grad_decay
            else:
                dcb[...] += grad_decay
        parts.append(total)
    grad_inputs = jnp.concatenate(parts, axis=1)
    grad_scores = dcb[...]
    grad_in = dot(grad_scores.astype(BF16), out_state) + dot(
        (inputs * tail_wide).astype(BF16), later[0]
    )
    grad_out = dot(grad_scores.T.astype(BF16), in_state) + dot(
        (wide_dy * entry_wide).astype(BF16), hin[0]
    )
    entry_last = jnp.broadcast_to(entry[length - 1 :], (8, LANES))
    later_wide = later[0].astype(F32)
    lane_ones = jnp.ones((8, nstate), BF16)
    through = head_sums(
        sum(dot(lane_ones, piece, NT) for piece in split2(later_wide * hin[0].astype(F32))), spread
    )
    born = head_sums(
        sum(dot(lane_ones, piece, NT) for piece in split2(later_wide * state[0].astype(F32))), spread
    )
    ending = (born + entry_last * through)[:1]
    grad_log = head_sums(wide_dy * full[0], spread) - head_sums(
        low_inputs.astype(F32) * grad_inputs, spread
    )
    grad_rate_step = running_sum(ones_upper, grad_log) + ending
    rate = prm[RATE : RATE + 1, :LANES]
    grad_step = head_sums(values * grad_inputs, spread) + rate * grad_rate_step
    gpre = grad_step * sigmoid(step_pre)
    lane = lax.broadcasted_iota(jnp.int32, (length, LANES), 1)
    gpre = jnp.where(lane < inner // size, gpre, 0.0)
    gpre_o[0] = gpre
    grad_values = step_wide * grad_inputs + prm[SKIP : SKIP + 1, :inner] * wide_dy
    px = pre[0, :, :inner]
    sig = sigmoid(px)
    gcx = grad_values * (sig * (1.0 + px * (1.0 - sig)))
    gcx_o[0] = gcx
    edge_o[0] = gcx[:EDGE]
    is_first = core == 0
    own_o[0] = jnp.where(is_first, grad_in, grad_out)
    send_o[0] = jnp.where(is_first, grad_out, grad_in).astype(BF16)
    ps = pre[0, :EDGE, pl.ds(pl.multiple_of(inner + core * nstate, LANES), nstate)]
    sig = sigmoid(ps)
    slope_o[0] = sig * (1.0 + ps * (1.0 - sig))
    rows = jnp.concatenate(
        [
            jnp.sum(gpre, axis=0, keepdims=True),
            rate * jnp.sum(step * grad_rate_step, axis=0, keepdims=True),
            jnp.zeros((6, LANES), F32),
        ],
        axis=0,
    )

    @pl.when(at == 0)
    def _():
        small_o[...] = rows

    @pl.when(at > 0)
    def _():
        small_o[...] += rows


def conv_kernel(
    sizes, gcx, own, recv, edge, edge_state, pre, xs, gpre, ggate, normed, prm, w,
    part_o, dx_o, small_o, acc, ext, gext,
):
    length, inner, nstate, size, taps = sizes
    at = pl.program_id(0)
    core = lax.axis_index("head")
    last = lax.axis_index("seq") == lax.axis_size("seq") - 1
    mine = pl.ds(pl.multiple_of(inner + core * nstate, LANES), nstate)
    channels = inner + nstate
    ps = pre[0, :, mine]
    sig = sigmoid(ps)
    gst = (own[0] + recv[0].astype(F32)) * (sig * (1.0 + ps * (1.0 - sig)))
    gext[:length, :inner] = gcx[0]
    gext[:length, inner:] = gst
    gext[length:, :inner] = jnp.where(last, 0.0, edge[0])
    gext[length:, inner:] = jnp.where(last, 0.0, edge_state[0])
    ext[:, :inner] = xs[0, :, :inner].astype(F32)
    ext[:, inner:] = xs[0, :, mine].astype(F32)
    grad_conv = gext[:length]
    grad_in = None
    rows = []
    for k in range(taps):
        row = jnp.concatenate(
            [prm[TAPS + k : TAPS + k + 1, :inner], prm[TAPS + k : TAPS + k + 1, mine]], axis=1
        )
        term = row * gext[taps - 1 - k : taps - 1 - k + length]
        grad_in = term if grad_in is None else grad_in + term
        start = HALO - taps + 1 + k
        rows.append(jnp.sum(ext[start : start + length] * grad_conv, axis=0, keepdims=True))
    rows.append(jnp.sum(grad_conv, axis=0, keepdims=True))
    rows.append(jnp.zeros((8 - taps - 1, channels), F32))
    rows = jnp.concatenate(rows, axis=0)
    low = grad_in.astype(BF16)
    low_pre = gpre[0].astype(BF16)
    part = dot(ggate[0], w[:, :inner], NT)
    part = part + dot(low[:, :inner], w[:, inner : 2 * inner], NT)
    wst = w[:, pl.ds(pl.multiple_of(2 * inner + core * nstate, LANES), nstate)]
    part = part + dot(low[:, inner:], wst, NT)
    part = part + dot(low_pre, w[:, 2 * inner + 2 * nstate :], NT)
    part_o[0] = part.astype(BF16)
    stacked = jnp.concatenate([low, low_pre], axis=1)
    term = dot(normed[0], stacked, TN)

    @pl.when(at == 0)
    def _():
        small_o[...] = rows
        acc[...] = term

    @pl.when(at > 0)
    def _():
        small_o[...] += rows
        acc[...] += term

    @pl.when(at == pl.num_programs(0) - 1)
    def _():
        dx_o[...] = acc[...].astype(BF16)


def tokens_kernel(sizes, tok, part, recv, g, prm, out_o, small_o, wide):
    at = pl.program_id(0)
    core = lax.axis_index("head")
    x = tok[0].astype(F32)
    model = x.shape[1]
    scale = lax.rsqrt(jnp.mean(x * x, axis=-1, keepdims=True) + EPSILON)
    unit = x * scale
    grad_normed = part[0].astype(F32) + recv[0].astype(F32)
    r = grad_normed * prm[GAIN : GAIN + 1, :model]
    wide[...] = scale * (r - unit * jnp.mean(r * unit, axis=-1, keepdims=True))
    half = model // 2
    out_o[0] = g[0].astype(F32) + wide[:, pl.ds(pl.multiple_of(core * half, LANES), half)]
    rows = jnp.concatenate(
        [jnp.sum(grad_normed * unit, axis=0, keepdims=True), jnp.zeros((7, model), F32)], axis=0
    )

    @pl.when(at == 0)
    def _():
        small_o[...] = rows

    @pl.when(at > 0)
    def _():
        small_o[...] += rows


def swap_heads(v):
    return lax.ppermute(v, "head", [(0, 1), (1, 0)])


def shift(v, distance):
    devices = range(lax.axis_size("seq"))
    return lax.ppermute(
        v, "seq", [(i - distance, i) for i in devices if i - distance in devices]
    )


def plain_gather(w_in, w_out, tokens, grads, tails):
    return (
        lax.all_gather(w_in, "seq", axis=0, tiled=True),
        lax.all_gather(w_out, "seq", axis=0, tiled=True),
        lax.all_gather(tokens, "head", axis=2, tiled=True),
        lax.all_gather(grads, "head", axis=2, tiled=True),
        lax.all_gather(shift(tails, 1), "head", axis=2, tiled=True),
    )


def plain_scan(state, decay, size, backward):
    count, place = lax.axis_size("seq"), lax.axis_index("seq")
    heads = state.shape[1] // size
    wide = jnp.repeat(decay[:, :heads, 0], size, axis=1)[..., None]
    states = lax.all_gather(state, "seq")
    decays = lax.all_gather(wide, "seq")

    def one(k, carried):
        at = count - 1 - k if backward else k
        reached = at > place if backward else at < place
        return jnp.where(reached, decays[at] * carried + states[at].astype(F32), carried)

    return lax.fori_loop(0, count, one, jnp.zeros(state.shape, F32)).astype(BF16)


def plain_states(send, own, slope, edge):
    recv = swap_heads(send)
    mine = (own[:, :EDGE] + recv[:, :EDGE].astype(F32)) * slope
    return recv, shift(edge, -1), shift(mine, -1)


def plain_sum(pieces, small, shared):
    totals = [
        lax.psum_scatter(p.astype(F32), "seq", scatter_dimension=0, tiled=True) for p in pieces
    ]
    shared = lax.psum(shared, ("seq", "head"))
    return totals, lax.psum(small, "seq"), shared


def plain_both(v):
    return lax.all_gather(v, "head", axis=1, tiled=True)


PLANE = 4
LINE = 4
OFFSETS = (0, -1, 1, -2, 2, -3, 3)


def place():
    s, c = lax.axis_index("seq"), lax.axis_index("head")
    return s, c, s // PLANE, (s // 2) % 2, s % 2


def remote(src, dst, send_sem, recv_sem, device):
    return pltpu.make_async_remote_copy(
        src_ref=src,
        dst_ref=dst,
        send_sem=send_sem,
        recv_sem=recv_sem,
        device_id=device,
        device_id_type=MESH,
    )


def greet(relations):
    barrier = pltpu.get_barrier_semaphore()
    total = 0
    for exists, device in relations:
        if exists is True:
            pl.semaphore_signal(barrier, inc=1, device_id=device, device_id_type=MESH)
            total = total + 1
        else:
            pl.when(exists)(
                functools.partial(
                    pl.semaphore_signal, barrier, inc=1, device_id=device, device_id_type=MESH
                )
            )
            total = total + jnp.where(exists, 1, 0)
    pl.semaphore_wait(barrier, total)


def comm_call(kernel, ins, outs, scratch, collective, name, anywhere=False):
    space = pl.ANY if anywhere else pltpu.VMEM
    return pl.pallas_call(
        kernel,
        in_specs=[pl.BlockSpec(memory_space=space) for _ in ins],
        out_specs=[pl.BlockSpec(memory_space=space) for _ in outs],
        out_shape=outs,
        scratch_shapes=list(scratch),
        compiler_params=pltpu.CompilerParams(
            collective_id=collective, has_side_effects=True, vmem_limit_bytes=VMEM_LIMIT
        ),
        name=name,
    )(*ins)


def dma(*dims):
    return pltpu.SemaphoreType.DMA(dims)


SUM_OFFSETS = (3, -3, 2, -2, 1, -1, 0)


class Refs:
    def __init__(self, names, refs):
        self.__dict__.update(zip(names, refs))


def fused_call(body, steps, ins, outs, scratch, collective, name):
    names = list(ins) + list(outs) + list(scratch)

    def kernel(*refs):
        body(Refs(names, refs))

    results = pl.pallas_call(
        kernel,
        grid=(steps,) if steps else (),
        in_specs=[spec for _, spec in ins.values()],
        out_specs=[spec for _, spec in outs.values()],
        out_shape=[shaped for shaped, _ in outs.values()],
        scratch_shapes=list(scratch.values()),
        compiler_params=pltpu.CompilerParams(
            collective_id=collective,
            has_side_effects=True,
            vmem_limit_bytes=VMEM_LIMIT,
            dimension_semantics=("arbitrary",) if steps else None,
        ),
        name=name,
    )(*[array for array, _ in ins.values()])
    return Refs(list(outs), results)


ANYWHERE = pl.BlockSpec(memory_space=pl.ANY)
INSIDE = pl.BlockSpec(memory_space=pltpu.VMEM)


def stepped(array, index):
    rank = len(array.shape)
    return pl.BlockSpec((1,) + tuple(array.shape[1:]), lambda k: (index(k),) + (0,) * (rank - 1))


def during(first, count=4):
    return lambda k: jnp.clip(k - first, 0, count - 1)


def cyclic(last, count=4):
    return lambda k: jnp.where(k < last, k % count, count - 1)


def either(core, own, other):
    low = jnp.where(core == 0, own, other)
    return jnp.concatenate([low, jnp.where(core == 0, other, own)], axis=1)


class Gather:
    def __init__(self, pieces, rows, sems):
        self.pieces, self.rows = pieces, rows
        self.local, self.zs, self.zr, self.as_, self.ar, self.bs, self.br = sems
        self.s, self.c, self.z, self.y, self.x = place()
        s, c = self.s, self.c
        self.up, self.down = self.z < LINE - 1, self.z > 0
        self.to_x, self.to_y = (s + 1 - 2 * self.x, c), (s + 2 - 4 * self.y, c)
        self.to_up, self.to_down = (s + PLANE, c), (s - PLANE, c)
        self.span = range(len(pieces))

    @staticmethod
    def semaphores(n):
        return dict(
            g0=dma(n), g1=dma(n, 2, 4), g2=dma(n, 4), g3=dma(n, 4), g4=dma(n, 4), g5=dma(n, 4, 2),
            g6=dma(n, 4, 2),
        )

    def at(self, p, index, count=1):
        src, dst, start, width, order = self.pieces[p]
        begin = pl.multiple_of(index * self.rows, 16)
        return dst.at[pl.ds(begin, count * self.rows), pl.ds(start, width)]

    def own(self, p):
        src, dst, start, width, order = self.pieces[p]
        return src.at[:, pl.ds(start, width)]

    def local_copy(self, p):
        return pltpu.make_async_copy(self.own(p), self.at(p, self.s), self.local.at[p])

    def z_copy(self, p, off):
        zz = self.z + off
        dst = self.at(p, zz * PLANE + self.y * 2 + self.x)
        src = self.own(p) if off == 0 else dst
        step = abs(off)
        moves = []
        if off <= 0:
            sems = self.zs.at[p, 0, step], self.zr.at[p, zz]
            moves.append((self.up, remote(src, dst, *sems, self.to_up)))
        if off >= 0:
            sems = self.zs.at[p, 1, step], self.zr.at[p, zz]
            moves.append((self.down, remote(src, dst, *sems, self.to_down)))
        return moves

    def first_copy(self, p, off):
        zz = self.z + off
        dst = self.at(p, zz * PLANE + self.y * 2 + self.x)
        src = self.own(p) if off == 0 else dst
        device = self.to_x if self.pieces[p][4] else self.to_y
        return remote(src, dst, self.as_.at[p, zz], self.ar.at[p, zz], device)

    def second_copies(self, p, off):
        zz = self.z + off
        if self.pieces[p][4]:
            pair = self.at(p, zz * PLANE + self.y * 2, 2)
            return [remote(pair, pair, self.bs.at[p, zz, 0], self.br.at[p, zz, 0], self.to_y)]
        copies = []
        for k in range(2):
            block = self.at(p, zz * PLANE + k * 2 + self.x)
            copies.append(
                remote(block, block, self.bs.at[p, zz, k], self.br.at[p, zz, k], self.to_x)
            )
        return copies

    def exists(self, off):
        zz = self.z + off
        return (zz >= 0) & (zz < LINE)

    def begin(self):
        for p in self.span:
            for there, copy in self.z_copy(p, 0):
                pl.when(there)(copy.start)
            self.first_copy(p, 0).start()
            self.local_copy(p).start()

    def z_arrived(self, *offs):
        for off in offs:

            @pl.when(self.exists(off))
            def _():
                for p in self.span:
                    for there, copy in self.z_copy(p, off):
                        copy.wait_recv()
                        pl.when(there)(copy.start)
                    self.first_copy(p, off).start()

    def first_arrived(self, *offs):
        for off in offs:

            @pl.when(self.exists(off))
            def _():
                for p in self.span:
                    if off == 0:
                        self.local_copy(p).wait()
                    self.first_copy(p, off).wait_recv()
                    for copy in self.second_copies(p, off):
                        copy.start()

    def finish(self):
        for off in OFFSETS:

            @pl.when(self.exists(off))
            def _():
                for p in self.span:
                    for copy in self.second_copies(p, off):
                        copy.wait()
                    self.first_copy(p, off).wait_send()
                    for there, copy in self.z_copy(p, off):
                        pl.when(there)(copy.wait_send)


class Scan:
    def __init__(self, backward, size, state, decay, out, refs):
        self.state, self.decay, self.out, self.size = state, decay, out, size
        (
            self.slots, self.rates, self.total, self.through, self.arriving, self.leaving,
            self.staged, self.s1, self.r1, self.s2, self.r2, self.zs, self.zr, self.s3, self.r3,
        ) = refs
        s, c, z, y, x = place()
        self.c, self.p = c, s % PLANE
        self.base = s - self.p
        self.order = tuple(range(PLANE - 1, -1, -1)) if backward else tuple(range(PLANE))
        self.rows = state.shape[1] // PLANE
        self.place = LINE - 1 - z if backward else z
        self.before, self.after = self.place > 0, self.place < LINE - 1
        self.step = -PLANE if backward else PLANE
        self.s = s

    @staticmethod
    def scratch(count, rows, nstate, heads):
        quarter = rows // PLANE
        return dict(
            slots=pltpu.VMEM((count, PLANE, quarter, nstate), BF16),
            rates=pltpu.VMEM((count, PLANE, heads, nstate), F32),
            total=pltpu.VMEM((count, quarter, nstate), F32),
            through=pltpu.VMEM((count, 8, nstate), F32),
            arriving=pltpu.VMEM((count, quarter, nstate), BF16),
            leaving=pltpu.VMEM((count, quarter, nstate), BF16),
            staged=pltpu.VMEM((count, PLANE, quarter, nstate), BF16),
            s1=dma(count, PLANE), r1=dma(count, PLANE),
            s2=dma(count, PLANE), r2=dma(count, PLANE),
            zs=dma(count), zr=dma(count),
            s3=dma(count, PLANE), r3=dma(count, PLANE),
        )

    def relations(self):
        plane = [(self.p != j, (self.base + j, self.c)) for j in range(PLANE)]
        return plane + [
            (self.before, (self.s - self.step, self.c)),
            (self.after, (self.s + self.step, self.c)),
        ]

    def part(self, j):
        return pl.ds(pl.multiple_of(j * self.rows, 16), self.rows)

    def first(self, i, j, slot):
        device = (self.base + j, self.c)
        return [
            remote(
                self.state.at[i, self.part(j)], self.slots.at[i, slot],
                self.s1.at[i, j], self.r1.at[i, slot], device,
            ),
            remote(
                self.decay.at[i], self.rates.at[i, slot], self.s2.at[i, j], self.r2.at[i, slot],
                device,
            ),
        ]

    def z_copy(self, i):
        return remote(
            self.leaving.at[i], self.arriving.at[i], self.zs.at[i], self.zr.at[i],
            (self.s + self.step, self.c),
        )

    def last(self, i, j, quarter):
        return remote(
            self.staged.at[i, j], self.out.at[i, self.part(quarter)],
            self.s3.at[i, j], self.r3.at[i, quarter], (self.base + j, self.c),
        )

    def others(self, act):
        for j in range(PLANE):
            pl.when(self.p != j)(functools.partial(act, j))

    def start(self, i):
        def send(j):
            for copy in self.first(i, j, self.p):
                copy.start()

        self.others(send)
        self.slots[i, self.p] = self.state[i, self.part(self.p)]
        self.rates[i, self.p] = self.decay[i]

    def pieces(self):
        for n in range(self.rows // self.size):
            yield n, slice(n * self.size, (n + 1) * self.size)

    def rate(self, i, j, n):
        return self.rates[i, j, pl.ds(self.p * (self.rows // self.size) + n, 1)]

    def fold(self, i):
        def arrived(j):
            for copy in self.first(i, j, j):
                copy.wait_recv()

        self.others(arrived)
        for n, rows in self.pieces():
            held = self.slots[i, self.order[0], rows].astype(F32)
            rate = self.rate(i, self.order[0], n)
            for j in self.order[1:]:
                own = self.rate(i, j, n)
                held = own * held + self.slots[i, j, rows].astype(F32)
                rate = own * rate
            self.total[i, rows] = held
            self.through[i, n : n + 1] = rate

    def chain(self, i):
        @pl.when(self.before)
        def _():
            self.z_copy(i).wait_recv()

        @pl.when(jnp.logical_not(self.before))
        def _():
            self.arriving[i] = jnp.zeros(self.arriving.shape[1:], BF16)

        for n, rows in self.pieces():
            self.leaving[i, rows] = (
                self.total[i, rows]
                + self.through[i, n : n + 1] * self.arriving[i, rows].astype(F32)
            ).astype(BF16)
        pl.when(self.after)(self.z_copy(i).start)
        for n, rows in self.pieces():
            held = self.arriving[i, rows].astype(F32)
            for at, j in enumerate(self.order):
                self.staged[i, j, rows] = held.astype(BF16)
                if at < PLANE - 1:
                    held = self.rate(i, j, n) * held + self.slots[i, j, rows].astype(F32)
        self.others(lambda j: self.last(i, j, self.p).start())
        self.out[i, self.part(self.p)] = self.staged[i, self.p]

    def events(self, k):
        count = self.state.shape[0]
        pl.when((k >= 0) & (k < count))(lambda: self.start(k))
        pl.when((k >= 1) & (k <= count))(lambda: self.fold(k - 1))
        at = k - 1 - self.place
        pl.when((at >= 0) & (at < count))(lambda: self.chain(at))

    def arrived(self, i):
        self.others(lambda j: self.last(i, j, j).wait_recv())

    def finish(self):
        @pl.loop(0, self.state.shape[0])
        def _(i):
            def close(j):
                for copy in self.first(i, j, self.p):
                    copy.wait_send()
                self.last(i, j, self.p).wait_send()

            self.others(close)
            pl.when(self.after)(self.z_copy(i).wait_send)


class Reduce:
    def __init__(self, pieces, rows, refs):
        self.pieces, self.rows = pieces, rows
        (
            self.near, self.mid, self.above, self.below, self.mid_send, self.kept,
            self.s1, self.r1, self.s2, self.r2, self.sz, self.rz,
        ) = refs
        self.s, self.c, self.z, self.y, self.x = place()
        s, c = self.s, self.c
        self.up, self.down = self.z < LINE - 1, self.z > 0
        self.to_x, self.to_y = (s + 1 - 2 * self.x, c), (s + 2 - 4 * self.y, c)
        self.to_up, self.to_down = (s + PLANE, c), (s - PLANE, c)
        self.span = range(len(pieces))

    @staticmethod
    def scratch(n, rows, wide):
        return dict(
            near=pltpu.VMEM((LINE, 2 * rows, wide), BF16),
            mid=pltpu.VMEM((LINE, rows, wide), BF16),
            above=pltpu.VMEM((LINE, rows, wide), BF16),
            below=pltpu.VMEM((LINE, rows, wide), BF16),
            mid_send=pltpu.VMEM((LINE, rows, wide), BF16),
            kept=pltpu.VMEM((LINE, rows, wide), F32),
            t1=dma(n, LINE, 2), u1=dma(n, LINE, 2), t2=dma(n, LINE),
            u2=dma(n, LINE), tz=dma(n, LINE), uz=dma(n, 2, LINE),
        )

    def columns(self, p):
        return pl.ds(self.pieces[p][6], self.pieces[p][2])

    def source(self, p, index, count=1):
        ref, start, width = self.pieces[p][:3]
        begin = pl.multiple_of(index * self.rows, 16)
        return ref.at[pl.ds(begin, count * self.rows), pl.ds(start, width)]

    def index(self, zz, yy, xx):
        return zz * PLANE + yy * 2 + xx

    def near_copies(self, p, zz):
        if self.pieces[p][3]:
            return [
                remote(
                    self.source(p, self.index(zz, 1 - self.y, 0), 2),
                    self.near.at[zz, :, self.columns(p)],
                    self.s1.at[p, zz, 0], self.r1.at[p, zz, 0], self.to_y,
                )
            ]
        return [
            remote(
                self.source(p, self.index(zz, k, 1 - self.x)),
                self.near.at[zz, pl.ds(k * self.rows, self.rows), self.columns(p)],
                self.s1.at[p, zz, k], self.r1.at[p, zz, k], self.to_x,
            )
            for k in range(2)
        ]

    def mid_copy(self, p, zz):
        at = self.columns(p)
        return remote(
            self.mid_send.at[zz, :, at], self.mid.at[zz, :, at],
            self.s2.at[p, zz], self.r2.at[p, zz], self.to_x if self.pieces[p][3] else self.to_y,
        )

    def line_copy(self, p, zz, upward):
        at = self.columns(p)
        target = self.above if upward else self.below
        return remote(
            self.mid_send.at[zz, :, at], target.at[zz, :, at],
            self.sz.at[p, zz], self.rz.at[p, 0 if upward else 1, zz],
            self.to_up if upward else self.to_down,
        )

    def exists(self, off):
        zz = self.z + off
        return (zz >= 0) & (zz < LINE)

    def rows_of(self, k):
        return pl.ds(pl.multiple_of(k * self.rows, 16), self.rows)

    def begin(self, *pieces):
        for off in SUM_OFFSETS:

            @pl.when(self.exists(off))
            def _():
                for p in pieces or self.span:
                    for copy in self.near_copies(p, self.z + off):
                        copy.start()

    def second(self, *offs):
        for off in offs:

            @pl.when(self.exists(off))
            def _():
                zz = self.z + off
                y, x = self.y, self.x
                for p in self.span:
                    for copy in self.near_copies(p, zz):
                        copy.wait_recv()
                    own = self.index(zz, y, x)
                    if self.pieces[p][3]:
                        other, mine = self.index(zz, y, 1 - x), x
                    else:
                        other, mine = self.index(zz, 1 - y, x), y
                    at = self.columns(p)
                    sent = self.source(p, other)[...].astype(F32) + self.near[
                        zz, self.rows_of(1 - mine), at
                    ].astype(F32)
                    self.mid_send[zz, :, at] = sent.astype(BF16)
                    self.mid_copy(p, zz).start()
                    self.kept[zz, :, at] = self.source(p, own)[...].astype(F32) + self.near[
                        zz, self.rows_of(mine), at
                    ].astype(F32)

    def third(self, *offs, only=None):
        for off in offs:

            @pl.when(self.exists(off))
            def _():
                zz = self.z + off
                for p in self.span if only is None else only:
                    at = self.columns(p)
                    self.mid_copy(p, zz).wait_recv()
                    self.kept[zz, :, at] = self.kept[zz, :, at] + self.mid[zz, :, at].astype(F32)
                    if off >= 0:

                        @pl.when(self.down)
                        def _():
                            self.line_copy(p, zz, True).wait_recv()
                            self.kept[zz, :, at] = self.kept[zz, :, at] + self.above[
                                zz, :, at
                            ].astype(F32)

                    if off <= 0:

                        @pl.when(self.up)
                        def _():
                            self.line_copy(p, zz, False).wait_recv()
                            self.kept[zz, :, at] = self.kept[zz, :, at] + self.below[
                                zz, :, at
                            ].astype(F32)

                    if off == 0:
                        _, _, width, _, out, start, _ = self.pieces[p]
                        out[:, start : start + width] = self.kept[zz, :, at]
                    else:
                        self.mid_copy(p, zz).wait_send()
                        self.mid_send[zz, :, at] = self.kept[zz, :, at].astype(BF16)
                        self.line_copy(p, zz, off > 0).start()

    def finish(self):
        for off in SUM_OFFSETS:

            @pl.when(self.exists(off))
            def _():
                zz = self.z + off
                for p in self.span:
                    for copy in self.near_copies(p, zz):
                        copy.wait_send()
                    if off == 0:
                        self.mid_copy(p, zz).wait_send()
                    else:
                        self.line_copy(p, zz, off > 0).wait_send()


def picked(r, names):
    return tuple(r.__dict__[n] for n in names)


GATHER_REFS = tuple(Gather.semaphores(1))
SCAN_REFS = tuple(Scan.scratch(1, PLANE, 1, 1))
REDUCE_REFS = tuple(Reduce.scratch(1, 16, 1))


def main_body(sizes, total_inner, r):
    length, inner, nstate, size, taps = sizes
    channels = inner + 2 * nstate
    heads = inner // size
    count = r.tok.shape[0]
    half = r.tok.shape[2]
    s, c, z, y, x = place()
    to_core, to_prv = (s, 1 - c), (s - 1, c)
    nxt, prv = s < LINE * PLANE - 1, s > 0
    first_gather = Gather(
        ((r.w1, r.w, 0, 640, True), (r.w1, r.w, 640, r.w1.shape[1] - 640, False)),
        r.w1.shape[0],
        picked(r, GATHER_REFS),
    )
    second_gather = Gather(
        ((r.w2, r.w2_full, 0, inner, True), (r.w2, r.w2_full, inner, inner, False)),
        r.w2.shape[0],
        picked(r, SECOND_REFS),
    )
    prefix = Scan(False, size, r.state, r.dec, r.hin, picked(r, SCAN_REFS))
    suffix = Scan(True, size, r.prior, r.dec, r.later, picked(r, SUFFIX_REFS))
    reduce_ = Reduce(
        ((r.dout, 0, inner, True, r.g_out, 0, 0), (r.dgate, 0, inner, False, r.g_gate, 0, inner)),
        r.g_out.shape[0],
        picked(r, REDUCE_REFS),
    )
    spread = head_spread(inner, size)
    mine = pl.ds(pl.multiple_of(inner + c * nstate, LANES), nstate)
    side = pl.ds(pl.multiple_of(c * half, LANES), half)
    other_side = pl.ds(pl.multiple_of((1 - c) * half, LANES), half)
    log_at, step_at, pre_at, entry_at, tail_at = (
        slice(n * LANES, (n + 1) * LANES) for n in range(5)
    )
    own_at, slope_at, gpre_at = (
        slice(half + n * nstate, half + (n + 1) * nstate) for n in range(3)
    )
    left = lax.broadcasted_iota(jnp.int32, (length, LANES), 1) < size

    def swap(n, source, target):
        return lambda i: remote(
            source.at[i], target.at[i], r.ss.at[n, i], r.rs.at[n, i], to_core
        )

    swap_tokens = swap(0, r.tok, r.tok_in)
    swap_grads = swap(1, r.g, r.g_in)
    swap_sums = swap(2, r.sums, r.sums_in)
    swap_out = swap(3, r.osend, r.out_in)
    swap_states = swap(4, r.bsend, r.brecv)

    def send_edge(i):
        return remote(r.edge.at[i], r.edge_in.at[i], r.ss.at[5, i], r.rs.at[5, i], to_prv)

    def halo_copy(k):
        tails = r.tok.at[:, pl.ds(length - HALO, HALO), :]
        device = (s + 1, c if k == 0 else 1 - c)
        return remote(tails, r.halo.at[:, :, side], r.hs.at[k], r.hr.at[k], device)

    stores = dict(
        normed=lambda i: (r.normed_s.at[i, pl.ds(HALO, length)], r.normed.at[i]),
        xs=lambda i: (r.xs_s.at[i], r.xs.at[i]),
        ggate=lambda i: (r.ggate_s.at[i], r.ggate.at[i]),
        keep=lambda i: (r.gate.at[i, :, pl.ds(0, half)], r.keep.at[i]),
        gcx=lambda i: (r.gn.at[i], r.gcx.at[i]),
        gpre=lambda i: (r.gate.at[i, :, gpre_at], r.gpre.at[i]),
        gst=lambda i: (r.gate.at[i, :, own_at], r.gst.at[i]),
        w=lambda i: (r.w, r.w_out),
        w2=lambda i: (r.w2_full.at[:, pl.ds(0, inner)], r.w2_out),
    )

    def store(name, i):
        source, target = stores[name](i)
        n = tuple(stores).index(name)
        return pltpu.make_async_copy(source, target, r.store.at[n, i])

    def bias_row(at):
        return r.prm[BIAS : BIAS + 1, at]

    def conv(at):
        pre = r.prm[BIAS : BIAS + 1, at]
        for t in range(taps):
            start = HALO - taps + 1 + t
            pre = pre + r.prm[TAPS + t : TAPS + t + 1, at] * r.ext[start : start + length, at]
        return pre

    greet(
        prefix.relations()
        + [
            (True, to_core),
            (nxt, (s + 1, c)),
            (nxt, (s + 1, 1 - c)),
            (prv, (s - 1, c)),
            (prv, (s - 1, 1 - c)),
        ]
    )
    first_gather.begin()
    for k in range(2):
        pl.when(nxt)(halo_copy(k).start)
    for i in range(count):
        swap_tokens(i).start()
    r.small[...] = jnp.zeros_like(r.small)
    first_gather.z_arrived(-1, 1)
    first_gather.first_arrived(0)
    for i in range(count):
        swap_grads(i).start()

    @pl.loop(0, count)
    def _(i):
        swap_tokens(i).wait()
        own, other = r.tok[i].astype(F32), r.tok_in[i].astype(F32)
        scale = lax.rsqrt(
            jnp.mean(own * own + other * other, axis=-1, keepdims=True) * 0.5 + EPSILON
        )
        gain_own = r.prm[GAIN : GAIN + 1, side]
        gain_other = r.prm[GAIN : GAIN + 1, other_side]
        r.normed_s[i, HALO:, side] = (own * scale * gain_own).astype(BF16)
        r.normed_s[i, HALO:, other_side] = (other * scale * gain_other).astype(BF16)

    first_gather.z_arrived(-2, 2)
    first_gather.first_arrived(-1, 1)
    for k in range(2):
        pl.when(nxt)(halo_copy(k).wait_send)
        pl.when(prv)(halo_copy(k).wait_recv)

    @pl.when(prv)
    def _():
        for i in range(count):
            edge = r.halo[i].astype(F32)
            scale = lax.rsqrt(jnp.mean(edge * edge, axis=-1, keepdims=True) + EPSILON)
            r.normed_s[i, :HALO] = (
                edge * scale * r.prm[GAIN : GAIN + 1, : edge.shape[1]]
            ).astype(BF16)

    @pl.when(jnp.logical_not(prv))
    def _():
        for i in range(count):
            r.normed_s[i, :HALO] = jnp.zeros((HALO, 2 * half), BF16)

    first_gather.z_arrived(-3, 3)
    first_gather.first_arrived(-2, 2, -3, 3)
    second_gather.begin()
    first_gather.finish()
    store("w", 0).start()
    kept, ones = triangle(length)

    @pl.loop(0, count)
    def _(i):
        xs = dot(r.normed_s[i], r.w[:, :channels]).astype(BF16)
        r.xs_s[i] = xs
        r.ext[...] = xs.astype(F32)
        pre = conv(slice(0, channels))
        act = (pre * sigmoid(pre)).astype(BF16)
        r.act[i] = act
        step_pre = (
            dot(r.normed_s[i, HALO:], r.w[:, channels:])
            + r.prm[STEP_BIAS : STEP_BIAS + 1, :LANES]
        )
        step = softplus(step_pre)
        log_decay = running_sum(ones, step * r.prm[RATE : RATE + 1, :LANES])
        doc_col, doc_row = doc_numbers(r.doc[i], ones)
        entry = jnp.where(doc_col == 0.0, jnp.exp(log_decay), 0.0)
        last = log_decay[length - 1 :]
        tail = jnp.where(doc_col == doc_col[length - 1 :], jnp.exp(last - log_decay), 0.0)
        r.aux[i, :, log_at] = log_decay
        r.aux[i, :, step_at] = step
        r.aux[i, :, pre_at] = step_pre
        r.aux[i, :, entry_at] = entry
        r.aux[i, :, tail_at] = tail
        log_rows = log_decay.T
        whole_decay = jnp.where(
            doc_row[:, length - 1 :] == 0.0, jnp.exp(log_rows[:HEAD_ROWS, length - 1 :]), 0.0
        )
        r.dec[i] = jnp.broadcast_to(whole_decay, (HEAD_ROWS, LANES))
        inputs = act[:, :inner].astype(F32) * expand(step, spread)
        r.low[i] = inputs.astype(BF16)
        r.state[i] = dot(
            (inputs * expand(tail, spread)).astype(BF16), act[:, inner : inner + nstate], TN
        ).astype(BF16)
        prefix.events(i)
        store("normed", i).start()
        store("xs", i).start()

        @pl.when(i == 1)
        def _():
            second_gather.z_arrived(-1, 1)
            second_gather.first_arrived(0)

        @pl.when(i == 2)
        def _():
            second_gather.z_arrived(-2, 2)
            second_gather.first_arrived(-1, 1)

        @pl.when(i == 3)
        def _():
            second_gather.z_arrived(-3, 3)
            second_gather.first_arrived(-2, 2)

    @pl.loop(0, count)
    def _(i):
        log_decay = r.aux[i, :, log_at]
        log_rows = log_decay.T
        doc_col, doc_row = doc_numbers(r.doc[i], ones)
        closed = jnp.where(kept & (doc_col == doc_row), 0.0, MASKED)
        scores = dot(r.act[i, :, inner + nstate :], r.act[i, :, inner : inner + nstate], NT)
        for pair in range(inner // LANES):
            columns = slice(pair * LANES, (pair + 1) * LANES)
            part = r.low[i, :, columns]
            total = None
            for h in (2 * pair, 2 * pair + 1):
                decay = jnp.exp(log_decay[:, h : h + 1] - log_rows[h : h + 1] + closed)
                own = jnp.where(left if h % 2 == 0 else ~left, part, jnp.zeros_like(part))
                term = dot((scores * decay).astype(BF16), own)
                total = term if total is None else total + term
            r.full[i, :, columns] = total
        prefix.events(i + count)

        @pl.when(i == 0)
        def _():
            second_gather.first_arrived(-3, 3)

    second_gather.finish()
    store("w2", 0).start()
    for i in range(count):
        swap_grads(i).wait()

    @pl.loop(0, count)
    def _(i):
        r.gate[i] = dot(r.normed_s[i, HALO:], r.w2_full[:, :inner])
        r.gn[i] = dot(either(c, r.g[i], r.g_in[i]), r.w2_full[:, inner:])

    @pl.loop(0, count)
    def _(i):
        prefix.arrived(i)
        values = r.act[i, :, :inner].astype(F32)
        entry = expand(r.aux[i, :, entry_at], spread)
        scanned = r.full[i] + dot(r.act[i, :, inner + nstate :], r.hin[i], NT) * entry
        r.full[i] = scanned
        mixed = scanned + r.prm[SKIP : SKIP + 1, :inner] * values
        gate = r.gate[i]
        gated = mixed * (gate * sigmoid(gate))
        squares = jnp.sum(gated * gated, axis=-1, keepdims=True)
        cross = jnp.sum(
            r.gn[i] * r.prm[INNER_GAIN : INNER_GAIN + 1, :inner] * gated, axis=-1, keepdims=True
        )
        lane = lax.broadcasted_iota(jnp.int32, (length, LANES), 1)
        r.sums[i] = jnp.where(lane == 0, squares, jnp.where(lane == 1, cross, 0.0))
        swap_sums(i).start()

    prefix.finish()

    @pl.loop(0, count)
    def _(i):
        swap_sums(i).wait_recv()
        values = r.act[i, :, :inner].astype(F32)
        mixed = r.full[i] + r.prm[SKIP : SKIP + 1, :inner] * values
        gate = r.gate[i]
        sig = sigmoid(gate)
        swish = gate * sig
        gated = mixed * swish
        both = r.sums[i] + r.sums_in[i]
        inner_scale = lax.rsqrt(both[:, 0:1] / total_inner + EPSILON)
        gain = r.prm[INNER_GAIN : INNER_GAIN + 1, :inner]
        unit = gated * inner_scale
        r.normal[i] = (unit * gain).astype(BF16)
        grad_norm = r.gn[i]
        grad_inner = jnp.sum(grad_norm * unit, axis=0, keepdims=True)
        grad_gated = inner_scale * (grad_norm * gain) - unit * (
            inner_scale * inner_scale * (both[:, 1:2] / total_inner)
        )
        dy = grad_gated * swish
        r.dy[i] = dy.astype(BF16)
        r.ggate_s[i] = (
            grad_gated * mixed * (sig * (1.0 + gate * (1.0 - sig)))
        ).astype(BF16)
        entry = expand(r.aux[i, :, entry_at], spread)
        r.prior[i] = dot(
            (dy * entry).astype(BF16), r.act[i, :, inner + nstate :], TN
        ).astype(BF16)
        suffix.events(i)
        r.small[1:2, :inner] += grad_inner
        per_head = head_sums(
            jnp.broadcast_to(jnp.sum(dy * values, axis=0, keepdims=True), (8, inner)), spread
        )
        r.small[2:3, :LANES] += per_head[:1]
        store("ggate", i).start()

    @pl.loop(0, count)
    def _(i):
        r.ginputs[...] = dot(r.normal[i], r.w2_full[:, inner:], NT)
        r.gate[i, :, :half] = r.ginputs[:, side]
        r.osend[i] = r.ginputs[:, other_side].astype(BF16)
        swap_out(i).start()
        store("keep", i).start()
        suffix.events(i + count)

    def weights_gradient(source, target, values, rows):
        for n in range(inner // 256):
            at = slice(n * 256, (n + 1) * 256)
            total = None
            for i in range(count):
                term = dot(source(i), values[i, :, at], TN)
                total = term if total is None else total + term
            target[rows, at] = total.astype(BF16)

    weights_gradient(lambda i: r.g[i], r.dout, r.normal, side)
    weights_gradient(lambda i: r.g_in[i], r.dout, r.normal, other_side)
    reduce_.begin(0)
    weights_gradient(lambda i: r.normed_s[i, HALO:], r.dgate, r.ggate_s, slice(None))
    reduce_.begin(1)

    @pl.loop(0, count)
    def _(i):
        suffix.arrived(i)
        log_decay = r.aux[i, :, log_at]
        step = r.aux[i, :, step_at]
        entry = r.aux[i, :, entry_at]
        values = r.act[i, :, :inner].astype(F32)
        in_state = r.act[i, :, inner : inner + nstate]
        out_state = r.act[i, :, inner + nstate :]
        later = r.later[i]
        wide_dy = r.dy[i].astype(F32)
        step_wide = expand(step, spread)
        tail_wide = expand(r.aux[i, :, tail_at], spread)
        entry_wide = expand(entry, spread)
        upper, ones_upper = triangle(length, True)
        doc_col, doc_row = doc_numbers(r.doc[i], ones)
        closed = jnp.where(upper & (doc_col == doc_row), 0.0, MASKED)
        scores = dot(in_state, out_state, NT)
        log_rows = log_decay.T
        r.ginputs[...] = tail_wide * dot(in_state, later, NT)
        for pair in range(inner // LANES):
            columns = slice(pair * LANES, (pair + 1) * LANES)
            pair_dy = r.dy[i, :, columns]
            pair_in = r.low[i, :, columns]
            total = r.ginputs[:, columns]
            for h in (2 * pair, 2 * pair + 1):
                chosen = left if h % 2 == 0 else ~left
                own_dy = jnp.where(chosen, pair_dy, jnp.zeros_like(pair_dy))
                decay = jnp.exp(log_rows[h : h + 1] - log_decay[:, h : h + 1] + closed)
                total = total + dot((scores * decay).astype(BF16), own_dy)
                grad_decay = dot(pair_in, own_dy, NT) * decay
                if h == 0:
                    r.dcb[...] = grad_decay
                else:
                    r.dcb[...] += grad_decay
            r.ginputs[:, columns] = total
        grad_inputs = r.ginputs[...]
        grad_scores = r.dcb[...]
        inputs = values * step_wide
        grad_in = dot(grad_scores.astype(BF16), out_state) + dot(
            (inputs * tail_wide).astype(BF16), later
        )
        grad_out = dot(grad_scores.T.astype(BF16), in_state) + dot(
            (wide_dy * entry_wide).astype(BF16), r.hin[i]
        )
        is_first = c == 0
        r.gate[i, :, own_at] = jnp.where(is_first, grad_in, grad_out)
        r.bsend[i] = jnp.where(is_first, grad_out, grad_in).astype(BF16)
        swap_states(i).start()
        entry_last = jnp.broadcast_to(entry[length - 1 :], (8, LANES))
        later_wide = later.astype(F32)
        lane_ones = jnp.ones((8, nstate), BF16)

        def state_sums(other):
            pieces = split2(later_wide * other.astype(F32))
            return head_sums(sum(dot(lane_ones, piece, NT) for piece in pieces), spread)

        ending = (state_sums(r.state[i]) + entry_last * state_sums(r.hin[i]))[:1]
        grad_log = head_sums(wide_dy * r.full[i], spread) - head_sums(
            r.low[i].astype(F32) * grad_inputs, spread
        )
        grad_rate_step = running_sum(ones_upper, grad_log) + ending
        rate = r.prm[RATE : RATE + 1, :LANES]
        grad_step = head_sums(values * grad_inputs, spread) + rate * grad_rate_step
        lane = lax.broadcasted_iota(jnp.int32, (length, LANES), 1)
        gpre = jnp.where(lane < heads, grad_step * sigmoid(r.aux[i, :, pre_at]), 0.0)
        r.gate[i, :, gpre_at] = gpre
        store("gpre", i).start()
        grad_values = step_wide * grad_inputs + r.prm[SKIP : SKIP + 1, :inner] * wide_dy
        r.ext[...] = r.xs_s[i].astype(F32)
        px = conv(slice(0, inner))
        sig = sigmoid(px)
        gcx = grad_values * (sig * (1.0 + px * (1.0 - sig)))
        r.gn[i] = gcx
        store("gcx", i).start()
        r.edge[i, :, :inner] = gcx[:EDGE]
        ps = conv(mine)
        sig = sigmoid(ps)
        r.gate[i, :, slope_at] = sig * (1.0 + ps * (1.0 - sig))
        r.small[3:4, :LANES] += jnp.sum(gpre, axis=0, keepdims=True)
        r.small[4:5, :LANES] += rate * jnp.sum(step * grad_rate_step, axis=0, keepdims=True)

        def finish_states(n):
            swap_states(n).wait_recv()
            gst = (r.gate[n, :, own_at] + r.brecv[n].astype(F32)) * r.gate[n, :, slope_at]
            r.gate[n, :, own_at] = gst
            store("gst", n).start()
            r.edge[n, :, inner:] = gst[:EDGE]
            pl.when(prv)(send_edge(n).start)

        pl.when(i > 0)(lambda: finish_states(i - 1))

        @pl.when(i == 0)
        def _():
            reduce_.second(3, -3, 2, -2)

        @pl.when(i == 1)
        def _():
            reduce_.second(1, -1, 0)
            reduce_.third(3, -3)

        @pl.when(i == 2)
        def _():
            reduce_.third(2, -2)

        @pl.when(i == count - 1)
        def _():
            finish_states(i)
            reduce_.third(1, -1)

    reduce_.third(0)
    reduce_.finish()
    suffix.finish()

    @pl.loop(0, count)
    def _(i):
        swap_sums(i).wait_send()
        swap_out(i).wait()
        swap_states(i).wait_send()
        pl.when(prv)(send_edge(i).wait_send)
        pl.when(nxt)(send_edge(i).wait_recv)
        for name in stores:
            if name not in SINGLE:
                store(name, i).wait()

    for name in SINGLE:
        store(name, 0).wait()


SINGLE = tuple(dict(w=0, w2=0))
SECOND_REFS = tuple("s" + n for n in GATHER_REFS)
SHARED_REFS = tuple(dict(total=0, through=0, leaving=0, staged=0))
SUFFIX_REFS = tuple(n if n in SHARED_REFS else "s" + n for n in SCAN_REFS)


def main_call(sizes, total_inner, tok, g, doc, prm, w1, w2):
    length, inner, nstate, size, taps = sizes
    count, _, half = tok.shape
    model = 2 * half
    channels = inner + 2 * nstate
    rows = w1.shape[0]
    ins = dict(
        tok=(tok, INSIDE), g=(g, INSIDE), doc=(doc, INSIDE), prm=(prm, INSIDE),
        w1=(w1, ANYWHERE), w2=(w2, ANYWHERE),
    )
    outs = dict(
        normed=(shape((count, length, model), BF16), ANYWHERE),
        xs=(shape((count, HALO + length, channels), BF16), ANYWHERE),
        ggate=(shape((count, length, inner), BF16), ANYWHERE),
        keep=(shape((count, length, half), F32), ANYWHERE),
        gpre=(shape((count, length, LANES), F32), ANYWHERE),
        gcx=(shape((count, length, inner), F32), ANYWHERE),
        gst=(shape((count, length, nstate), F32), ANYWHERE),
        out_in=(shape((count, length, half), BF16), ANYWHERE),
        edge_in=(shape((count, EDGE, inner + nstate), F32), ANYWHERE),
        w_out=(shape((model, w1.shape[1]), BF16), ANYWHERE),
        w2_out=(shape((model, inner), BF16), ANYWHERE),
        tok_in=(shape(tok.shape, BF16), INSIDE),
        small=(shape((8, channels), F32), INSIDE),
        g_out=(shape((rows, inner), F32), INSIDE),
        g_gate=(shape((rows, inner), F32), INSIDE),
    )

    def vmem(*dims, dtype=F32):
        return pltpu.VMEM(dims, dtype)

    def low(*dims):
        return pltpu.VMEM(dims, BF16)

    scratch = dict(
        g_in=low(count, length, half),
        halo=low(count, HALO, model),
        w=low(model, w1.shape[1]),
        w2_full=low(model, 2 * inner),
        normed_s=low(count, HALO + length, model),
        xs_s=low(count, HALO + length, channels),
        act=low(count, length, channels),
        aux=vmem(count, length, 5 * LANES),
        low=low(count, length, inner),
        dec=vmem(count, HEAD_ROWS, LANES),
        state=low(count, inner, nstate),
        hin=low(count, inner, nstate),
        prior=low(count, inner, nstate),
        later=low(count, inner, nstate),
        full=vmem(count, length, inner),
        gate=vmem(count, length, inner),
        gn=vmem(count, length, inner),
        sums=vmem(count, length, LANES),
        sums_in=vmem(count, length, LANES),
        normal=low(count, length, inner),
        dy=low(count, length, inner),
        ggate_s=low(count, length, inner),
        osend=low(count, length, half),
        dout=low(model, inner),
        dgate=low(model, inner),
        ext=vmem(HALO + length, channels),
        ginputs=vmem(length, inner),
        dcb=vmem(length, length),
        bsend=low(count, length, nstate),
        brecv=low(count, length, nstate),
        edge=vmem(count, EDGE, inner + nstate),
        ss=dma(6, count),
        rs=dma(6, count),
        hs=dma(2),
        hr=dma(2),
        store=dma(9, count),
    )
    scan = Scan.scratch(count, inner, nstate, HEAD_ROWS)
    gather = Gather.semaphores(2)
    scratch.update(zip(SUFFIX_REFS, scan.values()))
    scratch.update(scan)
    scratch.update(gather)
    scratch.update(zip(SECOND_REFS, gather.values()))
    scratch.update(Reduce.scratch(2, rows, 2 * inner))
    return fused_call(
        functools.partial(main_body, sizes, total_inner), None, ins, outs, scratch, 1, "main"
    )


def back_body(sizes, r):
    length, inner, nstate, size, taps = sizes
    k = pl.program_id(0)
    s, c, z, y, x = place()
    to_core = (s, 1 - c)
    wide = inner + nstate + LANES
    reduce_ = Reduce(
        (
            (r.dx, 0, wide // 2, True, r.g_x, 0, 0),
            (r.dx, wide // 2, wide // 2, False, r.g_x, wide // 2, wide // 2),
        ),
        r.g_x.shape[0],
        picked(r, REDUCE_REFS),
    )
    lines = [(z != j, (s + (j - z) * PLANE, c)) for j in range(LINE)]

    def swap_part(i):
        return remote(r.part.at[i], r.part_in.at[i], r.ps.at[i], r.pr.at[i], to_core)

    def small_copy(src, dst, at, device):
        return remote(src, dst, r.qs.at[at], r.qr.at[at], device)

    core_copy = small_copy(r.bc, r.bc_in, 0, to_core)
    x_copy = small_copy(r.work.at[0], r.from_x, 1, reduce_.to_x)
    y_copy = small_copy(r.work.at[1], r.from_y, 2, reduce_.to_y)
    states_copy = small_copy(r.states_s.at[c], r.states_s.at[c], 7, to_core)

    def z_small(j, slot):
        return remote(
            r.work.at[2], r.from_z.at[slot], r.qs.at[3 + j], r.qr.at[3 + slot],
            (s + (j - z) * PLANE, c),
        )

    @pl.when(k == 0)
    def _():
        greet([(True, reduce_.to_x), (True, reduce_.to_y), (True, to_core)] + lines)

    @pl.when(k < 4)
    def _():
        last = s == lax.axis_size("seq") - 1
        mine = pl.ds(pl.multiple_of(inner + c * nstate, LANES), nstate)
        r.gext[:length, :inner] = r.gcx[0]
        r.gext[:length, inner:] = r.gst[0]
        r.gext[length:] = jnp.where(last, 0.0, r.edge_in[0])
        r.ext[:, :inner] = r.xs[0, :, :inner].astype(F32)
        r.ext[:, inner:] = r.xs[0, :, mine].astype(F32)
        grad_conv = r.gext[:length]
        grad_in = None
        rows = []
        for t in range(taps):
            row = jnp.concatenate(
                [r.prm[TAPS + t : TAPS + t + 1, :inner], r.prm[TAPS + t : TAPS + t + 1, mine]],
                axis=1,
            )
            term = row * r.gext[taps - 1 - t : taps - 1 - t + length]
            grad_in = term if grad_in is None else grad_in + term
            start = HALO - taps + 1 + t
            rows.append(
                jnp.sum(r.ext[start : start + length] * grad_conv, axis=0, keepdims=True)
            )
        rows.append(jnp.sum(grad_conv, axis=0, keepdims=True))
        rows.append(jnp.zeros((8 - taps - 1, inner + nstate), F32))
        rows = jnp.concatenate(rows, axis=0)
        low = grad_in.astype(BF16)
        low_pre = r.gpre[0].astype(BF16)
        part = dot(r.ggate[0], r.w2[:, :inner], NT)
        part = part + dot(low[:, :inner], r.w[:, :inner], NT)
        part = part + dot(low[:, inner:], r.w[:, mine], NT)
        part = part + dot(low_pre, r.w[:, inner + 2 * nstate :], NT)
        r.part[k] = part.astype(BF16)
        swap_part(k).start()
        stacked = jnp.concatenate([low, low_pre], axis=1)
        term = dot(r.normed[0], stacked, TN)

        @pl.when(k == 0)
        def _():
            r.conv_rows[...] = rows
            r.acc[...] = term

        @pl.when(k > 0)
        def _():
            r.conv_rows[...] += rows
            r.acc[...] += term

    @pl.when(k == 3)
    def _():
        r.dx[...] = r.acc[...].astype(BF16)
        reduce_.begin()
        own = r.conv_rows[:, inner:]
        r.bc[:, :nstate] = jnp.where(c == 0, own, 0.0)
        r.bc[:, nstate:] = jnp.where(c == 1, own, 0.0)
        core_copy.start()

    @pl.when(k >= 4)
    def _():
        i = k - 4
        swap_part(i).wait_recv()
        own_tok = r.tok[0].astype(F32)
        tok = either(c, own_tok, r.tok_in[0].astype(F32))
        model = tok.shape[1]
        scale = lax.rsqrt(jnp.mean(tok * tok, axis=-1, keepdims=True) + EPSILON)
        unit = tok * scale
        grad_normed = r.part[i].astype(F32) + r.part_in[i].astype(F32)
        grad = grad_normed * r.prm[GAIN : GAIN + 1, :model]
        r.wide[...] = scale * (grad - unit * jnp.mean(grad * unit, axis=-1, keepdims=True))
        half = model // 2
        r.tokens_grad[0] = (
            r.g[0].astype(F32) + r.wide[:, pl.ds(pl.multiple_of(c * half, LANES), half)]
        )
        r.mixed[0] = (own_tok + (r.keep[0] + r.out_in[0].astype(F32))).astype(BF16)
        gain = jnp.sum(grad_normed * unit, axis=0, keepdims=True)

        @pl.when(i == 0)
        def _():
            r.gain_row[...] = gain

        @pl.when(i > 0)
        def _():
            r.gain_row[...] += gain

    @pl.when(k == 4)
    def _():
        reduce_.second(3, -3, 2, -2)

    @pl.when(k == 5)
    def _():
        reduce_.second(1, -1, 0)
        reduce_.third(3, -3)

    @pl.when(k == 6)
    def _():
        reduce_.third(2, -2)

    @pl.when(k == 7)
    def _():
        core_copy.wait_recv()
        r.work[0] = jnp.zeros(r.work.shape[1:], F32)
        r.work[0, 0:8] = r.small[...]
        r.work[0, 0:1, :inner] = r.gain_row[...]
        r.work[0, 8:16, :inner] = r.conv_rows[:, :inner]
        r.work[0, 16:24, : 2 * nstate] = r.bc[...] + r.bc_in[...]
        x_copy.start()
        reduce_.third(1, -1)
        x_copy.wait_recv()
        r.work[1] = r.work[0] + r.from_x[...]
        y_copy.start()
        reduce_.third(0, only=(1,))
        r.states_s[c] = r.g_x[:, inner : inner + nstate]
        states_copy.start()
        y_copy.wait_recv()
        r.work[2] = r.work[1] + r.from_y[...]
        for j in range(LINE):
            pl.when(z != j)(z_small(j, z).start)
        r.from_z[z] = r.work[2]
        reduce_.third(0, only=(0,))
        for j in range(LINE):
            pl.when(z != j)(z_small(j, j).wait_recv)
        r.sums[...] = (r.from_z[0] + r.from_z[1]) + (r.from_z[2] + r.from_z[3])
        states_copy.wait()
        r.states[...] = r.states_s[...]
        core_copy.wait_send()
        x_copy.wait_send()
        y_copy.wait_send()
        for j in range(LINE):
            pl.when(z != j)(z_small(j, z).wait_send)
        reduce_.finish()

        @pl.loop(0, 4)
        def _(i):
            swap_part(i).wait_send()


def back_call(sizes, m, tok, g, prm):
    length, inner, nstate, size, taps = sizes
    count, _, half = g.shape
    model = 2 * half
    channels = inner + 2 * nstate
    rows = model // lax.axis_size("seq")
    wide = inner + nstate + LANES
    first, second = during(0), during(4)
    ins = dict(
        gcx=(m.gcx, stepped(m.gcx, first)),
        gst=(m.gst, stepped(m.gst, first)),
        gpre=(m.gpre, stepped(m.gpre, first)),
        ggate=(m.ggate, stepped(m.ggate, first)),
        edge_in=(m.edge_in, stepped(m.edge_in, first)),
        xs=(m.xs, stepped(m.xs, first)),
        normed=(m.normed, stepped(m.normed, first)),
        tok=(tok, stepped(tok, second)),
        tok_in=(m.tok_in, stepped(m.tok_in, second)),
        g=(g, stepped(g, second)),
        keep=(m.keep, stepped(m.keep, second)),
        out_in=(m.out_in, stepped(m.out_in, second)),
        small=(m.small, whole(m.small)),
        prm=(prm, whole(prm)),
        w=(m.w_out, whole(m.w_out)),
        w2=(m.w2_out, whole(m.w2_out)),
    )
    grads = shape((count, length, half), F32)
    mixed = shape((count, length, half), BF16)
    g_x = shape((rows, wide), F32)
    states = shape((2, rows, nstate), F32)
    sums = shape((24, channels), F32)
    outs = dict(
        tokens_grad=(grads, stepped(grads, second)),
        mixed=(mixed, stepped(mixed, second)),
        g_x=(g_x, whole(g_x)),
        sums=(sums, whole(sums)),
        states=(states, whole(states)),
    )
    scratch = dict(
        part=pltpu.VMEM((count, length, model), BF16),
        part_in=pltpu.VMEM((count, length, model), BF16),
        acc=pltpu.VMEM((model, wide), F32),
        dx=pltpu.VMEM((model, wide), BF16),
        conv_rows=pltpu.VMEM((8, inner + nstate), F32),
        gain_row=pltpu.VMEM((1, model), F32),
        ext=pltpu.VMEM((HALO + length, inner + nstate), F32),
        gext=pltpu.VMEM((length + EDGE, inner + nstate), F32),
        wide=pltpu.VMEM((length, model), F32),
        states_s=pltpu.VMEM((2, rows, nstate), F32),
        bc=pltpu.VMEM((8, 2 * nstate), F32),
        bc_in=pltpu.VMEM((8, 2 * nstate), F32),
        work=pltpu.VMEM((3, 24, channels), F32),
        from_x=pltpu.VMEM((24, channels), F32),
        from_y=pltpu.VMEM((24, channels), F32),
        from_z=pltpu.VMEM((LINE, 24, channels), F32),
        ps=dma(count), pr=dma(count), qs=dma(8), qr=dma(8),
    )
    scratch.update(Reduce.scratch(2, rows, wide))
    return fused_call(functools.partial(back_body, sizes), 8, ins, outs, scratch, 4, "back")


def fused_layer(sizes, total_inner, heads, tok, g, doc, prm, w, w2):
    length, inner, nstate, size, taps = sizes
    model = 2 * tok.shape[2]
    m = main_call(sizes, total_inner, tok, g, doc, prm, w, w2)
    b = back_call(sizes, m, tok, g, prm)
    sums = b.sums
    return (
        b.mixed,
        b.tokens_grad,
        sums[0, :model],
        jnp.stack([m.g_gate, b.g_x[:, :inner]], axis=1),
        jnp.concatenate([b.states[0], b.states[1]], axis=1),
        b.g_x[:, inner + nstate : inner + nstate + heads],
        sums[8 : 8 + taps, :inner],
        sums[8 + taps, :inner],
        sums[16 : 16 + taps, : 2 * nstate],
        sums[16 + taps, : 2 * nstate],
        sums[3, :heads],
        sums[4, :heads],
        sums[2, :heads],
        sums[1, :inner],
        m.g_out.T,
    )


def shards(
    tokens, doc_starts, norm_gain, input_gate_features, input_state_weight, input_step_weight,
    conv_taps_x, conv_bias_x, conv_taps_bc, conv_bias_bc, step_bias, decay_log, skip_gain,
    inner_gain, output_projection, out_grad,
):
    micro, seqs, length, half = tokens.shape
    count = micro * seqs
    model = 2 * half
    heads = step_bias.shape[0]
    inner = inner_gain.shape[0]
    size = inner // heads
    nstate = conv_taps_bc.shape[1] // 2
    taps = conv_taps_x.shape[0]
    channels = inner + 2 * nstate
    rows = input_gate_features.shape[0]
    total_inner = inner * lax.axis_size("head")
    sizes = (length, inner, nstate, size, taps)
    core = lax.axis_index("head")

    tok = tokens.reshape(count, length, half)
    g = out_grad.reshape(count, length, half)
    doc = jnp.broadcast_to(
        doc_starts.reshape(count, 1, length).astype(F32), (count, 8, length)
    )

    def row(v):
        return jnp.pad(v, (0, channels - v.shape[0]))[None]

    prm = jnp.concatenate(
        [
            row(norm_gain),
            row(inner_gain),
            row(jnp.repeat(skip_gain, size)),
            row(jnp.concatenate([conv_bias_x, conv_bias_bc])),
            row(step_bias),
            row(-jnp.exp(decay_log)),
            jnp.concatenate([conv_taps_x, conv_taps_bc], axis=1),
        ],
        axis=0,
    )
    prm = jnp.pad(prm, ((0, 16 - prm.shape[0]), (0, 0)))
    w_own = jnp.concatenate(
        [
            input_gate_features.reshape(rows, 2 * inner),
            input_state_weight,
            jnp.pad(input_step_weight, ((0, 0), (0, LANES - heads))),
        ],
        axis=1,
    )
    w_out_own = output_projection.T

    if lax.axis_size("seq") == PLANE * LINE and lax.axis_size("head") == 2:
        outputs = fused_layer(
            sizes, total_inner, heads, tok, g, doc, prm, w_own[:, inner:],
            jnp.concatenate([w_own[:, :inner], w_out_own], axis=1),
        )
        return tuple(
            o.reshape(tokens.shape) if n < 2 else o for n, o in enumerate(outputs)
        )

    w_in, w_out, tok_full, g_full, halo = plain_gather(
        w_own, w_out_own, tok, g, tok[:, length - HALO :]
    )
    grid = (count,)
    outs = [
        shape((count, length, model), BF16),
        shape((count, length, inner), F32),
        shape((count, HALO + length, channels), BF16),
        shape((count, length, channels), F32),
        shape((count, length, channels), BF16),
        shape((count, length, inner), F32),
        shape((count, inner, nstate), BF16),
        shape((count, length, 5 * LANES), F32),
        shape((count, HEAD_ROWS, LANES), F32),
    ]
    normed, gate, xs, pre, act, scan, state, aux, dec = call(
        functools.partial(forward_kernel, sizes),
        grid,
        [per_seq(tok_full), per_seq(halo), per_seq(doc), whole(prm), whole(w_in)],
        [per_seq(o) for o in outs],
        outs,
        [pltpu.VMEM((HALO + length, channels), F32)],
        name="forward",
    )(tok_full, halo, doc, prm, w_in)

    hin = plain_scan(state, dec, size, False)

    outs = [
        shape((count, length, inner), F32),
        shape((count, length, inner), F32),
        shape((count, length, LANES), F32),
    ]
    ins = (scan, act, aux, gate, hin, g_full)
    full, grad_norm, sums = call(
        functools.partial(gate_kernel, sizes),
        grid,
        [per_seq(a) for a in ins] + [whole(prm), whole(w_out)],
        [per_seq(o) for o in outs],
        outs,
        name="gate",
    )(*ins, prm, w_out)

    sums_in = swap_heads(sums)

    outs = [
        shape((count, length, half), F32),
        shape((count, length, half), BF16),
        shape((count, length, inner), BF16),
        shape((count, length, inner), BF16),
        shape((count, inner, nstate), BF16),
        shape((8, inner), F32),
        shape((model, inner), BF16),
        shape((model, inner), BF16),
    ]
    ins = (full, act, aux, gate, grad_norm, sums, sums_in, g_full, normed)
    keep, send, dy, ggate, prior, small_out, dout, dgate = call(
        functools.partial(output_kernel, sizes, total_inner),
        grid,
        [per_seq(a) for a in ins] + [whole(prm), whole(w_out)],
        [per_seq(o) for o in outs[:5]] + [whole(o) for o in outs[5:]],
        outs,
        [
            pltpu.VMEM((model, inner), F32),
            pltpu.VMEM((model, inner), F32),
            pltpu.VMEM((length, model), F32),
        ],
        name="output",
    )(*ins, prm, w_out)

    mixed = (tok.astype(F32) + (keep + swap_heads(send).astype(F32))).astype(BF16)
    later = plain_scan(prior, dec, size, True)

    outs = [
        shape((count, length, inner), F32),
        shape((count, length, nstate), F32),
        shape((count, length, nstate), BF16),
        shape((count, length, LANES), F32),
        shape((8, LANES), F32),
        shape((count, EDGE, inner), F32),
        shape((count, EDGE, nstate), F32),
    ]
    ins = (full, act, aux, dy, hin, later, state, doc, pre)
    gcx, own, other, gpre, small_scan, edge, slope = call(
        functools.partial(backward_kernel, sizes),
        grid,
        [per_seq(a) for a in ins] + [whole(prm)],
        [per_seq(o) if len(o.shape) == 3 else whole(o) for o in outs],
        outs,
        [pltpu.VMEM((length, length), F32)],
        name="backward",
    )(*ins, prm)

    recv, edge_in, edge_state = plain_states(other, own, slope, edge)

    outs = [
        shape((count, length, model), BF16),
        shape((model, inner + nstate + LANES), BF16),
        shape((8, inner + nstate), F32),
    ]
    ins = (gcx, own, recv, edge_in, edge_state, pre, xs, gpre, ggate, normed)
    part, dx, small_conv = call(
        functools.partial(conv_kernel, sizes),
        grid,
        [per_seq(a) for a in ins] + [whole(prm), whole(w_in)],
        [per_seq(outs[0]), whole(outs[1]), whole(outs[2])],
        outs,
        [
            pltpu.VMEM((model, inner + nstate + LANES), F32),
            pltpu.VMEM((HALO + length, inner + nstate), F32),
            pltpu.VMEM((length + EDGE, inner + nstate), F32),
        ],
        name="conv",
    )(*ins, prm, w_in)

    part_in = swap_heads(part)

    outs = [shape((count, length, half), F32), shape((8, model), F32)]
    ins = (tok_full, part, part_in, g)
    tokens_grad, small_norm = call(
        functools.partial(tokens_kernel, sizes),
        grid,
        [per_seq(a) for a in ins] + [whole(prm)],
        [per_seq(outs[0]), whole(outs[1])],
        outs,
        [pltpu.VMEM((length, model), F32)],
        name="tokens",
    )(*ins, prm)

    small = jnp.concatenate(
        [
            row(small_norm[0]),
            row(small_out[0]),
            row(small_out[1]),
            row(jnp.concatenate([small_scan[0], small_scan[1]])),
            jnp.pad(small_conv[: taps + 1, :inner], ((0, 0), (0, channels - inner))),
            jnp.zeros((16 - 5 - taps, channels), F32),
        ],
        axis=0,
    )
    own_states = small_conv[:, inner:]
    shared = jnp.concatenate(
        [jnp.where(core == 0, own_states, 0.0), jnp.where(core == 1, own_states, 0.0)], axis=1
    )
    (g_out, g_gate, g_x), small, shared = plain_sum((dout, dgate, dx), small, shared)
    g_states = plain_both(g_x[:, inner : inner + nstate])
    return (
        mixed.reshape(tokens.shape),
        tokens_grad.reshape(tokens.shape),
        small[0, :model],
        jnp.stack([g_gate, g_x[:, :inner]], axis=1),
        g_states,
        g_x[:, inner + nstate : inner + nstate + heads],
        small[4 : 4 + taps, :inner],
        small[4 + taps, :inner],
        shared[:taps],
        shared[taps],
        small[3, :heads],
        small[3, LANES : LANES + heads],
        small[2, :inner].reshape(heads, size).sum(axis=1),
        small[1, :inner],
        g_out.T,
    )


def solution(mesh):
    placed = (
        P(None, None, "seq", "head"),
        P(None, None, "seq"),
        P(),
        P("seq", None, "head"),
        P("seq", None),
        P("seq", "head"),
        P(None, "head"),
        P("head"),
        P(),
        P(),
        P("head"),
        P("head"),
        P("head"),
        P("head"),
        P("head", "seq"),
        P(None, None, "seq", "head"),
    )
    return jax.shard_map(
        shards,
        mesh=mesh,
        in_specs=placed,
        out_specs=(
            P(None, None, "seq", "head"),
            P(None, None, "seq", "head"),
            P(),
            P("seq", None, "head"),
            P("seq", None),
            P("seq", "head"),
            P(None, "head"),
            P("head"),
            P(),
            P(),
            P("head"),
            P("head"),
            P("head"),
            P("head"),
            P("head", "seq"),
        ),
        check_vma=False,
    )
```

```python
import functools

import jax
import jax.numpy as jnp
from jax import lax
from jax.experimental import pallas as pl
from jax.experimental.pallas import tpu as pltpu
from jax.sharding import PartitionSpec as P

F32 = jnp.float32
BF16 = jnp.bfloat16
EPSILON = 1e-05
MASKED = -1e30
HALO = 16
EDGE = 8
HEAD_ROWS = 16
LANES = 128
MESH = pl.DeviceIdType.MESH
NN = ((1,), (0,))
NT = ((1,), (1,))
TN = ((0,), (0,))
VMEM_LIMIT = 62 * 2**20

GAIN, INNER_GAIN, SKIP, BIAS, STEP_BIAS, RATE, TAPS = 0, 1, 2, 3, 4, 5, 6


def dot(a, b, dims=NN):
    return lax.dot_general(a, b, (dims, ((), ())), preferred_element_type=F32)


def split2(v):
    high = v.astype(BF16)
    return high, (v - high.astype(F32)).astype(BF16)


def split3(v):
    high = v.astype(BF16)
    rest = v - high.astype(F32)
    middle = rest.astype(BF16)
    return high, middle, (rest - middle.astype(F32)).astype(BF16)


def sigmoid(v):
    return 1.0 / (1.0 + jnp.exp(-v))


def softplus(v):
    return jnp.maximum(v, 0.0) + jnp.log1p(jnp.exp(-jnp.abs(v)))


def head_spread(inner, size):
    rows = lax.broadcasted_iota(jnp.int32, (LANES, inner), 0)
    columns = lax.broadcasted_iota(jnp.int32, (LANES, inner), 1)
    return jnp.where(rows == columns // size, 1.0, 0.0).astype(BF16)


def expand(per_head, spread):
    high, low = split2(per_head)
    return dot(high, spread) + dot(low, spread)


def head_sums(wide, spread):
    high, low = split2(wide)
    return dot(high, spread, NT) + dot(low, spread, NT)


def triangle(length, upper=False):
    rows = lax.broadcasted_iota(jnp.int32, (length, length), 0)
    columns = lax.broadcasted_iota(jnp.int32, (length, length), 1)
    kept = rows <= columns if upper else rows >= columns
    return kept, jnp.where(kept, 1.0, 0.0).astype(BF16)


def running_sum(ones, v):
    a, b, c = split3(v)
    return dot(ones, a) + dot(ones, b) + dot(ones, c)


def doc_numbers(doc, ones):
    flags = doc.astype(BF16)
    return dot(ones, flags, NT)[:, :1], dot(flags, ones, NT)[:1]


def call(kernel, grid, in_specs, out_specs, out_shape, scratch=(), name=None, flops=10**9):
    return pl.pallas_call(
        kernel,
        grid=grid,
        in_specs=in_specs,
        out_specs=out_specs,
        out_shape=out_shape,
        scratch_shapes=list(scratch),
        compiler_params=pltpu.CompilerParams(
            vmem_limit_bytes=VMEM_LIMIT, dimension_semantics=("arbitrary",) * len(grid)
        ),
        cost_estimate=pl.CostEstimate(flops=flops, bytes_accessed=10**7, transcendentals=0),
        name=name,
    )


def whole(array):
    rank = len(array.shape)
    return pl.BlockSpec(array.shape, lambda i: (0,) * rank)


def per_seq(array):
    rank = len(array.shape)
    return pl.BlockSpec((1,) + tuple(array.shape[1:]), lambda i: (i,) + (0,) * (rank - 1))


def shape(dims, dtype):
    return jax.ShapeDtypeStruct(tuple(dims), dtype)


def forward_kernel(
    sizes, tok, halo, doc, prm, w, normed_o, gate_o, xs_o, pre_o, act_o, scan_o, state_o, aux_o,
    dec_o, ext,
):
    length, inner, nstate, size, taps = sizes
    channels = inner + 2 * nstate
    first = lax.axis_index("seq") == 0
    edge = jnp.where(first, 0.0, halo[0].astype(F32))
    x = jnp.concatenate([edge, tok[0].astype(F32)], axis=0)
    scale = lax.rsqrt(jnp.mean(x * x, axis=-1, keepdims=True) + EPSILON)
    normed = (x * scale * prm[GAIN : GAIN + 1, : x.shape[1]]).astype(BF16)
    normed_o[0] = normed[HALO:]
    gate_o[0] = dot(normed[HALO:], w[:, :inner])
    xs = dot(normed, w[:, inner : inner + channels]).astype(BF16)
    xs_o[0] = xs
    ext[...] = xs.astype(F32)
    pre = prm[BIAS : BIAS + 1, :channels]
    for k in range(taps):
        start = HALO - taps + 1 + k
        pre = pre + prm[TAPS + k : TAPS + k + 1, :channels] * ext[start : start + length]
    pre_o[0] = pre
    act = (pre * sigmoid(pre)).astype(BF16)
    act_o[0] = act
    step_pre = (
        dot(normed[HALO:], w[:, inner + channels :]) + prm[STEP_BIAS : STEP_BIAS + 1, :LANES]
    )
    step = softplus(step_pre)
    kept, ones = triangle(length)
    log_decay = running_sum(ones, step * prm[RATE : RATE + 1, :LANES])
    doc_col, doc_row = doc_numbers(doc[0], ones)
    entry = jnp.where(doc_col == 0.0, jnp.exp(log_decay), 0.0)
    last = log_decay[length - 1 :]
    tail = jnp.where(doc_col == doc_col[length - 1 :], jnp.exp(last - log_decay), 0.0)
    aux_o[0, :, 0:LANES] = log_decay
    aux_o[0, :, LANES : 2 * LANES] = step
    aux_o[0, :, 2 * LANES : 3 * LANES] = step_pre
    aux_o[0, :, 3 * LANES : 4 * LANES] = entry
    aux_o[0, :, 4 * LANES :] = tail
    spread = head_spread(inner, size)
    values = act[:, :inner].astype(F32)
    inputs = values * expand(step, spread)
    low_inputs = inputs.astype(BF16)
    in_state = act[:, inner : inner + nstate]
    out_state = act[:, inner + nstate :]
    state_o[0] = dot((inputs * expand(tail, spread)).astype(BF16), in_state, TN).astype(BF16)
    scores = dot(out_state, in_state, NT)
    closed = jnp.where(kept & (doc_col == doc_row), 0.0, MASKED)
    log_rows = log_decay.T
    whole_decay = jnp.where(doc_row[:, length - 1 :] == 0.0, jnp.exp(log_rows[:HEAD_ROWS, length - 1 :]), 0.0)
    dec_o[0] = jnp.broadcast_to(whole_decay, (HEAD_ROWS, LANES))
    left = lax.broadcasted_iota(jnp.int32, (length, LANES), 1) < size
    for pair in range(inner // LANES):
        columns = slice(pair * LANES, (pair + 1) * LANES)
        part = low_inputs[:, columns]
        total = None
        for side in range(2):
            h = 2 * pair + side
            decay = jnp.exp(log_decay[:, h : h + 1] - log_rows[h : h + 1] + closed)
            own = jnp.where(left if side == 0 else ~left, part, jnp.zeros_like(part))
            term = dot((scores * decay).astype(BF16), own)
            total = term if total is None else total + term
        scan_o[0, :, columns] = total


def gate_kernel(sizes, scan, act, aux, gate, hin, g, prm, wout, full_o, gn_o, sums_o):
    length, inner, nstate, size, taps = sizes
    spread = head_spread(inner, size)
    values = act[0, :, :inner].astype(F32)
    out_state = act[0, :, inner + nstate :]
    scanned = scan[0] + dot(out_state, hin[0], NT) * expand(aux[0, :, 3 * LANES : 4 * LANES], spread)
    full_o[0] = scanned
    mixed = scanned + prm[SKIP : SKIP + 1, :inner] * values
    gated = mixed * (gate[0] * sigmoid(gate[0]))
    grad_norm = dot(g[0], wout[...])
    gn_o[0] = grad_norm
    squares = jnp.sum(gated * gated, axis=-1, keepdims=True)
    cross = jnp.sum(
        grad_norm * prm[INNER_GAIN : INNER_GAIN + 1, :inner] * gated, axis=-1, keepdims=True
    )
    lane = lax.broadcasted_iota(jnp.int32, (length, LANES), 1)
    sums_o[0] = jnp.where(lane == 0, squares, jnp.where(lane == 1, cross, 0.0))


def output_kernel(
    sizes, total_inner, full, act, aux, gate, gn, sums, sums_in, g, normed, prm, wout,
    keep_o, send_o, dy_o, ggate_o, prior_o, small_o, dout_o, dgate_o, acc_out, acc_gate, wide,
):
    length, inner, nstate, size, taps = sizes
    at = pl.program_id(0)
    spread = head_spread(inner, size)
    values = act[0, :, :inner].astype(F32)
    out_state = act[0, :, inner + nstate :]
    mixed = full[0] + prm[SKIP : SKIP + 1, :inner] * values
    z = gate[0]
    sig = sigmoid(z)
    swish = z * sig
    gated = mixed * swish
    both = sums[0] + sums_in[0]
    inner_scale = lax.rsqrt(both[:, 0:1] / total_inner + EPSILON)
    gain = prm[INNER_GAIN : INNER_GAIN + 1, :inner]
    unit = gated * inner_scale
    normal = (unit * gain).astype(BF16)
    wide[...] = dot(normal, wout[...], NT)
    half = wide.shape[1] // 2
    core = lax.axis_index("head")
    keep_o[0] = wide[:, pl.ds(pl.multiple_of(core * half, LANES), half)]
    send_o[0] = wide[:, pl.ds(pl.multiple_of((1 - core) * half, LANES), half)].astype(BF16)
    grad_norm = gn[0]
    grad_inner = jnp.sum(grad_norm * unit, axis=0, keepdims=True)
    grad_gated = inner_scale * (grad_norm * gain) - unit * (
        inner_scale * inner_scale * (both[:, 1:2] / total_inner)
    )
    dy = grad_gated * swish
    low_dy = dy.astype(BF16)
    dy_o[0] = low_dy
    ggate = (grad_gated * mixed * (sig * (1.0 + z * (1.0 - sig)))).astype(BF16)
    ggate_o[0] = ggate
    grad_skip = jnp.sum(dy * values, axis=0, keepdims=True)
    entry = expand(aux[0, :, 3 * LANES : 4 * LANES], spread)
    prior_o[0] = dot((dy * entry).astype(BF16), out_state, TN).astype(BF16)
    rows = jnp.concatenate([grad_inner, grad_skip, jnp.zeros((6, inner), F32)], axis=0)
    term_out = dot(g[0], normal, TN)
    term_gate = dot(normed[0], ggate, TN)

    @pl.when(at == 0)
    def _():
        small_o[...] = rows
        acc_out[...] = term_out
        acc_gate[...] = term_gate

    @pl.when(at > 0)
    def _():
        small_o[...] += rows
        acc_out[...] += term_out
        acc_gate[...] += term_gate

    @pl.when(at == pl.num_programs(0) - 1)
    def _():
        dout_o[...] = acc_out[...].astype(BF16)
        dgate_o[...] = acc_gate[...].astype(BF16)


def backward_kernel(
    sizes, full, act, aux, dy, hin, later, state, doc, pre, prm,
    gcx_o, own_o, send_o, gpre_o, small_o, edge_o, slope_o, dcb,
):
    length, inner, nstate, size, taps = sizes
    at = pl.program_id(0)
    core = lax.axis_index("head")
    spread = head_spread(inner, size)
    log_decay = aux[0, :, 0:LANES]
    step = aux[0, :, LANES : 2 * LANES]
    step_pre = aux[0, :, 2 * LANES : 3 * LANES]
    entry = aux[0, :, 3 * LANES : 4 * LANES]
    tail = aux[0, :, 4 * LANES :]
    values = act[0, :, :inner].astype(F32)
    in_state = act[0, :, inner : inner + nstate]
    out_state = act[0, :, inner + nstate :]
    low_dy = dy[0]
    wide_dy = low_dy.astype(F32)
    step_wide = expand(step, spread)
    tail_wide = expand(tail, spread)
    entry_wide = expand(entry, spread)
    inputs = values * step_wide
    low_inputs = inputs.astype(BF16)
    kept, ones = triangle(length)
    upper, ones_upper = triangle(length, True)
    doc_col, doc_row = doc_numbers(doc[0], ones)
    closed = jnp.where(upper & (doc_col == doc_row), 0.0, MASKED)
    scores = dot(in_state, out_state, NT)
    log_rows = log_decay.T
    left = lax.broadcasted_iota(jnp.int32, (length, LANES), 1) < size
    grad_inputs = tail_wide * dot(in_state, later[0], NT)
    parts = []
    for pair in range(inner // LANES):
        columns = slice(pair * LANES, (pair + 1) * LANES)
        pair_dy = low_dy[:, columns]
        pair_in = low_inputs[:, columns]
        total = grad_inputs[:, columns]
        for side in range(2):
            h = 2 * pair + side
            chosen = left if side == 0 else ~left
            own_dy = jnp.where(chosen, pair_dy, jnp.zeros_like(pair_dy))
            decay = jnp.exp(log_rows[h : h + 1] - log_decay[:, h : h + 1] + closed)
            total = total + dot((scores * decay).astype(BF16), own_dy)
            grad_decay = dot(pair_in, own_dy, NT) * decay
            if h == 0:
                dcb[...] = grad_decay
            else:
                dcb[...] += grad_decay
        parts.append(total)
    grad_inputs = jnp.concatenate(parts, axis=1)
    grad_scores = dcb[...]
    grad_in = dot(grad_scores.astype(BF16), out_state) + dot(
        (inputs * tail_wide).astype(BF16), later[0]
    )
    grad_out = dot(grad_scores.T.astype(BF16), in_state) + dot(
        (wide_dy * entry_wide).astype(BF16), hin[0]
    )
    entry_last = jnp.broadcast_to(entry[length - 1 :], (8, LANES))
    later_wide = later[0].astype(F32)
    lane_ones = jnp.ones((8, nstate), BF16)
    through = head_sums(
        sum(dot(lane_ones, piece, NT) for piece in split2(later_wide * hin[0].astype(F32))), spread
    )
    born = head_sums(
        sum(dot(lane_ones, piece, NT) for piece in split2(later_wide * state[0].astype(F32))), spread
    )
    ending = (born + entry_last * through)[:1]
    grad_log = head_sums(wide_dy * full[0], spread) - head_sums(
        low_inputs.astype(F32) * grad_inputs, spread
    )
    grad_rate_step = running_sum(ones_upper, grad_log) + ending
    rate = prm[RATE : RATE + 1, :LANES]
    grad_step = head_sums(values * grad_inputs, spread) + rate * grad_rate_step
    gpre = grad_step * sigmoid(step_pre)
    lane = lax.broadcasted_iota(jnp.int32, (length, LANES), 1)
    gpre = jnp.where(lane < inner // size, gpre, 0.0)
    gpre_o[0] = gpre
    grad_values = step_wide * grad_inputs + prm[SKIP : SKIP + 1, :inner] * wide_dy
    px = pre[0, :, :inner]
    sig = sigmoid(px)
    gcx = grad_values * (sig * (1.0 + px * (1.0 - sig)))
    gcx_o[0] = gcx
    edge_o[0] = gcx[:EDGE]
    is_first = core == 0
    own_o[0] = jnp.where(is_first, grad_in, grad_out)
    send_o[0] = jnp.where(is_first, grad_out, grad_in).astype(BF16)
    ps = pre[0, :EDGE, pl.ds(pl.multiple_of(inner + core * nstate, LANES), nstate)]
    sig = sigmoid(ps)
    slope_o[0] = sig * (1.0 + ps * (1.0 - sig))
    rows = jnp.concatenate(
        [
            jnp.sum(gpre, axis=0, keepdims=True),
            rate * jnp.sum(step * grad_rate_step, axis=0, keepdims=True),
            jnp.zeros((6, LANES), F32),
        ],
        axis=0,
    )

    @pl.when(at == 0)
    def _():
        small_o[...] = rows

    @pl.when(at > 0)
    def _():
        small_o[...] += rows


def conv_kernel(
    sizes, gcx, own, recv, edge, edge_state, pre, xs, gpre, ggate, normed, prm, w,
    part_o, dx_o, small_o, acc, ext, gext,
):
    length, inner, nstate, size, taps = sizes
    at = pl.program_id(0)
    core = lax.axis_index("head")
    last = lax.axis_index("seq") == lax.axis_size("seq") - 1
    mine = pl.ds(pl.multiple_of(inner + core * nstate, LANES), nstate)
    channels = inner + nstate
    ps = pre[0, :, mine]
    sig = sigmoid(ps)
    gst = (own[0] + recv[0].astype(F32)) * (sig * (1.0 + ps * (1.0 - sig)))
    gext[:length, :inner] = gcx[0]
    gext[:length, inner:] = gst
    gext[length:, :inner] = jnp.where(last, 0.0, edge[0])
    gext[length:, inner:] = jnp.where(last, 0.0, edge_state[0])
    ext[:, :inner] = xs[0, :, :inner].astype(F32)
    ext[:, inner:] = xs[0, :, mine].astype(F32)
    grad_conv = gext[:length]
    grad_in = None
    rows = []
    for k in range(taps):
        row = jnp.concatenate(
            [prm[TAPS + k : TAPS + k + 1, :inner], prm[TAPS + k : TAPS + k + 1, mine]], axis=1
        )
        term = row * gext[taps - 1 - k : taps - 1 - k + length]
        grad_in = term if grad_in is None else grad_in + term
        start = HALO - taps + 1 + k
        rows.append(jnp.sum(ext[start : start + length] * grad_conv, axis=0, keepdims=True))
    rows.append(jnp.sum(grad_conv, axis=0, keepdims=True))
    rows.append(jnp.zeros((8 - taps - 1, channels), F32))
    rows = jnp.concatenate(rows, axis=0)
    low = grad_in.astype(BF16)
    low_pre = gpre[0].astype(BF16)
    part = dot(ggate[0], w[:, :inner], NT)
    part = part + dot(low[:, :inner], w[:, inner : 2 * inner], NT)
    wst = w[:, pl.ds(pl.multiple_of(2 * inner + core * nstate, LANES), nstate)]
    part = part + dot(low[:, inner:], wst, NT)
    part = part + dot(low_pre, w[:, 2 * inner + 2 * nstate :], NT)
    part_o[0] = part.astype(BF16)
    stacked = jnp.concatenate([low, low_pre], axis=1)
    term = dot(normed[0], stacked, TN)

    @pl.when(at == 0)
    def _():
        small_o[...] = rows
        acc[...] = term

    @pl.when(at > 0)
    def _():
        small_o[...] += rows
        acc[...] += term

    @pl.when(at == pl.num_programs(0) - 1)
    def _():
        dx_o[...] = acc[...].astype(BF16)


def tokens_kernel(sizes, tok, part, recv, g, prm, out_o, small_o, wide):
    at = pl.program_id(0)
    core = lax.axis_index("head")
    x = tok[0].astype(F32)
    model = x.shape[1]
    scale = lax.rsqrt(jnp.mean(x * x, axis=-1, keepdims=True) + EPSILON)
    unit = x * scale
    grad_normed = part[0].astype(F32) + recv[0].astype(F32)
    r = grad_normed * prm[GAIN : GAIN + 1, :model]
    wide[...] = scale * (r - unit * jnp.mean(r * unit, axis=-1, keepdims=True))
    half = model // 2
    out_o[0] = g[0].astype(F32) + wide[:, pl.ds(pl.multiple_of(core * half, LANES), half)]
    rows = jnp.concatenate(
        [jnp.sum(grad_normed * unit, axis=0, keepdims=True), jnp.zeros((7, model), F32)], axis=0
    )

    @pl.when(at == 0)
    def _():
        small_o[...] = rows

    @pl.when(at > 0)
    def _():
        small_o[...] += rows


def swap_heads(v):
    return lax.ppermute(v, "head", [(0, 1), (1, 0)])


def shift(v, distance):
    devices = range(lax.axis_size("seq"))
    return lax.ppermute(
        v, "seq", [(i - distance, i) for i in devices if i - distance in devices]
    )


def plain_gather(w_in, w_out, tokens, grads, tails):
    return (
        lax.all_gather(w_in, "seq", axis=0, tiled=True),
        lax.all_gather(w_out, "seq", axis=0, tiled=True),
        lax.all_gather(tokens, "head", axis=2, tiled=True),
        lax.all_gather(grads, "head", axis=2, tiled=True),
        lax.all_gather(shift(tails, 1), "head", axis=2, tiled=True),
    )


def plain_scan(state, decay, size, backward):
    count, place = lax.axis_size("seq"), lax.axis_index("seq")
    heads = state.shape[1] // size
    wide = jnp.repeat(decay[:, :heads, 0], size, axis=1)[..., None]
    states = lax.all_gather(state, "seq")
    decays = lax.all_gather(wide, "seq")

    def one(k, carried):
        at = count - 1 - k if backward else k
        reached = at > place if backward else at < place
        return jnp.where(reached, decays[at] * carried + states[at].astype(F32), carried)

    return lax.fori_loop(0, count, one, jnp.zeros(state.shape, F32)).astype(BF16)


def plain_states(send, own, slope, edge):
    recv = swap_heads(send)
    mine = (own[:, :EDGE] + recv[:, :EDGE].astype(F32)) * slope
    return recv, shift(edge, -1), shift(mine, -1)


def plain_sum(pieces, small, shared):
    totals = [
        lax.psum_scatter(p.astype(F32), "seq", scatter_dimension=0, tiled=True) for p in pieces
    ]
    shared = lax.psum(shared, ("seq", "head"))
    return totals, lax.psum(small, "seq"), shared


def plain_both(v):
    return lax.all_gather(v, "head", axis=1, tiled=True)


PLANE = 4
LINE = 4
OFFSETS = (0, -1, 1, -2, 2, -3, 3)


def place():
    s, c = lax.axis_index("seq"), lax.axis_index("head")
    return s, c, s // PLANE, (s // 2) % 2, s % 2


def remote(src, dst, send_sem, recv_sem, device):
    return pltpu.make_async_remote_copy(
        src_ref=src,
        dst_ref=dst,
        send_sem=send_sem,
        recv_sem=recv_sem,
        device_id=device,
        device_id_type=MESH,
    )


def greet(relations):
    barrier = pltpu.get_barrier_semaphore()
    total = 0
    for exists, device in relations:
        if exists is True:
            pl.semaphore_signal(barrier, inc=1, device_id=device, device_id_type=MESH)
            total = total + 1
        else:
            pl.when(exists)(
                functools.partial(
                    pl.semaphore_signal, barrier, inc=1, device_id=device, device_id_type=MESH
                )
            )
            total = total + jnp.where(exists, 1, 0)
    pl.semaphore_wait(barrier, total)


def comm_call(kernel, ins, outs, scratch, collective, name, anywhere=False):
    space = pl.ANY if anywhere else pltpu.VMEM
    return pl.pallas_call(
        kernel,
        in_specs=[pl.BlockSpec(memory_space=space) for _ in ins],
        out_specs=[pl.BlockSpec(memory_space=space) for _ in outs],
        out_shape=outs,
        scratch_shapes=list(scratch),
        compiler_params=pltpu.CompilerParams(
            collective_id=collective, has_side_effects=True, vmem_limit_bytes=VMEM_LIMIT
        ),
        name=name,
    )(*ins)


def dma(*dims):
    return pltpu.SemaphoreType.DMA(dims)


SUM_OFFSETS = (3, -3, 2, -2, 1, -1, 0)


class Refs:
    def __init__(self, names, refs):
        self.__dict__.update(zip(names, refs))


def fused_call(body, steps, ins, outs, scratch, collective, name):
    names = list(ins) + list(outs) + list(scratch)

    def kernel(*refs):
        body(Refs(names, refs))

    results = pl.pallas_call(
        kernel,
        grid=(steps,) if steps else (),
        in_specs=[spec for _, spec in ins.values()],
        out_specs=[spec for _, spec in outs.values()],
        out_shape=[shaped for shaped, _ in outs.values()],
        scratch_shapes=list(scratch.values()),
        compiler_params=pltpu.CompilerParams(
            collective_id=collective,
            has_side_effects=True,
            vmem_limit_bytes=VMEM_LIMIT,
            dimension_semantics=("arbitrary",) if steps else None,
        ),
        name=name,
    )(*[array for array, _ in ins.values()])
    return Refs(list(outs), results)


ANYWHERE = pl.BlockSpec(memory_space=pl.ANY)
INSIDE = pl.BlockSpec(memory_space=pltpu.VMEM)


def stepped(array, index):
    rank = len(array.shape)
    return pl.BlockSpec((1,) + tuple(array.shape[1:]), lambda k: (index(k),) + (0,) * (rank - 1))


def during(first, count=4):
    return lambda k: jnp.clip(k - first, 0, count - 1)


def cyclic(last, count=4):
    return lambda k: jnp.where(k < last, k % count, count - 1)


def either(core, own, other):
    low = jnp.where(core == 0, own, other)
    return jnp.concatenate([low, jnp.where(core == 0, other, own)], axis=1)


class Gather:
    def __init__(self, pieces, rows, sems):
        self.pieces, self.rows = pieces, rows
        self.local, self.zs, self.zr, self.as_, self.ar, self.bs, self.br = sems
        self.s, self.c, self.z, self.y, self.x = place()
        s, c = self.s, self.c
        self.up, self.down = self.z < LINE - 1, self.z > 0
        self.to_x, self.to_y = (s + 1 - 2 * self.x, c), (s + 2 - 4 * self.y, c)
        self.to_up, self.to_down = (s + PLANE, c), (s - PLANE, c)
        self.span = range(len(pieces))

    @staticmethod
    def semaphores(n):
        return dict(
            g0=dma(n), g1=dma(n, 2, 4), g2=dma(n, 4), g3=dma(n, 4), g4=dma(n, 4), g5=dma(n, 4, 2),
            g6=dma(n, 4, 2),
        )

    def at(self, p, index, count=1):
        src, dst, start, width, order = self.pieces[p]
        begin = pl.multiple_of(index * self.rows, 16)
        return dst.at[pl.ds(begin, count * self.rows), pl.ds(start, width)]

    def own(self, p):
        src, dst, start, width, order = self.pieces[p]
        return src.at[:, pl.ds(start, width)]

    def local_copy(self, p):
        return pltpu.make_async_copy(self.own(p), self.at(p, self.s), self.local.at[p])

    def z_copy(self, p, off):
        zz = self.z + off
        dst = self.at(p, zz * PLANE + self.y * 2 + self.x)
        src = self.own(p) if off == 0 else dst
        step = abs(off)
        moves = []
        if off <= 0:
            sems = self.zs.at[p, 0, step], self.zr.at[p, zz]
            moves.append((self.up, remote(src, dst, *sems, self.to_up)))
        if off >= 0:
            sems = self.zs.at[p, 1, step], self.zr.at[p, zz]
            moves.append((self.down, remote(src, dst, *sems, self.to_down)))
        return moves

    def first_copy(self, p, off):
        zz = self.z + off
        dst = self.at(p, zz * PLANE + self.y * 2 + self.x)
        src = self.own(p) if off == 0 else dst
        device = self.to_x if self.pieces[p][4] else self.to_y
        return remote(src, dst, self.as_.at[p, zz], self.ar.at[p, zz], device)

    def second_copies(self, p, off):
        zz = self.z + off
        if self.pieces[p][4]:
            pair = self.at(p, zz * PLANE + self.y * 2, 2)
            return [remote(pair, pair, self.bs.at[p, zz, 0], self.br.at[p, zz, 0], self.to_y)]
        copies = []
        for k in range(2):
            block = self.at(p, zz * PLANE + k * 2 + self.x)
            copies.append(
                remote(block, block, self.bs.at[p, zz, k], self.br.at[p, zz, k], self.to_x)
            )
        return copies

    def exists(self, off):
        zz = self.z + off
        return (zz >= 0) & (zz < LINE)

    def begin(self):
        for p in self.span:
            for there, copy in self.z_copy(p, 0):
                pl.when(there)(copy.start)
            self.first_copy(p, 0).start()
            self.local_copy(p).start()

    def z_arrived(self, *offs):
        for off in offs:

            @pl.when(self.exists(off))
            def _():
                for p in self.span:
                    for there, copy in self.z_copy(p, off):
                        copy.wait_recv()
                        pl.when(there)(copy.start)
                    self.first_copy(p, off).start()

    def first_arrived(self, *offs):
        for off in offs:

            @pl.when(self.exists(off))
            def _():
                for p in self.span:
                    if off == 0:
                        self.local_copy(p).wait()
                    self.first_copy(p, off).wait_recv()
                    for copy in self.second_copies(p, off):
                        copy.start()

    def finish(self):
        for off in OFFSETS:

            @pl.when(self.exists(off))
            def _():
                for p in self.span:
                    for copy in self.second_copies(p, off):
                        copy.wait()
                    self.first_copy(p, off).wait_send()
                    for there, copy in self.z_copy(p, off):
                        pl.when(there)(copy.wait_send)


class Scan:
    def __init__(self, backward, size, state, decay, out, refs):
        self.state, self.decay, self.out, self.size = state, decay, out, size
        (
            self.slots, self.rates, self.total, self.through, self.pair, self.pair_through,
            self.far, self.leaving, self.staged, self.s1, self.r1, self.s2, self.r2, self.zs,
            self.zr, self.s3, self.r3,
        ) = refs
        s, c, z, y, x = place()
        self.s, self.c, self.p = s, c, s % PLANE
        self.base = s - self.p
        self.order = tuple(range(PLANE - 1, -1, -1)) if backward else tuple(range(PLANE))
        self.rows = state.shape[1] // PLANE
        self.place = LINE - 1 - z if backward else z
        self.step = -PLANE if backward else PLANE

    @staticmethod
    def scratch(count, rows, nstate, heads):
        quarter = rows // PLANE
        return dict(
            slots=pltpu.VMEM((count, PLANE, quarter, nstate), BF16),
            rates=pltpu.VMEM((count, PLANE, heads, nstate), F32),
            total=pltpu.VMEM((count, quarter, nstate), F32),
            through=pltpu.VMEM((count, 8, nstate), F32),
            pair=pltpu.VMEM((count, quarter, nstate), BF16),
            pair_through=pltpu.VMEM((count, 8, nstate), F32),
            far=pltpu.VMEM((count, quarter, nstate), BF16),
            leaving=pltpu.VMEM((count, quarter, nstate), BF16),
            staged=pltpu.VMEM((count, PLANE, quarter, nstate), BF16),
            s1=dma(count, PLANE), r1=dma(count, PLANE),
            s2=dma(count, PLANE), r2=dma(count, PLANE),
            zs=dma(count, 3), zr=dma(count, 3),
            s3=dma(count, PLANE), r3=dma(count, PLANE),
        )

    def relations(self):
        plane = [(self.p != j, (self.base + j, self.c)) for j in range(PLANE)]
        s, c, at, step = self.s, self.c, self.place, self.step
        return plane + [
            (at > 0, (s - step, c)),
            (at < LINE - 1, (s + step, c)),
            (at == 1, (s + 2 * step, c)),
            (at == 3, (s - 2 * step, c)),
        ]

    def part(self, j):
        return pl.ds(pl.multiple_of(j * self.rows, 16), self.rows)

    def first(self, i, j, slot):
        device = (self.base + j, self.c)
        return [
            remote(
                self.state.at[i, self.part(j)], self.slots.at[i, slot],
                self.s1.at[i, j], self.r1.at[i, slot], device,
            ),
            remote(
                self.decay.at[i], self.rates.at[i, slot], self.s2.at[i, j], self.r2.at[i, slot],
                device,
            ),
        ]

    def to_pair(self, i):
        device = (self.s + self.step, self.c)
        return [
            remote(self.leaving.at[i], self.pair.at[i], self.zs.at[i, 0], self.zr.at[i, 0], device),
            remote(
                self.through.at[i], self.pair_through.at[i], self.zs.at[i, 1], self.zr.at[i, 1],
                device,
            ),
        ]

    def to_far(self, i, n):
        return remote(
            self.leaving.at[i], self.far.at[i], self.zs.at[i, 0 if n == 1 else 2],
            self.zr.at[i, 2], (self.s + n * self.step, self.c),
        )

    def last(self, i, j, quarter):
        return remote(
            self.staged.at[i, j], self.out.at[i, self.part(quarter)],
            self.s3.at[i, j], self.r3.at[i, quarter], (self.base + j, self.c),
        )

    def others(self, act):
        for j in range(PLANE):
            pl.when(self.p != j)(functools.partial(act, j))

    def start(self, i):
        def send(j):
            for copy in self.first(i, j, self.p):
                copy.start()

        self.others(send)
        self.slots[i, self.p] = self.state[i, self.part(self.p)]
        self.rates[i, self.p] = self.decay[i]

    def pieces(self):
        for n in range(self.rows // self.size):
            yield n, slice(n * self.size, (n + 1) * self.size)

    def rate(self, i, j, n):
        return self.rates[i, j, pl.ds(self.p * (self.rows // self.size) + n, 1)]

    def deliver(self, i, entering):
        for n, rows in self.pieces():
            held = entering(n, rows)
            for at, j in enumerate(self.order):
                self.staged[i, j, rows] = held.astype(BF16)
                if at < PLANE - 1:
                    held = self.rate(i, j, n) * held + self.slots[i, j, rows].astype(F32)
        self.others(lambda j: self.last(i, j, self.p).start())
        self.out[i, self.part(self.p)] = self.staged[i, self.p]

    def fold(self, i):
        def arrived(j):
            for copy in self.first(i, j, j):
                copy.wait_recv()

        self.others(arrived)
        for n, rows in self.pieces():
            held = self.slots[i, self.order[0], rows].astype(F32)
            rate = self.rate(i, self.order[0], n)
            for j in self.order[1:]:
                own = self.rate(i, j, n)
                held = own * held + self.slots[i, j, rows].astype(F32)
                rate = own * rate
            self.total[i, rows] = held
            self.through[i, n : n + 1] = rate

        @pl.when((self.place == 0) | (self.place == 2))
        def _():
            self.leaving[i] = self.total[i].astype(BF16)
            for copy in self.to_pair(i):
                copy.start()

        @pl.when(self.place == 0)
        def _():
            self.deliver(i, lambda n, rows: jnp.zeros((self.size, self.out.shape[2]), F32))

    def join(self, i):
        @pl.when(self.place == 1)
        def _():
            for copy in self.to_pair(i):
                copy.wait_recv()
            for n, rows in self.pieces():
                self.leaving[i, rows] = (
                    self.total[i, rows]
                    + self.through[i, n : n + 1] * self.pair[i, rows].astype(F32)
                ).astype(BF16)
            for n in (1, 2):
                self.to_far(i, n).start()
            self.deliver(i, lambda n, rows: self.pair[i, rows].astype(F32))

    def close(self, i):
        @pl.when(self.place == 2)
        def _():
            self.to_far(i, 1).wait_recv()
            self.deliver(i, lambda n, rows: self.far[i, rows].astype(F32))

        @pl.when(self.place == 3)
        def _():
            for copy in self.to_pair(i):
                copy.wait_recv()
            self.to_far(i, 1).wait_recv()
            self.deliver(
                i,
                lambda n, rows: self.pair[i, rows].astype(F32)
                + self.pair_through[i, n : n + 1] * self.far[i, rows].astype(F32),
            )

    def arrived(self, i):
        self.others(lambda j: self.last(i, j, j).wait_recv())

    def finish(self):
        @pl.loop(0, self.state.shape[0])
        def _(i):
            def close(j):
                for copy in self.first(i, j, self.p):
                    copy.wait_send()
                self.last(i, j, self.p).wait_send()

            self.others(close)

            @pl.when((self.place == 0) | (self.place == 2))
            def _():
                for copy in self.to_pair(i):
                    copy.wait_send()

            @pl.when(self.place == 1)
            def _():
                for n in (1, 2):
                    self.to_far(i, n).wait_send()


class Reduce:
    def __init__(self, pieces, rows, refs):
        self.pieces, self.rows = pieces, rows
        (
            self.near, self.mid, self.above, self.below, self.mid_send, self.kept,
            self.s1, self.r1, self.s2, self.r2, self.sz, self.rz,
        ) = refs
        self.s, self.c, self.z, self.y, self.x = place()
        s, c = self.s, self.c
        self.up, self.down = self.z < LINE - 1, self.z > 0
        self.to_x, self.to_y = (s + 1 - 2 * self.x, c), (s + 2 - 4 * self.y, c)
        self.to_up, self.to_down = (s + PLANE, c), (s - PLANE, c)
        self.span = range(len(pieces))

    @staticmethod
    def scratch(n, rows, wide):
        return dict(
            near=pltpu.VMEM((LINE, 2 * rows, wide), BF16),
            mid=pltpu.VMEM((LINE, rows, wide), BF16),
            above=pltpu.VMEM((LINE, rows, wide), BF16),
            below=pltpu.VMEM((LINE, rows, wide), BF16),
            mid_send=pltpu.VMEM((LINE, rows, wide), BF16),
            kept=pltpu.VMEM((LINE, rows, wide), F32),
            t1=dma(n, LINE, 2), u1=dma(n, LINE, 2), t2=dma(n, LINE),
            u2=dma(n, LINE), tz=dma(n, LINE), uz=dma(n, 2, LINE),
        )

    def columns(self, p):
        return pl.ds(self.pieces[p][6], self.pieces[p][2])

    def source(self, p, index, count=1):
        ref, start, width = self.pieces[p][:3]
        begin = pl.multiple_of(index * self.rows, 16)
        return ref.at[pl.ds(begin, count * self.rows), pl.ds(start, width)]

    def index(self, zz, yy, xx):
        return zz * PLANE + yy * 2 + xx

    def near_copies(self, p, zz):
        if self.pieces[p][3]:
            return [
                remote(
                    self.source(p, self.index(zz, 1 - self.y, 0), 2),
                    self.near.at[zz, :, self.columns(p)],
                    self.s1.at[p, zz, 0], self.r1.at[p, zz, 0], self.to_y,
                )
            ]
        return [
            remote(
                self.source(p, self.index(zz, k, 1 - self.x)),
                self.near.at[zz, pl.ds(k * self.rows, self.rows), self.columns(p)],
                self.s1.at[p, zz, k], self.r1.at[p, zz, k], self.to_x,
            )
            for k in range(2)
        ]

    def mid_copy(self, p, zz):
        at = self.columns(p)
        return remote(
            self.mid_send.at[zz, :, at], self.mid.at[zz, :, at],
            self.s2.at[p, zz], self.r2.at[p, zz], self.to_x if self.pieces[p][3] else self.to_y,
        )

    def line_copy(self, p, zz, upward):
        at = self.columns(p)
        target = self.above if upward else self.below
        return remote(
            self.mid_send.at[zz, :, at], target.at[zz, :, at],
            self.sz.at[p, zz], self.rz.at[p, 0 if upward else 1, zz],
            self.to_up if upward else self.to_down,
        )

    def exists(self, off):
        zz = self.z + off
        return (zz >= 0) & (zz < LINE)

    def rows_of(self, k):
        return pl.ds(pl.multiple_of(k * self.rows, 16), self.rows)

    def begin(self, *pieces):
        for off in SUM_OFFSETS:

            @pl.when(self.exists(off))
            def _():
                for p in pieces or self.span:
                    for copy in self.near_copies(p, self.z + off):
                        copy.start()

    def second(self, *offs):
        for off in offs:

            @pl.when(self.exists(off))
            def _():
                zz = self.z + off
                y, x = self.y, self.x
                for p in self.span:
                    for copy in self.near_copies(p, zz):
                        copy.wait_recv()
                    own = self.index(zz, y, x)
                    if self.pieces[p][3]:
                        other, mine = self.index(zz, y, 1 - x), x
                    else:
                        other, mine = self.index(zz, 1 - y, x), y
                    at = self.columns(p)
                    sent = self.source(p, other)[...].astype(F32) + self.near[
                        zz, self.rows_of(1 - mine), at
                    ].astype(F32)
                    self.mid_send[zz, :, at] = sent.astype(BF16)
                    self.mid_copy(p, zz).start()
                    self.kept[zz, :, at] = self.source(p, own)[...].astype(F32) + self.near[
                        zz, self.rows_of(mine), at
                    ].astype(F32)

    def third(self, *offs, only=None):
        for off in offs:

            @pl.when(self.exists(off))
            def _():
                zz = self.z + off
                for p in self.span if only is None else only:
                    at = self.columns(p)
                    self.mid_copy(p, zz).wait_recv()
                    self.kept[zz, :, at] = self.kept[zz, :, at] + self.mid[zz, :, at].astype(F32)
                    if off >= 0:

                        @pl.when(self.down)
                        def _():
                            self.line_copy(p, zz, True).wait_recv()
                            self.kept[zz, :, at] = self.kept[zz, :, at] + self.above[
                                zz, :, at
                            ].astype(F32)

                    if off <= 0:

                        @pl.when(self.up)
                        def _():
                            self.line_copy(p, zz, False).wait_recv()
                            self.kept[zz, :, at] = self.kept[zz, :, at] + self.below[
                                zz, :, at
                            ].astype(F32)

                    if off == 0:
                        _, _, width, _, out, start, _ = self.pieces[p]
                        out[:, start : start + width] = self.kept[zz, :, at]
                    else:
                        self.mid_copy(p, zz).wait_send()
                        self.mid_send[zz, :, at] = self.kept[zz, :, at].astype(BF16)
                        self.line_copy(p, zz, off > 0).start()

    def finish(self):
        for off in SUM_OFFSETS:

            @pl.when(self.exists(off))
            def _():
                zz = self.z + off
                for p in self.span:
                    for copy in self.near_copies(p, zz):
                        copy.wait_send()
                    if off == 0:
                        self.mid_copy(p, zz).wait_send()
                    else:
                        self.line_copy(p, zz, off > 0).wait_send()


def picked(r, names):
    return tuple(r.__dict__[n] for n in names)


GATHER_REFS = tuple(Gather.semaphores(1))
SCAN_REFS = tuple(Scan.scratch(1, PLANE, 1, 1))
REDUCE_REFS = tuple(Reduce.scratch(1, 16, 1))


def main_body(sizes, total_inner, r):
    length, inner, nstate, size, taps = sizes
    channels = inner + 2 * nstate
    heads = inner // size
    count = r.tok.shape[0]
    half = r.tok.shape[2]
    s, c, z, y, x = place()
    to_core, to_prv = (s, 1 - c), (s - 1, c)
    nxt, prv = s < LINE * PLANE - 1, s > 0
    first_gather = Gather(
        ((r.w1, r.w, 0, 640, True), (r.w1, r.w, 640, r.w1.shape[1] - 640, False)),
        r.w1.shape[0],
        picked(r, GATHER_REFS),
    )
    second_gather = Gather(
        ((r.w2, r.w2_full, 0, inner, True), (r.w2, r.w2_full, inner, inner, False)),
        r.w2.shape[0],
        picked(r, SECOND_REFS),
    )
    prefix = Scan(False, size, r.state, r.dec, r.hin, picked(r, SCAN_REFS))
    suffix = Scan(True, size, r.prior, r.dec, r.later, picked(r, SUFFIX_REFS))
    reduce_ = Reduce(
        ((r.dout, 0, inner, True, r.g_out, 0, 0), (r.dgate, 0, inner, False, r.g_gate, 0, inner)),
        r.g_out.shape[0],
        picked(r, REDUCE_REFS),
    )
    wide = inner + nstate + LANES
    late = Reduce(
        (
            (r.dout, 0, wide // 2, True, r.g_x, 0, 0),
            (r.dgate, 0, wide // 2, False, r.g_x, wide // 2, wide // 2),
        ),
        r.g_x.shape[0],
        picked(r, LATE_REFS),
    )
    spread = head_spread(inner, size)
    mine = pl.ds(pl.multiple_of(inner + c * nstate, LANES), nstate)
    side = pl.ds(pl.multiple_of(c * half, LANES), half)
    other_side = pl.ds(pl.multiple_of((1 - c) * half, LANES), half)
    log_at, step_at, pre_at, entry_at = (
        slice(n * LANES, (n + 1) * LANES) for n in range(4)
    )
    scores_at = slice(half, half + length)
    own_at, slope_at, gpre_at = (
        slice(half + n * nstate, half + (n + 1) * nstate) for n in range(3)
    )
    left = lax.broadcasted_iota(jnp.int32, (length, LANES), 1) < size

    def swap(n, source, target):
        return lambda i: remote(
            source.at[i], target.at[i], r.ss.at[n, i], r.rs.at[n, i], to_core
        )

    swap_tokens = swap(0, r.tok, r.tok_in)
    swap_grads = swap(1, r.g, r.g_in)
    swap_sums = swap(2, r.sums, r.sums_in)
    swap_out = swap(3, r.osend, r.out_in)
    swap_states = swap(4, r.bsend, r.brecv)
    swap_part = swap(6, r.normal, r.low)

    def send_edge(i):
        return remote(r.edge.at[i], r.edge_in.at[i], r.ss.at[5, i], r.rs.at[5, i], to_prv)

    def halo_copy(k):
        tails = r.tok.at[:, pl.ds(length - HALO, HALO), :]
        device = (s + 1, c if k == 0 else 1 - c)
        return remote(tails, r.halo.at[:, :, side], r.hs.at[k], r.hr.at[k], device)

    def store_grad(i):
        return pltpu.make_async_copy(
            r.full.at[i, :, pl.ds(0, half)], r.tokens_grad.at[i], r.store.at[0, i]
        )

    def store_mixed(i):
        return pltpu.make_async_copy(r.g_in.at[i], r.mixed.at[i], r.store.at[1, i])

    def conv(at):
        pre = r.prm[BIAS : BIAS + 1, at]
        for t in range(taps):
            start = HALO - taps + 1 + t
            pre = pre + r.prm[TAPS + t : TAPS + t + 1, at] * r.ext[start : start + length, at]
        return pre

    greet(
        prefix.relations()
        + [(z != j, (s + (j - z) * PLANE, c)) for j in range(LINE)]
        + [
            (True, to_core),
            (nxt, (s + 1, c)),
            (nxt, (s + 1, 1 - c)),
            (prv, (s - 1, c)),
            (prv, (s - 1, 1 - c)),
        ]
    )
    first_gather.begin()
    for k in range(2):
        pl.when(nxt)(halo_copy(k).start)
    for i in range(count):
        swap_tokens(i).start()
    r.small[...] = jnp.zeros_like(r.small)
    first_gather.z_arrived(-1, 1)
    first_gather.first_arrived(0)
    for i in range(count):
        swap_grads(i).start()

    @pl.loop(0, count)
    def _(i):
        swap_tokens(i).wait()
        own, other = r.tok[i].astype(F32), r.tok_in[i].astype(F32)
        scale = lax.rsqrt(
            jnp.mean(own * own + other * other, axis=-1, keepdims=True) * 0.5 + EPSILON
        )
        gain_own = r.prm[GAIN : GAIN + 1, side]
        gain_other = r.prm[GAIN : GAIN + 1, other_side]
        r.normed_s[i, HALO:, side] = (own * scale * gain_own).astype(BF16)
        r.normed_s[i, HALO:, other_side] = (other * scale * gain_other).astype(BF16)

    first_gather.z_arrived(-2, 2)
    first_gather.first_arrived(-1, 1)
    for k in range(2):
        pl.when(nxt)(halo_copy(k).wait_send)
        pl.when(prv)(halo_copy(k).wait_recv)

    @pl.when(prv)
    def _():
        for i in range(count):
            edge = r.halo[i].astype(F32)
            scale = lax.rsqrt(jnp.mean(edge * edge, axis=-1, keepdims=True) + EPSILON)
            r.normed_s[i, :HALO] = (
                edge * scale * r.prm[GAIN : GAIN + 1, : edge.shape[1]]
            ).astype(BF16)

    @pl.when(jnp.logical_not(prv))
    def _():
        for i in range(count):
            r.normed_s[i, :HALO] = jnp.zeros((HALO, 2 * half), BF16)

    first_gather.z_arrived(-3, 3)
    first_gather.first_arrived(-2, 2, -3, 3)
    second_gather.begin()
    first_gather.finish()
    kept, ones = triangle(length)

    def project(i):
        xs = dot(r.normed_s[i], r.w[:, :channels]).astype(BF16)
        r.xs_s[i] = xs
        r.ext[...] = xs.astype(F32)
        pre = conv(slice(0, channels))
        act = (pre * sigmoid(pre)).astype(BF16)
        r.act[i] = act
        step_pre = (
            dot(r.normed_s[i, HALO:], r.w[:, channels:])
            + r.prm[STEP_BIAS : STEP_BIAS + 1, :LANES]
        )
        step = softplus(step_pre)
        log_decay = running_sum(ones, step * r.prm[RATE : RATE + 1, :LANES])
        doc_col, doc_row = doc_numbers(r.doc[i], ones)
        entry = jnp.where(doc_col == 0.0, jnp.exp(log_decay), 0.0)
        last = log_decay[length - 1 :]
        tail = jnp.where(doc_col == doc_col[length - 1 :], jnp.exp(last - log_decay), 0.0)
        r.aux[i, :, log_at] = log_decay
        r.aux[i, :, step_at] = step
        r.aux[i, :, pre_at] = step_pre
        r.aux[i, :, entry_at] = entry
        log_rows = log_decay.T
        whole_decay = jnp.where(
            doc_row[:, length - 1 :] == 0.0, jnp.exp(log_rows[:HEAD_ROWS, length - 1 :]), 0.0
        )
        r.dec[i] = jnp.broadcast_to(whole_decay, (HEAD_ROWS, LANES))
        inputs = act[:, :inner].astype(F32) * expand(step, spread)
        r.low[i] = inputs.astype(BF16)
        r.state[i] = dot(
            (inputs * expand(tail, spread)).astype(BF16), act[:, inner : inner + nstate], TN
        ).astype(BF16)
        prefix.start(i)

    @pl.loop(0, count)
    def _(i):
        project(i)

        @pl.when(i == 1)
        def _():
            second_gather.z_arrived(-1, 1)
            second_gather.first_arrived(0)

        @pl.when(i == 2)
        def _():
            prefix.fold(0)
            second_gather.z_arrived(-2, 2)
            second_gather.first_arrived(-1, 1)

        @pl.when(i == 3)
        def _():
            prefix.fold(1)
            second_gather.z_arrived(-3, 3)
            second_gather.first_arrived(-2, 2)

    def inside(i):
        log_decay = r.aux[i, :, log_at]
        log_rows = log_decay.T
        doc_col, doc_row = doc_numbers(r.doc[i], ones)
        closed = jnp.where(kept & (doc_col == doc_row), 0.0, MASKED)
        scores = dot(r.act[i, :, inner + nstate :], r.act[i, :, inner : inner + nstate], NT)
        for pair in range(inner // LANES):
            columns = slice(pair * LANES, (pair + 1) * LANES)
            part = r.low[i, :, columns]
            total = None
            for h in (2 * pair, 2 * pair + 1):
                decay = jnp.exp(log_decay[:, h : h + 1] - log_rows[h : h + 1] + closed)
                own = jnp.where(left if h % 2 == 0 else ~left, part, jnp.zeros_like(part))
                term = dot((scores * decay).astype(BF16), own)
                total = term if total is None else total + term
            r.full[i, :, columns] = total

    @pl.loop(0, count)
    def _(i):
        inside(i)

        @pl.when(i == 0)
        def _():
            prefix.join(0)
            second_gather.first_arrived(-3, 3)

        @pl.when(i == 1)
        def _():
            prefix.fold(2)
            prefix.join(1)

        @pl.when(i == 2)
        def _():
            prefix.fold(3)
            prefix.close(0)

        @pl.when(i == 3)
        def _():
            prefix.join(2)
            prefix.close(1)

    second_gather.finish()
    for i in range(count):
        swap_grads(i).wait()

    def gates(i):
        r.gate[i] = dot(r.normed_s[i, HALO:], r.w2_full[:, :inner])
        r.gn[i] = dot(either(c, r.g[i], r.g_in[i]), r.w2_full[:, inner:])

    @pl.loop(0, count)
    def _(i):
        gates(i)

        @pl.when(i == 0)
        def _():
            prefix.join(3)

        @pl.when(i == 1)
        def _():
            prefix.close(2)

    def combine(i):
        prefix.arrived(i)
        values = r.act[i, :, :inner].astype(F32)
        entry = expand(r.aux[i, :, entry_at], spread)
        scanned = r.full[i] + dot(r.act[i, :, inner + nstate :], r.hin[i], NT) * entry
        r.full[i] = scanned
        mixed = scanned + r.prm[SKIP : SKIP + 1, :inner] * values
        gate = r.gate[i]
        gated = mixed * (gate * sigmoid(gate))
        squares = jnp.sum(gated * gated, axis=-1, keepdims=True)
        cross = jnp.sum(
            r.gn[i] * r.prm[INNER_GAIN : INNER_GAIN + 1, :inner] * gated, axis=-1, keepdims=True
        )
        lane = lax.broadcasted_iota(jnp.int32, (length, LANES), 1)
        r.sums[i] = jnp.where(lane == 0, squares, jnp.where(lane == 1, cross, 0.0)).T[:EDGE]
        swap_sums(i).start()

    def norm_back(i):
        swap_sums(i).wait_recv()
        values = r.act[i, :, :inner].astype(F32)
        mixed = r.full[i] + r.prm[SKIP : SKIP + 1, :inner] * values
        gate = r.gate[i]
        sig = sigmoid(gate)
        swish = gate * sig
        gated = mixed * swish
        both = jnp.concatenate(
            [r.sums[i] + r.sums_in[i], jnp.zeros((LANES - EDGE, length), F32)], axis=0
        ).T
        inner_scale = lax.rsqrt(both[:, 0:1] / total_inner + EPSILON)
        gain = r.prm[INNER_GAIN : INNER_GAIN + 1, :inner]
        unit = gated * inner_scale
        r.normal[i] = (unit * gain).astype(BF16)
        grad_norm = r.gn[i]
        grad_inner = jnp.sum(grad_norm * unit, axis=0, keepdims=True)
        grad_gated = inner_scale * (grad_norm * gain) - unit * (
            inner_scale * inner_scale * (both[:, 1:2] / total_inner)
        )
        dy = grad_gated * swish
        r.dy[i] = dy.astype(BF16)
        r.ggate_s[i] = (
            grad_gated * mixed * (sig * (1.0 + gate * (1.0 - sig)))
        ).astype(BF16)
        entry = expand(r.aux[i, :, entry_at], spread)
        r.prior[i] = dot(
            (dy * entry).astype(BF16), r.act[i, :, inner + nstate :], TN
        ).astype(BF16)
        suffix.start(i)
        r.small[0:1, :inner] += grad_inner
        per_head = head_sums(
            jnp.broadcast_to(jnp.sum(dy * values, axis=0, keepdims=True), (8, inner)), spread
        )
        r.small[1:2, :LANES] += per_head[:1]

    combine(0)
    combine(1)
    prefix.close(3)
    norm_back(0)
    combine(2)
    norm_back(1)
    combine(3)
    prefix.finish()
    norm_back(2)
    suffix.fold(0)
    norm_back(3)
    suffix.fold(1)

    def outputs(i):
        r.ginputs[...] = dot(r.normal[i], r.w2_full[:, inner:], NT)
        r.gate[i, :, :half] = r.ginputs[:, side]
        r.osend[i] = r.ginputs[:, other_side].astype(BF16)
        swap_out(i).start()

    pl.loop(0, count)(outputs)
    suffix.join(0)

    def weights_gradient(source, target, values, rows):
        for n in range(inner // 256):
            at = slice(n * 256, (n + 1) * 256)
            total = None
            for i in range(count):
                term = dot(source(i), values[i, :, at], TN)
                total = term if total is None else total + term
            target[rows, at] = total.astype(BF16)

    weights_gradient(lambda i: r.g[i], r.dout, r.normal, side)
    suffix.fold(2)
    weights_gradient(lambda i: r.g_in[i], r.dout, r.normal, other_side)
    reduce_.begin(0)
    suffix.fold(3)
    suffix.join(1)
    suffix.close(0)
    weights_gradient(lambda i: r.normed_s[i, HALO:], r.dgate, r.ggate_s, slice(None))
    reduce_.begin(1)
    suffix.join(2)

    upper, ones_upper = triangle(length, True)

    def back_inside(i):
        log_decay = r.aux[i, :, log_at]
        in_state = r.act[i, :, inner : inner + nstate]
        out_state = r.act[i, :, inner + nstate :]
        doc_col, doc_row = doc_numbers(r.doc[i], ones)
        closed = jnp.where(upper & (doc_col == doc_row), 0.0, MASKED)
        scores = dot(in_state, out_state, NT)
        log_rows = log_decay.T
        for pair in range(inner // LANES):
            columns = slice(pair * LANES, (pair + 1) * LANES)
            pair_dy = r.dy[i, :, columns]
            pair_in = r.low[i, :, columns]
            total = None
            for h in (2 * pair, 2 * pair + 1):
                chosen = left if h % 2 == 0 else ~left
                own_dy = jnp.where(chosen, pair_dy, jnp.zeros_like(pair_dy))
                decay = jnp.exp(log_rows[h : h + 1] - log_decay[:, h : h + 1] + closed)
                term = dot((scores * decay).astype(BF16), own_dy)
                total = term if total is None else total + term
                grad_decay = dot(pair_in, own_dy, NT) * decay
                if h == 0:
                    r.gate[i, :, scores_at] = grad_decay
                else:
                    r.gate[i, :, scores_at] += grad_decay
            r.gn[i, :, columns] = total

    @pl.loop(0, count)
    def _(i):
        back_inside(i)

        @pl.when(i == 0)
        def _():
            suffix.close(1)
            suffix.join(3)

        @pl.when(i == 1)
        def _():
            suffix.close(2)

        @pl.when(i == 2)
        def _():
            suffix.close(3)
            reduce_.second(3, -3)

        @pl.when(i == 3)
        def _():
            reduce_.second(2, -2)

    def back_rest(i):
        suffix.arrived(i)
        step = r.aux[i, :, step_at]
        entry = r.aux[i, :, entry_at]
        values = r.act[i, :, :inner].astype(F32)
        in_state = r.act[i, :, inner : inner + nstate]
        out_state = r.act[i, :, inner + nstate :]
        later = r.later[i]
        wide_dy = r.dy[i].astype(F32)
        step_wide = expand(step, spread)
        log_decay = r.aux[i, :, log_at]
        doc_col, doc_row = doc_numbers(r.doc[i], ones)
        tail = jnp.where(
            doc_col == doc_col[length - 1 :], jnp.exp(log_decay[length - 1 :] - log_decay), 0.0
        )
        tail_wide = expand(tail, spread)
        entry_wide = expand(entry, spread)
        inputs = values * step_wide
        grad_inputs = r.gn[i] + tail_wide * dot(in_state, later, NT)
        grad_scores = r.gate[i, :, scores_at]
        grad_in = dot(grad_scores.astype(BF16), out_state) + dot(
            (inputs * tail_wide).astype(BF16), later
        )
        grad_out = dot(grad_scores.T.astype(BF16), in_state) + dot(
            (wide_dy * entry_wide).astype(BF16), r.hin[i]
        )
        is_first = c == 0
        r.gate[i, :, own_at] = jnp.where(is_first, grad_in, grad_out)
        r.bsend[i] = jnp.where(is_first, grad_out, grad_in).astype(BF16)
        entry_last = jnp.broadcast_to(entry[length - 1 :], (8, LANES))
        later_wide = later.astype(F32)
        lane_ones = jnp.ones((8, nstate), BF16)

        def state_sums(other):
            pieces = split2(later_wide * other.astype(F32))
            return head_sums(sum(dot(lane_ones, piece, NT) for piece in pieces), spread)

        ending = (state_sums(r.state[i]) + entry_last * state_sums(r.hin[i]))[:1]
        grad_log = head_sums(wide_dy * r.full[i], spread) - head_sums(
            r.low[i].astype(F32) * grad_inputs, spread
        )
        swap_states(i).start()
        grad_rate_step = running_sum(ones_upper, grad_log) + ending
        rate = r.prm[RATE : RATE + 1, :LANES]
        grad_step = head_sums(values * grad_inputs, spread) + rate * grad_rate_step
        lane = lax.broadcasted_iota(jnp.int32, (length, LANES), 1)
        gpre = jnp.where(lane < heads, grad_step * sigmoid(r.aux[i, :, pre_at]), 0.0)
        r.gate[i, :, gpre_at] = gpre
        grad_values = step_wide * grad_inputs + r.prm[SKIP : SKIP + 1, :inner] * wide_dy
        r.ext[...] = r.xs_s[i].astype(F32)
        px = conv(slice(0, inner))
        sig = sigmoid(px)
        gcx = grad_values * (sig * (1.0 + px * (1.0 - sig)))
        r.gn[i] = gcx
        r.edge[i, :, :inner] = gcx[:EDGE]
        ps = conv(mine)
        sig = sigmoid(ps)
        r.gate[i, :, slope_at] = sig * (1.0 + ps * (1.0 - sig))
        r.small[1:2, LANES : 2 * LANES] += jnp.sum(gpre, axis=0, keepdims=True)
        r.small[1:2, 2 * LANES : 3 * LANES] += rate * jnp.sum(
            step * grad_rate_step, axis=0, keepdims=True
        )


    def finish_states(n):
        swap_states(n).wait_recv()
        gst = (r.gate[n, :, own_at] + r.brecv[n].astype(F32)) * r.gate[n, :, slope_at]
        r.gate[n, :, own_at] = gst
        r.edge[n, :, inner:] = gst[:EDGE]
        pl.when(prv)(send_edge(n).start)

    @pl.loop(0, count)
    def _(i):
        back_rest(i)
        pl.when(i > 0)(lambda: finish_states(i - 1))

        @pl.when(i == 0)
        def _():
            reduce_.second(1, -1)

        @pl.when(i == 1)
        def _():
            reduce_.second(0)
            reduce_.third(3, -3)

        @pl.when(i == 2)
        def _():
            reduce_.third(2, -2)

        @pl.when(i == 3)
        def _():
            reduce_.third(1, -1)

    r.conv_rows[...] = jnp.zeros_like(r.conv_rows)
    r.bc[...] = jnp.zeros_like(r.bc)

    def conv_back(i):
        pl.when(nxt)(send_edge(i).wait_recv)
        r.gext[:length, :inner] = r.gn[i]
        r.gext[:length, inner:] = r.gate[i, :, own_at]
        r.gext[length:] = jnp.where(nxt, r.edge_in[i], 0.0)
        r.ext[:, :inner] = r.xs_s[i, :, :inner].astype(F32)
        r.ext[:, inner : inner + nstate] = r.xs_s[i, :, mine].astype(F32)
        grad_conv = r.gext[:length]
        grad_in = None
        for t in range(taps):
            row = jnp.concatenate(
                [r.prm[TAPS + t : TAPS + t + 1, :inner], r.prm[TAPS + t : TAPS + t + 1, mine]],
                axis=1,
            )
            term = row * r.gext[taps - 1 - t : taps - 1 - t + length]
            grad_in = term if grad_in is None else grad_in + term
            start = HALO - taps + 1 + t
            r.conv_rows[t : t + 1] += jnp.sum(
                r.ext[start : start + length, : inner + nstate] * grad_conv, axis=0, keepdims=True
            )
        r.conv_rows[taps : taps + 1] += jnp.sum(grad_conv, axis=0, keepdims=True)
        low = grad_in.astype(BF16)
        low_pre = r.gate[i, :, gpre_at].astype(BF16)
        part = dot(r.ggate_s[i], r.w2_full[:, :inner], NT)
        part = part + dot(low[:, :inner], r.w[:, :inner], NT)
        part = part + dot(low[:, inner:], r.w[:, mine], NT)
        part = part + dot(low_pre, r.w[:, channels:], NT)
        low_part = part.astype(BF16)
        r.normal[i] = low_part
        swap_part(i).start()
        r.dy[i] = low[:, :inner]
        r.gtail[i, :, :nstate] = low[:, inner:]
        r.gtail[i, :, nstate:] = low_pre
        tok = either(c, r.tok[i].astype(F32), r.tok_in[i].astype(F32))
        unit = tok * lax.rsqrt(jnp.mean(tok * tok, axis=-1, keepdims=True) + EPSILON)
        r.bc[0:1, :inner] += jnp.sum(low_part.astype(F32) * unit, axis=0, keepdims=True)

    @pl.loop(0, count)
    def _(i):
        conv_back(i)

        @pl.when(i == 0)
        def _():
            finish_states(count - 1)

        @pl.when(i == 1)
        def _():
            reduce_.third(0)

    def small_copy(source, target, at, device):
        return remote(source, target, r.qs.at[at], r.qr.at[at], device)

    core_copy = small_copy(r.bc, r.bc_in, 0, to_core)
    x_copy = small_copy(r.work.at[0], r.from_x, 1, late.to_x)
    y_copy = small_copy(r.work.at[1], r.from_y, 2, late.to_y)
    states_copy = small_copy(r.states_s.at[c], r.states_s.at[c], 7, to_core)

    def z_small(j, slot):
        return remote(
            r.work.at[2], r.from_z.at[slot], r.qs.at[3 + j], r.qr.at[3 + slot],
            (s + (j - z) * PLANE, c),
        )

    for t in range(taps + 1):
        begin = (t % 3) * 2 * nstate
        own = r.conv_rows[t : t + 1, inner:]
        row = 1 + t // 3
        r.bc[row : row + 1, begin : begin + nstate] = jnp.where(c == 0, own, 0.0)
        r.bc[row : row + 1, begin + nstate : begin + 2 * nstate] = jnp.where(c == 1, own, 0.0)
    core_copy.start()

    def gradient_block(source, at, target, start):
        total = None
        for i in range(count):
            term = dot(r.normed_s[i, HALO:], source[i, :, at : at + 256], TN)
            total = term if total is None else total + term
        target[:, start : start + 256] = total.astype(BF16)

    reduce_.finish()
    gradient_block(r.dy, 0, r.dout, 0)
    core_copy.wait_recv()
    r.work[0, 0:2] = r.small[0:2]
    r.work[0, 2 : 3 + taps] = r.conv_rows[: taps + 1, :inner]
    r.work[0, 3 + taps : 8] = jnp.zeros((5 - taps, inner), F32)
    r.work[0, 8:16] = r.bc[...] + r.bc_in[...]
    x_copy.start()
    gradient_block(r.dy, 256, r.dout, 256)
    late.begin(0)
    gradient_block(r.dy, 512, r.dgate, 0)
    gradient_block(r.gtail, 0, r.dgate, 256)
    late.begin(1)

    def tokens_back(i):
        swap_part(i).wait_recv()
        swap_out(i).wait_recv()
        own_tok = r.tok[i].astype(F32)
        tok = either(c, own_tok, r.tok_in[i].astype(F32))
        scale = lax.rsqrt(jnp.mean(tok * tok, axis=-1, keepdims=True) + EPSILON)
        unit = tok * scale
        grad_normed = r.normal[i].astype(F32) + r.low[i].astype(F32)
        grad = grad_normed * r.prm[GAIN : GAIN + 1, : 2 * half]
        r.ginputs[...] = scale * (grad - unit * jnp.mean(grad * unit, axis=-1, keepdims=True))
        r.full[i, :, :half] = r.g[i].astype(F32) + r.ginputs[:, side]
        store_grad(i).start()
        r.g_in[i] = (own_tok + (r.gate[i, :, :half] + r.out_in[i].astype(F32))).astype(BF16)
        store_mixed(i).start()

    @pl.loop(0, count)
    def _(i):
        tokens_back(i)

        @pl.when(i == 0)
        def _():
            x_copy.wait_recv()
            r.work[1] = r.work[0] + r.from_x[...]
            y_copy.start()

        @pl.when(i == 2)
        def _():
            y_copy.wait_recv()
            r.work[2] = r.work[1] + r.from_y[...]
            for j in range(LINE):
                pl.when(z != j)(z_small(j, z).start)
            r.from_z[z] = r.work[2]

    late.second(3, -3, 2, -2)
    late.third(3, -3)
    late.second(1, -1)
    late.third(2, -2)
    late.second(0)
    late.third(1, -1)
    late.third(0, only=(1,))
    r.states_s[c] = r.g_x[:, inner : inner + nstate]
    states_copy.start()
    late.third(0, only=(0,))
    for j in range(LINE):
        pl.when(z != j)(z_small(j, j).wait_recv)
    r.sums_out[...] = (r.from_z[0] + r.from_z[1]) + (r.from_z[2] + r.from_z[3])
    states_copy.wait()
    r.states[...] = r.states_s[...]
    core_copy.wait_send()
    x_copy.wait_send()
    y_copy.wait_send()
    for j in range(LINE):
        pl.when(z != j)(z_small(j, z).wait_send)
    late.finish()
    suffix.finish()

    @pl.loop(0, count)
    def _(i):
        swap_sums(i).wait_send()
        swap_out(i).wait_send()
        swap_states(i).wait_send()
        pl.when(prv)(send_edge(i).wait_send)
        swap_part(i).wait_send()
        store_grad(i).wait()
        store_mixed(i).wait()


LOCAL_REFS = tuple(dict(kept=0, mid_send=0))
LATE_REFS = tuple(n if n in LOCAL_REFS else "l" + n for n in REDUCE_REFS)
SECOND_REFS = tuple("s" + n for n in GATHER_REFS)
SHARED_REFS = tuple(dict(total=0, leaving=0, staged=0))
SUFFIX_REFS = tuple(n if n in SHARED_REFS else "s" + n for n in SCAN_REFS)


def main_call(sizes, total_inner, tok, g, doc, prm, w1, w2):
    length, inner, nstate, size, taps = sizes
    count, _, half = tok.shape
    model = 2 * half
    channels = inner + 2 * nstate
    rows = w1.shape[0]
    wide = inner + nstate + LANES
    ins = dict(
        tok=(tok, INSIDE), g=(g, INSIDE), doc=(doc, INSIDE), prm=(prm, INSIDE),
        w1=(w1, ANYWHERE), w2=(w2, ANYWHERE),
    )
    outs = dict(
        mixed=(shape((count, length, half), BF16), ANYWHERE),
        tokens_grad=(shape((count, length, half), F32), ANYWHERE),
        g_out=(shape((rows, inner), F32), INSIDE),
        g_gate=(shape((rows, inner), F32), INSIDE),
        g_x=(shape((rows, wide), F32), INSIDE),
        states=(shape((2, rows, nstate), F32), INSIDE),
        sums_out=(shape((16, inner), F32), INSIDE),
    )

    def vmem(*dims, dtype=F32):
        return pltpu.VMEM(dims, dtype)

    def low(*dims):
        return pltpu.VMEM(dims, BF16)

    scratch = dict(
        g_in=low(count, length, half),
        tok_in=low(count, length, half),
        out_in=low(count, length, half),
        edge_in=vmem(count, EDGE, inner + nstate),
        small=vmem(8, inner),
        gtail=low(count, length, nstate + LANES),
        gext=vmem(length + EDGE, inner + nstate),
        conv_rows=vmem(8, inner + nstate),
        states_s=vmem(2, rows, nstate),
        bc=vmem(8, inner),
        bc_in=vmem(8, inner),
        work=vmem(3, 16, inner),
        from_x=vmem(16, inner),
        from_y=vmem(16, inner),
        from_z=vmem(LINE, 16, inner),
        qs=dma(8),
        qr=dma(8),
        halo=low(count, HALO, model),
        w=low(model, w1.shape[1]),
        w2_full=low(model, 2 * inner),
        normed_s=low(count, HALO + length, model),
        xs_s=low(count, HALO + length, channels),
        act=low(count, length, channels),
        aux=vmem(count, length, 4 * LANES),
        low=low(count, length, inner),
        dec=vmem(count, HEAD_ROWS, LANES),
        state=low(count, inner, nstate),
        hin=low(count, inner, nstate),
        prior=low(count, inner, nstate),
        later=low(count, inner, nstate),
        full=vmem(count, length, inner),
        gate=vmem(count, length, inner),
        gn=vmem(count, length, inner),
        sums=vmem(count, EDGE, length),
        sums_in=vmem(count, EDGE, length),
        normal=low(count, length, inner),
        dy=low(count, length, inner),
        ggate_s=low(count, length, inner),
        osend=low(count, length, half),
        dout=low(model, inner),
        dgate=low(model, inner),
        ext=vmem(HALO + length, channels),
        ginputs=vmem(length, inner),
        bsend=low(count, length, nstate),
        brecv=low(count, length, nstate),
        edge=vmem(count, EDGE, inner + nstate),
        ss=dma(7, count),
        rs=dma(7, count),
        hs=dma(2),
        hr=dma(2),
        store=dma(2, count),
    )
    scan = Scan.scratch(count, inner, nstate, HEAD_ROWS)
    gather = Gather.semaphores(2)
    scratch.update(zip(SUFFIX_REFS, scan.values()))
    scratch.update(scan)
    scratch.update(gather)
    scratch.update(zip(SECOND_REFS, gather.values()))
    scratch.update(zip(LATE_REFS, Reduce.scratch(2, rows, wide).values()))
    scratch.update(Reduce.scratch(2, rows, 2 * inner))
    return fused_call(
        functools.partial(main_body, sizes, total_inner), None, ins, outs, scratch, 1, "main"
    )


def fused_layer(sizes, total_inner, heads, tok, g, doc, prm, w, w2):
    length, inner, nstate, size, taps = sizes
    model = 2 * tok.shape[2]
    m = main_call(sizes, total_inner, tok, g, doc, prm, w, w2)
    sums = m.sums_out
    shared = sums[9:11].reshape(-1)[: (taps + 1) * 2 * nstate].reshape(taps + 1, 2 * nstate)
    return (
        m.mixed,
        m.tokens_grad,
        sums[8, :model],
        jnp.stack([m.g_gate, m.g_x[:, :inner]], axis=1),
        jnp.concatenate([m.states[0], m.states[1]], axis=1),
        m.g_x[:, inner + nstate : inner + nstate + heads],
        sums[2 : 2 + taps],
        sums[2 + taps],
        shared[:taps],
        shared[taps],
        sums[1, LANES : LANES + heads],
        sums[1, 2 * LANES : 2 * LANES + heads],
        sums[1, :heads],
        sums[0],
        m.g_out.T,
    )


def shards(
    tokens, doc_starts, norm_gain, input_gate_features, input_state_weight, input_step_weight,
    conv_taps_x, conv_bias_x, conv_taps_bc, conv_bias_bc, step_bias, decay_log, skip_gain,
    inner_gain, output_projection, out_grad,
):
    micro, seqs, length, half = tokens.shape
    count = micro * seqs
    model = 2 * half
    heads = step_bias.shape[0]
    inner = inner_gain.shape[0]
    size = inner // heads
    nstate = conv_taps_bc.shape[1] // 2
    taps = conv_taps_x.shape[0]
    channels = inner + 2 * nstate
    rows = input_gate_features.shape[0]
    total_inner = inner * lax.axis_size("head")
    sizes = (length, inner, nstate, size, taps)
    core = lax.axis_index("head")

    tok = tokens.reshape(count, length, half)
    g = out_grad.reshape(count, length, half)
    doc = jnp.broadcast_to(
        doc_starts.reshape(count, 1, length).astype(F32), (count, 8, length)
    )

    def row(v):
        return jnp.pad(v, (0, channels - v.shape[0]))[None]

    prm = jnp.concatenate(
        [
            row(norm_gain),
            row(inner_gain),
            row(jnp.repeat(skip_gain, size)),
            row(jnp.concatenate([conv_bias_x, conv_bias_bc])),
            row(step_bias),
            row(-jnp.exp(decay_log)),
            jnp.concatenate([conv_taps_x, conv_taps_bc], axis=1),
        ],
        axis=0,
    )
    prm = jnp.pad(prm, ((0, 16 - prm.shape[0]), (0, 0)))
    w_own = jnp.concatenate(
        [
            input_gate_features.reshape(rows, 2 * inner),
            input_state_weight,
            jnp.pad(input_step_weight, ((0, 0), (0, LANES - heads))),
        ],
        axis=1,
    )
    w_out_own = output_projection.T

    if lax.axis_size("seq") == PLANE * LINE and lax.axis_size("head") == 2:
        outputs = fused_layer(
            sizes, total_inner, heads, tok, g, doc, prm, w_own[:, inner:],
            jnp.concatenate([w_own[:, :inner], w_out_own], axis=1),
        )
        return tuple(
            o.reshape(tokens.shape) if n < 2 else o for n, o in enumerate(outputs)
        )

    w_in, w_out, tok_full, g_full, halo = plain_gather(
        w_own, w_out_own, tok, g, tok[:, length - HALO :]
    )
    grid = (count,)
    outs = [
        shape((count, length, model), BF16),
        shape((count, length, inner), F32),
        shape((count, HALO + length, channels), BF16),
        shape((count, length, channels), F32),
        shape((count, length, channels), BF16),
        shape((count, length, inner), F32),
        shape((count, inner, nstate), BF16),
        shape((count, length, 5 * LANES), F32),
        shape((count, HEAD_ROWS, LANES), F32),
    ]
    normed, gate, xs, pre, act, scan, state, aux, dec = call(
        functools.partial(forward_kernel, sizes),
        grid,
        [per_seq(tok_full), per_seq(halo), per_seq(doc), whole(prm), whole(w_in)],
        [per_seq(o) for o in outs],
        outs,
        [pltpu.VMEM((HALO + length, channels), F32)],
        name="forward",
    )(tok_full, halo, doc, prm, w_in)

    hin = plain_scan(state, dec, size, False)

    outs = [
        shape((count, length, inner), F32),
        shape((count, length, inner), F32),
        shape((count, length, LANES), F32),
    ]
    ins = (scan, act, aux, gate, hin, g_full)
    full, grad_norm, sums = call(
        functools.partial(gate_kernel, sizes),
        grid,
        [per_seq(a) for a in ins] + [whole(prm), whole(w_out)],
        [per_seq(o) for o in outs],
        outs,
        name="gate",
    )(*ins, prm, w_out)

    sums_in = swap_heads(sums)

    outs = [
        shape((count, length, half), F32),
        shape((count, length, half), BF16),
        shape((count, length, inner), BF16),
        shape((count, length, inner), BF16),
        shape((count, inner, nstate), BF16),
        shape((8, inner), F32),
        shape((model, inner), BF16),
        shape((model, inner), BF16),
    ]
    ins = (full, act, aux, gate, grad_norm, sums, sums_in, g_full, normed)
    keep, send, dy, ggate, prior, small_out, dout, dgate = call(
        functools.partial(output_kernel, sizes, total_inner),
        grid,
        [per_seq(a) for a in ins] + [whole(prm), whole(w_out)],
        [per_seq(o) for o in outs[:5]] + [whole(o) for o in outs[5:]],
        outs,
        [
            pltpu.VMEM((model, inner), F32),
            pltpu.VMEM((model, inner), F32),
            pltpu.VMEM((length, model), F32),
        ],
        name="output",
    )(*ins, prm, w_out)

    mixed = (tok.astype(F32) + (keep + swap_heads(send).astype(F32))).astype(BF16)
    later = plain_scan(prior, dec, size, True)

    outs = [
        shape((count, length, inner), F32),
        shape((count, length, nstate), F32),
        shape((count, length, nstate), BF16),
        shape((count, length, LANES), F32),
        shape((8, LANES), F32),
        shape((count, EDGE, inner), F32),
        shape((count, EDGE, nstate), F32),
    ]
    ins = (full, act, aux, dy, hin, later, state, doc, pre)
    gcx, own, other, gpre, small_scan, edge, slope = call(
        functools.partial(backward_kernel, sizes),
        grid,
        [per_seq(a) for a in ins] + [whole(prm)],
        [per_seq(o) if len(o.shape) == 3 else whole(o) for o in outs],
        outs,
        [pltpu.VMEM((length, length), F32)],
        name="backward",
    )(*ins, prm)

    recv, edge_in, edge_state = plain_states(other, own, slope, edge)

    outs = [
        shape((count, length, model), BF16),
        shape((model, inner + nstate + LANES), BF16),
        shape((8, inner + nstate), F32),
    ]
    ins = (gcx, own, recv, edge_in, edge_state, pre, xs, gpre, ggate, normed)
    part, dx, small_conv = call(
        functools.partial(conv_kernel, sizes),
        grid,
        [per_seq(a) for a in ins] + [whole(prm), whole(w_in)],
        [per_seq(outs[0]), whole(outs[1]), whole(outs[2])],
        outs,
        [
            pltpu.VMEM((model, inner + nstate + LANES), F32),
            pltpu.VMEM((HALO + length, inner + nstate), F32),
            pltpu.VMEM((length + EDGE, inner + nstate), F32),
        ],
        name="conv",
    )(*ins, prm, w_in)

    part_in = swap_heads(part)

    outs = [shape((count, length, half), F32), shape((8, model), F32)]
    ins = (tok_full, part, part_in, g)
    tokens_grad, small_norm = call(
        functools.partial(tokens_kernel, sizes),
        grid,
        [per_seq(a) for a in ins] + [whole(prm)],
        [per_seq(outs[0]), whole(outs[1])],
        outs,
        [pltpu.VMEM((length, model), F32)],
        name="tokens",
    )(*ins, prm)

    small = jnp.concatenate(
        [
            row(small_norm[0]),
            row(small_out[0]),
            row(small_out[1]),
            row(jnp.concatenate([small_scan[0], small_scan[1]])),
            jnp.pad(small_conv[: taps + 1, :inner], ((0, 0), (0, channels - inner))),
            jnp.zeros((16 - 5 - taps, channels), F32),
        ],
        axis=0,
    )
    own_states = small_conv[:, inner:]
    shared = jnp.concatenate(
        [jnp.where(core == 0, own_states, 0.0), jnp.where(core == 1, own_states, 0.0)], axis=1
    )
    (g_out, g_gate, g_x), small, shared = plain_sum((dout, dgate, dx), small, shared)
    g_states = plain_both(g_x[:, inner : inner + nstate])
    return (
        mixed.reshape(tokens.shape),
        tokens_grad.reshape(tokens.shape),
        small[0, :model],
        jnp.stack([g_gate, g_x[:, :inner]], axis=1),
        g_states,
        g_x[:, inner + nstate : inner + nstate + heads],
        small[4 : 4 + taps, :inner],
        small[4 + taps, :inner],
        shared[:taps],
        shared[taps],
        small[3, :heads],
        small[3, LANES : LANES + heads],
        small[2, :inner].reshape(heads, size).sum(axis=1),
        small[1, :inner],
        g_out.T,
    )


def solution(mesh):
    placed = (
        P(None, None, "seq", "head"),
        P(None, None, "seq"),
        P(),
        P("seq", None, "head"),
        P("seq", None),
        P("seq", "head"),
        P(None, "head"),
        P("head"),
        P(),
        P(),
        P("head"),
        P("head"),
        P("head"),
        P("head"),
        P("head", "seq"),
        P(None, None, "seq", "head"),
    )
    return jax.shard_map(
        shards,
        mesh=mesh,
        in_specs=placed,
        out_specs=(
            P(None, None, "seq", "head"),
            P(None, None, "seq", "head"),
            P(),
            P("seq", None, "head"),
            P("seq", None),
            P("seq", "head"),
            P(None, "head"),
            P("head"),
            P(),
            P(),
            P("head"),
            P("head"),
            P("head"),
            P("head"),
            P("head", "seq"),
        ),
        check_vma=False,
    )
```

```python
import functools

import jax
import jax.numpy as jnp
from jax import lax
from jax.experimental import pallas as pl
from jax.experimental.pallas import tpu as pltpu
from jax.sharding import PartitionSpec as P

F32 = jnp.float32
BF16 = jnp.bfloat16
EPSILON = 1e-05
MASKED = -1e30
HALO = 16
EDGE = 8
HEAD_ROWS = 16
LANES = 128
MESH = pl.DeviceIdType.MESH
NN = ((1,), (0,))
NT = ((1,), (1,))
TN = ((0,), (0,))
VMEM_LIMIT = 62 * 2**20

GAIN, INNER_GAIN, SKIP, BIAS, STEP_BIAS, RATE, TAPS = 0, 1, 2, 3, 4, 5, 6


def dot(a, b, dims=NN):
    return lax.dot_general(a, b, (dims, ((), ())), preferred_element_type=F32)


def split2(v):
    high = v.astype(BF16)
    return high, (v - high.astype(F32)).astype(BF16)


def split3(v):
    high = v.astype(BF16)
    rest = v - high.astype(F32)
    middle = rest.astype(BF16)
    return high, middle, (rest - middle.astype(F32)).astype(BF16)


def sigmoid(v):
    return 0.5 * jnp.tanh(0.5 * v) + 0.5


def softplus(v):
    return jnp.maximum(v, 0.0) + jnp.log1p(jnp.exp(-jnp.abs(v)))


def head_spread(inner, size):
    rows = lax.broadcasted_iota(jnp.int32, (LANES, inner), 0)
    columns = lax.broadcasted_iota(jnp.int32, (LANES, inner), 1)
    return jnp.where(rows == columns // size, 1.0, 0.0).astype(BF16)


def expand(per_head, spread):
    high, low = split2(per_head)
    return dot(high, spread) + dot(low, spread)


def head_sums(wide, spread):
    high, low = split2(wide)
    return dot(high, spread, NT) + dot(low, spread, NT)


def triangle(length, upper=False):
    rows = lax.broadcasted_iota(jnp.int32, (length, length), 0)
    columns = lax.broadcasted_iota(jnp.int32, (length, length), 1)
    kept = rows <= columns if upper else rows >= columns
    return kept, jnp.where(kept, 1.0, 0.0).astype(BF16)


def running_sum(ones, v):
    a, b, c = split3(v)
    return dot(ones, a) + dot(ones, b) + dot(ones, c)


def doc_numbers(doc, ones):
    flags = doc.astype(BF16)
    return dot(ones, flags, NT)[:, :1], dot(flags, ones, NT)[:1]


def call(kernel, grid, in_specs, out_specs, out_shape, scratch=(), name=None, flops=10**9):
    return pl.pallas_call(
        kernel,
        grid=grid,
        in_specs=in_specs,
        out_specs=out_specs,
        out_shape=out_shape,
        scratch_shapes=list(scratch),
        compiler_params=pltpu.CompilerParams(
            vmem_limit_bytes=VMEM_LIMIT, dimension_semantics=("arbitrary",) * len(grid)
        ),
        cost_estimate=pl.CostEstimate(flops=flops, bytes_accessed=10**7, transcendentals=0),
        name=name,
    )


def whole(array):
    rank = len(array.shape)
    return pl.BlockSpec(array.shape, lambda i: (0,) * rank)


def per_seq(array):
    rank = len(array.shape)
    return pl.BlockSpec((1,) + tuple(array.shape[1:]), lambda i: (i,) + (0,) * (rank - 1))


def shape(dims, dtype):
    return jax.ShapeDtypeStruct(tuple(dims), dtype)


def forward_kernel(
    sizes, tok, halo, doc, prm, w, normed_o, gate_o, xs_o, pre_o, act_o, scan_o, state_o, aux_o,
    dec_o, ext,
):
    length, inner, nstate, size, taps = sizes
    channels = inner + 2 * nstate
    first = lax.axis_index("seq") == 0
    edge = jnp.where(first, 0.0, halo[0].astype(F32))
    x = jnp.concatenate([edge, tok[0].astype(F32)], axis=0)
    scale = lax.rsqrt(jnp.mean(x * x, axis=-1, keepdims=True) + EPSILON)
    normed = (x * scale * prm[GAIN : GAIN + 1, : x.shape[1]]).astype(BF16)
    normed_o[0] = normed[HALO:]
    gate_o[0] = dot(normed[HALO:], w[:, :inner])
    xs = dot(normed, w[:, inner : inner + channels]).astype(BF16)
    xs_o[0] = xs
    ext[...] = xs.astype(F32)
    pre = prm[BIAS : BIAS + 1, :channels]
    for k in range(taps):
        start = HALO - taps + 1 + k
        pre = pre + prm[TAPS + k : TAPS + k + 1, :channels] * ext[start : start + length]
    pre_o[0] = pre
    act = (pre * sigmoid(pre)).astype(BF16)
    act_o[0] = act
    step_pre = (
        dot(normed[HALO:], w[:, inner + channels :]) + prm[STEP_BIAS : STEP_BIAS + 1, :LANES]
    )
    step = softplus(step_pre)
    kept, ones = triangle(length)
    log_decay = running_sum(ones, step * prm[RATE : RATE + 1, :LANES])
    doc_col, doc_row = doc_numbers(doc[0], ones)
    entry = jnp.where(doc_col == 0.0, jnp.exp(log_decay), 0.0)
    last = log_decay[length - 1 :]
    tail = jnp.where(doc_col == doc_col[length - 1 :], jnp.exp(last - log_decay), 0.0)
    aux_o[0, :, 0:LANES] = log_decay
    aux_o[0, :, LANES : 2 * LANES] = step
    aux_o[0, :, 2 * LANES : 3 * LANES] = step_pre
    aux_o[0, :, 3 * LANES : 4 * LANES] = entry
    aux_o[0, :, 4 * LANES :] = tail
    spread = head_spread(inner, size)
    values = act[:, :inner].astype(F32)
    inputs = values * expand(step, spread)
    low_inputs = inputs.astype(BF16)
    in_state = act[:, inner : inner + nstate]
    out_state = act[:, inner + nstate :]
    state_o[0] = dot((inputs * expand(tail, spread)).astype(BF16), in_state, TN).astype(BF16)
    scores = dot(out_state, in_state, NT)
    closed = jnp.where(kept & (doc_col == doc_row), 0.0, MASKED)
    log_rows = log_decay.T
    whole_decay = jnp.where(doc_row[:, length - 1 :] == 0.0, jnp.exp(log_rows[:HEAD_ROWS, length - 1 :]), 0.0)
    dec_o[0] = jnp.broadcast_to(whole_decay, (HEAD_ROWS, LANES))
    left = lax.broadcasted_iota(jnp.int32, (length, LANES), 1) < size
    for pair in range(inner // LANES):
        columns = slice(pair * LANES, (pair + 1) * LANES)
        part = low_inputs[:, columns]
        total = None
        for side in range(2):
            h = 2 * pair + side
            decay = jnp.exp(log_decay[:, h : h + 1] - log_rows[h : h + 1] + closed)
            own = jnp.where(left if side == 0 else ~left, part, jnp.zeros_like(part))
            term = dot((scores * decay).astype(BF16), own)
            total = term if total is None else total + term
        scan_o[0, :, columns] = total


def gate_kernel(sizes, scan, act, aux, gate, hin, g, prm, wout, full_o, gn_o, sums_o):
    length, inner, nstate, size, taps = sizes
    spread = head_spread(inner, size)
    values = act[0, :, :inner].astype(F32)
    out_state = act[0, :, inner + nstate :]
    scanned = scan[0] + dot(out_state, hin[0], NT) * expand(aux[0, :, 3 * LANES : 4 * LANES], spread)
    full_o[0] = scanned
    mixed = scanned + prm[SKIP : SKIP + 1, :inner] * values
    gated = mixed * (gate[0] * sigmoid(gate[0]))
    grad_norm = dot(g[0], wout[...])
    gn_o[0] = grad_norm
    squares = jnp.sum(gated * gated, axis=-1, keepdims=True)
    cross = jnp.sum(
        grad_norm * prm[INNER_GAIN : INNER_GAIN + 1, :inner] * gated, axis=-1, keepdims=True
    )
    lane = lax.broadcasted_iota(jnp.int32, (length, LANES), 1)
    sums_o[0] = jnp.where(lane == 0, squares, jnp.where(lane == 1, cross, 0.0))


def output_kernel(
    sizes, total_inner, full, act, aux, gate, gn, sums, sums_in, g, normed, prm, wout,
    keep_o, send_o, dy_o, ggate_o, prior_o, small_o, dout_o, dgate_o, acc_out, acc_gate, wide,
):
    length, inner, nstate, size, taps = sizes
    at = pl.program_id(0)
    spread = head_spread(inner, size)
    values = act[0, :, :inner].astype(F32)
    out_state = act[0, :, inner + nstate :]
    mixed = full[0] + prm[SKIP : SKIP + 1, :inner] * values
    z = gate[0]
    sig = sigmoid(z)
    swish = z * sig
    gated = mixed * swish
    both = sums[0] + sums_in[0]
    inner_scale = lax.rsqrt(both[:, 0:1] / total_inner + EPSILON)
    gain = prm[INNER_GAIN : INNER_GAIN + 1, :inner]
    unit = gated * inner_scale
    normal = (unit * gain).astype(BF16)
    wide[...] = dot(normal, wout[...], NT)
    half = wide.shape[1] // 2
    core = lax.axis_index("head")
    keep_o[0] = wide[:, pl.ds(pl.multiple_of(core * half, LANES), half)]
    send_o[0] = wide[:, pl.ds(pl.multiple_of((1 - core) * half, LANES), half)].astype(BF16)
    grad_norm = gn[0]
    grad_inner = jnp.sum(grad_norm * unit, axis=0, keepdims=True)
    grad_gated = inner_scale * (grad_norm * gain) - unit * (
        inner_scale * inner_scale * (both[:, 1:2] / total_inner)
    )
    dy = grad_gated * swish
    low_dy = dy.astype(BF16)
    dy_o[0] = low_dy
    ggate = (grad_gated * mixed * (sig * (1.0 + z * (1.0 - sig)))).astype(BF16)
    ggate_o[0] = ggate
    grad_skip = jnp.sum(dy * values, axis=0, keepdims=True)
    entry = expand(aux[0, :, 3 * LANES : 4 * LANES], spread)
    prior_o[0] = dot((dy * entry).astype(BF16), out_state, TN).astype(BF16)
    rows = jnp.concatenate([grad_inner, grad_skip, jnp.zeros((6, inner), F32)], axis=0)
    term_out = dot(g[0], normal, TN)
    term_gate = dot(normed[0], ggate, TN)

    @pl.when(at == 0)
    def _():
        small_o[...] = rows
        acc_out[...] = term_out
        acc_gate[...] = term_gate

    @pl.when(at > 0)
    def _():
        small_o[...] += rows
        acc_out[...] += term_out
        acc_gate[...] += term_gate

    @pl.when(at == pl.num_programs(0) - 1)
    def _():
        dout_o[...] = acc_out[...].astype(BF16)
        dgate_o[...] = acc_gate[...].astype(BF16)


def backward_kernel(
    sizes, full, act, aux, dy, hin, later, state, doc, pre, prm,
    gcx_o, own_o, send_o, gpre_o, small_o, edge_o, slope_o, dcb,
):
    length, inner, nstate, size, taps = sizes
    at = pl.program_id(0)
    core = lax.axis_index("head")
    spread = head_spread(inner, size)
    log_decay = aux[0, :, 0:LANES]
    step = aux[0, :, LANES : 2 * LANES]
    step_pre = aux[0, :, 2 * LANES : 3 * LANES]
    entry = aux[0, :, 3 * LANES : 4 * LANES]
    tail = aux[0, :, 4 * LANES :]
    values = act[0, :, :inner].astype(F32)
    in_state = act[0, :, inner : inner + nstate]
    out_state = act[0, :, inner + nstate :]
    low_dy = dy[0]
    wide_dy = low_dy.astype(F32)
    step_wide = expand(step, spread)
    tail_wide = expand(tail, spread)
    entry_wide = expand(entry, spread)
    inputs = values * step_wide
    low_inputs = inputs.astype(BF16)
    kept, ones = triangle(length)
    upper, ones_upper = triangle(length, True)
    doc_col, doc_row = doc_numbers(doc[0], ones)
    closed = jnp.where(upper & (doc_col == doc_row), 0.0, MASKED)
    scores = dot(in_state, out_state, NT)
    log_rows = log_decay.T
    left = lax.broadcasted_iota(jnp.int32, (length, LANES), 1) < size
    grad_inputs = tail_wide * dot(in_state, later[0], NT)
    parts = []
    for pair in range(inner // LANES):
        columns = slice(pair * LANES, (pair + 1) * LANES)
        pair_dy = low_dy[:, columns]
        pair_in = low_inputs[:, columns]
        total = grad_inputs[:, columns]
        for side in range(2):
            h = 2 * pair + side
            chosen = left if side == 0 else ~left
            own_dy = jnp.where(chosen, pair_dy, jnp.zeros_like(pair_dy))
            decay = jnp.exp(log_rows[h : h + 1] - log_decay[:, h : h + 1] + closed)
            total = total + dot((scores * decay).astype(BF16), own_dy)
            grad_decay = dot(pair_in, own_dy, NT) * decay
            if h == 0:
                dcb[...] = grad_decay
            else:
                dcb[...] += grad_decay
        parts.append(total)
    grad_inputs = jnp.concatenate(parts, axis=1)
    grad_scores = dcb[...]
    grad_in = dot(grad_scores.astype(BF16), out_state) + dot(
        (inputs * tail_wide).astype(BF16), later[0]
    )
    grad_out = dot(grad_scores.T.astype(BF16), in_state) + dot(
        (wide_dy * entry_wide).astype(BF16), hin[0]
    )
    entry_last = jnp.broadcast_to(entry[length - 1 :], (8, LANES))
    later_wide = later[0].astype(F32)
    lane_ones = jnp.ones((8, nstate), BF16)
    through = head_sums(
        sum(dot(lane_ones, piece, NT) for piece in split2(later_wide * hin[0].astype(F32))), spread
    )
    born = head_sums(
        sum(dot(lane_ones, piece, NT) for piece in split2(later_wide * state[0].astype(F32))), spread
    )
    ending = (born + entry_last * through)[:1]
    grad_log = head_sums(wide_dy * full[0], spread) - head_sums(
        low_inputs.astype(F32) * grad_inputs, spread
    )
    grad_rate_step = running_sum(ones_upper, grad_log) + ending
    rate = prm[RATE : RATE + 1, :LANES]
    grad_step = head_sums(values * grad_inputs, spread) + rate * grad_rate_step
    gpre = grad_step * sigmoid(step_pre)
    lane = lax.broadcasted_iota(jnp.int32, (length, LANES), 1)
    gpre = jnp.where(lane < inner // size, gpre, 0.0)
    gpre_o[0] = gpre
    grad_values = step_wide * grad_inputs + prm[SKIP : SKIP + 1, :inner] * wide_dy
    px = pre[0, :, :inner]
    sig = sigmoid(px)
    gcx = grad_values * (sig * (1.0 + px * (1.0 - sig)))
    gcx_o[0] = gcx
    edge_o[0] = gcx[:EDGE]
    is_first = core == 0
    own_o[0] = jnp.where(is_first, grad_in, grad_out)
    send_o[0] = jnp.where(is_first, grad_out, grad_in).astype(BF16)
    ps = pre[0, :EDGE, pl.ds(pl.multiple_of(inner + core * nstate, LANES), nstate)]
    sig = sigmoid(ps)
    slope_o[0] = sig * (1.0 + ps * (1.0 - sig))
    rows = jnp.concatenate(
        [
            jnp.sum(gpre, axis=0, keepdims=True),
            rate * jnp.sum(step * grad_rate_step, axis=0, keepdims=True),
            jnp.zeros((6, LANES), F32),
        ],
        axis=0,
    )

    @pl.when(at == 0)
    def _():
        small_o[...] = rows

    @pl.when(at > 0)
    def _():
        small_o[...] += rows


def conv_kernel(
    sizes, gcx, own, recv, edge, edge_state, pre, xs, gpre, ggate, normed, prm, w,
    part_o, dx_o, small_o, acc, ext, gext,
):
    length, inner, nstate, size, taps = sizes
    at = pl.program_id(0)
    core = lax.axis_index("head")
    last = lax.axis_index("seq") == lax.axis_size("seq") - 1
    mine = pl.ds(pl.multiple_of(inner + core * nstate, LANES), nstate)
    channels = inner + nstate
    ps = pre[0, :, mine]
    sig = sigmoid(ps)
    gst = (own[0] + recv[0].astype(F32)) * (sig * (1.0 + ps * (1.0 - sig)))
    gext[:length, :inner] = gcx[0]
    gext[:length, inner:] = gst
    gext[length:, :inner] = jnp.where(last, 0.0, edge[0])
    gext[length:, inner:] = jnp.where(last, 0.0, edge_state[0])
    ext[:, :inner] = xs[0, :, :inner].astype(F32)
    ext[:, inner:] = xs[0, :, mine].astype(F32)
    grad_conv = gext[:length]
    grad_in = None
    rows = []
    for k in range(taps):
        row = jnp.concatenate(
            [prm[TAPS + k : TAPS + k + 1, :inner], prm[TAPS + k : TAPS + k + 1, mine]], axis=1
        )
        term = row * gext[taps - 1 - k : taps - 1 - k + length]
        grad_in = term if grad_in is None else grad_in + term
        start = HALO - taps + 1 + k
        rows.append(jnp.sum(ext[start : start + length] * grad_conv, axis=0, keepdims=True))
    rows.append(jnp.sum(grad_conv, axis=0, keepdims=True))
    rows.append(jnp.zeros((8 - taps - 1, channels), F32))
    rows = jnp.concatenate(rows, axis=0)
    low = grad_in.astype(BF16)
    low_pre = gpre[0].astype(BF16)
    part = dot(ggate[0], w[:, :inner], NT)
    part = part + dot(low[:, :inner], w[:, inner : 2 * inner], NT)
    wst = w[:, pl.ds(pl.multiple_of(2 * inner + core * nstate, LANES), nstate)]
    part = part + dot(low[:, inner:], wst, NT)
    part = part + dot(low_pre, w[:, 2 * inner + 2 * nstate :], NT)
    part_o[0] = part.astype(BF16)
    stacked = jnp.concatenate([low, low_pre], axis=1)
    term = dot(normed[0], stacked, TN)

    @pl.when(at == 0)
    def _():
        small_o[...] = rows
        acc[...] = term

    @pl.when(at > 0)
    def _():
        small_o[...] += rows
        acc[...] += term

    @pl.when(at == pl.num_programs(0) - 1)
    def _():
        dx_o[...] = acc[...].astype(BF16)


def tokens_kernel(sizes, tok, part, recv, g, prm, out_o, small_o, wide):
    at = pl.program_id(0)
    core = lax.axis_index("head")
    x = tok[0].astype(F32)
    model = x.shape[1]
    scale = lax.rsqrt(jnp.mean(x * x, axis=-1, keepdims=True) + EPSILON)
    unit = x * scale
    grad_normed = part[0].astype(F32) + recv[0].astype(F32)
    r = grad_normed * prm[GAIN : GAIN + 1, :model]
    wide[...] = scale * (r - unit * jnp.mean(r * unit, axis=-1, keepdims=True))
    half = model // 2
    out_o[0] = g[0].astype(F32) + wide[:, pl.ds(pl.multiple_of(core * half, LANES), half)]
    rows = jnp.concatenate(
        [jnp.sum(grad_normed * unit, axis=0, keepdims=True), jnp.zeros((7, model), F32)], axis=0
    )

    @pl.when(at == 0)
    def _():
        small_o[...] = rows

    @pl.when(at > 0)
    def _():
        small_o[...] += rows


def swap_heads(v):
    return lax.ppermute(v, "head", [(0, 1), (1, 0)])


def shift(v, distance):
    devices = range(lax.axis_size("seq"))
    return lax.ppermute(
        v, "seq", [(i - distance, i) for i in devices if i - distance in devices]
    )


def plain_gather(w_in, w_out, tokens, grads, tails):
    return (
        lax.all_gather(w_in, "seq", axis=0, tiled=True),
        lax.all_gather(w_out, "seq", axis=0, tiled=True),
        lax.all_gather(tokens, "head", axis=2, tiled=True),
        lax.all_gather(grads, "head", axis=2, tiled=True),
        lax.all_gather(shift(tails, 1), "head", axis=2, tiled=True),
    )


def plain_scan(state, decay, size, backward):
    count, place = lax.axis_size("seq"), lax.axis_index("seq")
    heads = state.shape[1] // size
    wide = jnp.repeat(decay[:, :heads, 0], size, axis=1)[..., None]
    states = lax.all_gather(state, "seq")
    decays = lax.all_gather(wide, "seq")

    def one(k, carried):
        at = count - 1 - k if backward else k
        reached = at > place if backward else at < place
        return jnp.where(reached, decays[at] * carried + states[at].astype(F32), carried)

    return lax.fori_loop(0, count, one, jnp.zeros(state.shape, F32)).astype(BF16)


def plain_states(send, own, slope, edge):
    recv = swap_heads(send)
    mine = (own[:, :EDGE] + recv[:, :EDGE].astype(F32)) * slope
    return recv, shift(edge, -1), shift(mine, -1)


def plain_sum(pieces, small, shared):
    totals = [
        lax.psum_scatter(p.astype(F32), "seq", scatter_dimension=0, tiled=True) for p in pieces
    ]
    shared = lax.psum(shared, ("seq", "head"))
    return totals, lax.psum(small, "seq"), shared


def plain_both(v):
    return lax.all_gather(v, "head", axis=1, tiled=True)


PLANE = 4
LINE = 4
OFFSETS = (0, -1, 1, -2, 2, -3, 3)


def place():
    s, c = lax.axis_index("seq"), lax.axis_index("head")
    return s, c, s // PLANE, (s // 2) % 2, s % 2


def remote(src, dst, send_sem, recv_sem, device):
    return pltpu.make_async_remote_copy(
        src_ref=src,
        dst_ref=dst,
        send_sem=send_sem,
        recv_sem=recv_sem,
        device_id=device,
        device_id_type=MESH,
    )


def greet(relations):
    barrier = pltpu.get_barrier_semaphore()
    total = 0
    for exists, device in relations:
        if exists is True:
            pl.semaphore_signal(barrier, inc=1, device_id=device, device_id_type=MESH)
            total = total + 1
        else:
            pl.when(exists)(
                functools.partial(
                    pl.semaphore_signal, barrier, inc=1, device_id=device, device_id_type=MESH
                )
            )
            total = total + jnp.where(exists, 1, 0)
    pl.semaphore_wait(barrier, total)


def comm_call(kernel, ins, outs, scratch, collective, name, anywhere=False):
    space = pl.ANY if anywhere else pltpu.VMEM
    return pl.pallas_call(
        kernel,
        in_specs=[pl.BlockSpec(memory_space=space) for _ in ins],
        out_specs=[pl.BlockSpec(memory_space=space) for _ in outs],
        out_shape=outs,
        scratch_shapes=list(scratch),
        compiler_params=pltpu.CompilerParams(
            collective_id=collective, has_side_effects=True, vmem_limit_bytes=VMEM_LIMIT
        ),
        name=name,
    )(*ins)


def dma(*dims):
    return pltpu.SemaphoreType.DMA(dims)


SUM_OFFSETS = (3, -3, 2, -2, 1, -1, 0)


class Refs:
    def __init__(self, names, refs):
        self.__dict__.update(zip(names, refs))


def fused_call(body, steps, ins, outs, scratch, collective, name):
    names = list(ins) + list(outs) + list(scratch)

    def kernel(*refs):
        body(Refs(names, refs))

    results = pl.pallas_call(
        kernel,
        grid=(steps,) if steps else (),
        in_specs=[spec for _, spec in ins.values()],
        out_specs=[spec for _, spec in outs.values()],
        out_shape=[shaped for shaped, _ in outs.values()],
        scratch_shapes=list(scratch.values()),
        compiler_params=pltpu.CompilerParams(
            collective_id=collective,
            has_side_effects=True,
            vmem_limit_bytes=VMEM_LIMIT,
            dimension_semantics=("arbitrary",) if steps else None,
        ),
        name=name,
    )(*[array for array, _ in ins.values()])
    return Refs(list(outs), results)


ANYWHERE = pl.BlockSpec(memory_space=pl.ANY)
INSIDE = pl.BlockSpec(memory_space=pltpu.VMEM)


def stepped(array, index):
    rank = len(array.shape)
    return pl.BlockSpec((1,) + tuple(array.shape[1:]), lambda k: (index(k),) + (0,) * (rank - 1))


def during(first, count=4):
    return lambda k: jnp.clip(k - first, 0, count - 1)


def cyclic(last, count=4):
    return lambda k: jnp.where(k < last, k % count, count - 1)


def either(core, own, other):
    low = jnp.where(core == 0, own, other)
    return jnp.concatenate([low, jnp.where(core == 0, other, own)], axis=1)


LINE_X, LINE_Y, PLANE_X, PLANE_Y = range(4)


class Gather:
    def __init__(self, pieces, rows, sems):
        self.pieces, self.rows = pieces, rows
        self.local, self.zs, self.zr, self.as_, self.ar, self.bs, self.br = sems
        self.s, self.c, self.z, self.y, self.x = place()
        s, c = self.s, self.c
        self.up, self.down = self.z < LINE - 1, self.z > 0
        self.to_x, self.to_y = (s + 1 - 2 * self.x, c), (s + 2 - 4 * self.y, c)
        self.to_up, self.to_down = (s + PLANE, c), (s - PLANE, c)
        kinds = [piece[4] for piece in pieces]
        self.span = range(len(pieces))
        self.lines = [p for p in self.span if kinds[p] in (LINE_X, LINE_Y)]
        self.planes = [p for p in self.span if kinds[p] in (PLANE_X, PLANE_Y)]
        self.x_first = [kind in (LINE_X, PLANE_X) for kind in kinds]

    @staticmethod
    def semaphores(n):
        return dict(
            g0=dma(n), g1=dma(n, 2, 4), g2=dma(n, 4), g3=dma(n, 4), g4=dma(n, 4), g5=dma(n, 4, 2),
            g6=dma(n, 4, 2),
        )

    def at(self, p, index, count=1):
        src, dst, start, width, order = self.pieces[p]
        begin = pl.multiple_of(index * self.rows, 16)
        return dst.at[pl.ds(begin, count * self.rows), pl.ds(start, width)]

    def own(self, p):
        src, dst, start, width, order = self.pieces[p]
        return src.at[:, pl.ds(start, width)]

    def local_copy(self, p):
        return pltpu.make_async_copy(self.own(p), self.at(p, self.s), self.local.at[p])

    def block(self, p, zz):
        if p in self.planes:
            return self.at(p, zz * PLANE, PLANE)
        return self.at(p, zz * PLANE + self.y * 2 + self.x)

    def z_copy(self, p, off):
        zz = self.z + off
        dst = self.block(p, zz)
        src = self.own(p) if off == 0 and p in self.lines else dst
        step = abs(off)
        moves = []
        if off <= 0:
            sems = self.zs.at[p, 0, step], self.zr.at[p, zz]
            moves.append((self.up, remote(src, dst, *sems, self.to_up)))
        if off >= 0:
            sems = self.zs.at[p, 1, step], self.zr.at[p, zz]
            moves.append((self.down, remote(src, dst, *sems, self.to_down)))
        return moves

    def first_copy(self, p, off):
        zz = self.z + off
        dst = self.at(p, zz * PLANE + self.y * 2 + self.x)
        src = self.own(p) if off == 0 else dst
        device = self.to_x if self.x_first[p] else self.to_y
        return remote(src, dst, self.as_.at[p, zz], self.ar.at[p, zz], device)

    def second_copies(self, p, off):
        zz = self.z + off
        if self.x_first[p]:
            pair = self.at(p, zz * PLANE + self.y * 2, 2)
            return [remote(pair, pair, self.bs.at[p, zz, 0], self.br.at[p, zz, 0], self.to_y)]
        copies = []
        for k in range(2):
            block = self.at(p, zz * PLANE + k * 2 + self.x)
            copies.append(
                remote(block, block, self.bs.at[p, zz, k], self.br.at[p, zz, k], self.to_x)
            )
        return copies

    def exists(self, off):
        zz = self.z + off
        return (zz >= 0) & (zz < LINE)

    def begin(self):
        for p in self.span:
            if p in self.lines:
                for there, copy in self.z_copy(p, 0):
                    pl.when(there)(copy.start)
            self.first_copy(p, 0).start()
            self.local_copy(p).start()

    def z_arrived(self, *offs):
        for off in offs:

            @pl.when(self.exists(off))
            def _():
                for p in self.lines:
                    for there, copy in self.z_copy(p, off):
                        copy.wait_recv()
                        pl.when(there)(copy.start)
                    self.first_copy(p, off).start()

    def first_arrived(self, *offs):
        for off in offs:

            @pl.when(self.exists(off))
            def _():
                for p in self.lines:
                    if off == 0:
                        self.local_copy(p).wait()
                    self.first_copy(p, off).wait_recv()
                    for copy in self.second_copies(p, off):
                        copy.start()

    def plane_first(self):
        for p in self.planes:
            self.local_copy(p).wait()
            self.first_copy(p, 0).wait_recv()
            for copy in self.second_copies(p, 0):
                copy.start()

    def plane_second(self):
        for p in self.planes:
            for copy in self.second_copies(p, 0):
                copy.wait_recv()
            for there, copy in self.z_copy(p, 0):
                pl.when(there)(copy.start)

    def plane_arrived(self, *offs):
        for off in offs:

            @pl.when(self.exists(off))
            def _():
                for p in self.planes:
                    for there, copy in self.z_copy(p, off):
                        copy.wait_recv()
                        pl.when(there)(copy.start)

    def finish(self):
        for off in OFFSETS:

            @pl.when(self.exists(off))
            def _():
                for p in self.lines:
                    for copy in self.second_copies(p, off):
                        copy.wait()
                    self.first_copy(p, off).wait_send()
                for p in self.span:
                    for there, copy in self.z_copy(p, off):
                        pl.when(there)(copy.wait_send)

        for p in self.planes:
            self.first_copy(p, 0).wait_send()
            for copy in self.second_copies(p, 0):
                copy.wait_send()


class Scan:
    def __init__(self, backward, size, state, decay, out, refs):
        self.state, self.decay, self.out, self.size = state, decay, out, size
        (
            self.slots, self.rates, self.total, self.through, self.pair, self.pair_through,
            self.far, self.leaving, self.staged, self.s1, self.r1, self.s2, self.r2, self.zs,
            self.zr, self.s3, self.r3,
        ) = refs
        s, c, z, y, x = place()
        self.s, self.c, self.p = s, c, s % PLANE
        self.base = s - self.p
        self.order = tuple(range(PLANE - 1, -1, -1)) if backward else tuple(range(PLANE))
        self.rows = state.shape[1] // PLANE
        self.place = LINE - 1 - z if backward else z
        self.step = -PLANE if backward else PLANE

    @staticmethod
    def scratch(count, rows, nstate, heads):
        quarter = rows // PLANE
        return dict(
            slots=pltpu.VMEM((count, PLANE, quarter, nstate), BF16),
            rates=pltpu.VMEM((count, PLANE, heads, nstate), F32),
            total=pltpu.VMEM((count, quarter, nstate), F32),
            through=pltpu.VMEM((count, 8, nstate), F32),
            pair=pltpu.VMEM((count, quarter, nstate), BF16),
            pair_through=pltpu.VMEM((count, 8, nstate), F32),
            far=pltpu.VMEM((count, quarter, nstate), BF16),
            leaving=pltpu.VMEM((count, quarter, nstate), BF16),
            staged=pltpu.VMEM((count, PLANE, quarter, nstate), BF16),
            s1=dma(count, PLANE), r1=dma(count, PLANE),
            s2=dma(count, PLANE), r2=dma(count, PLANE),
            zs=dma(count, 3), zr=dma(count, 3),
            s3=dma(count, PLANE), r3=dma(count, PLANE),
        )

    def relations(self):
        plane = [(self.p != j, (self.base + j, self.c)) for j in range(PLANE)]
        s, c, at, step = self.s, self.c, self.place, self.step
        return plane + [
            (at > 0, (s - step, c)),
            (at < LINE - 1, (s + step, c)),
            (at == 1, (s + 2 * step, c)),
            (at == 3, (s - 2 * step, c)),
        ]

    def part(self, j):
        return pl.ds(pl.multiple_of(j * self.rows, 16), self.rows)

    def first(self, i, j, slot):
        device = (self.base + j, self.c)
        return [
            remote(
                self.state.at[i, self.part(j)], self.slots.at[i, slot],
                self.s1.at[i, j], self.r1.at[i, slot], device,
            ),
            remote(
                self.decay.at[i], self.rates.at[i, slot], self.s2.at[i, j], self.r2.at[i, slot],
                device,
            ),
        ]

    def to_pair(self, i):
        device = (self.s + self.step, self.c)
        return [
            remote(self.leaving.at[i], self.pair.at[i], self.zs.at[i, 0], self.zr.at[i, 0], device),
            remote(
                self.through.at[i], self.pair_through.at[i], self.zs.at[i, 1], self.zr.at[i, 1],
                device,
            ),
        ]

    def to_far(self, i, n):
        return remote(
            self.leaving.at[i], self.far.at[i], self.zs.at[i, 0 if n == 1 else 2],
            self.zr.at[i, 2], (self.s + n * self.step, self.c),
        )

    def last(self, i, j, quarter):
        return remote(
            self.staged.at[i, j], self.out.at[i, self.part(quarter)],
            self.s3.at[i, j], self.r3.at[i, quarter], (self.base + j, self.c),
        )

    def others(self, act):
        for j in range(PLANE):
            pl.when(self.p != j)(functools.partial(act, j))

    def start(self, i):
        def send(j):
            for copy in self.first(i, j, self.p):
                copy.start()

        self.others(send)
        self.slots[i, self.p] = self.state[i, self.part(self.p)]
        self.rates[i, self.p] = self.decay[i]

    def pieces(self):
        for n in range(self.rows // self.size):
            yield n, slice(n * self.size, (n + 1) * self.size)

    def rate(self, i, j, n):
        return self.rates[i, j, pl.ds(self.p * (self.rows // self.size) + n, 1)]

    def deliver(self, i, entering):
        for n, rows in self.pieces():
            held = entering(n, rows)
            for at, j in enumerate(self.order):
                self.staged[i, j, rows] = held.astype(BF16)
                if at < PLANE - 1:
                    held = self.rate(i, j, n) * held + self.slots[i, j, rows].astype(F32)
        self.others(lambda j: self.last(i, j, self.p).start())
        self.out[i, self.part(self.p)] = self.staged[i, self.p]

    def fold(self, i):
        def arrived(j):
            for copy in self.first(i, j, j):
                copy.wait_recv()

        self.others(arrived)
        for n, rows in self.pieces():
            held = self.slots[i, self.order[0], rows].astype(F32)
            rate = self.rate(i, self.order[0], n)
            for j in self.order[1:]:
                own = self.rate(i, j, n)
                held = own * held + self.slots[i, j, rows].astype(F32)
                rate = own * rate
            self.total[i, rows] = held
            self.through[i, n : n + 1] = rate

        @pl.when((self.place == 0) | (self.place == 2))
        def _():
            self.leaving[i] = self.total[i].astype(BF16)
            for copy in self.to_pair(i):
                copy.start()

        @pl.when(self.place == 0)
        def _():
            self.deliver(i, lambda n, rows: jnp.zeros((self.size, self.out.shape[2]), F32))

    def join(self, i):
        @pl.when(self.place == 1)
        def _():
            for copy in self.to_pair(i):
                copy.wait_recv()
            for n, rows in self.pieces():
                self.leaving[i, rows] = (
                    self.total[i, rows]
                    + self.through[i, n : n + 1] * self.pair[i, rows].astype(F32)
                ).astype(BF16)
            for n in (1, 2):
                self.to_far(i, n).start()
            self.deliver(i, lambda n, rows: self.pair[i, rows].astype(F32))

    def close(self, i):
        @pl.when(self.place == 2)
        def _():
            self.to_far(i, 1).wait_recv()
            self.deliver(i, lambda n, rows: self.far[i, rows].astype(F32))

        @pl.when(self.place == 3)
        def _():
            for copy in self.to_pair(i):
                copy.wait_recv()
            self.to_far(i, 1).wait_recv()
            self.deliver(
                i,
                lambda n, rows: self.pair[i, rows].astype(F32)
                + self.pair_through[i, n : n + 1] * self.far[i, rows].astype(F32),
            )

    def arrived(self, i):
        self.others(lambda j: self.last(i, j, j).wait_recv())

    def finish(self):
        @pl.loop(0, self.state.shape[0])
        def _(i):
            def close(j):
                for copy in self.first(i, j, self.p):
                    copy.wait_send()
                self.last(i, j, self.p).wait_send()

            self.others(close)

            @pl.when((self.place == 0) | (self.place == 2))
            def _():
                for copy in self.to_pair(i):
                    copy.wait_send()

            @pl.when(self.place == 1)
            def _():
                for n in (1, 2):
                    self.to_far(i, n).wait_send()


class Reduce:
    def __init__(self, pieces, rows, refs):
        self.pieces, self.rows = pieces, rows
        (
            self.near, self.mid, self.above, self.below, self.mid_send, self.kept,
            self.s1, self.r1, self.s2, self.r2, self.sz, self.rz,
        ) = refs
        self.s, self.c, self.z, self.y, self.x = place()
        s, c = self.s, self.c
        self.up, self.down = self.z < LINE - 1, self.z > 0
        self.to_x, self.to_y = (s + 1 - 2 * self.x, c), (s + 2 - 4 * self.y, c)
        self.to_up, self.to_down = (s + PLANE, c), (s - PLANE, c)
        self.span = range(len(pieces))

    @staticmethod
    def scratch(n, rows, wide):
        return dict(
            near=pltpu.VMEM((LINE, 2 * rows, wide), BF16),
            mid=pltpu.VMEM((LINE, rows, wide), BF16),
            above=pltpu.VMEM((LINE, rows, wide), BF16),
            below=pltpu.VMEM((LINE, rows, wide), BF16),
            mid_send=pltpu.VMEM((LINE, rows, wide), BF16),
            kept=pltpu.VMEM((LINE, rows, wide), F32),
            t1=dma(n, LINE, 2), u1=dma(n, LINE, 2), t2=dma(n, LINE),
            u2=dma(n, LINE), tz=dma(n, LINE), uz=dma(n, 2, LINE),
        )

    def columns(self, p):
        return pl.ds(self.pieces[p][6], self.pieces[p][2])

    def source(self, p, index, count=1):
        ref, start, width = self.pieces[p][:3]
        begin = pl.multiple_of(index * self.rows, 16)
        return ref.at[pl.ds(begin, count * self.rows), pl.ds(start, width)]

    def index(self, zz, yy, xx):
        return zz * PLANE + yy * 2 + xx

    def near_copies(self, p, zz):
        if self.pieces[p][3]:
            return [
                remote(
                    self.source(p, self.index(zz, 1 - self.y, 0), 2),
                    self.near.at[zz, :, self.columns(p)],
                    self.s1.at[p, zz, 0], self.r1.at[p, zz, 0], self.to_y,
                )
            ]
        return [
            remote(
                self.source(p, self.index(zz, k, 1 - self.x)),
                self.near.at[zz, pl.ds(k * self.rows, self.rows), self.columns(p)],
                self.s1.at[p, zz, k], self.r1.at[p, zz, k], self.to_x,
            )
            for k in range(2)
        ]

    def mid_copy(self, p, zz):
        at = self.columns(p)
        return remote(
            self.mid_send.at[zz, :, at], self.mid.at[zz, :, at],
            self.s2.at[p, zz], self.r2.at[p, zz], self.to_x if self.pieces[p][3] else self.to_y,
        )

    def line_copy(self, p, zz, upward):
        at = self.columns(p)
        target = self.above if upward else self.below
        return remote(
            self.mid_send.at[zz, :, at], target.at[zz, :, at],
            self.sz.at[p, zz], self.rz.at[p, 0 if upward else 1, zz],
            self.to_up if upward else self.to_down,
        )

    def exists(self, off):
        zz = self.z + off
        return (zz >= 0) & (zz < LINE)

    def rows_of(self, k):
        return pl.ds(pl.multiple_of(k * self.rows, 16), self.rows)

    def begin(self, *pieces):
        for off in SUM_OFFSETS:

            @pl.when(self.exists(off))
            def _():
                for p in pieces or self.span:
                    for copy in self.near_copies(p, self.z + off):
                        copy.start()

    def second(self, *offs):
        for off in offs:

            @pl.when(self.exists(off))
            def _():
                zz = self.z + off
                y, x = self.y, self.x
                for p in self.span:
                    for copy in self.near_copies(p, zz):
                        copy.wait_recv()
                    own = self.index(zz, y, x)
                    if self.pieces[p][3]:
                        other, mine = self.index(zz, y, 1 - x), x
                    else:
                        other, mine = self.index(zz, 1 - y, x), y
                    at = self.columns(p)
                    sent = self.source(p, other)[...].astype(F32) + self.near[
                        zz, self.rows_of(1 - mine), at
                    ].astype(F32)
                    self.mid_send[zz, :, at] = sent.astype(BF16)
                    self.mid_copy(p, zz).start()
                    self.kept[zz, :, at] = self.source(p, own)[...].astype(F32) + self.near[
                        zz, self.rows_of(mine), at
                    ].astype(F32)

    def third(self, *offs, only=None):
        for off in offs:

            @pl.when(self.exists(off))
            def _():
                zz = self.z + off
                for p in self.span if only is None else only:
                    at = self.columns(p)
                    self.mid_copy(p, zz).wait_recv()
                    self.kept[zz, :, at] = self.kept[zz, :, at] + self.mid[zz, :, at].astype(F32)
                    if off >= 0:

                        @pl.when(self.down)
                        def _():
                            self.line_copy(p, zz, True).wait_recv()
                            self.kept[zz, :, at] = self.kept[zz, :, at] + self.above[
                                zz, :, at
                            ].astype(F32)

                    if off <= 0:

                        @pl.when(self.up)
                        def _():
                            self.line_copy(p, zz, False).wait_recv()
                            self.kept[zz, :, at] = self.kept[zz, :, at] + self.below[
                                zz, :, at
                            ].astype(F32)

                    if off == 0:
                        _, _, width, _, out, start, _ = self.pieces[p]
                        out[:, start : start + width] = self.kept[zz, :, at]
                    else:
                        self.mid_copy(p, zz).wait_send()
                        self.mid_send[zz, :, at] = self.kept[zz, :, at].astype(BF16)
                        self.line_copy(p, zz, off > 0).start()

    def finish(self):
        for off in SUM_OFFSETS:

            @pl.when(self.exists(off))
            def _():
                zz = self.z + off
                for p in self.span:
                    for copy in self.near_copies(p, zz):
                        copy.wait_send()
                    if off == 0:
                        self.mid_copy(p, zz).wait_send()
                    else:
                        self.line_copy(p, zz, off > 0).wait_send()


def picked(r, names):
    return tuple(r.__dict__[n] for n in names)


GATHER_REFS = tuple(Gather.semaphores(1))
SCAN_REFS = tuple(Scan.scratch(1, PLANE, 1, 1))
REDUCE_REFS = tuple(Reduce.scratch(1, 16, 1))


def main_body(sizes, total_inner, r):
    length, inner, nstate, size, taps = sizes
    channels = inner + 2 * nstate
    heads = inner // size
    count = r.tok.shape[0]
    half = r.tok.shape[2]
    s, c, z, y, x = place()
    to_core, to_prv = (s, 1 - c), (s - 1, c)
    nxt, prv = s < LINE * PLANE - 1, s > 0
    first_gather = Gather(
        (
            (r.w1, r.w, 0, 512, LINE_X),
            (r.w1, r.w, 512, 384, LINE_Y),
            (r.w1, r.w, 896, 128, PLANE_X),
            (r.w1, r.w, 1024, 128, PLANE_Y),
        ),
        r.w1.shape[0],
        picked(r, GATHER_REFS),
    )
    second_gather = Gather(
        (
            (r.w2, r.w2_full, 0, 512, LINE_X),
            (r.w2, r.w2_full, 512, 512, LINE_Y),
            (r.w2, r.w2_full, 1024, 256, PLANE_X),
            (r.w2, r.w2_full, 1280, 256, PLANE_Y),
        ),
        r.w2.shape[0],
        picked(r, SECOND_REFS),
    )
    prefix = Scan(False, size, r.state, r.dec, r.hin, picked(r, SCAN_REFS))
    suffix = Scan(True, size, r.prior, r.dec, r.later, picked(r, SUFFIX_REFS))
    reduce_ = Reduce(
        ((r.dout, 0, inner, True, r.g_out, 0, 0), (r.dgate, 0, inner, False, r.g_gate, 0, inner)),
        r.g_out.shape[0],
        picked(r, REDUCE_REFS),
    )
    wide = inner + nstate + LANES
    late = Reduce(
        (
            (r.dout, 0, wide // 2, True, r.g_x, 0, 0),
            (r.dgate, 0, wide // 2, False, r.g_x, wide // 2, wide // 2),
        ),
        r.g_x.shape[0],
        picked(r, LATE_REFS),
    )
    spread = head_spread(inner, size)
    mine = pl.ds(pl.multiple_of(inner + c * nstate, LANES), nstate)
    side = pl.ds(pl.multiple_of(c * half, LANES), half)
    other_side = pl.ds(pl.multiple_of((1 - c) * half, LANES), half)
    log_at, step_at, pre_at, entry_at = (
        slice(n * LANES, (n + 1) * LANES) for n in range(4)
    )
    scores_at = slice(half, half + length)
    own_at, slope_at, gpre_at = (
        slice(half + n * nstate, half + (n + 1) * nstate) for n in range(3)
    )
    left = lax.broadcasted_iota(jnp.int32, (length, LANES), 1) < size

    def swap(n, source, target):
        return lambda i: remote(
            source.at[i], target.at[i], r.ss.at[n, i], r.rs.at[n, i], to_core
        )

    swap_tokens = swap(0, r.tok, r.tok_in)
    swap_grads = swap(1, r.g, r.g_in)
    swap_sums = swap(2, r.sums, r.sums_in)
    swap_out = swap(3, r.osend, r.out_in)
    swap_states = swap(4, r.bsend, r.brecv)
    swap_part = swap(6, r.normal, r.low)

    def send_edge(i):
        return remote(r.edge.at[i], r.edge_in.at[i], r.ss.at[5, i], r.rs.at[5, i], to_prv)

    def halo_copy(k):
        tails = r.tok.at[:, pl.ds(length - HALO, HALO), :]
        device = (s + 1, c if k == 0 else 1 - c)
        return remote(tails, r.halo.at[:, :, side], r.hs.at[k], r.hr.at[k], device)

    def store_grad(i):
        return pltpu.make_async_copy(
            r.full.at[i, :, pl.ds(0, half)], r.tokens_grad.at[i], r.store.at[0, i]
        )

    def store_mixed(i):
        return pltpu.make_async_copy(r.g_in.at[i], r.mixed.at[i], r.store.at[1, i])

    def conv(at):
        pre = r.prm[BIAS : BIAS + 1, at]
        for t in range(taps):
            start = HALO - taps + 1 + t
            pre = pre + r.prm[TAPS + t : TAPS + t + 1, at] * r.ext[start : start + length, at]
        return pre

    greet(
        prefix.relations()
        + [(z != j, (s + (j - z) * PLANE, c)) for j in range(LINE)]
        + [
            (True, to_core),
            (nxt, (s + 1, c)),
            (nxt, (s + 1, 1 - c)),
            (prv, (s - 1, c)),
            (prv, (s - 1, 1 - c)),
        ]
    )
    first_gather.begin()
    for k in range(2):
        pl.when(nxt)(halo_copy(k).start)
    for i in range(count):
        swap_tokens(i).start()
    r.small[...] = jnp.zeros_like(r.small)
    first_gather.z_arrived(-1, 1)
    first_gather.plane_first()
    first_gather.first_arrived(0)
    second_gather.begin()
    for i in range(count):
        swap_grads(i).start()

    @pl.loop(0, count)
    def _(i):
        swap_tokens(i).wait()
        own, other = r.tok[i].astype(F32), r.tok_in[i].astype(F32)
        scale = lax.rsqrt(
            jnp.mean(own * own + other * other, axis=-1, keepdims=True) * 0.5 + EPSILON
        )
        gain_own = r.prm[GAIN : GAIN + 1, side]
        gain_other = r.prm[GAIN : GAIN + 1, other_side]
        r.normed_s[i, HALO:, side] = (own * scale * gain_own).astype(BF16)
        r.normed_s[i, HALO:, other_side] = (other * scale * gain_other).astype(BF16)

    first_gather.z_arrived(-2, 2)
    first_gather.plane_second()
    first_gather.first_arrived(-1, 1)
    for k in range(2):
        pl.when(nxt)(halo_copy(k).wait_send)
        pl.when(prv)(halo_copy(k).wait_recv)

    @pl.when(prv)
    def _():
        for i in range(count):
            edge = r.halo[i].astype(F32)
            scale = lax.rsqrt(jnp.mean(edge * edge, axis=-1, keepdims=True) + EPSILON)
            r.normed_s[i, :HALO] = (
                edge * scale * r.prm[GAIN : GAIN + 1, : edge.shape[1]]
            ).astype(BF16)

    @pl.when(jnp.logical_not(prv))
    def _():
        for i in range(count):
            r.normed_s[i, :HALO] = jnp.zeros((HALO, 2 * half), BF16)

    first_gather.z_arrived(-3, 3)
    first_gather.plane_arrived(-1, 1)
    first_gather.first_arrived(-2, 2)
    second_gather.z_arrived(-1, 1)
    second_gather.plane_first()
    first_gather.plane_arrived(-2, 2)
    first_gather.first_arrived(-3, 3)
    second_gather.first_arrived(0)
    first_gather.plane_arrived(-3, 3)
    first_gather.finish()
    kept, ones = triangle(length)

    def project(i):
        xs = dot(r.normed_s[i], r.w[:, :channels]).astype(BF16)
        r.xs_s[i] = xs
        r.ext[...] = xs.astype(F32)
        pre = conv(slice(0, channels))
        act = (pre * sigmoid(pre)).astype(BF16)
        r.act[i] = act
        step_pre = (
            dot(r.normed_s[i, HALO:], r.w[:, channels:])
            + r.prm[STEP_BIAS : STEP_BIAS + 1, :LANES]
        )
        step = softplus(step_pre)
        log_decay = running_sum(ones, step * r.prm[RATE : RATE + 1, :LANES])
        doc_col, doc_row = doc_numbers(r.doc[i], ones)
        entry = jnp.where(doc_col == 0.0, jnp.exp(log_decay), 0.0)
        last = log_decay[length - 1 :]
        tail = jnp.where(doc_col == doc_col[length - 1 :], jnp.exp(last - log_decay), 0.0)
        r.aux[i, :, log_at] = log_decay
        r.aux[i, :, step_at] = step
        r.aux[i, :, pre_at] = step_pre
        r.aux[i, :, entry_at] = entry
        log_rows = log_decay.T
        whole_decay = jnp.where(
            doc_row[:, length - 1 :] == 0.0, jnp.exp(log_rows[:HEAD_ROWS, length - 1 :]), 0.0
        )
        r.dec[i] = jnp.broadcast_to(whole_decay, (HEAD_ROWS, LANES))
        inputs = act[:, :inner].astype(F32) * expand(step, spread)
        r.low[i] = inputs.astype(BF16)
        r.state[i] = dot(
            (inputs * expand(tail, spread)).astype(BF16), act[:, inner : inner + nstate], TN
        ).astype(BF16)
        prefix.start(i)

    @pl.loop(0, count)
    def _(i):
        project(i)

        @pl.when(i == 0)
        def _():
            second_gather.z_arrived(-2, 2)
            second_gather.plane_second()
            second_gather.first_arrived(-1, 1)

        @pl.when(i == 1)
        def _():
            second_gather.z_arrived(-3, 3)
            second_gather.first_arrived(-2, 2)

        @pl.when(i == 2)
        def _():
            prefix.fold(0)
            second_gather.plane_arrived(-1, 1)
            second_gather.first_arrived(-3, 3)

        @pl.when(i == 3)
        def _():
            prefix.fold(1)
            second_gather.plane_arrived(-2, 2)

    def inside(i):
        log_decay = r.aux[i, :, log_at]
        log_rows = log_decay.T
        doc_col, doc_row = doc_numbers(r.doc[i], ones)
        closed = jnp.where(kept & (doc_col == doc_row), 0.0, MASKED)
        scores = dot(r.act[i, :, inner + nstate :], r.act[i, :, inner : inner + nstate], NT)
        for pair in range(inner // LANES):
            columns = slice(pair * LANES, (pair + 1) * LANES)
            part = r.low[i, :, columns]
            total = None
            for h in (2 * pair, 2 * pair + 1):
                decay = jnp.exp(log_decay[:, h : h + 1] - log_rows[h : h + 1] + closed)
                own = jnp.where(left if h % 2 == 0 else ~left, part, jnp.zeros_like(part))
                term = dot((scores * decay).astype(BF16), own)
                total = term if total is None else total + term
            r.full[i, :, columns] = total

    @pl.loop(0, count)
    def _(i):
        inside(i)

        @pl.when(i == 0)
        def _():
            prefix.join(0)
            second_gather.plane_arrived(-3, 3)

        @pl.when(i == 1)
        def _():
            prefix.fold(2)
            prefix.join(1)

        @pl.when(i == 2)
        def _():
            prefix.fold(3)
            prefix.close(0)

        @pl.when(i == 3)
        def _():
            prefix.join(2)
            prefix.close(1)

    second_gather.finish()
    for i in range(count):
        swap_grads(i).wait()

    def gates(i):
        r.gate[i] = dot(r.normed_s[i, HALO:], r.w2_full[:, :inner])
        r.gn[i] = dot(either(c, r.g[i], r.g_in[i]), r.w2_full[:, inner:])

    @pl.loop(0, count)
    def _(i):
        gates(i)

        @pl.when(i == 0)
        def _():
            prefix.join(3)

        @pl.when(i == 1)
        def _():
            prefix.close(2)

    def combine(i):
        prefix.arrived(i)
        values = r.act[i, :, :inner].astype(F32)
        entry = expand(r.aux[i, :, entry_at], spread)
        scanned = r.full[i] + dot(r.act[i, :, inner + nstate :], r.hin[i], NT) * entry
        r.full[i] = scanned
        mixed = scanned + r.prm[SKIP : SKIP + 1, :inner] * values
        gate = r.gate[i]
        gated = mixed * (gate * sigmoid(gate))
        squares = jnp.sum(gated * gated, axis=-1, keepdims=True)
        cross = jnp.sum(
            r.gn[i] * r.prm[INNER_GAIN : INNER_GAIN + 1, :inner] * gated, axis=-1, keepdims=True
        )
        lane = lax.broadcasted_iota(jnp.int32, (length, LANES), 1)
        r.sums[i] = jnp.where(lane == 0, squares, jnp.where(lane == 1, cross, 0.0)).T[:EDGE]
        swap_sums(i).start()

    def norm_back(i):
        swap_sums(i).wait_recv()
        values = r.act[i, :, :inner].astype(F32)
        mixed = r.full[i] + r.prm[SKIP : SKIP + 1, :inner] * values
        gate = r.gate[i]
        sig = sigmoid(gate)
        swish = gate * sig
        gated = mixed * swish
        both = jnp.concatenate(
            [r.sums[i] + r.sums_in[i], jnp.zeros((LANES - EDGE, length), F32)], axis=0
        ).T
        inner_scale = lax.rsqrt(both[:, 0:1] / total_inner + EPSILON)
        gain = r.prm[INNER_GAIN : INNER_GAIN + 1, :inner]
        unit = gated * inner_scale
        r.normal[i] = (unit * gain).astype(BF16)
        grad_norm = r.gn[i]
        grad_inner = jnp.sum(grad_norm * unit, axis=0, keepdims=True)
        grad_gated = inner_scale * (grad_norm * gain) - unit * (
            inner_scale * inner_scale * (both[:, 1:2] / total_inner)
        )
        dy = grad_gated * swish
        r.dy[i] = dy.astype(BF16)
        r.ggate_s[i] = (
            grad_gated * mixed * (sig * (1.0 + gate * (1.0 - sig)))
        ).astype(BF16)
        entry = expand(r.aux[i, :, entry_at], spread)
        r.prior[i] = dot(
            (dy * entry).astype(BF16), r.act[i, :, inner + nstate :], TN
        ).astype(BF16)
        suffix.start(i)
        r.small[0:1, :inner] += grad_inner
        per_head = head_sums(
            jnp.broadcast_to(jnp.sum(dy * values, axis=0, keepdims=True), (8, inner)), spread
        )
        r.small[1:2, :LANES] += per_head[:1]

    combine(0)
    combine(1)
    prefix.close(3)
    norm_back(0)
    combine(2)
    norm_back(1)
    combine(3)
    prefix.finish()
    norm_back(2)
    suffix.fold(0)
    norm_back(3)
    suffix.fold(1)

    def outputs(i):
        r.ginputs[...] = dot(r.normal[i], r.w2_full[:, inner:], NT)
        r.gate[i, :, :half] = r.ginputs[:, side]
        r.osend[i] = r.ginputs[:, other_side].astype(BF16)
        swap_out(i).start()

    pl.loop(0, count)(outputs)
    suffix.join(0)

    def weights_gradient(source, target, values, start, rows, step):
        for n in range(0, rows, step):
            total = None
            for i in range(count):
                term = dot(source(i, n, step), values[i], TN)
                total = term if total is None else total + term
            target[pl.ds(pl.multiple_of(start + n, LANES), step), :] = total.astype(BF16)

    def normed_block(i, n, step):
        return r.normed_s[i, HALO:, n : n + step]

    weights_gradient(
        lambda i, n, step: r.g[i, :, n : n + step], r.dout, r.normal, c * half, half, LANES
    )
    suffix.fold(2)
    weights_gradient(
        lambda i, n, step: r.g_in[i, :, n : n + step], r.dout, r.normal, (1 - c) * half, half,
        LANES,
    )
    reduce_.begin(0)
    suffix.fold(3)
    suffix.join(1)
    suffix.close(0)
    weights_gradient(normed_block, r.dgate, r.ggate_s, 0, 2 * half, 256)
    reduce_.begin(1)
    suffix.join(2)

    upper, ones_upper = triangle(length, True)

    def back_inside(i):
        log_decay = r.aux[i, :, log_at]
        in_state = r.act[i, :, inner : inner + nstate]
        out_state = r.act[i, :, inner + nstate :]
        doc_col, doc_row = doc_numbers(r.doc[i], ones)
        closed = jnp.where(upper & (doc_col == doc_row), 0.0, MASKED)
        scores = dot(in_state, out_state, NT)
        log_rows = log_decay.T
        for pair in range(inner // LANES):
            columns = slice(pair * LANES, (pair + 1) * LANES)
            pair_dy = r.dy[i, :, columns]
            pair_in = r.low[i, :, columns]
            total = None
            for h in (2 * pair, 2 * pair + 1):
                chosen = left if h % 2 == 0 else ~left
                own_dy = jnp.where(chosen, pair_dy, jnp.zeros_like(pair_dy))
                decay = jnp.exp(log_rows[h : h + 1] - log_decay[:, h : h + 1] + closed)
                term = dot((scores * decay).astype(BF16), own_dy)
                total = term if total is None else total + term
                grad_decay = dot(pair_in, own_dy, NT) * decay
                if h == 0:
                    r.gate[i, :, scores_at] = grad_decay
                else:
                    r.gate[i, :, scores_at] += grad_decay
            r.gn[i, :, columns] = total

    @pl.loop(0, count)
    def _(i):
        back_inside(i)

        @pl.when(i == 0)
        def _():
            suffix.close(1)
            suffix.join(3)

        @pl.when(i == 1)
        def _():
            suffix.close(2)

        @pl.when(i == 2)
        def _():
            suffix.close(3)
            reduce_.second(3, -3)

        @pl.when(i == 3)
        def _():
            reduce_.second(2, -2)

    def back_rest(i):
        suffix.arrived(i)
        step = r.aux[i, :, step_at]
        entry = r.aux[i, :, entry_at]
        values = r.act[i, :, :inner].astype(F32)
        in_state = r.act[i, :, inner : inner + nstate]
        out_state = r.act[i, :, inner + nstate :]
        later = r.later[i]
        wide_dy = r.dy[i].astype(F32)
        step_wide = expand(step, spread)
        log_decay = r.aux[i, :, log_at]
        doc_col, doc_row = doc_numbers(r.doc[i], ones)
        tail = jnp.where(
            doc_col == doc_col[length - 1 :], jnp.exp(log_decay[length - 1 :] - log_decay), 0.0
        )
        tail_wide = expand(tail, spread)
        entry_wide = expand(entry, spread)
        inputs = values * step_wide
        grad_inputs = r.gn[i] + tail_wide * dot(in_state, later, NT)
        grad_scores = r.gate[i, :, scores_at]
        grad_in = dot(grad_scores.astype(BF16), out_state) + dot(
            (inputs * tail_wide).astype(BF16), later
        )
        grad_out = dot(grad_scores.T.astype(BF16), in_state) + dot(
            (wide_dy * entry_wide).astype(BF16), r.hin[i]
        )
        is_first = c == 0
        r.gate[i, :, own_at] = jnp.where(is_first, grad_in, grad_out)
        r.bsend[i] = jnp.where(is_first, grad_out, grad_in).astype(BF16)
        entry_last = jnp.broadcast_to(entry[length - 1 :], (8, LANES))
        later_wide = later.astype(F32)
        lane_ones = jnp.ones((8, nstate), BF16)

        def state_sums(other):
            pieces = split2(later_wide * other.astype(F32))
            return head_sums(sum(dot(lane_ones, piece, NT) for piece in pieces), spread)

        ending = (state_sums(r.state[i]) + entry_last * state_sums(r.hin[i]))[:1]
        grad_log = head_sums(wide_dy * r.full[i], spread) - head_sums(
            r.low[i].astype(F32) * grad_inputs, spread
        )
        swap_states(i).start()
        grad_rate_step = running_sum(ones_upper, grad_log) + ending
        rate = r.prm[RATE : RATE + 1, :LANES]
        grad_step = head_sums(values * grad_inputs, spread) + rate * grad_rate_step
        lane = lax.broadcasted_iota(jnp.int32, (length, LANES), 1)
        gpre = jnp.where(lane < heads, grad_step * sigmoid(r.aux[i, :, pre_at]), 0.0)
        r.gate[i, :, gpre_at] = gpre
        grad_values = step_wide * grad_inputs + r.prm[SKIP : SKIP + 1, :inner] * wide_dy
        r.ext[...] = r.xs_s[i].astype(F32)
        px = conv(slice(0, inner))
        sig = sigmoid(px)
        gcx = grad_values * (sig * (1.0 + px * (1.0 - sig)))
        r.gn[i] = gcx
        r.edge[i, :, :inner] = gcx[:EDGE]
        ps = conv(mine)
        sig = sigmoid(ps)
        r.gate[i, :, slope_at] = sig * (1.0 + ps * (1.0 - sig))
        r.small[1:2, LANES : 2 * LANES] += jnp.sum(gpre, axis=0, keepdims=True)
        r.small[1:2, 2 * LANES : 3 * LANES] += rate * jnp.sum(
            step * grad_rate_step, axis=0, keepdims=True
        )


    def finish_states(n):
        swap_states(n).wait_recv()
        gst = (r.gate[n, :, own_at] + r.brecv[n].astype(F32)) * r.gate[n, :, slope_at]
        r.gate[n, :, own_at] = gst
        r.edge[n, :, inner:] = gst[:EDGE]
        pl.when(prv)(send_edge(n).start)

    @pl.loop(0, count)
    def _(i):
        back_rest(i)
        pl.when(i > 0)(lambda: finish_states(i - 1))

        @pl.when(i == 0)
        def _():
            reduce_.second(1, -1)

        @pl.when(i == 1)
        def _():
            reduce_.second(0)
            reduce_.third(3, -3)

        @pl.when(i == 2)
        def _():
            reduce_.third(2, -2)

        @pl.when(i == 3)
        def _():
            reduce_.third(1, -1)

    r.conv_rows[...] = jnp.zeros_like(r.conv_rows)
    r.bc[...] = jnp.zeros_like(r.bc)

    def conv_back(i):
        pl.when(nxt)(send_edge(i).wait_recv)
        r.gext[:length, :inner] = r.gn[i]
        r.gext[:length, inner:] = r.gate[i, :, own_at]
        r.gext[length:] = jnp.where(nxt, r.edge_in[i], 0.0)
        r.ext[:, :inner] = r.xs_s[i, :, :inner].astype(F32)
        r.ext[:, inner : inner + nstate] = r.xs_s[i, :, mine].astype(F32)
        grad_conv = r.gext[:length]
        grad_in = None
        for t in range(taps):
            row = jnp.concatenate(
                [r.prm[TAPS + t : TAPS + t + 1, :inner], r.prm[TAPS + t : TAPS + t + 1, mine]],
                axis=1,
            )
            term = row * r.gext[taps - 1 - t : taps - 1 - t + length]
            grad_in = term if grad_in is None else grad_in + term
            start = HALO - taps + 1 + t
            r.conv_rows[t : t + 1] += jnp.sum(
                r.ext[start : start + length, : inner + nstate] * grad_conv, axis=0, keepdims=True
            )
        r.conv_rows[taps : taps + 1] += jnp.sum(grad_conv, axis=0, keepdims=True)
        low = grad_in.astype(BF16)
        low_pre = r.gate[i, :, gpre_at].astype(BF16)
        r.dy[i] = low[:, :inner]
        r.gtail[i, :, :nstate] = low[:, inner:]
        r.gtail[i, :, nstate:] = low_pre

    @pl.loop(0, count)
    def _(i):
        conv_back(i)

        @pl.when(i == 0)
        def _():
            finish_states(count - 1)

        @pl.when(i == 1)
        def _():
            reduce_.third(0)

    def small_copy(source, target, at, device):
        return remote(source, target, r.qs.at[at], r.qr.at[at], device)

    core_copy = small_copy(r.bc, r.bc_in, 0, to_core)
    x_copy = small_copy(r.work.at[0], r.from_x, 1, late.to_x)
    y_copy = small_copy(r.work.at[1], r.from_y, 2, late.to_y)
    states_copy = small_copy(r.states_s.at[c], r.states_s.at[c], 7, to_core)

    def z_small(j, slot):
        return remote(
            r.work.at[2], r.from_z.at[slot], r.qs.at[3 + j], r.qr.at[3 + slot],
            (s + (j - z) * PLANE, c),
        )

    for t in range(taps + 1):
        begin = (t % 3) * 2 * nstate
        own = r.conv_rows[t : t + 1, inner:]
        row = 1 + t // 3
        r.bc[row : row + 1, begin : begin + nstate] = jnp.where(c == 0, own, 0.0)
        r.bc[row : row + 1, begin + nstate : begin + 2 * nstate] = jnp.where(c == 1, own, 0.0)

    half_wide = wide // 2

    def last_gradient(values, target):
        for n in range(0, 2 * half, 256):
            total = None
            for i in range(count):
                term = dot(normed_block(i, n, 256), values(i), TN)
                total = term if total is None else total + term
            target[n : n + 256, :half_wide] = total.astype(BF16)

    reduce_.finish()
    last_gradient(lambda i: r.dy[i, :, :half_wide], r.dout)
    late.begin(0)
    last_gradient(
        lambda i: jnp.concatenate([r.dy[i, :, half_wide:], r.gtail[i]], axis=1), r.dgate
    )
    late.begin(1)

    def part_back(i):
        part = dot(r.ggate_s[i], r.w2_full[:, :inner], NT)
        part = part + dot(r.dy[i], r.w[:, :inner], NT)
        part = part + dot(r.gtail[i, :, :nstate], r.w[:, mine], NT)
        part = part + dot(r.gtail[i, :, nstate:], r.w[:, channels:], NT)
        low_part = part.astype(BF16)
        r.normal[i] = low_part
        swap_part(i).start()
        tok = either(c, r.tok[i].astype(F32), r.tok_in[i].astype(F32))
        unit = tok * lax.rsqrt(jnp.mean(tok * tok, axis=-1, keepdims=True) + EPSILON)
        r.bc[0:1, :inner] += jnp.sum(low_part.astype(F32) * unit, axis=0, keepdims=True)

    pl.loop(0, count)(part_back)
    core_copy.start()

    def tokens_back(i):
        swap_part(i).wait_recv()
        swap_out(i).wait_recv()
        own_tok = r.tok[i].astype(F32)
        tok = either(c, own_tok, r.tok_in[i].astype(F32))
        scale = lax.rsqrt(jnp.mean(tok * tok, axis=-1, keepdims=True) + EPSILON)
        unit = tok * scale
        grad_normed = r.normal[i].astype(F32) + r.low[i].astype(F32)
        grad = grad_normed * r.prm[GAIN : GAIN + 1, : 2 * half]
        r.ginputs[...] = scale * (grad - unit * jnp.mean(grad * unit, axis=-1, keepdims=True))
        r.full[i, :, :half] = r.g[i].astype(F32) + r.ginputs[:, side]
        store_grad(i).start()
        r.g_in[i] = (own_tok + (r.gate[i, :, :half] + r.out_in[i].astype(F32))).astype(BF16)
        store_mixed(i).start()

    @pl.loop(0, count)
    def _(i):
        tokens_back(i)

        @pl.when(i == 0)
        def _():
            core_copy.wait_recv()
            r.work[0, 0:2] = r.small[0:2]
            r.work[0, 2 : 3 + taps] = r.conv_rows[: taps + 1, :inner]
            r.work[0, 3 + taps : 8] = jnp.zeros((5 - taps, inner), F32)
            r.work[0, 8:16] = r.bc[...] + r.bc_in[...]
            x_copy.start()

        @pl.when(i == 1)
        def _():
            late.second(3, -3)

        @pl.when(i == 2)
        def _():
            x_copy.wait_recv()
            r.work[1] = r.work[0] + r.from_x[...]
            y_copy.start()
            late.second(2, -2)

    late.third(3, -3)
    late.second(1, -1)
    y_copy.wait_recv()
    r.work[2] = r.work[1] + r.from_y[...]
    for j in range(LINE):
        pl.when(z != j)(z_small(j, z).start)
    r.from_z[z] = r.work[2]
    late.third(2, -2)
    late.second(0)
    late.third(1, -1)
    late.third(0, only=(1,))
    r.states_s[c] = r.g_x[:, inner : inner + nstate]
    states_copy.start()
    late.third(0, only=(0,))
    for j in range(LINE):
        pl.when(z != j)(z_small(j, j).wait_recv)
    r.sums_out[...] = (r.from_z[0] + r.from_z[1]) + (r.from_z[2] + r.from_z[3])
    states_copy.wait()
    r.states[...] = r.states_s[...]
    core_copy.wait_send()
    x_copy.wait_send()
    y_copy.wait_send()
    for j in range(LINE):
        pl.when(z != j)(z_small(j, z).wait_send)
    late.finish()
    suffix.finish()

    @pl.loop(0, count)
    def _(i):
        swap_sums(i).wait_send()
        swap_out(i).wait_send()
        swap_states(i).wait_send()
        pl.when(prv)(send_edge(i).wait_send)
        swap_part(i).wait_send()
        store_grad(i).wait()
        store_mixed(i).wait()


LOCAL_REFS = tuple(dict(kept=0, mid_send=0))
LATE_REFS = tuple(n if n in LOCAL_REFS else "l" + n for n in REDUCE_REFS)
SECOND_REFS = tuple("s" + n for n in GATHER_REFS)
SHARED_REFS = tuple(dict(total=0, leaving=0, staged=0))
SUFFIX_REFS = tuple(n if n in SHARED_REFS else "s" + n for n in SCAN_REFS)


def main_call(sizes, total_inner, tok, g, doc, prm, w1, w2):
    length, inner, nstate, size, taps = sizes
    count, _, half = tok.shape
    model = 2 * half
    channels = inner + 2 * nstate
    rows = w1.shape[0]
    wide = inner + nstate + LANES
    ins = dict(
        tok=(tok, INSIDE), g=(g, INSIDE), doc=(doc, INSIDE), prm=(prm, INSIDE),
        w1=(w1, ANYWHERE), w2=(w2, ANYWHERE),
    )
    outs = dict(
        mixed=(shape((count, length, half), BF16), ANYWHERE),
        tokens_grad=(shape((count, length, half), F32), ANYWHERE),
        g_out=(shape((rows, inner), F32), INSIDE),
        g_gate=(shape((rows, inner), F32), INSIDE),
        g_x=(shape((rows, wide), F32), INSIDE),
        states=(shape((2, rows, nstate), F32), INSIDE),
        sums_out=(shape((16, inner), F32), INSIDE),
    )

    def vmem(*dims, dtype=F32):
        return pltpu.VMEM(dims, dtype)

    def low(*dims):
        return pltpu.VMEM(dims, BF16)

    scratch = dict(
        g_in=low(count, length, half),
        tok_in=low(count, length, half),
        out_in=low(count, length, half),
        edge_in=vmem(count, EDGE, inner + nstate),
        small=vmem(8, inner),
        gtail=low(count, length, nstate + LANES),
        gext=vmem(length + EDGE, inner + nstate),
        conv_rows=vmem(8, inner + nstate),
        states_s=vmem(2, rows, nstate),
        bc=vmem(8, inner),
        bc_in=vmem(8, inner),
        work=vmem(3, 16, inner),
        from_x=vmem(16, inner),
        from_y=vmem(16, inner),
        from_z=vmem(LINE, 16, inner),
        qs=dma(8),
        qr=dma(8),
        halo=low(count, HALO, model),
        w=low(model, w1.shape[1]),
        w2_full=low(model, 2 * inner),
        normed_s=low(count, HALO + length, model),
        xs_s=low(count, HALO + length, channels),
        act=low(count, length, channels),
        aux=vmem(count, length, 4 * LANES),
        low=low(count, length, inner),
        dec=vmem(count, HEAD_ROWS, LANES),
        state=low(count, inner, nstate),
        hin=low(count, inner, nstate),
        prior=low(count, inner, nstate),
        later=low(count, inner, nstate),
        full=vmem(count, length, inner),
        gate=vmem(count, length, inner),
        gn=vmem(count, length, inner),
        sums=vmem(count, EDGE, length),
        sums_in=vmem(count, EDGE, length),
        normal=low(count, length, inner),
        dy=low(count, length, inner),
        ggate_s=low(count, length, inner),
        osend=low(count, length, half),
        dout=low(model, inner),
        dgate=low(model, inner),
        ext=vmem(HALO + length, channels),
        ginputs=vmem(length, inner),
        bsend=low(count, length, nstate),
        brecv=low(count, length, nstate),
        edge=vmem(count, EDGE, inner + nstate),
        ss=dma(7, count),
        rs=dma(7, count),
        hs=dma(2),
        hr=dma(2),
        store=dma(2, count),
    )
    scan = Scan.scratch(count, inner, nstate, HEAD_ROWS)
    gather = Gather.semaphores(4)
    scratch.update(zip(SUFFIX_REFS, scan.values()))
    scratch.update(scan)
    scratch.update(gather)
    scratch.update(zip(SECOND_REFS, gather.values()))
    scratch.update(zip(LATE_REFS, Reduce.scratch(2, rows, wide).values()))
    scratch.update(Reduce.scratch(2, rows, 2 * inner))
    return fused_call(
        functools.partial(main_body, sizes, total_inner), None, ins, outs, scratch, 1, "main"
    )


def local_call(body, ins, outs, name):
    names = list(ins) + list(outs)

    def kernel(*refs):
        body(Refs(names, refs))

    results = pl.pallas_call(
        kernel,
        in_specs=[INSIDE for _ in ins],
        out_specs=[INSIDE for _ in outs],
        out_shape=list(outs.values()),
        name=name,
    )(*ins.values())
    return Refs(list(outs), results)


def pack_body(sizes, r):
    length, inner, nstate, size, taps = sizes
    heads = inner // size
    channels = inner + 2 * nstate
    model = r.norm_gain.shape[0]

    def line(v):
        return v.reshape(1, v.shape[0])

    r.prm[...] = jnp.zeros_like(r.prm)
    r.prm[GAIN : GAIN + 1, :model] = line(r.norm_gain[...])
    r.prm[INNER_GAIN : INNER_GAIN + 1, :inner] = line(r.inner_gain[...])
    r.prm[BIAS : BIAS + 1, :inner] = line(r.conv_bias_x[...])
    r.prm[BIAS : BIAS + 1, inner:] = line(r.conv_bias_bc[...])
    r.prm[STEP_BIAS : STEP_BIAS + 1, :heads] = line(r.step_bias[...])
    r.prm[RATE : RATE + 1, :heads] = -jnp.exp(line(r.decay_log[...]))
    r.prm[TAPS : TAPS + taps, :inner] = r.conv_taps_x[...]
    r.prm[TAPS : TAPS + taps, inner:] = r.conv_taps_bc[...]
    r.prm[SKIP : SKIP + 1, :heads] = line(r.skip_gain[...])
    skip = jnp.broadcast_to(r.prm[SKIP : SKIP + 1, :LANES], (8, LANES))
    spread = head_spread(inner, size)
    r.prm[SKIP : SKIP + 1, :inner] = sum(dot(v, spread) for v in split3(skip))[:1]
    r.w2[:, :inner] = r.features[:, 0, :]
    same = lax.broadcasted_iota(jnp.int32, (heads, LANES), 0) == lax.broadcasted_iota(
        jnp.int32, (heads, LANES), 1
    )
    r.w2[:, inner:] = r.output_projection[...]
    r.w1[:, :inner] = r.features[:, 1, :]
    r.w1[:, inner:channels] = r.state_weight[...]
    r.w1[:, channels:] = dot(
        r.step_weight[...], jnp.where(same, 1.0, 0.0).astype(BF16), TN
    ).astype(BF16)
    seqs = r.starts.shape[1]
    for i in range(r.doc.shape[0]):
        flags = r.starts[i // seqs, i % seqs : i % seqs + 1].astype(F32)
        r.doc[i] = jnp.broadcast_to(flags, (8, length))


def results_body(sizes, r):
    length, inner, nstate, size, taps = sizes
    heads = inner // size
    r.norm_gain[...] = r.sums[8]
    r.gate_x[:, 0, :] = r.g_gate[...]
    r.gate_x[:, 1, :] = r.g_x[:, :inner]
    r.state_weight[:, :nstate] = r.states[0]
    r.state_weight[:, nstate:] = r.states[1]
    r.step_weight[...] = r.g_x[:, inner + nstate :].T[:heads]
    r.taps_x[...] = r.sums[2 : 2 + taps]
    r.bias_x[...] = r.sums[2 + taps]
    for t in range(taps + 1):
        begin = (t % 3) * 2 * nstate
        row = r.sums[9 + t // 3, begin : begin + 2 * nstate]
        if t < taps:
            r.taps_bc[t] = row
        else:
            r.bias_bc[...] = row
    r.step_bias[...] = r.sums[1, LANES : LANES + heads]
    r.decay_log[...] = r.sums[1, 2 * LANES : 2 * LANES + heads]
    r.skip_gain[...] = r.sums[1, :heads]
    r.inner_gain[...] = r.sums[0]


def fused_layer(
    sizes, total_inner, tok, g, starts, norm_gain, features, state_weight, step_weight, conv_taps_x,
    conv_bias_x, conv_taps_bc, conv_bias_bc, step_bias, decay_log, skip_gain, inner_gain,
    output_projection,
):
    length, inner, nstate, size, taps = sizes
    heads = inner // size
    count, _, half = tok.shape
    model = 2 * half
    rows = features.shape[0]
    channels = inner + 2 * nstate
    packed = local_call(
        functools.partial(pack_body, sizes),
        dict(
            norm_gain=norm_gain, inner_gain=inner_gain, conv_bias_x=conv_bias_x,
            conv_bias_bc=conv_bias_bc, step_bias=step_bias, decay_log=decay_log,
            conv_taps_x=conv_taps_x, conv_taps_bc=conv_taps_bc, skip_gain=skip_gain,
            features=features, state_weight=state_weight, step_weight=step_weight.T,
            output_projection=output_projection.T, starts=starts,
        ),
        dict(
            prm=shape((16, channels), F32),
            w1=shape((rows, channels + LANES), BF16),
            w2=shape((rows, 2 * inner), BF16),
            doc=shape((count, 8, length), F32),
        ),
        "pack",
    )
    m = main_call(sizes, total_inner, tok, g, packed.doc, packed.prm, packed.w1, packed.w2)
    o = local_call(
        functools.partial(results_body, sizes),
        dict(sums=m.sums_out, g_x=m.g_x, g_gate=m.g_gate, states=m.states),
        dict(
            norm_gain=shape((model,), F32),
            gate_x=shape((rows, 2, inner), F32),
            state_weight=shape((rows, 2 * nstate), F32),
            step_weight=shape((heads, rows), F32),
            taps_x=shape((taps, inner), F32),
            bias_x=shape((inner,), F32),
            taps_bc=shape((taps, 2 * nstate), F32),
            bias_bc=shape((2 * nstate,), F32),
            step_bias=shape((heads,), F32),
            decay_log=shape((heads,), F32),
            skip_gain=shape((heads,), F32),
            inner_gain=shape((inner,), F32),
        ),
        "results",
    )
    o.step_weight = o.step_weight.T
    return (m.mixed, m.tokens_grad) + tuple(o.__dict__.values()) + (m.g_out.T,)


def shards(
    tokens, doc_starts, norm_gain, input_gate_features, input_state_weight, input_step_weight,
    conv_taps_x, conv_bias_x, conv_taps_bc, conv_bias_bc, step_bias, decay_log, skip_gain,
    inner_gain, output_projection, out_grad,
):
    micro, seqs, length, half = tokens.shape
    count = micro * seqs
    model = 2 * half
    heads = step_bias.shape[0]
    inner = inner_gain.shape[0]
    size = inner // heads
    nstate = conv_taps_bc.shape[1] // 2
    taps = conv_taps_x.shape[0]
    channels = inner + 2 * nstate
    rows = input_gate_features.shape[0]
    total_inner = inner * lax.axis_size("head")
    sizes = (length, inner, nstate, size, taps)
    core = lax.axis_index("head")

    tok = tokens.reshape(count, length, half)
    g = out_grad.reshape(count, length, half)
    if lax.axis_size("seq") == PLANE * LINE and lax.axis_size("head") == 2:
        outputs = fused_layer(
            sizes, total_inner, tok, g, doc_starts, norm_gain, input_gate_features,
            input_state_weight, input_step_weight, conv_taps_x, conv_bias_x, conv_taps_bc,
            conv_bias_bc, step_bias, decay_log, skip_gain, inner_gain, output_projection,
        )
        return tuple(o.reshape(tokens.shape) if n < 2 else o for n, o in enumerate(outputs))

    doc = jnp.broadcast_to(
        doc_starts.reshape(count, 1, length).astype(F32), (count, 8, length)
    )

    def row(v):
        return jnp.pad(v, (0, channels - v.shape[0]))[None]

    prm = jnp.concatenate(
        [
            row(norm_gain),
            row(inner_gain),
            row(jnp.repeat(skip_gain, size)),
            row(jnp.concatenate([conv_bias_x, conv_bias_bc])),
            row(step_bias),
            row(-jnp.exp(decay_log)),
            jnp.concatenate([conv_taps_x, conv_taps_bc], axis=1),
        ],
        axis=0,
    )
    prm = jnp.pad(prm, ((0, 16 - prm.shape[0]), (0, 0)))
    w_own = jnp.concatenate(
        [
            input_gate_features.reshape(rows, 2 * inner),
            input_state_weight,
            jnp.pad(input_step_weight, ((0, 0), (0, LANES - heads))),
        ],
        axis=1,
    )
    w_out_own = output_projection.T

    w_in, w_out, tok_full, g_full, halo = plain_gather(
        w_own, w_out_own, tok, g, tok[:, length - HALO :]
    )
    grid = (count,)
    outs = [
        shape((count, length, model), BF16),
        shape((count, length, inner), F32),
        shape((count, HALO + length, channels), BF16),
        shape((count, length, channels), F32),
        shape((count, length, channels), BF16),
        shape((count, length, inner), F32),
        shape((count, inner, nstate), BF16),
        shape((count, length, 5 * LANES), F32),
        shape((count, HEAD_ROWS, LANES), F32),
    ]
    normed, gate, xs, pre, act, scan, state, aux, dec = call(
        functools.partial(forward_kernel, sizes),
        grid,
        [per_seq(tok_full), per_seq(halo), per_seq(doc), whole(prm), whole(w_in)],
        [per_seq(o) for o in outs],
        outs,
        [pltpu.VMEM((HALO + length, channels), F32)],
        name="forward",
    )(tok_full, halo, doc, prm, w_in)

    hin = plain_scan(state, dec, size, False)

    outs = [
        shape((count, length, inner), F32),
        shape((count, length, inner), F32),
        shape((count, length, LANES), F32),
    ]
    ins = (scan, act, aux, gate, hin, g_full)
    full, grad_norm, sums = call(
        functools.partial(gate_kernel, sizes),
        grid,
        [per_seq(a) for a in ins] + [whole(prm), whole(w_out)],
        [per_seq(o) for o in outs],
        outs,
        name="gate",
    )(*ins, prm, w_out)

    sums_in = swap_heads(sums)

    outs = [
        shape((count, length, half), F32),
        shape((count, length, half), BF16),
        shape((count, length, inner), BF16),
        shape((count, length, inner), BF16),
        shape((count, inner, nstate), BF16),
        shape((8, inner), F32),
        shape((model, inner), BF16),
        shape((model, inner), BF16),
    ]
    ins = (full, act, aux, gate, grad_norm, sums, sums_in, g_full, normed)
    keep, send, dy, ggate, prior, small_out, dout, dgate = call(
        functools.partial(output_kernel, sizes, total_inner),
        grid,
        [per_seq(a) for a in ins] + [whole(prm), whole(w_out)],
        [per_seq(o) for o in outs[:5]] + [whole(o) for o in outs[5:]],
        outs,
        [
            pltpu.VMEM((model, inner), F32),
            pltpu.VMEM((model, inner), F32),
            pltpu.VMEM((length, model), F32),
        ],
        name="output",
    )(*ins, prm, w_out)

    mixed = (tok.astype(F32) + (keep + swap_heads(send).astype(F32))).astype(BF16)
    later = plain_scan(prior, dec, size, True)

    outs = [
        shape((count, length, inner), F32),
        shape((count, length, nstate), F32),
        shape((count, length, nstate), BF16),
        shape((count, length, LANES), F32),
        shape((8, LANES), F32),
        shape((count, EDGE, inner), F32),
        shape((count, EDGE, nstate), F32),
    ]
    ins = (full, act, aux, dy, hin, later, state, doc, pre)
    gcx, own, other, gpre, small_scan, edge, slope = call(
        functools.partial(backward_kernel, sizes),
        grid,
        [per_seq(a) for a in ins] + [whole(prm)],
        [per_seq(o) if len(o.shape) == 3 else whole(o) for o in outs],
        outs,
        [pltpu.VMEM((length, length), F32)],
        name="backward",
    )(*ins, prm)

    recv, edge_in, edge_state = plain_states(other, own, slope, edge)

    outs = [
        shape((count, length, model), BF16),
        shape((model, inner + nstate + LANES), BF16),
        shape((8, inner + nstate), F32),
    ]
    ins = (gcx, own, recv, edge_in, edge_state, pre, xs, gpre, ggate, normed)
    part, dx, small_conv = call(
        functools.partial(conv_kernel, sizes),
        grid,
        [per_seq(a) for a in ins] + [whole(prm), whole(w_in)],
        [per_seq(outs[0]), whole(outs[1]), whole(outs[2])],
        outs,
        [
            pltpu.VMEM((model, inner + nstate + LANES), F32),
            pltpu.VMEM((HALO + length, inner + nstate), F32),
            pltpu.VMEM((length + EDGE, inner + nstate), F32),
        ],
        name="conv",
    )(*ins, prm, w_in)

    part_in = swap_heads(part)

    outs = [shape((count, length, half), F32), shape((8, model), F32)]
    ins = (tok_full, part, part_in, g)
    tokens_grad, small_norm = call(
        functools.partial(tokens_kernel, sizes),
        grid,
        [per_seq(a) for a in ins] + [whole(prm)],
        [per_seq(outs[0]), whole(outs[1])],
        outs,
        [pltpu.VMEM((length, model), F32)],
        name="tokens",
    )(*ins, prm)

    small = jnp.concatenate(
        [
            row(small_norm[0]),
            row(small_out[0]),
            row(small_out[1]),
            row(jnp.concatenate([small_scan[0], small_scan[1]])),
            jnp.pad(small_conv[: taps + 1, :inner], ((0, 0), (0, channels - inner))),
            jnp.zeros((16 - 5 - taps, channels), F32),
        ],
        axis=0,
    )
    own_states = small_conv[:, inner:]
    shared = jnp.concatenate(
        [jnp.where(core == 0, own_states, 0.0), jnp.where(core == 1, own_states, 0.0)], axis=1
    )
    (g_out, g_gate, g_x), small, shared = plain_sum((dout, dgate, dx), small, shared)
    g_states = plain_both(g_x[:, inner : inner + nstate])
    return (
        mixed.reshape(tokens.shape),
        tokens_grad.reshape(tokens.shape),
        small[0, :model],
        jnp.stack([g_gate, g_x[:, :inner]], axis=1),
        g_states,
        g_x[:, inner + nstate : inner + nstate + heads],
        small[4 : 4 + taps, :inner],
        small[4 + taps, :inner],
        shared[:taps],
        shared[taps],
        small[3, :heads],
        small[3, LANES : LANES + heads],
        small[2, :inner].reshape(heads, size).sum(axis=1),
        small[1, :inner],
        g_out.T,
    )


def solution(mesh):
    placed = (
        P(None, None, "seq", "head"),
        P(None, None, "seq"),
        P(),
        P("seq", None, "head"),
        P("seq", None),
        P("seq", "head"),
        P(None, "head"),
        P("head"),
        P(),
        P(),
        P("head"),
        P("head"),
        P("head"),
        P("head"),
        P("head", "seq"),
        P(None, None, "seq", "head"),
    )
    return jax.shard_map(
        shards,
        mesh=mesh,
        in_specs=placed,
        out_specs=(
            P(None, None, "seq", "head"),
            P(None, None, "seq", "head"),
            P(),
            P("seq", None, "head"),
            P("seq", None),
            P("seq", "head"),
            P(None, "head"),
            P("head"),
            P(),
            P(),
            P("head"),
            P("head"),
            P("head"),
            P("head"),
            P("head", "seq"),
        ),
        check_vma=False,
    )
```

```python
import functools

import jax
import jax.numpy as jnp
from jax import lax
from jax.experimental import pallas as pl
from jax.experimental.pallas import tpu as pltpu
from jax.sharding import PartitionSpec as P

F32 = jnp.float32
BF16 = jnp.bfloat16
EPSILON = 1e-05
MASKED = -1e30
HALO = 16
EDGE = 8
HEAD_ROWS = 16
LANES = 128
MESH = pl.DeviceIdType.MESH
NN = ((1,), (0,))
NT = ((1,), (1,))
TN = ((0,), (0,))
VMEM_LIMIT = 62 * 2**20

GAIN, INNER_GAIN, SKIP, BIAS, STEP_BIAS, RATE, TAPS = 0, 1, 2, 3, 4, 5, 6


def dot(a, b, dims=NN):
    return lax.dot_general(a, b, (dims, ((), ())), preferred_element_type=F32)


def split2(v):
    high = v.astype(BF16)
    return high, (v - high.astype(F32)).astype(BF16)


def split3(v):
    high = v.astype(BF16)
    rest = v - high.astype(F32)
    middle = rest.astype(BF16)
    return high, middle, (rest - middle.astype(F32)).astype(BF16)


def sigmoid(v):
    return 0.5 * jnp.tanh(0.5 * v) + 0.5


def softplus(v):
    return jnp.maximum(v, 0.0) + jnp.log1p(jnp.exp(-jnp.abs(v)))


def head_spread(inner, size):
    rows = lax.broadcasted_iota(jnp.int32, (LANES, inner), 0)
    columns = lax.broadcasted_iota(jnp.int32, (LANES, inner), 1)
    return jnp.where(rows == columns // size, 1.0, 0.0).astype(BF16)


def expand(per_head, spread):
    high, low = split2(per_head)
    return dot(high, spread) + dot(low, spread)


def head_sums(wide, spread):
    high, low = split2(wide)
    return dot(high, spread, NT) + dot(low, spread, NT)


def triangle(length, upper=False):
    rows = lax.broadcasted_iota(jnp.int32, (length, length), 0)
    columns = lax.broadcasted_iota(jnp.int32, (length, length), 1)
    kept = rows <= columns if upper else rows >= columns
    return kept, jnp.where(kept, 1.0, 0.0).astype(BF16)


def running_sum(ones, v):
    a, b, c = split3(v)
    return dot(ones, a) + dot(ones, b) + dot(ones, c)


def doc_numbers(doc, ones):
    flags = doc.astype(BF16)
    return dot(ones, flags, NT)[:, :1], dot(flags, ones, NT)[:1]


def call(kernel, grid, in_specs, out_specs, out_shape, scratch=(), name=None, flops=10**9):
    return pl.pallas_call(
        kernel,
        grid=grid,
        in_specs=in_specs,
        out_specs=out_specs,
        out_shape=out_shape,
        scratch_shapes=list(scratch),
        compiler_params=pltpu.CompilerParams(
            vmem_limit_bytes=VMEM_LIMIT, dimension_semantics=("arbitrary",) * len(grid)
        ),
        cost_estimate=pl.CostEstimate(flops=flops, bytes_accessed=10**7, transcendentals=0),
        name=name,
    )


def whole(array):
    rank = len(array.shape)
    return pl.BlockSpec(array.shape, lambda i: (0,) * rank)


def per_seq(array):
    rank = len(array.shape)
    return pl.BlockSpec((1,) + tuple(array.shape[1:]), lambda i: (i,) + (0,) * (rank - 1))


def shape(dims, dtype):
    return jax.ShapeDtypeStruct(tuple(dims), dtype)


def forward_kernel(
    sizes, tok, halo, doc, prm, w, normed_o, gate_o, xs_o, pre_o, act_o, scan_o, state_o, aux_o,
    dec_o, ext,
):
    length, inner, nstate, size, taps = sizes
    channels = inner + 2 * nstate
    first = lax.axis_index("seq") == 0
    edge = jnp.where(first, 0.0, halo[0].astype(F32))
    x = jnp.concatenate([edge, tok[0].astype(F32)], axis=0)
    scale = lax.rsqrt(jnp.mean(x * x, axis=-1, keepdims=True) + EPSILON)
    normed = (x * scale * prm[GAIN : GAIN + 1, : x.shape[1]]).astype(BF16)
    normed_o[0] = normed[HALO:]
    gate_o[0] = dot(normed[HALO:], w[:, :inner])
    xs = dot(normed, w[:, inner : inner + channels]).astype(BF16)
    xs_o[0] = xs
    ext[...] = xs.astype(F32)
    pre = prm[BIAS : BIAS + 1, :channels]
    for k in range(taps):
        start = HALO - taps + 1 + k
        pre = pre + prm[TAPS + k : TAPS + k + 1, :channels] * ext[start : start + length]
    pre_o[0] = pre
    act = (pre * sigmoid(pre)).astype(BF16)
    act_o[0] = act
    step_pre = (
        dot(normed[HALO:], w[:, inner + channels :]) + prm[STEP_BIAS : STEP_BIAS + 1, :LANES]
    )
    step = softplus(step_pre)
    kept, ones = triangle(length)
    log_decay = running_sum(ones, step * prm[RATE : RATE + 1, :LANES])
    doc_col, doc_row = doc_numbers(doc[0], ones)
    entry = jnp.where(doc_col == 0.0, jnp.exp(log_decay), 0.0)
    last = log_decay[length - 1 :]
    tail = jnp.where(doc_col == doc_col[length - 1 :], jnp.exp(last - log_decay), 0.0)
    aux_o[0, :, 0:LANES] = log_decay
    aux_o[0, :, LANES : 2 * LANES] = step
    aux_o[0, :, 2 * LANES : 3 * LANES] = step_pre
    aux_o[0, :, 3 * LANES : 4 * LANES] = entry
    aux_o[0, :, 4 * LANES :] = tail
    spread = head_spread(inner, size)
    values = act[:, :inner].astype(F32)
    inputs = values * expand(step, spread)
    low_inputs = inputs.astype(BF16)
    in_state = act[:, inner : inner + nstate]
    out_state = act[:, inner + nstate :]
    state_o[0] = dot((inputs * expand(tail, spread)).astype(BF16), in_state, TN).astype(BF16)
    scores = dot(out_state, in_state, NT)
    closed = jnp.where(kept & (doc_col == doc_row), 0.0, MASKED)
    log_rows = log_decay.T
    whole_decay = jnp.where(doc_row[:, length - 1 :] == 0.0, jnp.exp(log_rows[:HEAD_ROWS, length - 1 :]), 0.0)
    dec_o[0] = jnp.broadcast_to(whole_decay, (HEAD_ROWS, LANES))
    left = lax.broadcasted_iota(jnp.int32, (length, LANES), 1) < size
    for pair in range(inner // LANES):
        columns = slice(pair * LANES, (pair + 1) * LANES)
        part = low_inputs[:, columns]
        total = None
        for side in range(2):
            h = 2 * pair + side
            decay = jnp.exp(log_decay[:, h : h + 1] - log_rows[h : h + 1] + closed)
            own = jnp.where(left if side == 0 else ~left, part, jnp.zeros_like(part))
            term = dot((scores * decay).astype(BF16), own)
            total = term if total is None else total + term
        scan_o[0, :, columns] = total


def gate_kernel(sizes, scan, act, aux, gate, hin, g, prm, wout, full_o, gn_o, sums_o):
    length, inner, nstate, size, taps = sizes
    spread = head_spread(inner, size)
    values = act[0, :, :inner].astype(F32)
    out_state = act[0, :, inner + nstate :]
    scanned = scan[0] + dot(out_state, hin[0], NT) * expand(aux[0, :, 3 * LANES : 4 * LANES], spread)
    full_o[0] = scanned
    mixed = scanned + prm[SKIP : SKIP + 1, :inner] * values
    gated = mixed * (gate[0] * sigmoid(gate[0]))
    grad_norm = dot(g[0], wout[...])
    gn_o[0] = grad_norm
    squares = jnp.sum(gated * gated, axis=-1, keepdims=True)
    cross = jnp.sum(
        grad_norm * prm[INNER_GAIN : INNER_GAIN + 1, :inner] * gated, axis=-1, keepdims=True
    )
    lane = lax.broadcasted_iota(jnp.int32, (length, LANES), 1)
    sums_o[0] = jnp.where(lane == 0, squares, jnp.where(lane == 1, cross, 0.0))


def output_kernel(
    sizes, total_inner, full, act, aux, gate, gn, sums, sums_in, g, normed, prm, wout,
    keep_o, send_o, dy_o, ggate_o, prior_o, small_o, dout_o, dgate_o, acc_out, acc_gate, wide,
):
    length, inner, nstate, size, taps = sizes
    at = pl.program_id(0)
    spread = head_spread(inner, size)
    values = act[0, :, :inner].astype(F32)
    out_state = act[0, :, inner + nstate :]
    mixed = full[0] + prm[SKIP : SKIP + 1, :inner] * values
    z = gate[0]
    sig = sigmoid(z)
    swish = z * sig
    gated = mixed * swish
    both = sums[0] + sums_in[0]
    inner_scale = lax.rsqrt(both[:, 0:1] / total_inner + EPSILON)
    gain = prm[INNER_GAIN : INNER_GAIN + 1, :inner]
    unit = gated * inner_scale
    normal = (unit * gain).astype(BF16)
    wide[...] = dot(normal, wout[...], NT)
    half = wide.shape[1] // 2
    core = lax.axis_index("head")
    keep_o[0] = wide[:, pl.ds(pl.multiple_of(core * half, LANES), half)]
    send_o[0] = wide[:, pl.ds(pl.multiple_of((1 - core) * half, LANES), half)].astype(BF16)
    grad_norm = gn[0]
    grad_inner = jnp.sum(grad_norm * unit, axis=0, keepdims=True)
    grad_gated = inner_scale * (grad_norm * gain) - unit * (
        inner_scale * inner_scale * (both[:, 1:2] / total_inner)
    )
    dy = grad_gated * swish
    low_dy = dy.astype(BF16)
    dy_o[0] = low_dy
    ggate = (grad_gated * mixed * (sig * (1.0 + z * (1.0 - sig)))).astype(BF16)
    ggate_o[0] = ggate
    grad_skip = jnp.sum(dy * values, axis=0, keepdims=True)
    entry = expand(aux[0, :, 3 * LANES : 4 * LANES], spread)
    prior_o[0] = dot((dy * entry).astype(BF16), out_state, TN).astype(BF16)
    rows = jnp.concatenate([grad_inner, grad_skip, jnp.zeros((6, inner), F32)], axis=0)
    term_out = dot(g[0], normal, TN)
    term_gate = dot(normed[0], ggate, TN)

    @pl.when(at == 0)
    def _():
        small_o[...] = rows
        acc_out[...] = term_out
        acc_gate[...] = term_gate

    @pl.when(at > 0)
    def _():
        small_o[...] += rows
        acc_out[...] += term_out
        acc_gate[...] += term_gate

    @pl.when(at == pl.num_programs(0) - 1)
    def _():
        dout_o[...] = acc_out[...].astype(BF16)
        dgate_o[...] = acc_gate[...].astype(BF16)


def backward_kernel(
    sizes, full, act, aux, dy, hin, later, state, doc, pre, prm,
    gcx_o, own_o, send_o, gpre_o, small_o, edge_o, slope_o, dcb,
):
    length, inner, nstate, size, taps = sizes
    at = pl.program_id(0)
    core = lax.axis_index("head")
    spread = head_spread(inner, size)
    log_decay = aux[0, :, 0:LANES]
    step = aux[0, :, LANES : 2 * LANES]
    step_pre = aux[0, :, 2 * LANES : 3 * LANES]
    entry = aux[0, :, 3 * LANES : 4 * LANES]
    tail = aux[0, :, 4 * LANES :]
    values = act[0, :, :inner].astype(F32)
    in_state = act[0, :, inner : inner + nstate]
    out_state = act[0, :, inner + nstate :]
    low_dy = dy[0]
    wide_dy = low_dy.astype(F32)
    step_wide = expand(step, spread)
    tail_wide = expand(tail, spread)
    entry_wide = expand(entry, spread)
    inputs = values * step_wide
    low_inputs = inputs.astype(BF16)
    kept, ones = triangle(length)
    upper, ones_upper = triangle(length, True)
    doc_col, doc_row = doc_numbers(doc[0], ones)
    closed = jnp.where(upper & (doc_col == doc_row), 0.0, MASKED)
    scores = dot(in_state, out_state, NT)
    log_rows = log_decay.T
    left = lax.broadcasted_iota(jnp.int32, (length, LANES), 1) < size
    grad_inputs = tail_wide * dot(in_state, later[0], NT)
    parts = []
    for pair in range(inner // LANES):
        columns = slice(pair * LANES, (pair + 1) * LANES)
        pair_dy = low_dy[:, columns]
        pair_in = low_inputs[:, columns]
        total = grad_inputs[:, columns]
        for side in range(2):
            h = 2 * pair + side
            chosen = left if side == 0 else ~left
            own_dy = jnp.where(chosen, pair_dy, jnp.zeros_like(pair_dy))
            decay = jnp.exp(log_rows[h : h + 1] - log_decay[:, h : h + 1] + closed)
            total = total + dot((scores * decay).astype(BF16), own_dy)
            grad_decay = dot(pair_in, own_dy, NT) * decay
            if h == 0:
                dcb[...] = grad_decay
            else:
                dcb[...] += grad_decay
        parts.append(total)
    grad_inputs = jnp.concatenate(parts, axis=1)
    grad_scores = dcb[...]
    grad_in = dot(grad_scores.astype(BF16), out_state) + dot(
        (inputs * tail_wide).astype(BF16), later[0]
    )
    grad_out = dot(grad_scores.T.astype(BF16), in_state) + dot(
        (wide_dy * entry_wide).astype(BF16), hin[0]
    )
    entry_last = jnp.broadcast_to(entry[length - 1 :], (8, LANES))
    later_wide = later[0].astype(F32)
    lane_ones = jnp.ones((8, nstate), BF16)
    through = head_sums(
        sum(dot(lane_ones, piece, NT) for piece in split2(later_wide * hin[0].astype(F32))), spread
    )
    born = head_sums(
        sum(dot(lane_ones, piece, NT) for piece in split2(later_wide * state[0].astype(F32))), spread
    )
    ending = (born + entry_last * through)[:1]
    grad_log = head_sums(wide_dy * full[0], spread) - head_sums(
        low_inputs.astype(F32) * grad_inputs, spread
    )
    grad_rate_step = running_sum(ones_upper, grad_log) + ending
    rate = prm[RATE : RATE + 1, :LANES]
    grad_step = head_sums(values * grad_inputs, spread) + rate * grad_rate_step
    gpre = grad_step * sigmoid(step_pre)
    lane = lax.broadcasted_iota(jnp.int32, (length, LANES), 1)
    gpre = jnp.where(lane < inner // size, gpre, 0.0)
    gpre_o[0] = gpre
    grad_values = step_wide * grad_inputs + prm[SKIP : SKIP + 1, :inner] * wide_dy
    px = pre[0, :, :inner]
    sig = sigmoid(px)
    gcx = grad_values * (sig * (1.0 + px * (1.0 - sig)))
    gcx_o[0] = gcx
    edge_o[0] = gcx[:EDGE]
    is_first = core == 0
    own_o[0] = jnp.where(is_first, grad_in, grad_out)
    send_o[0] = jnp.where(is_first, grad_out, grad_in).astype(BF16)
    ps = pre[0, :EDGE, pl.ds(pl.multiple_of(inner + core * nstate, LANES), nstate)]
    sig = sigmoid(ps)
    slope_o[0] = sig * (1.0 + ps * (1.0 - sig))
    rows = jnp.concatenate(
        [
            jnp.sum(gpre, axis=0, keepdims=True),
            rate * jnp.sum(step * grad_rate_step, axis=0, keepdims=True),
            jnp.zeros((6, LANES), F32),
        ],
        axis=0,
    )

    @pl.when(at == 0)
    def _():
        small_o[...] = rows

    @pl.when(at > 0)
    def _():
        small_o[...] += rows


def conv_kernel(
    sizes, gcx, own, recv, edge, edge_state, pre, xs, gpre, ggate, normed, prm, w,
    part_o, dx_o, small_o, acc, ext, gext,
):
    length, inner, nstate, size, taps = sizes
    at = pl.program_id(0)
    core = lax.axis_index("head")
    last = lax.axis_index("seq") == lax.axis_size("seq") - 1
    mine = pl.ds(pl.multiple_of(inner + core * nstate, LANES), nstate)
    channels = inner + nstate
    ps = pre[0, :, mine]
    sig = sigmoid(ps)
    gst = (own[0] + recv[0].astype(F32)) * (sig * (1.0 + ps * (1.0 - sig)))
    gext[:length, :inner] = gcx[0]
    gext[:length, inner:] = gst
    gext[length:, :inner] = jnp.where(last, 0.0, edge[0])
    gext[length:, inner:] = jnp.where(last, 0.0, edge_state[0])
    ext[:, :inner] = xs[0, :, :inner].astype(F32)
    ext[:, inner:] = xs[0, :, mine].astype(F32)
    grad_conv = gext[:length]
    grad_in = None
    rows = []
    for k in range(taps):
        row = jnp.concatenate(
            [prm[TAPS + k : TAPS + k + 1, :inner], prm[TAPS + k : TAPS + k + 1, mine]], axis=1
        )
        term = row * gext[taps - 1 - k : taps - 1 - k + length]
        grad_in = term if grad_in is None else grad_in + term
        start = HALO - taps + 1 + k
        rows.append(jnp.sum(ext[start : start + length] * grad_conv, axis=0, keepdims=True))
    rows.append(jnp.sum(grad_conv, axis=0, keepdims=True))
    rows.append(jnp.zeros((8 - taps - 1, channels), F32))
    rows = jnp.concatenate(rows, axis=0)
    low = grad_in.astype(BF16)
    low_pre = gpre[0].astype(BF16)
    part = dot(ggate[0], w[:, :inner], NT)
    part = part + dot(low[:, :inner], w[:, inner : 2 * inner], NT)
    wst = w[:, pl.ds(pl.multiple_of(2 * inner + core * nstate, LANES), nstate)]
    part = part + dot(low[:, inner:], wst, NT)
    part = part + dot(low_pre, w[:, 2 * inner + 2 * nstate :], NT)
    part_o[0] = part.astype(BF16)
    stacked = jnp.concatenate([low, low_pre], axis=1)
    term = dot(normed[0], stacked, TN)

    @pl.when(at == 0)
    def _():
        small_o[...] = rows
        acc[...] = term

    @pl.when(at > 0)
    def _():
        small_o[...] += rows
        acc[...] += term

    @pl.when(at == pl.num_programs(0) - 1)
    def _():
        dx_o[...] = acc[...].astype(BF16)


def tokens_kernel(sizes, tok, part, recv, g, prm, out_o, small_o, wide):
    at = pl.program_id(0)
    core = lax.axis_index("head")
    x = tok[0].astype(F32)
    model = x.shape[1]
    scale = lax.rsqrt(jnp.mean(x * x, axis=-1, keepdims=True) + EPSILON)
    unit = x * scale
    grad_normed = part[0].astype(F32) + recv[0].astype(F32)
    r = grad_normed * prm[GAIN : GAIN + 1, :model]
    wide[...] = scale * (r - unit * jnp.mean(r * unit, axis=-1, keepdims=True))
    half = model // 2
    out_o[0] = g[0].astype(F32) + wide[:, pl.ds(pl.multiple_of(core * half, LANES), half)]
    rows = jnp.concatenate(
        [jnp.sum(grad_normed * unit, axis=0, keepdims=True), jnp.zeros((7, model), F32)], axis=0
    )

    @pl.when(at == 0)
    def _():
        small_o[...] = rows

    @pl.when(at > 0)
    def _():
        small_o[...] += rows


def swap_heads(v):
    return lax.ppermute(v, "head", [(0, 1), (1, 0)])


def shift(v, distance):
    devices = range(lax.axis_size("seq"))
    return lax.ppermute(
        v, "seq", [(i - distance, i) for i in devices if i - distance in devices]
    )


def plain_gather(w_in, w_out, tokens, grads, tails):
    return (
        lax.all_gather(w_in, "seq", axis=0, tiled=True),
        lax.all_gather(w_out, "seq", axis=0, tiled=True),
        lax.all_gather(tokens, "head", axis=2, tiled=True),
        lax.all_gather(grads, "head", axis=2, tiled=True),
        lax.all_gather(shift(tails, 1), "head", axis=2, tiled=True),
    )


def plain_scan(state, decay, size, backward):
    count, place = lax.axis_size("seq"), lax.axis_index("seq")
    heads = state.shape[1] // size
    wide = jnp.repeat(decay[:, :heads, 0], size, axis=1)[..., None]
    states = lax.all_gather(state, "seq")
    decays = lax.all_gather(wide, "seq")

    def one(k, carried):
        at = count - 1 - k if backward else k
        reached = at > place if backward else at < place
        return jnp.where(reached, decays[at] * carried + states[at].astype(F32), carried)

    return lax.fori_loop(0, count, one, jnp.zeros(state.shape, F32)).astype(BF16)


def plain_states(send, own, slope, edge):
    recv = swap_heads(send)
    mine = (own[:, :EDGE] + recv[:, :EDGE].astype(F32)) * slope
    return recv, shift(edge, -1), shift(mine, -1)


def plain_sum(pieces, small, shared):
    totals = [
        lax.psum_scatter(p.astype(F32), "seq", scatter_dimension=0, tiled=True) for p in pieces
    ]
    shared = lax.psum(shared, ("seq", "head"))
    return totals, lax.psum(small, "seq"), shared


def plain_both(v):
    return lax.all_gather(v, "head", axis=1, tiled=True)


PLANE = 4
LINE = 4
OFFSETS = (0, -1, 1, -2, 2, -3, 3)


def place():
    s, c = lax.axis_index("seq"), lax.axis_index("head")
    return s, c, s // PLANE, (s // 2) % 2, s % 2


def remote(src, dst, send_sem, recv_sem, device):
    return pltpu.make_async_remote_copy(
        src_ref=src,
        dst_ref=dst,
        send_sem=send_sem,
        recv_sem=recv_sem,
        device_id=device,
        device_id_type=MESH,
    )


def greet(relations):
    barrier = pltpu.get_barrier_semaphore()
    total = 0
    for exists, device in relations:
        if exists is True:
            pl.semaphore_signal(barrier, inc=1, device_id=device, device_id_type=MESH)
            total = total + 1
        else:
            pl.when(exists)(
                functools.partial(
                    pl.semaphore_signal, barrier, inc=1, device_id=device, device_id_type=MESH
                )
            )
            total = total + jnp.where(exists, 1, 0)
    pl.semaphore_wait(barrier, total)


def comm_call(kernel, ins, outs, scratch, collective, name, anywhere=False):
    space = pl.ANY if anywhere else pltpu.VMEM
    return pl.pallas_call(
        kernel,
        in_specs=[pl.BlockSpec(memory_space=space) for _ in ins],
        out_specs=[pl.BlockSpec(memory_space=space) for _ in outs],
        out_shape=outs,
        scratch_shapes=list(scratch),
        compiler_params=pltpu.CompilerParams(
            collective_id=collective, has_side_effects=True, vmem_limit_bytes=VMEM_LIMIT
        ),
        name=name,
    )(*ins)


def dma(*dims):
    return pltpu.SemaphoreType.DMA(dims)


SUM_OFFSETS = (3, -3, 2, -2, 1, -1, 0)


class Refs:
    def __init__(self, names, refs):
        self.__dict__.update(zip(names, refs))


def fused_call(body, steps, ins, outs, scratch, collective, name):
    names = list(ins) + list(outs) + list(scratch)

    def kernel(*refs):
        body(Refs(names, refs))

    results = pl.pallas_call(
        kernel,
        grid=(steps,) if steps else (),
        in_specs=[spec for _, spec in ins.values()],
        out_specs=[spec for _, spec in outs.values()],
        out_shape=[shaped for shaped, _ in outs.values()],
        scratch_shapes=list(scratch.values()),
        compiler_params=pltpu.CompilerParams(
            collective_id=collective,
            has_side_effects=True,
            vmem_limit_bytes=VMEM_LIMIT,
            dimension_semantics=("arbitrary",) if steps else None,
        ),
        name=name,
    )(*[array for array, _ in ins.values()])
    return Refs(list(outs), results)


ANYWHERE = pl.BlockSpec(memory_space=pl.ANY)
INSIDE = pl.BlockSpec(memory_space=pltpu.VMEM)


def stepped(array, index):
    rank = len(array.shape)
    return pl.BlockSpec((1,) + tuple(array.shape[1:]), lambda k: (index(k),) + (0,) * (rank - 1))


def during(first, count=4):
    return lambda k: jnp.clip(k - first, 0, count - 1)


def cyclic(last, count=4):
    return lambda k: jnp.where(k < last, k % count, count - 1)


def either(core, own, other):
    low = jnp.where(core == 0, own, other)
    return jnp.concatenate([low, jnp.where(core == 0, other, own)], axis=1)


LINE_X, LINE_Y, PLANE_X, PLANE_Y = range(4)


class Gather:
    def __init__(self, pieces, rows, sems):
        self.pieces, self.rows = pieces, rows
        self.local, self.zs, self.zr, self.as_, self.ar, self.bs, self.br = sems
        self.s, self.c, self.z, self.y, self.x = place()
        s, c = self.s, self.c
        self.up, self.down = self.z < LINE - 1, self.z > 0
        self.to_x, self.to_y = (s + 1 - 2 * self.x, c), (s + 2 - 4 * self.y, c)
        self.to_up, self.to_down = (s + PLANE, c), (s - PLANE, c)
        kinds = [piece[4] for piece in pieces]
        self.span = range(len(pieces))
        self.lines = [p for p in self.span if kinds[p] in (LINE_X, LINE_Y)]
        self.planes = [p for p in self.span if kinds[p] in (PLANE_X, PLANE_Y)]
        self.x_first = [kind in (LINE_X, PLANE_X) for kind in kinds]

    @staticmethod
    def semaphores(n):
        return dict(
            g0=dma(n), g1=dma(n, 2, 4), g2=dma(n, 4), g3=dma(n, 4), g4=dma(n, 4), g5=dma(n, 4, 2),
            g6=dma(n, 4, 2),
        )

    def at(self, p, index, count=1):
        src, dst, start, width, order = self.pieces[p]
        begin = pl.multiple_of(index * self.rows, 16)
        return dst.at[pl.ds(begin, count * self.rows), pl.ds(start, width)]

    def own(self, p):
        src, dst, start, width, order = self.pieces[p]
        return src.at[:, pl.ds(start, width)]

    def local_copy(self, p):
        return pltpu.make_async_copy(self.own(p), self.at(p, self.s), self.local.at[p])

    def block(self, p, zz):
        if p in self.planes:
            return self.at(p, zz * PLANE, PLANE)
        return self.at(p, zz * PLANE + self.y * 2 + self.x)

    def z_copy(self, p, off):
        zz = self.z + off
        dst = self.block(p, zz)
        src = self.own(p) if off == 0 and p in self.lines else dst
        step = abs(off)
        moves = []
        if off <= 0:
            sems = self.zs.at[p, 0, step], self.zr.at[p, zz]
            moves.append((self.up, remote(src, dst, *sems, self.to_up)))
        if off >= 0:
            sems = self.zs.at[p, 1, step], self.zr.at[p, zz]
            moves.append((self.down, remote(src, dst, *sems, self.to_down)))
        return moves

    def first_copy(self, p, off):
        zz = self.z + off
        dst = self.at(p, zz * PLANE + self.y * 2 + self.x)
        src = self.own(p) if off == 0 else dst
        device = self.to_x if self.x_first[p] else self.to_y
        return remote(src, dst, self.as_.at[p, zz], self.ar.at[p, zz], device)

    def second_copies(self, p, off):
        zz = self.z + off
        if self.x_first[p]:
            pair = self.at(p, zz * PLANE + self.y * 2, 2)
            return [remote(pair, pair, self.bs.at[p, zz, 0], self.br.at[p, zz, 0], self.to_y)]
        copies = []
        for k in range(2):
            block = self.at(p, zz * PLANE + k * 2 + self.x)
            copies.append(
                remote(block, block, self.bs.at[p, zz, k], self.br.at[p, zz, k], self.to_x)
            )
        return copies

    def exists(self, off):
        zz = self.z + off
        return (zz >= 0) & (zz < LINE)

    def begin(self):
        for p in self.span:
            if p in self.lines:
                for there, copy in self.z_copy(p, 0):
                    pl.when(there)(copy.start)
            self.first_copy(p, 0).start()
            self.local_copy(p).start()

    def z_arrived(self, *offs):
        for off in offs:

            @pl.when(self.exists(off))
            def _():
                for p in self.lines:
                    for there, copy in self.z_copy(p, off):
                        copy.wait_recv()
                        pl.when(there)(copy.start)
                    self.first_copy(p, off).start()

    def first_arrived(self, *offs):
        for off in offs:

            @pl.when(self.exists(off))
            def _():
                for p in self.lines:
                    if off == 0:
                        self.local_copy(p).wait()
                    self.first_copy(p, off).wait_recv()
                    for copy in self.second_copies(p, off):
                        copy.start()

    def plane_first(self):
        for p in self.planes:
            self.local_copy(p).wait()
            self.first_copy(p, 0).wait_recv()
            for copy in self.second_copies(p, 0):
                copy.start()

    def plane_second(self):
        for p in self.planes:
            for copy in self.second_copies(p, 0):
                copy.wait_recv()
            for there, copy in self.z_copy(p, 0):
                pl.when(there)(copy.start)

    def plane_arrived(self, *offs):
        for off in offs:

            @pl.when(self.exists(off))
            def _():
                for p in self.planes:
                    for there, copy in self.z_copy(p, off):
                        copy.wait_recv()
                        pl.when(there)(copy.start)

    def received(self):
        for off in OFFSETS:

            @pl.when(self.exists(off))
            def _():
                for p in self.lines:
                    for copy in self.second_copies(p, off):
                        copy.wait_recv()

    def drain(self):
        for off in OFFSETS:

            @pl.when(self.exists(off))
            def _():
                for p in self.lines:
                    for copy in self.second_copies(p, off):
                        copy.wait_send()
                    self.first_copy(p, off).wait_send()
                for p in self.span:
                    for there, copy in self.z_copy(p, off):
                        pl.when(there)(copy.wait_send)

        for p in self.planes:
            self.first_copy(p, 0).wait_send()
            for copy in self.second_copies(p, 0):
                copy.wait_send()


class Scan:
    def __init__(self, backward, size, state, decay, out, refs):
        self.state, self.decay, self.out, self.size = state, decay, out, size
        (
            self.slots, self.rates, self.total, self.through, self.pair, self.pair_through,
            self.far, self.leaving, self.staged, self.s1, self.r1, self.s2, self.r2, self.zs,
            self.zr, self.s3, self.r3,
        ) = refs
        s, c, z, y, x = place()
        self.s, self.c, self.p = s, c, s % PLANE
        self.base = s - self.p
        self.order = tuple(range(PLANE - 1, -1, -1)) if backward else tuple(range(PLANE))
        self.rows = state.shape[1] // PLANE
        self.place = LINE - 1 - z if backward else z
        self.step = -PLANE if backward else PLANE

    @staticmethod
    def scratch(count, rows, nstate, heads):
        quarter = rows // PLANE
        return dict(
            slots=pltpu.VMEM((count, PLANE, quarter, nstate), BF16),
            rates=pltpu.VMEM((count, PLANE, heads, nstate), F32),
            total=pltpu.VMEM((count, quarter, nstate), F32),
            through=pltpu.VMEM((count, 8, nstate), F32),
            pair=pltpu.VMEM((count, quarter, nstate), BF16),
            pair_through=pltpu.VMEM((count, 8, nstate), F32),
            far=pltpu.VMEM((count, quarter, nstate), BF16),
            leaving=pltpu.VMEM((count, quarter, nstate), BF16),
            staged=pltpu.VMEM((count, PLANE, quarter, nstate), BF16),
            s1=dma(count, PLANE), r1=dma(count, PLANE),
            s2=dma(count, PLANE), r2=dma(count, PLANE),
            zs=dma(count, 3), zr=dma(count, 3),
            s3=dma(count, PLANE), r3=dma(count, PLANE),
        )

    def relations(self):
        plane = [(self.p != j, (self.base + j, self.c)) for j in range(PLANE)]
        s, c, at, step = self.s, self.c, self.place, self.step
        return plane + [
            (at > 0, (s - step, c)),
            (at < LINE - 1, (s + step, c)),
            (at == 1, (s + 2 * step, c)),
            (at == 3, (s - 2 * step, c)),
        ]

    def part(self, j):
        return pl.ds(pl.multiple_of(j * self.rows, 16), self.rows)

    def first(self, i, j, slot):
        device = (self.base + j, self.c)
        return [
            remote(
                self.state.at[i, self.part(j)], self.slots.at[i, slot],
                self.s1.at[i, j], self.r1.at[i, slot], device,
            ),
            remote(
                self.decay.at[i], self.rates.at[i, slot], self.s2.at[i, j], self.r2.at[i, slot],
                device,
            ),
        ]

    def to_pair(self, i):
        device = (self.s + self.step, self.c)
        return [
            remote(self.leaving.at[i], self.pair.at[i], self.zs.at[i, 0], self.zr.at[i, 0], device),
            remote(
                self.through.at[i], self.pair_through.at[i], self.zs.at[i, 1], self.zr.at[i, 1],
                device,
            ),
        ]

    def to_far(self, i, n):
        return remote(
            self.leaving.at[i], self.far.at[i], self.zs.at[i, 0 if n == 1 else 2],
            self.zr.at[i, 2], (self.s + n * self.step, self.c),
        )

    def last(self, i, j, quarter):
        return remote(
            self.staged.at[i, j], self.out.at[i, self.part(quarter)],
            self.s3.at[i, j], self.r3.at[i, quarter], (self.base + j, self.c),
        )

    def others(self, act):
        for j in range(PLANE):
            pl.when(self.p != j)(functools.partial(act, j))

    def start(self, i):
        def send(j):
            for copy in self.first(i, j, self.p):
                copy.start()

        self.others(send)
        self.slots[i, self.p] = self.state[i, self.part(self.p)]
        self.rates[i, self.p] = self.decay[i]

    def pieces(self):
        for n in range(self.rows // self.size):
            yield n, slice(n * self.size, (n + 1) * self.size)

    def rate(self, i, j, n):
        return self.rates[i, j, pl.ds(self.p * (self.rows // self.size) + n, 1)]

    def deliver(self, i, entering):
        for n, rows in self.pieces():
            held = entering(n, rows)
            for at, j in enumerate(self.order):
                self.staged[i, j, rows] = held.astype(BF16)
                if at < PLANE - 1:
                    held = self.rate(i, j, n) * held + self.slots[i, j, rows].astype(F32)
        self.others(lambda j: self.last(i, j, self.p).start())
        self.out[i, self.part(self.p)] = self.staged[i, self.p]

    def fold(self, i):
        def arrived(j):
            for copy in self.first(i, j, j):
                copy.wait_recv()

        self.others(arrived)
        for n, rows in self.pieces():
            held = self.slots[i, self.order[0], rows].astype(F32)
            rate = self.rate(i, self.order[0], n)
            for j in self.order[1:]:
                own = self.rate(i, j, n)
                held = own * held + self.slots[i, j, rows].astype(F32)
                rate = own * rate
            self.total[i, rows] = held
            self.through[i, n : n + 1] = rate

        @pl.when((self.place == 0) | (self.place == 2))
        def _():
            self.leaving[i] = self.total[i].astype(BF16)
            for copy in self.to_pair(i):
                copy.start()

        @pl.when(self.place == 0)
        def _():
            self.deliver(i, lambda n, rows: jnp.zeros((self.size, self.out.shape[2]), F32))

    def join(self, i):
        @pl.when(self.place == 1)
        def _():
            for copy in self.to_pair(i):
                copy.wait_recv()
            for n, rows in self.pieces():
                self.leaving[i, rows] = (
                    self.total[i, rows]
                    + self.through[i, n : n + 1] * self.pair[i, rows].astype(F32)
                ).astype(BF16)
            for n in (1, 2):
                self.to_far(i, n).start()
            self.deliver(i, lambda n, rows: self.pair[i, rows].astype(F32))

    def close(self, i):
        @pl.when(self.place == 2)
        def _():
            self.to_far(i, 1).wait_recv()
            self.deliver(i, lambda n, rows: self.far[i, rows].astype(F32))

        @pl.when(self.place == 3)
        def _():
            for copy in self.to_pair(i):
                copy.wait_recv()
            self.to_far(i, 1).wait_recv()
            self.deliver(
                i,
                lambda n, rows: self.pair[i, rows].astype(F32)
                + self.pair_through[i, n : n + 1] * self.far[i, rows].astype(F32),
            )

    def arrived(self, i):
        self.others(lambda j: self.last(i, j, j).wait_recv())

    def finish(self):
        @pl.loop(0, self.state.shape[0])
        def _(i):
            def close(j):
                for copy in self.first(i, j, self.p):
                    copy.wait_send()
                self.last(i, j, self.p).wait_send()

            self.others(close)

            @pl.when((self.place == 0) | (self.place == 2))
            def _():
                for copy in self.to_pair(i):
                    copy.wait_send()

            @pl.when(self.place == 1)
            def _():
                for n in (1, 2):
                    self.to_far(i, n).wait_send()


class Reduce:
    def __init__(self, pieces, rows, refs):
        self.pieces, self.rows = pieces, rows
        (
            self.near, self.mid, self.above, self.below, self.mid_send, self.kept,
            self.s1, self.r1, self.s2, self.r2, self.sz, self.rz,
        ) = refs
        self.s, self.c, self.z, self.y, self.x = place()
        s, c = self.s, self.c
        self.up, self.down = self.z < LINE - 1, self.z > 0
        self.to_x, self.to_y = (s + 1 - 2 * self.x, c), (s + 2 - 4 * self.y, c)
        self.to_up, self.to_down = (s + PLANE, c), (s - PLANE, c)
        self.span = range(len(pieces))

    @staticmethod
    def scratch(n, rows, wide):
        return dict(
            near=pltpu.VMEM((LINE, 2 * rows, wide), BF16),
            mid=pltpu.VMEM((LINE, rows, wide), BF16),
            above=pltpu.VMEM((LINE, rows, wide), BF16),
            below=pltpu.VMEM((LINE, rows, wide), BF16),
            mid_send=pltpu.VMEM((LINE, rows, wide), BF16),
            kept=pltpu.VMEM((LINE, rows, wide), F32),
            t1=dma(n, LINE, 2), u1=dma(n, LINE, 2), t2=dma(n, LINE),
            u2=dma(n, LINE), tz=dma(n, LINE), uz=dma(n, 2, LINE),
        )

    def columns(self, p):
        return pl.ds(self.pieces[p][6], self.pieces[p][2])

    def source(self, p, index, count=1):
        ref, start, width = self.pieces[p][:3]
        begin = pl.multiple_of(index * self.rows, 16)
        return ref.at[pl.ds(begin, count * self.rows), pl.ds(start, width)]

    def index(self, zz, yy, xx):
        return zz * PLANE + yy * 2 + xx

    def near_copies(self, p, zz):
        if self.pieces[p][3]:
            return [
                remote(
                    self.source(p, self.index(zz, 1 - self.y, 0), 2),
                    self.near.at[zz, :, self.columns(p)],
                    self.s1.at[p, zz, 0], self.r1.at[p, zz, 0], self.to_y,
                )
            ]
        return [
            remote(
                self.source(p, self.index(zz, k, 1 - self.x)),
                self.near.at[zz, pl.ds(k * self.rows, self.rows), self.columns(p)],
                self.s1.at[p, zz, k], self.r1.at[p, zz, k], self.to_x,
            )
            for k in range(2)
        ]

    def mid_copy(self, p, zz):
        at = self.columns(p)
        return remote(
            self.mid_send.at[zz, :, at], self.mid.at[zz, :, at],
            self.s2.at[p, zz], self.r2.at[p, zz], self.to_x if self.pieces[p][3] else self.to_y,
        )

    def line_copy(self, p, zz, upward):
        at = self.columns(p)
        target = self.above if upward else self.below
        return remote(
            self.mid_send.at[zz, :, at], target.at[zz, :, at],
            self.sz.at[p, zz], self.rz.at[p, 0 if upward else 1, zz],
            self.to_up if upward else self.to_down,
        )

    def exists(self, off):
        zz = self.z + off
        return (zz >= 0) & (zz < LINE)

    def rows_of(self, k):
        return pl.ds(pl.multiple_of(k * self.rows, 16), self.rows)

    def begin(self, *pieces):
        for off in SUM_OFFSETS:

            @pl.when(self.exists(off))
            def _():
                for p in pieces or self.span:
                    for copy in self.near_copies(p, self.z + off):
                        copy.start()

    def second(self, *offs):
        for off in offs:

            @pl.when(self.exists(off))
            def _():
                zz = self.z + off
                y, x = self.y, self.x
                for p in self.span:
                    for copy in self.near_copies(p, zz):
                        copy.wait_recv()
                    own = self.index(zz, y, x)
                    if self.pieces[p][3]:
                        other, mine = self.index(zz, y, 1 - x), x
                    else:
                        other, mine = self.index(zz, 1 - y, x), y
                    at = self.columns(p)
                    sent = self.source(p, other)[...].astype(F32) + self.near[
                        zz, self.rows_of(1 - mine), at
                    ].astype(F32)
                    self.mid_send[zz, :, at] = sent.astype(BF16)
                    self.mid_copy(p, zz).start()
                    self.kept[zz, :, at] = self.source(p, own)[...].astype(F32) + self.near[
                        zz, self.rows_of(mine), at
                    ].astype(F32)

    def third(self, *offs, only=None):
        for off in offs:

            @pl.when(self.exists(off))
            def _():
                zz = self.z + off
                for p in self.span if only is None else only:
                    at = self.columns(p)
                    self.mid_copy(p, zz).wait_recv()
                    self.kept[zz, :, at] = self.kept[zz, :, at] + self.mid[zz, :, at].astype(F32)
                    if off >= 0:

                        @pl.when(self.down)
                        def _():
                            self.line_copy(p, zz, True).wait_recv()
                            self.kept[zz, :, at] = self.kept[zz, :, at] + self.above[
                                zz, :, at
                            ].astype(F32)

                    if off <= 0:

                        @pl.when(self.up)
                        def _():
                            self.line_copy(p, zz, False).wait_recv()
                            self.kept[zz, :, at] = self.kept[zz, :, at] + self.below[
                                zz, :, at
                            ].astype(F32)

                    if off == 0:
                        _, _, width, _, out, start, _ = self.pieces[p]
                        out[:, start : start + width] = self.kept[zz, :, at]
                    else:
                        self.mid_copy(p, zz).wait_send()
                        self.mid_send[zz, :, at] = self.kept[zz, :, at].astype(BF16)
                        self.line_copy(p, zz, off > 0).start()

    def near_sent(self):
        for off in SUM_OFFSETS:

            @pl.when(self.exists(off))
            def _():
                for p in self.span:
                    for copy in self.near_copies(p, self.z + off):
                        copy.wait_send()

    def finish(self):
        for off in SUM_OFFSETS:

            @pl.when(self.exists(off))
            def _():
                zz = self.z + off
                for p in self.span:
                    if off == 0:
                        self.mid_copy(p, zz).wait_send()
                    else:
                        self.line_copy(p, zz, off > 0).wait_send()


def picked(r, names):
    return tuple(r.__dict__[n] for n in names)


GATHER_REFS = tuple(Gather.semaphores(1))
SCAN_REFS = tuple(Scan.scratch(1, PLANE, 1, 1))
REDUCE_REFS = tuple(Reduce.scratch(1, 16, 1))


def main_body(sizes, total_inner, r):
    length, inner, nstate, size, taps = sizes
    channels = inner + 2 * nstate
    heads = inner // size
    count = r.tok.shape[0]
    half = r.tok.shape[2]
    s, c, z, y, x = place()
    to_core, to_prv = (s, 1 - c), (s - 1, c)
    nxt, prv = s < LINE * PLANE - 1, s > 0
    first_gather = Gather(
        (
            (r.w1, r.w, 0, 512, LINE_X),
            (r.w1, r.w, 512, 384, LINE_Y),
            (r.w1, r.w, 896, 128, PLANE_X),
            (r.w1, r.w, 1024, 128, PLANE_Y),
        ),
        r.w1.shape[0],
        picked(r, GATHER_REFS),
    )
    second_gather = Gather(
        (
            (r.w2, r.w2_full, 0, 512, LINE_X),
            (r.w2, r.w2_full, 512, 512, LINE_Y),
            (r.w2, r.w2_full, 1024, 256, PLANE_X),
            (r.w2, r.w2_full, 1280, 256, PLANE_Y),
        ),
        r.w2.shape[0],
        picked(r, SECOND_REFS),
    )
    prefix = Scan(False, size, r.state, r.dec, r.hin, picked(r, SCAN_REFS))
    suffix = Scan(True, size, r.prior, r.dec, r.later, picked(r, SUFFIX_REFS))
    reduce_ = Reduce(
        ((r.dout, 0, inner, True, r.g_out, 0, 0), (r.dgate, 0, inner, False, r.g_gate, 0, inner)),
        r.g_out.shape[0],
        picked(r, REDUCE_REFS),
    )
    wide = inner + nstate + LANES
    late = Reduce(
        (
            (r.dout, 0, wide // 2, True, r.g_x, 0, 0),
            (r.dgate, 0, wide // 2, False, r.g_x, wide // 2, wide // 2),
        ),
        r.g_x.shape[0],
        picked(r, LATE_REFS),
    )
    spread = head_spread(inner, size)
    mine = pl.ds(pl.multiple_of(inner + c * nstate, LANES), nstate)
    side = pl.ds(pl.multiple_of(c * half, LANES), half)
    other_side = pl.ds(pl.multiple_of((1 - c) * half, LANES), half)
    log_at, step_at, pre_at, entry_at = (
        slice(n * LANES, (n + 1) * LANES) for n in range(4)
    )
    scores_at = slice(half, half + length)
    own_at, slope_at, gpre_at = (
        slice(half + n * nstate, half + (n + 1) * nstate) for n in range(3)
    )
    left = lax.broadcasted_iota(jnp.int32, (length, LANES), 1) < size

    def swap(n, source, target):
        return lambda i: remote(
            source.at[i], target.at[i], r.ss.at[n, i], r.rs.at[n, i], to_core
        )

    swap_tokens = swap(0, r.tok, r.tok_in)
    swap_grads = swap(1, r.g, r.g_in)
    swap_sums = swap(2, r.sums, r.sums_in)
    swap_out = swap(3, r.osend, r.out_in)
    swap_states = swap(4, r.bsend, r.brecv)
    swap_part = swap(6, r.normal, r.low)

    def send_edge(i):
        return remote(r.edge.at[i], r.edge_in.at[i], r.ss.at[5, i], r.rs.at[5, i], to_prv)

    def halo_copy(k):
        tails = r.tok.at[:, pl.ds(length - HALO, HALO), :]
        device = (s + 1, c if k == 0 else 1 - c)
        return remote(tails, r.halo.at[:, :, side], r.hs.at[k], r.hr.at[k], device)

    def store_grad(i):
        return pltpu.make_async_copy(
            r.full.at[i, :, pl.ds(0, half)], r.tokens_grad.at[i], r.store.at[0, i]
        )

    def store_mixed(i):
        return pltpu.make_async_copy(r.g_in.at[i], r.mixed.at[i], r.store.at[1, i])

    def conv(at):
        pre = r.prm[BIAS : BIAS + 1, at]
        for t in range(taps):
            start = HALO - taps + 1 + t
            pre = pre + r.prm[TAPS + t : TAPS + t + 1, at] * r.ext[start : start + length, at]
        return pre

    greet(
        prefix.relations()
        + [(z != j, (s + (j - z) * PLANE, c)) for j in range(LINE)]
        + [
            (True, to_core),
            (nxt, (s + 1, c)),
            (nxt, (s + 1, 1 - c)),
            (prv, (s - 1, c)),
            (prv, (s - 1, 1 - c)),
        ]
    )
    first_gather.begin()
    for k in range(2):
        pl.when(nxt)(halo_copy(k).start)
    for i in range(count):
        swap_tokens(i).start()
    r.small[...] = jnp.zeros_like(r.small)
    first_gather.z_arrived(-1, 1)
    first_gather.plane_first()
    first_gather.first_arrived(0)
    second_gather.begin()
    for i in range(count):
        swap_grads(i).start()

    @pl.loop(0, count)
    def _(i):
        swap_tokens(i).wait()
        own, other = r.tok[i].astype(F32), r.tok_in[i].astype(F32)
        scale = lax.rsqrt(
            jnp.mean(own * own + other * other, axis=-1, keepdims=True) * 0.5 + EPSILON
        )
        gain_own = r.prm[GAIN : GAIN + 1, side]
        gain_other = r.prm[GAIN : GAIN + 1, other_side]
        r.normed_s[i, HALO:, side] = (own * scale * gain_own).astype(BF16)
        r.normed_s[i, HALO:, other_side] = (other * scale * gain_other).astype(BF16)

    first_gather.z_arrived(-2, 2)
    first_gather.plane_second()
    first_gather.first_arrived(-1, 1)
    for k in range(2):
        pl.when(nxt)(halo_copy(k).wait_send)
        pl.when(prv)(halo_copy(k).wait_recv)

    @pl.when(prv)
    def _():
        for i in range(count):
            edge = r.halo[i].astype(F32)
            scale = lax.rsqrt(jnp.mean(edge * edge, axis=-1, keepdims=True) + EPSILON)
            r.normed_s[i, :HALO] = (
                edge * scale * r.prm[GAIN : GAIN + 1, : edge.shape[1]]
            ).astype(BF16)

    @pl.when(jnp.logical_not(prv))
    def _():
        for i in range(count):
            r.normed_s[i, :HALO] = jnp.zeros((HALO, 2 * half), BF16)

    first_gather.z_arrived(-3, 3)
    first_gather.plane_arrived(-1, 1)
    first_gather.first_arrived(-2, 2)
    second_gather.z_arrived(-1, 1)
    second_gather.plane_first()
    first_gather.plane_arrived(-2, 2)
    first_gather.first_arrived(-3, 3)
    second_gather.first_arrived(0)
    first_gather.plane_arrived(-3, 3)
    first_gather.received()
    kept, ones = triangle(length)

    chunk = 2 * LANES
    chunks = [slice(n, n + chunk) for n in range(0, inner, chunk)]

    def spread_of(pieces, at):
        return sum(dot(piece, spread[:, at]) for piece in pieces)

    def tail_of(log_decay, doc_col):
        return jnp.where(
            doc_col == doc_col[length - 1 :], jnp.exp(log_decay[length - 1 :] - log_decay), 0.0
        )

    def project_chunk(i, at):
        xs = dot(r.normed_s[i], r.w[:, at]).astype(BF16)
        r.xs_s[i, :, at] = xs
        r.ext[:, at] = xs.astype(F32)
        pre = conv(at)
        act = (pre * sigmoid(pre)).astype(BF16)
        r.act[i, :, at] = act
        return act

    def project(i):
        project_chunk(i, slice(inner, channels))
        step_pre = (
            dot(r.normed_s[i, HALO:], r.w[:, channels:])
            + r.prm[STEP_BIAS : STEP_BIAS + 1, :LANES]
        )
        step = softplus(step_pre)
        log_decay = running_sum(ones, step * r.prm[RATE : RATE + 1, :LANES])
        doc_col, doc_row = doc_numbers(r.doc[i], ones)
        r.aux[i, :, log_at] = log_decay
        r.aux[i, :, step_at] = step
        r.aux[i, :, pre_at] = step_pre
        r.aux[i, :, entry_at] = jnp.where(doc_col == 0.0, jnp.exp(log_decay), 0.0)
        log_rows = log_decay.T
        whole_decay = jnp.where(
            doc_row[:, length - 1 :] == 0.0, jnp.exp(log_rows[:HEAD_ROWS, length - 1 :]), 0.0
        )
        r.dec[i] = jnp.broadcast_to(whole_decay, (HEAD_ROWS, LANES))
        steps, tails = split2(step), split2(tail_of(log_decay, doc_col))
        for at in chunks:
            act = project_chunk(i, at)
            inputs = act.astype(F32) * spread_of(steps, at)
            r.low[i, :, at] = inputs.astype(BF16)
            r.state[i, at] = dot(
                (inputs * spread_of(tails, at)).astype(BF16),
                r.act[i, :, inner : inner + nstate],
                TN,
            ).astype(BF16)
        prefix.start(i)

    @pl.loop(0, count)
    def _(i):
        project(i)

        @pl.when(i == 0)
        def _():
            second_gather.z_arrived(-2, 2)
            second_gather.plane_second()
            second_gather.first_arrived(-1, 1)

        @pl.when(i == 1)
        def _():
            second_gather.z_arrived(-3, 3)
            second_gather.first_arrived(-2, 2)

        @pl.when(i == 2)
        def _():
            prefix.fold(0)
            second_gather.plane_arrived(-1, 1)
            second_gather.first_arrived(-3, 3)

        @pl.when(i == 3)
        def _():
            prefix.fold(1)
            second_gather.plane_arrived(-2, 2)

    middle = length // 2
    below = ((slice(0, middle), slice(0, middle)), (slice(middle, length), slice(0, length)))
    above = ((slice(0, middle), slice(0, length)), (slice(middle, length), slice(middle, length)))

    def inside(i):
        log_decay = r.aux[i, :, log_at]
        log_rows = log_decay.T
        doc_col, doc_row = doc_numbers(r.doc[i], ones)
        scores = dot(r.act[i, :, inner + nstate :], r.act[i, :, inner : inner + nstate], NT)
        scores = jnp.where(kept & (doc_col == doc_row), scores, 0.0)
        for pair in range(inner // LANES):
            columns = slice(pair * LANES, (pair + 1) * LANES)
            part = r.low[i, :, columns]
            sides = [jnp.where(chosen, part, jnp.zeros_like(part)) for chosen in (left, ~left)]
            for to, ahead in below:
                total = None
                for n in range(2):
                    h = 2 * pair + n
                    decay = jnp.exp(
                        jnp.minimum(log_decay[to, h : h + 1] - log_rows[h : h + 1, ahead], 0.0)
                    )
                    term = dot((scores[to, ahead] * decay).astype(BF16), sides[n][ahead])
                    total = term if total is None else total + term
                r.full[i, to, columns] = total

    @pl.loop(0, count)
    def _(i):
        inside(i)

        @pl.when(i == 0)
        def _():
            prefix.join(0)
            second_gather.plane_arrived(-3, 3)

        @pl.when(i == 1)
        def _():
            prefix.fold(2)
            prefix.join(1)

        @pl.when(i == 2)
        def _():
            prefix.fold(3)
            prefix.close(0)

        @pl.when(i == 3)
        def _():
            prefix.join(2)
            prefix.close(1)

    second_gather.received()
    for i in range(count):
        swap_grads(i).wait()

    def gates(i):
        r.gate[i] = dot(r.normed_s[i, HALO:], r.w2_full[:, :inner])
        r.gn[i] = dot(either(c, r.g[i], r.g_in[i]), r.w2_full[:, inner:])

    @pl.loop(0, count)
    def _(i):
        gates(i)

        @pl.when(i == 0)
        def _():
            prefix.join(3)

        @pl.when(i == 1)
        def _():
            prefix.close(2)

    def combine(i):
        prefix.arrived(i)
        entries = split2(r.aux[i, :, entry_at])
        squares, cross = jnp.zeros((length, chunk), F32), jnp.zeros((length, chunk), F32)
        for at in chunks:
            from_behind = dot(r.act[i, :, inner + nstate :], r.hin[i, at], NT)
            scanned = r.full[i, :, at] + from_behind * spread_of(entries, at)
            r.full[i, :, at] = scanned
            mixed = scanned + r.prm[SKIP : SKIP + 1, at] * r.act[i, :, at].astype(F32)
            gate = r.gate[i, :, at]
            gated = mixed * (gate * sigmoid(gate))
            squares += gated * gated
            cross += r.gn[i, :, at] * r.prm[INNER_GAIN : INNER_GAIN + 1, at] * gated
        squares = jnp.sum(squares, axis=-1, keepdims=True)
        cross = jnp.sum(cross, axis=-1, keepdims=True)
        lane = lax.broadcasted_iota(jnp.int32, (length, LANES), 1)
        r.sums[i] = jnp.where(lane == 0, squares, jnp.where(lane == 1, cross, 0.0)).T[:EDGE]
        swap_sums(i).start()

    def norm_back(i):
        swap_sums(i).wait_recv()
        both = jnp.concatenate(
            [r.sums[i] + r.sums_in[i], jnp.zeros((LANES - EDGE, length), F32)], axis=0
        ).T
        inner_scale = lax.rsqrt(both[:, 0:1] / total_inner + EPSILON)
        factor = inner_scale * inner_scale * (both[:, 1:2] / total_inner)
        entries = split2(r.aux[i, :, entry_at])
        per_head = None
        for at in chunks:
            values = r.act[i, :, at].astype(F32)
            mixed = r.full[i, :, at] + r.prm[SKIP : SKIP + 1, at] * values
            gate = r.gate[i, :, at]
            sig = sigmoid(gate)
            swish = gate * sig
            unit = mixed * swish * inner_scale
            gain = r.prm[INNER_GAIN : INNER_GAIN + 1, at]
            r.normal[i, :, at] = (unit * gain).astype(BF16)
            grad_norm = r.gn[i, :, at]
            r.small[0:1, at] += jnp.sum(grad_norm * unit, axis=0, keepdims=True)
            grad_gated = inner_scale * (grad_norm * gain) - unit * factor
            dy = grad_gated * swish
            r.dy[i, :, at] = dy.astype(BF16)
            r.ggate_s[i, :, at] = (
                grad_gated * mixed * (sig * (1.0 + gate * (1.0 - sig)))
            ).astype(BF16)
            r.prior[i, at] = dot(
                (dy * spread_of(entries, at)).astype(BF16), r.act[i, :, inner + nstate :], TN
            ).astype(BF16)
            term = head_sums(
                jnp.broadcast_to(jnp.sum(dy * values, axis=0, keepdims=True), (8, chunk)),
                spread[:, at],
            )
            per_head = term if per_head is None else per_head + term
        suffix.start(i)
        r.small[1:2, :LANES] += per_head[:1]

    combine(0)
    combine(1)
    prefix.close(3)
    norm_back(0)
    combine(2)
    norm_back(1)
    combine(3)
    prefix.finish()
    norm_back(2)
    suffix.fold(0)
    norm_back(3)
    suffix.fold(1)

    def outputs(i):
        r.ginputs[...] = dot(r.normal[i], r.w2_full[:, inner:], NT)
        r.gate[i, :, :half] = r.ginputs[:, side]
        r.osend[i] = r.ginputs[:, other_side].astype(BF16)
        swap_out(i).start()

    pl.loop(0, count)(outputs)
    suffix.join(0)

    def weights_gradient(source, target, values, start, rows, step):
        for n in range(0, rows, step):
            total = None
            for i in range(count):
                term = dot(source(i, n, step), values[i], TN)
                total = term if total is None else total + term
            target[pl.ds(pl.multiple_of(start + n, LANES), step), :] = total.astype(BF16)

    def normed_block(i, n, step):
        return r.normed_s[i, HALO:, n : n + step]

    weights_gradient(
        lambda i, n, step: r.g[i, :, n : n + step], r.dout, r.normal, c * half, half, LANES
    )
    suffix.fold(2)
    weights_gradient(
        lambda i, n, step: r.g_in[i, :, n : n + step], r.dout, r.normal, (1 - c) * half, half,
        LANES,
    )
    suffix.fold(3)
    suffix.join(1)
    suffix.close(0)
    weights_gradient(normed_block, r.dgate, r.ggate_s, 0, 2 * half, 256)
    suffix.join(2)

    upper, ones_upper = triangle(length, True)

    def back_inside(i):
        log_decay = r.aux[i, :, log_at]
        in_state = r.act[i, :, inner : inner + nstate]
        out_state = r.act[i, :, inner + nstate :]
        doc_col, doc_row = doc_numbers(r.doc[i], ones)
        scores = dot(in_state, out_state, NT)
        scores = jnp.where(upper & (doc_col == doc_row), scores, 0.0)
        log_rows = log_decay.T
        for pair in range(inner // LANES):
            columns = slice(pair * LANES, (pair + 1) * LANES)
            pair_dy = r.dy[i, :, columns]
            pair_in = r.low[i, :, columns]
            sides = [jnp.where(chosen, pair_dy, jnp.zeros_like(pair_dy)) for chosen in (left, ~left)]
            for to, after in above:
                total, grad = None, None
                for n in range(2):
                    h = 2 * pair + n
                    own_dy = sides[n][after]
                    decay = jnp.exp(
                        jnp.minimum(log_rows[h : h + 1, after] - log_decay[to, h : h + 1], 0.0)
                    )
                    term = dot((scores[to, after] * decay).astype(BF16), own_dy)
                    total = term if total is None else total + term
                    term = dot(pair_in[to], own_dy, NT) * decay
                    grad = term if grad is None else grad + term
                at = slice(half + after.start, half + after.stop)
                if pair == 0:
                    r.gate[i, to, at] = grad
                else:
                    r.gate[i, to, at] += grad
                r.gn[i, to, columns] = total

    @pl.loop(0, count)
    def _(i):
        back_inside(i)

        @pl.when(i == 0)
        def _():
            suffix.close(1)
            suffix.join(3)

        @pl.when(i == 1)
        def _():
            suffix.close(2)

        @pl.when(i == 2)
        def _():
            suffix.close(3)
            reduce_.begin(0, 1)

    def back_rest(i):
        suffix.arrived(i)
        doc_col, doc_row = doc_numbers(r.doc[i], ones)
        log_decay = r.aux[i, :, log_at]
        step = r.aux[i, :, step_at]
        in_state = r.act[i, :, inner : inner + nstate]
        out_state = r.act[i, :, inner + nstate :]
        steps, tails, entries = (
            split2(v) for v in (step, tail_of(log_decay, doc_col), r.aux[i, :, entry_at])
        )
        grad_scores = jnp.where(upper & (doc_col == doc_row), r.gate[i, :, scores_at], 0.0)
        grad_in = dot(grad_scores.astype(BF16), out_state)
        grad_out = dot(grad_scores.T.astype(BF16), in_state)
        grad_log = jnp.zeros((length, LANES), F32)
        grad_step = jnp.zeros((length, LANES), F32)
        state_rows = []
        for pair in range(inner // LANES):
            at = slice(pair * LANES, (pair + 1) * LANES)
            step_wide, tail_wide, entry_wide = (
                spread_of(v, at) for v in (steps, tails, entries)
            )
            values = r.act[i, :, at].astype(F32)
            dy = r.dy[i, :, at].astype(F32)
            later, hin = r.later[i, at], r.hin[i, at]
            grad_inputs = r.gn[i, :, at] + tail_wide * dot(in_state, later, NT)
            grad_in += dot((values * step_wide * tail_wide).astype(BF16), later)
            grad_out += dot((dy * entry_wide).astype(BF16), hin)
            grad_log += head_sums(
                dy * r.full[i, :, at] - r.low[i, :, at].astype(F32) * grad_inputs, spread[:, at]
            )
            grad_step += head_sums(values * grad_inputs, spread[:, at])
            grad_values = step_wide * grad_inputs + r.prm[SKIP : SKIP + 1, at] * dy
            r.ext[:, at] = r.xs_s[i, :, at].astype(F32)
            px = conv(at)
            sig = sigmoid(px)
            gcx = grad_values * (sig * (1.0 + px * (1.0 - sig)))
            r.gn[i, :, at] = gcx
            r.edge[i, :, at] = gcx[:EDGE]
            leaving = r.state[i, at].astype(F32)
            for n in range(LANES // size):
                rows = slice(n * size, (n + 1) * size)
                h = pair * (LANES // size) + n
                whole_state = leaving[rows] + r.dec[i, h : h + 1] * hin[rows].astype(F32)
                state_rows.append(
                    jnp.sum(later[rows].astype(F32) * whole_state, axis=0, keepdims=True)
                )
        is_first = c == 0
        r.gate[i, :, own_at] = jnp.where(is_first, grad_in, grad_out)
        r.bsend[i] = jnp.where(is_first, grad_out, grad_in).astype(BF16)
        swap_states(i).start()
        state_rows.append(jnp.zeros((LANES - heads, LANES), F32))
        pieces = split2(jnp.concatenate(state_rows, axis=0))
        ending = sum(dot(jnp.ones((8, LANES), BF16), piece, NT) for piece in pieces)[:1]
        grad_rate_step = running_sum(ones_upper, grad_log) + ending
        rate = r.prm[RATE : RATE + 1, :LANES]
        grad_step = grad_step + rate * grad_rate_step
        lane = lax.broadcasted_iota(jnp.int32, (length, LANES), 1)
        gpre = jnp.where(lane < heads, grad_step * sigmoid(r.aux[i, :, pre_at]), 0.0)
        r.gate[i, :, gpre_at] = gpre
        r.ext[:, mine] = r.xs_s[i, :, mine].astype(F32)
        ps = conv(mine)
        sig = sigmoid(ps)
        r.gate[i, :, slope_at] = sig * (1.0 + ps * (1.0 - sig))
        r.small[1:2, LANES : 2 * LANES] += jnp.sum(gpre, axis=0, keepdims=True)
        r.small[1:2, 2 * LANES : 3 * LANES] += rate * jnp.sum(
            step * grad_rate_step, axis=0, keepdims=True
        )

    def finish_states(n):
        swap_states(n).wait_recv()
        gst = (r.gate[n, :, own_at] + r.brecv[n].astype(F32)) * r.gate[n, :, slope_at]
        r.gate[n, :, own_at] = gst
        r.edge[n, :, inner:] = gst[:EDGE]
        pl.when(prv)(send_edge(n).start)

    @pl.loop(0, count)
    def _(i):
        back_rest(i)
        pl.when(i > 0)(lambda: finish_states(i - 1))

        @pl.when(i == 1)
        def _():
            reduce_.second(3, -3)

        @pl.when(i == 2)
        def _():
            reduce_.second(2, -2)

        @pl.when(i == 3)
        def _():
            reduce_.second(1, -1)

    r.conv_rows[...] = jnp.zeros_like(r.conv_rows)
    r.bc[...] = jnp.zeros_like(r.bc)

    def conv_back(i):
        pl.when(nxt)(send_edge(i).wait_recv)

        def channel_block(source, at, own):
            grad_conv = source[...]
            r.gext[:length, at] = grad_conv
            r.gext[length:, at] = jnp.where(nxt, r.edge_in[i, :, at], 0.0)
            r.ext[:, at] = r.xs_s[i, :, own].astype(F32)
            grad_in = None
            for t in range(taps):
                term = r.prm[TAPS + t : TAPS + t + 1, own] * r.gext[
                    taps - 1 - t : taps - 1 - t + length, at
                ]
                grad_in = term if grad_in is None else grad_in + term
                start = HALO - taps + 1 + t
                r.conv_rows[t : t + 1, at] += jnp.sum(
                    r.ext[start : start + length, at] * grad_conv, axis=0, keepdims=True
                )
            r.conv_rows[taps : taps + 1, at] += jnp.sum(grad_conv, axis=0, keepdims=True)
            return grad_in.astype(BF16)

        for n in range(0, inner, LANES):
            at = slice(n, n + LANES)
            r.dy[i, :, at] = channel_block(r.gn.at[i, :, at], at, at)
        r.gtail[i, :, :nstate] = channel_block(
            r.gate.at[i, :, own_at], slice(inner, inner + nstate), mine
        )
        r.gtail[i, :, nstate:] = r.gate[i, :, gpre_at].astype(BF16)

    @pl.loop(0, count)
    def _(i):
        conv_back(i)

        @pl.when(i == 0)
        def _():
            finish_states(count - 1)
            reduce_.second(0)

        @pl.when(i == 1)
        def _():
            reduce_.third(3, -3)

        @pl.when(i == 2)
        def _():
            reduce_.third(2, -2)

        @pl.when(i == 3)
        def _():
            reduce_.third(1, -1)

    def small_copy(source, target, at, device):
        return remote(source, target, r.qs.at[at], r.qr.at[at], device)

    core_copy = small_copy(r.bc, r.bc_in, 0, to_core)
    x_copy = small_copy(r.work.at[0], r.from_x, 1, late.to_x)
    y_copy = small_copy(r.work.at[1], r.from_y, 2, late.to_y)
    states_copy = small_copy(r.states_s.at[c], r.states_s.at[c], 7, to_core)

    def z_small(j, slot):
        return remote(
            r.work.at[2], r.from_z.at[slot], r.qs.at[3 + j], r.qr.at[3 + slot],
            (s + (j - z) * PLANE, c),
        )

    for t in range(taps + 1):
        begin = (t % 3) * 2 * nstate
        own = r.conv_rows[t : t + 1, inner:]
        row = 1 + t // 3
        r.bc[row : row + 1, begin : begin + nstate] = jnp.where(c == 0, own, 0.0)
        r.bc[row : row + 1, begin + nstate : begin + 2 * nstate] = jnp.where(c == 1, own, 0.0)

    half_wide = wide // 2

    def last_gradient(values, target):
        for n in range(0, 2 * half, 256):
            total = None
            for i in range(count):
                term = dot(normed_block(i, n, 256), values(i), TN)
                total = term if total is None else total + term
            target[n : n + 256, :half_wide] = total.astype(BF16)

    reduce_.near_sent()
    last_gradient(lambda i: r.dy[i, :, :half_wide], r.dout)
    late.begin(0)
    last_gradient(
        lambda i: jnp.concatenate([r.dy[i, :, half_wide:], r.gtail[i]], axis=1), r.dgate
    )
    late.begin(1)
    reduce_.third(0)
    reduce_.finish()

    def part_back(i):
        part = dot(r.ggate_s[i], r.w2_full[:, :inner], NT)
        part = part + dot(r.dy[i], r.w[:, :inner], NT)
        part = part + dot(r.gtail[i, :, :nstate], r.w[:, mine], NT)
        part = part + dot(r.gtail[i, :, nstate:], r.w[:, channels:], NT)
        low_part = part.astype(BF16)
        r.normal[i] = low_part
        swap_part(i).start()
        tok = either(c, r.tok[i].astype(F32), r.tok_in[i].astype(F32))
        unit = tok * lax.rsqrt(jnp.mean(tok * tok, axis=-1, keepdims=True) + EPSILON)
        r.bc[0:1, :inner] += jnp.sum(low_part.astype(F32) * unit, axis=0, keepdims=True)

    @pl.loop(0, count)
    def _(i):
        part_back(i)

        @pl.when(i == 1)
        def _():
            late.second(3, -3)

        @pl.when(i == 2)
        def _():
            late.second(2, -2)

    core_copy.start()

    def tokens_back(i):
        swap_part(i).wait_recv()
        swap_out(i).wait_recv()
        own_tok = r.tok[i].astype(F32)
        tok = either(c, own_tok, r.tok_in[i].astype(F32))
        scale = lax.rsqrt(jnp.mean(tok * tok, axis=-1, keepdims=True) + EPSILON)
        unit = tok * scale
        grad_normed = r.normal[i].astype(F32) + r.low[i].astype(F32)
        grad = grad_normed * r.prm[GAIN : GAIN + 1, : 2 * half]
        r.ginputs[...] = scale * (grad - unit * jnp.mean(grad * unit, axis=-1, keepdims=True))
        r.full[i, :, :half] = r.g[i].astype(F32) + r.ginputs[:, side]
        store_grad(i).start()
        r.g_in[i] = (own_tok + (r.gate[i, :, :half] + r.out_in[i].astype(F32))).astype(BF16)
        store_mixed(i).start()

    @pl.loop(0, count)
    def _(i):
        tokens_back(i)

        @pl.when(i == 0)
        def _():
            late.second(1, -1)

        @pl.when(i == 1)
        def _():
            core_copy.wait_recv()
            r.work[0, 0:2] = r.small[0:2]
            r.work[0, 2 : 3 + taps] = r.conv_rows[: taps + 1, :inner]
            r.work[0, 3 + taps : 8] = jnp.zeros((5 - taps, inner), F32)
            r.work[0, 8:16] = r.bc[...] + r.bc_in[...]
            x_copy.start()

        @pl.when(i == 3)
        def _():
            late.third(3, -3)

    late.second(0)
    x_copy.wait_recv()
    r.work[1] = r.work[0] + r.from_x[...]
    y_copy.start()
    late.third(2, -2)
    y_copy.wait_recv()
    r.work[2] = r.work[1] + r.from_y[...]
    for j in range(LINE):
        pl.when(z != j)(z_small(j, z).start)
    r.from_z[z] = r.work[2]
    late.third(1, -1)
    late.third(0, only=(1,))
    r.states_s[c] = r.g_x[:, inner : inner + nstate]
    states_copy.start()
    late.third(0, only=(0,))
    for j in range(LINE):
        pl.when(z != j)(z_small(j, j).wait_recv)
    r.sums_out[...] = (r.from_z[0] + r.from_z[1]) + (r.from_z[2] + r.from_z[3])
    states_copy.wait()
    r.states[...] = r.states_s[...]
    core_copy.wait_send()
    x_copy.wait_send()
    y_copy.wait_send()
    for j in range(LINE):
        pl.when(z != j)(z_small(j, z).wait_send)
    late.near_sent()
    late.finish()
    suffix.finish()
    for gather in (first_gather, second_gather):
        gather.drain()

    @pl.loop(0, count)
    def _(i):
        swap_sums(i).wait_send()
        swap_out(i).wait_send()
        swap_states(i).wait_send()
        pl.when(prv)(send_edge(i).wait_send)
        swap_part(i).wait_send()
        store_grad(i).wait()
        store_mixed(i).wait()


LOCAL_REFS = tuple(dict(kept=0, mid_send=0))
LATE_REFS = tuple(n if n in LOCAL_REFS else "l" + n for n in REDUCE_REFS)
SECOND_REFS = tuple("s" + n for n in GATHER_REFS)
SHARED_REFS = tuple(dict(total=0, leaving=0, staged=0))
SUFFIX_REFS = tuple(n if n in SHARED_REFS else "s" + n for n in SCAN_REFS)


def main_call(sizes, total_inner, tok, g, doc, prm, w1, w2):
    length, inner, nstate, size, taps = sizes
    count, _, half = tok.shape
    model = 2 * half
    channels = inner + 2 * nstate
    rows = w1.shape[0]
    wide = inner + nstate + LANES
    ins = dict(
        tok=(tok, INSIDE), g=(g, INSIDE), doc=(doc, INSIDE), prm=(prm, INSIDE),
        w1=(w1, ANYWHERE), w2=(w2, ANYWHERE),
    )
    outs = dict(
        mixed=(shape((count, length, half), BF16), ANYWHERE),
        tokens_grad=(shape((count, length, half), F32), ANYWHERE),
        g_out=(shape((rows, inner), F32), INSIDE),
        g_gate=(shape((rows, inner), F32), INSIDE),
        g_x=(shape((rows, wide), F32), INSIDE),
        states=(shape((2, rows, nstate), F32), INSIDE),
        sums_out=(shape((16, inner), F32), INSIDE),
    )

    def vmem(*dims, dtype=F32):
        return pltpu.VMEM(dims, dtype)

    def low(*dims):
        return pltpu.VMEM(dims, BF16)

    scratch = dict(
        g_in=low(count, length, half),
        tok_in=low(count, length, half),
        out_in=low(count, length, half),
        edge_in=vmem(count, EDGE, inner + nstate),
        small=vmem(8, inner),
        gtail=low(count, length, nstate + LANES),
        gext=vmem(length + EDGE, inner + nstate),
        conv_rows=vmem(8, inner + nstate),
        states_s=vmem(2, rows, nstate),
        bc=vmem(8, inner),
        bc_in=vmem(8, inner),
        work=vmem(3, 16, inner),
        from_x=vmem(16, inner),
        from_y=vmem(16, inner),
        from_z=vmem(LINE, 16, inner),
        qs=dma(8),
        qr=dma(8),
        halo=low(count, HALO, model),
        w=low(model, w1.shape[1]),
        w2_full=low(model, 2 * inner),
        normed_s=low(count, HALO + length, model),
        xs_s=low(count, HALO + length, channels),
        act=low(count, length, channels),
        aux=vmem(count, length, 4 * LANES),
        low=low(count, length, inner),
        dec=vmem(count, HEAD_ROWS, LANES),
        state=low(count, inner, nstate),
        hin=low(count, inner, nstate),
        prior=low(count, inner, nstate),
        later=low(count, inner, nstate),
        full=vmem(count, length, inner),
        gate=vmem(count, length, inner),
        gn=vmem(count, length, inner),
        sums=vmem(count, EDGE, length),
        sums_in=vmem(count, EDGE, length),
        normal=low(count, length, inner),
        dy=low(count, length, inner),
        ggate_s=low(count, length, inner),
        osend=low(count, length, half),
        dout=low(model, inner),
        dgate=low(model, inner),
        ext=vmem(HALO + length, channels),
        ginputs=vmem(length, inner),
        bsend=low(count, length, nstate),
        brecv=low(count, length, nstate),
        edge=vmem(count, EDGE, inner + nstate),
        ss=dma(7, count),
        rs=dma(7, count),
        hs=dma(2),
        hr=dma(2),
        store=dma(2, count),
    )
    scan = Scan.scratch(count, inner, nstate, HEAD_ROWS)
    gather = Gather.semaphores(4)
    scratch.update(zip(SUFFIX_REFS, scan.values()))
    scratch.update(scan)
    scratch.update(gather)
    scratch.update(zip(SECOND_REFS, gather.values()))
    scratch.update(zip(LATE_REFS, Reduce.scratch(2, rows, wide).values()))
    scratch.update(Reduce.scratch(2, rows, 2 * inner))
    return fused_call(
        functools.partial(main_body, sizes, total_inner), None, ins, outs, scratch, 1, "main"
    )


def local_call(body, ins, outs, name):
    names = list(ins) + list(outs)

    def kernel(*refs):
        body(Refs(names, refs))

    results = pl.pallas_call(
        kernel,
        in_specs=[INSIDE for _ in ins],
        out_specs=[INSIDE for _ in outs],
        out_shape=list(outs.values()),
        name=name,
    )(*ins.values())
    return Refs(list(outs), results)


def pack_body(sizes, r):
    length, inner, nstate, size, taps = sizes
    heads = inner // size
    channels = inner + 2 * nstate
    model = r.norm_gain.shape[0]

    def line(v):
        return v.reshape(1, v.shape[0])

    r.prm[...] = jnp.zeros_like(r.prm)
    r.prm[GAIN : GAIN + 1, :model] = line(r.norm_gain[...])
    r.prm[INNER_GAIN : INNER_GAIN + 1, :inner] = line(r.inner_gain[...])
    r.prm[BIAS : BIAS + 1, :inner] = line(r.conv_bias_x[...])
    r.prm[BIAS : BIAS + 1, inner:] = line(r.conv_bias_bc[...])
    r.prm[STEP_BIAS : STEP_BIAS + 1, :heads] = line(r.step_bias[...])
    r.prm[RATE : RATE + 1, :heads] = -jnp.exp(line(r.decay_log[...]))
    r.prm[TAPS : TAPS + taps, :inner] = r.conv_taps_x[...]
    r.prm[TAPS : TAPS + taps, inner:] = r.conv_taps_bc[...]
    r.prm[SKIP : SKIP + 1, :heads] = line(r.skip_gain[...])
    skip = jnp.broadcast_to(r.prm[SKIP : SKIP + 1, :LANES], (8, LANES))
    spread = head_spread(inner, size)
    r.prm[SKIP : SKIP + 1, :inner] = sum(dot(v, spread) for v in split3(skip))[:1]
    r.w2[:, :inner] = r.features[:, 0, :]
    same = lax.broadcasted_iota(jnp.int32, (heads, LANES), 0) == lax.broadcasted_iota(
        jnp.int32, (heads, LANES), 1
    )
    r.w2[:, inner:] = r.output_projection[...]
    r.w1[:, :inner] = r.features[:, 1, :]
    r.w1[:, inner:channels] = r.state_weight[...]
    r.w1[:, channels:] = dot(
        r.step_weight[...], jnp.where(same, 1.0, 0.0).astype(BF16), TN
    ).astype(BF16)
    seqs = r.starts.shape[1]
    for i in range(r.doc.shape[0]):
        flags = r.starts[i // seqs, i % seqs : i % seqs + 1].astype(F32)
        r.doc[i] = jnp.broadcast_to(flags, (8, length))


def results_body(sizes, r):
    length, inner, nstate, size, taps = sizes
    heads = inner // size
    r.norm_gain[...] = r.sums[8]
    r.gate_x[:, 0, :] = r.g_gate[...]
    r.gate_x[:, 1, :] = r.g_x[:, :inner]
    r.state_weight[:, :nstate] = r.states[0]
    r.state_weight[:, nstate:] = r.states[1]
    r.step_weight[...] = r.g_x[:, inner + nstate :].T[:heads]
    r.taps_x[...] = r.sums[2 : 2 + taps]
    r.bias_x[...] = r.sums[2 + taps]
    for t in range(taps + 1):
        begin = (t % 3) * 2 * nstate
        row = r.sums[9 + t // 3, begin : begin + 2 * nstate]
        if t < taps:
            r.taps_bc[t] = row
        else:
            r.bias_bc[...] = row
    r.step_bias[...] = r.sums[1, LANES : LANES + heads]
    r.decay_log[...] = r.sums[1, 2 * LANES : 2 * LANES + heads]
    r.skip_gain[...] = r.sums[1, :heads]
    r.inner_gain[...] = r.sums[0]


def fused_layer(
    sizes, total_inner, tok, g, starts, norm_gain, features, state_weight, step_weight, conv_taps_x,
    conv_bias_x, conv_taps_bc, conv_bias_bc, step_bias, decay_log, skip_gain, inner_gain,
    output_projection,
):
    length, inner, nstate, size, taps = sizes
    heads = inner // size
    count, _, half = tok.shape
    model = 2 * half
    rows = features.shape[0]
    channels = inner + 2 * nstate
    packed = local_call(
        functools.partial(pack_body, sizes),
        dict(
            norm_gain=norm_gain, inner_gain=inner_gain, conv_bias_x=conv_bias_x,
            conv_bias_bc=conv_bias_bc, step_bias=step_bias, decay_log=decay_log,
            conv_taps_x=conv_taps_x, conv_taps_bc=conv_taps_bc, skip_gain=skip_gain,
            features=features, state_weight=state_weight, step_weight=step_weight.T,
            output_projection=output_projection.T, starts=starts,
        ),
        dict(
            prm=shape((16, channels), F32),
            w1=shape((rows, channels + LANES), BF16),
            w2=shape((rows, 2 * inner), BF16),
            doc=shape((count, 8, length), F32),
        ),
        "pack",
    )
    m = main_call(sizes, total_inner, tok, g, packed.doc, packed.prm, packed.w1, packed.w2)
    o = local_call(
        functools.partial(results_body, sizes),
        dict(sums=m.sums_out, g_x=m.g_x, g_gate=m.g_gate, states=m.states),
        dict(
            norm_gain=shape((model,), F32),
            gate_x=shape((rows, 2, inner), F32),
            state_weight=shape((rows, 2 * nstate), F32),
            step_weight=shape((heads, rows), F32),
            taps_x=shape((taps, inner), F32),
            bias_x=shape((inner,), F32),
            taps_bc=shape((taps, 2 * nstate), F32),
            bias_bc=shape((2 * nstate,), F32),
            step_bias=shape((heads,), F32),
            decay_log=shape((heads,), F32),
            skip_gain=shape((heads,), F32),
            inner_gain=shape((inner,), F32),
        ),
        "results",
    )
    o.step_weight = o.step_weight.T
    return (m.mixed, m.tokens_grad) + tuple(o.__dict__.values()) + (m.g_out.T,)


def shards(
    tokens, doc_starts, norm_gain, input_gate_features, input_state_weight, input_step_weight,
    conv_taps_x, conv_bias_x, conv_taps_bc, conv_bias_bc, step_bias, decay_log, skip_gain,
    inner_gain, output_projection, out_grad,
):
    micro, seqs, length, half = tokens.shape
    count = micro * seqs
    model = 2 * half
    heads = step_bias.shape[0]
    inner = inner_gain.shape[0]
    size = inner // heads
    nstate = conv_taps_bc.shape[1] // 2
    taps = conv_taps_x.shape[0]
    channels = inner + 2 * nstate
    rows = input_gate_features.shape[0]
    total_inner = inner * lax.axis_size("head")
    sizes = (length, inner, nstate, size, taps)
    core = lax.axis_index("head")

    tok = tokens.reshape(count, length, half)
    g = out_grad.reshape(count, length, half)
    if lax.axis_size("seq") == PLANE * LINE and lax.axis_size("head") == 2:
        outputs = fused_layer(
            sizes, total_inner, tok, g, doc_starts, norm_gain, input_gate_features,
            input_state_weight, input_step_weight, conv_taps_x, conv_bias_x, conv_taps_bc,
            conv_bias_bc, step_bias, decay_log, skip_gain, inner_gain, output_projection,
        )
        return tuple(o.reshape(tokens.shape) if n < 2 else o for n, o in enumerate(outputs))

    doc = jnp.broadcast_to(
        doc_starts.reshape(count, 1, length).astype(F32), (count, 8, length)
    )

    def row(v):
        return jnp.pad(v, (0, channels - v.shape[0]))[None]

    prm = jnp.concatenate(
        [
            row(norm_gain),
            row(inner_gain),
            row(jnp.repeat(skip_gain, size)),
            row(jnp.concatenate([conv_bias_x, conv_bias_bc])),
            row(step_bias),
            row(-jnp.exp(decay_log)),
            jnp.concatenate([conv_taps_x, conv_taps_bc], axis=1),
        ],
        axis=0,
    )
    prm = jnp.pad(prm, ((0, 16 - prm.shape[0]), (0, 0)))
    w_own = jnp.concatenate(
        [
            input_gate_features.reshape(rows, 2 * inner),
            input_state_weight,
            jnp.pad(input_step_weight, ((0, 0), (0, LANES - heads))),
        ],
        axis=1,
    )
    w_out_own = output_projection.T

    w_in, w_out, tok_full, g_full, halo = plain_gather(
        w_own, w_out_own, tok, g, tok[:, length - HALO :]
    )
    grid = (count,)
    outs = [
        shape((count, length, model), BF16),
        shape((count, length, inner), F32),
        shape((count, HALO + length, channels), BF16),
        shape((count, length, channels), F32),
        shape((count, length, channels), BF16),
        shape((count, length, inner), F32),
        shape((count, inner, nstate), BF16),
        shape((count, length, 5 * LANES), F32),
        shape((count, HEAD_ROWS, LANES), F32),
    ]
    normed, gate, xs, pre, act, scan, state, aux, dec = call(
        functools.partial(forward_kernel, sizes),
        grid,
        [per_seq(tok_full), per_seq(halo), per_seq(doc), whole(prm), whole(w_in)],
        [per_seq(o) for o in outs],
        outs,
        [pltpu.VMEM((HALO + length, channels), F32)],
        name="forward",
    )(tok_full, halo, doc, prm, w_in)

    hin = plain_scan(state, dec, size, False)

    outs = [
        shape((count, length, inner), F32),
        shape((count, length, inner), F32),
        shape((count, length, LANES), F32),
    ]
    ins = (scan, act, aux, gate, hin, g_full)
    full, grad_norm, sums = call(
        functools.partial(gate_kernel, sizes),
        grid,
        [per_seq(a) for a in ins] + [whole(prm), whole(w_out)],
        [per_seq(o) for o in outs],
        outs,
        name="gate",
    )(*ins, prm, w_out)

    sums_in = swap_heads(sums)

    outs = [
        shape((count, length, half), F32),
        shape((count, length, half), BF16),
        shape((count, length, inner), BF16),
        shape((count, length, inner), BF16),
        shape((count, inner, nstate), BF16),
        shape((8, inner), F32),
        shape((model, inner), BF16),
        shape((model, inner), BF16),
    ]
    ins = (full, act, aux, gate, grad_norm, sums, sums_in, g_full, normed)
    keep, send, dy, ggate, prior, small_out, dout, dgate = call(
        functools.partial(output_kernel, sizes, total_inner),
        grid,
        [per_seq(a) for a in ins] + [whole(prm), whole(w_out)],
        [per_seq(o) for o in outs[:5]] + [whole(o) for o in outs[5:]],
        outs,
        [
            pltpu.VMEM((model, inner), F32),
            pltpu.VMEM((model, inner), F32),
            pltpu.VMEM((length, model), F32),
        ],
        name="output",
    )(*ins, prm, w_out)

    mixed = (tok.astype(F32) + (keep + swap_heads(send).astype(F32))).astype(BF16)
    later = plain_scan(prior, dec, size, True)

    outs = [
        shape((count, length, inner), F32),
        shape((count, length, nstate), F32),
        shape((count, length, nstate), BF16),
        shape((count, length, LANES), F32),
        shape((8, LANES), F32),
        shape((count, EDGE, inner), F32),
        shape((count, EDGE, nstate), F32),
    ]
    ins = (full, act, aux, dy, hin, later, state, doc, pre)
    gcx, own, other, gpre, small_scan, edge, slope = call(
        functools.partial(backward_kernel, sizes),
        grid,
        [per_seq(a) for a in ins] + [whole(prm)],
        [per_seq(o) if len(o.shape) == 3 else whole(o) for o in outs],
        outs,
        [pltpu.VMEM((length, length), F32)],
        name="backward",
    )(*ins, prm)

    recv, edge_in, edge_state = plain_states(other, own, slope, edge)

    outs = [
        shape((count, length, model), BF16),
        shape((model, inner + nstate + LANES), BF16),
        shape((8, inner + nstate), F32),
    ]
    ins = (gcx, own, recv, edge_in, edge_state, pre, xs, gpre, ggate, normed)
    part, dx, small_conv = call(
        functools.partial(conv_kernel, sizes),
        grid,
        [per_seq(a) for a in ins] + [whole(prm), whole(w_in)],
        [per_seq(outs[0]), whole(outs[1]), whole(outs[2])],
        outs,
        [
            pltpu.VMEM((model, inner + nstate + LANES), F32),
            pltpu.VMEM((HALO + length, inner + nstate), F32),
            pltpu.VMEM((length + EDGE, inner + nstate), F32),
        ],
        name="conv",
    )(*ins, prm, w_in)

    part_in = swap_heads(part)

    outs = [shape((count, length, half), F32), shape((8, model), F32)]
    ins = (tok_full, part, part_in, g)
    tokens_grad, small_norm = call(
        functools.partial(tokens_kernel, sizes),
        grid,
        [per_seq(a) for a in ins] + [whole(prm)],
        [per_seq(outs[0]), whole(outs[1])],
        outs,
        [pltpu.VMEM((length, model), F32)],
        name="tokens",
    )(*ins, prm)

    small = jnp.concatenate(
        [
            row(small_norm[0]),
            row(small_out[0]),
            row(small_out[1]),
            row(jnp.concatenate([small_scan[0], small_scan[1]])),
            jnp.pad(small_conv[: taps + 1, :inner], ((0, 0), (0, channels - inner))),
            jnp.zeros((16 - 5 - taps, channels), F32),
        ],
        axis=0,
    )
    own_states = small_conv[:, inner:]
    shared = jnp.concatenate(
        [jnp.where(core == 0, own_states, 0.0), jnp.where(core == 1, own_states, 0.0)], axis=1
    )
    (g_out, g_gate, g_x), small, shared = plain_sum((dout, dgate, dx), small, shared)
    g_states = plain_both(g_x[:, inner : inner + nstate])
    return (
        mixed.reshape(tokens.shape),
        tokens_grad.reshape(tokens.shape),
        small[0, :model],
        jnp.stack([g_gate, g_x[:, :inner]], axis=1),
        g_states,
        g_x[:, inner + nstate : inner + nstate + heads],
        small[4 : 4 + taps, :inner],
        small[4 + taps, :inner],
        shared[:taps],
        shared[taps],
        small[3, :heads],
        small[3, LANES : LANES + heads],
        small[2, :inner].reshape(heads, size).sum(axis=1),
        small[1, :inner],
        g_out.T,
    )


def solution(mesh):
    placed = (
        P(None, None, "seq", "head"),
        P(None, None, "seq"),
        P(),
        P("seq", None, "head"),
        P("seq", None),
        P("seq", "head"),
        P(None, "head"),
        P("head"),
        P(),
        P(),
        P("head"),
        P("head"),
        P("head"),
        P("head"),
        P("head", "seq"),
        P(None, None, "seq", "head"),
    )
    return jax.shard_map(
        shards,
        mesh=mesh,
        in_specs=placed,
        out_specs=(
            P(None, None, "seq", "head"),
            P(None, None, "seq", "head"),
            P(),
            P("seq", None, "head"),
            P("seq", None),
            P("seq", "head"),
            P(None, "head"),
            P("head"),
            P(),
            P(),
            P("head"),
            P("head"),
            P("head"),
            P("head"),
            P("head", "seq"),
        ),
        check_vma=False,
    )
```

```python
import functools

import jax
import jax.numpy as jnp
from jax import lax
from jax.experimental import pallas as pl
from jax.experimental.pallas import tpu as pltpu
from jax.sharding import PartitionSpec as P

F32 = jnp.float32
BF16 = jnp.bfloat16
EPSILON = 1e-05
MASKED = -1e30
HALO = 16
EDGE = 8
HEAD_ROWS = 16
LANES = 128
MESH = pl.DeviceIdType.MESH
NN = ((1,), (0,))
NT = ((1,), (1,))
TN = ((0,), (0,))
VMEM_LIMIT = 62 * 2**20

GAIN, INNER_GAIN, SKIP, BIAS, STEP_BIAS, RATE, TAPS = 0, 1, 2, 3, 4, 5, 6


def dot(a, b, dims=NN):
    return lax.dot_general(a, b, (dims, ((), ())), preferred_element_type=F32)


def split2(v):
    high = v.astype(BF16)
    return high, (v - high.astype(F32)).astype(BF16)


def split3(v):
    high = v.astype(BF16)
    rest = v - high.astype(F32)
    middle = rest.astype(BF16)
    return high, middle, (rest - middle.astype(F32)).astype(BF16)


def sigmoid(v):
    return 0.5 * jnp.tanh(0.5 * v) + 0.5


def softplus(v):
    return jnp.maximum(v, 0.0) + jnp.log1p(jnp.exp(-jnp.abs(v)))


def head_spread(inner, size):
    rows = lax.broadcasted_iota(jnp.int32, (LANES, inner), 0)
    columns = lax.broadcasted_iota(jnp.int32, (LANES, inner), 1)
    return jnp.where(rows == columns // size, 1.0, 0.0).astype(BF16)


def expand(per_head, spread):
    high, low = split2(per_head)
    return dot(high, spread) + dot(low, spread)


def head_sums(wide, spread):
    high, low = split2(wide)
    return dot(high, spread, NT) + dot(low, spread, NT)


def triangle(length, upper=False):
    rows = lax.broadcasted_iota(jnp.int32, (length, length), 0)
    columns = lax.broadcasted_iota(jnp.int32, (length, length), 1)
    kept = rows <= columns if upper else rows >= columns
    return kept, jnp.where(kept, 1.0, 0.0).astype(BF16)


def running_sum(ones, v):
    a, b, c = split3(v)
    return dot(ones, a) + dot(ones, b) + dot(ones, c)


def doc_numbers(doc, ones):
    flags = doc.astype(BF16)
    return dot(ones, flags, NT)[:, :1], dot(flags, ones, NT)[:1]


def call(kernel, grid, in_specs, out_specs, out_shape, scratch=(), name=None, flops=10**9):
    return pl.pallas_call(
        kernel,
        grid=grid,
        in_specs=in_specs,
        out_specs=out_specs,
        out_shape=out_shape,
        scratch_shapes=list(scratch),
        compiler_params=pltpu.CompilerParams(
            vmem_limit_bytes=VMEM_LIMIT, dimension_semantics=("arbitrary",) * len(grid)
        ),
        cost_estimate=pl.CostEstimate(flops=flops, bytes_accessed=10**7, transcendentals=0),
        name=name,
    )


def whole(array):
    rank = len(array.shape)
    return pl.BlockSpec(array.shape, lambda i: (0,) * rank)


def per_seq(array):
    rank = len(array.shape)
    return pl.BlockSpec((1,) + tuple(array.shape[1:]), lambda i: (i,) + (0,) * (rank - 1))


def shape(dims, dtype):
    return jax.ShapeDtypeStruct(tuple(dims), dtype)


def forward_kernel(
    sizes, tok, halo, doc, prm, w, normed_o, gate_o, xs_o, pre_o, act_o, scan_o, state_o, aux_o,
    dec_o, ext,
):
    length, inner, nstate, size, taps = sizes
    channels = inner + 2 * nstate
    first = lax.axis_index("seq") == 0
    edge = jnp.where(first, 0.0, halo[0].astype(F32))
    x = jnp.concatenate([edge, tok[0].astype(F32)], axis=0)
    scale = lax.rsqrt(jnp.mean(x * x, axis=-1, keepdims=True) + EPSILON)
    normed = (x * scale * prm[GAIN : GAIN + 1, : x.shape[1]]).astype(BF16)
    normed_o[0] = normed[HALO:]
    gate_o[0] = dot(normed[HALO:], w[:, :inner])
    xs = dot(normed, w[:, inner : inner + channels]).astype(BF16)
    xs_o[0] = xs
    ext[...] = xs.astype(F32)
    pre = prm[BIAS : BIAS + 1, :channels]
    for k in range(taps):
        start = HALO - taps + 1 + k
        pre = pre + prm[TAPS + k : TAPS + k + 1, :channels] * ext[start : start + length]
    pre_o[0] = pre
    act = (pre * sigmoid(pre)).astype(BF16)
    act_o[0] = act
    step_pre = (
        dot(normed[HALO:], w[:, inner + channels :]) + prm[STEP_BIAS : STEP_BIAS + 1, :LANES]
    )
    step = softplus(step_pre)
    kept, ones = triangle(length)
    log_decay = running_sum(ones, step * prm[RATE : RATE + 1, :LANES])
    doc_col, doc_row = doc_numbers(doc[0], ones)
    entry = jnp.where(doc_col == 0.0, jnp.exp(log_decay), 0.0)
    last = log_decay[length - 1 :]
    tail = jnp.where(doc_col == doc_col[length - 1 :], jnp.exp(last - log_decay), 0.0)
    aux_o[0, :, 0:LANES] = log_decay
    aux_o[0, :, LANES : 2 * LANES] = step
    aux_o[0, :, 2 * LANES : 3 * LANES] = step_pre
    aux_o[0, :, 3 * LANES : 4 * LANES] = entry
    aux_o[0, :, 4 * LANES :] = tail
    spread = head_spread(inner, size)
    values = act[:, :inner].astype(F32)
    inputs = values * expand(step, spread)
    low_inputs = inputs.astype(BF16)
    in_state = act[:, inner : inner + nstate]
    out_state = act[:, inner + nstate :]
    state_o[0] = dot((inputs * expand(tail, spread)).astype(BF16), in_state, TN).astype(BF16)
    scores = dot(out_state, in_state, NT)
    closed = jnp.where(kept & (doc_col == doc_row), 0.0, MASKED)
    log_rows = log_decay.T
    whole_decay = jnp.where(doc_row[:, length - 1 :] == 0.0, jnp.exp(log_rows[:HEAD_ROWS, length - 1 :]), 0.0)
    dec_o[0] = jnp.broadcast_to(whole_decay, (HEAD_ROWS, LANES))
    left = lax.broadcasted_iota(jnp.int32, (length, LANES), 1) < size
    for pair in range(inner // LANES):
        columns = slice(pair * LANES, (pair + 1) * LANES)
        part = low_inputs[:, columns]
        total = None
        for side in range(2):
            h = 2 * pair + side
            decay = jnp.exp(log_decay[:, h : h + 1] - log_rows[h : h + 1] + closed)
            own = jnp.where(left if side == 0 else ~left, part, jnp.zeros_like(part))
            term = dot((scores * decay).astype(BF16), own)
            total = term if total is None else total + term
        scan_o[0, :, columns] = total


def gate_kernel(sizes, scan, act, aux, gate, hin, g, prm, wout, full_o, gn_o, sums_o):
    length, inner, nstate, size, taps = sizes
    spread = head_spread(inner, size)
    values = act[0, :, :inner].astype(F32)
    out_state = act[0, :, inner + nstate :]
    scanned = scan[0] + dot(out_state, hin[0], NT) * expand(aux[0, :, 3 * LANES : 4 * LANES], spread)
    full_o[0] = scanned
    mixed = scanned + prm[SKIP : SKIP + 1, :inner] * values
    gated = mixed * (gate[0] * sigmoid(gate[0]))
    grad_norm = dot(g[0], wout[...])
    gn_o[0] = grad_norm
    squares = jnp.sum(gated * gated, axis=-1, keepdims=True)
    cross = jnp.sum(
        grad_norm * prm[INNER_GAIN : INNER_GAIN + 1, :inner] * gated, axis=-1, keepdims=True
    )
    lane = lax.broadcasted_iota(jnp.int32, (length, LANES), 1)
    sums_o[0] = jnp.where(lane == 0, squares, jnp.where(lane == 1, cross, 0.0))


def output_kernel(
    sizes, total_inner, full, act, aux, gate, gn, sums, sums_in, g, normed, prm, wout,
    keep_o, send_o, dy_o, ggate_o, prior_o, small_o, dout_o, dgate_o, acc_out, acc_gate, wide,
):
    length, inner, nstate, size, taps = sizes
    at = pl.program_id(0)
    spread = head_spread(inner, size)
    values = act[0, :, :inner].astype(F32)
    out_state = act[0, :, inner + nstate :]
    mixed = full[0] + prm[SKIP : SKIP + 1, :inner] * values
    z = gate[0]
    sig = sigmoid(z)
    swish = z * sig
    gated = mixed * swish
    both = sums[0] + sums_in[0]
    inner_scale = lax.rsqrt(both[:, 0:1] / total_inner + EPSILON)
    gain = prm[INNER_GAIN : INNER_GAIN + 1, :inner]
    unit = gated * inner_scale
    normal = (unit * gain).astype(BF16)
    wide[...] = dot(normal, wout[...], NT)
    half = wide.shape[1] // 2
    core = lax.axis_index("head")
    keep_o[0] = wide[:, pl.ds(pl.multiple_of(core * half, LANES), half)]
    send_o[0] = wide[:, pl.ds(pl.multiple_of((1 - core) * half, LANES), half)].astype(BF16)
    grad_norm = gn[0]
    grad_inner = jnp.sum(grad_norm * unit, axis=0, keepdims=True)
    grad_gated = inner_scale * (grad_norm * gain) - unit * (
        inner_scale * inner_scale * (both[:, 1:2] / total_inner)
    )
    dy = grad_gated * swish
    low_dy = dy.astype(BF16)
    dy_o[0] = low_dy
    ggate = (grad_gated * mixed * (sig * (1.0 + z * (1.0 - sig)))).astype(BF16)
    ggate_o[0] = ggate
    grad_skip = jnp.sum(dy * values, axis=0, keepdims=True)
    entry = expand(aux[0, :, 3 * LANES : 4 * LANES], spread)
    prior_o[0] = dot((dy * entry).astype(BF16), out_state, TN).astype(BF16)
    rows = jnp.concatenate([grad_inner, grad_skip, jnp.zeros((6, inner), F32)], axis=0)
    term_out = dot(g[0], normal, TN)
    term_gate = dot(normed[0], ggate, TN)

    @pl.when(at == 0)
    def _():
        small_o[...] = rows
        acc_out[...] = term_out
        acc_gate[...] = term_gate

    @pl.when(at > 0)
    def _():
        small_o[...] += rows
        acc_out[...] += term_out
        acc_gate[...] += term_gate

    @pl.when(at == pl.num_programs(0) - 1)
    def _():
        dout_o[...] = acc_out[...].astype(BF16)
        dgate_o[...] = acc_gate[...].astype(BF16)


def backward_kernel(
    sizes, full, act, aux, dy, hin, later, state, doc, pre, prm,
    gcx_o, own_o, send_o, gpre_o, small_o, edge_o, slope_o, dcb,
):
    length, inner, nstate, size, taps = sizes
    at = pl.program_id(0)
    core = lax.axis_index("head")
    spread = head_spread(inner, size)
    log_decay = aux[0, :, 0:LANES]
    step = aux[0, :, LANES : 2 * LANES]
    step_pre = aux[0, :, 2 * LANES : 3 * LANES]
    entry = aux[0, :, 3 * LANES : 4 * LANES]
    tail = aux[0, :, 4 * LANES :]
    values = act[0, :, :inner].astype(F32)
    in_state = act[0, :, inner : inner + nstate]
    out_state = act[0, :, inner + nstate :]
    low_dy = dy[0]
    wide_dy = low_dy.astype(F32)
    step_wide = expand(step, spread)
    tail_wide = expand(tail, spread)
    entry_wide = expand(entry, spread)
    inputs = values * step_wide
    low_inputs = inputs.astype(BF16)
    kept, ones = triangle(length)
    upper, ones_upper = triangle(length, True)
    doc_col, doc_row = doc_numbers(doc[0], ones)
    closed = jnp.where(upper & (doc_col == doc_row), 0.0, MASKED)
    scores = dot(in_state, out_state, NT)
    log_rows = log_decay.T
    left = lax.broadcasted_iota(jnp.int32, (length, LANES), 1) < size
    grad_inputs = tail_wide * dot(in_state, later[0], NT)
    parts = []
    for pair in range(inner // LANES):
        columns = slice(pair * LANES, (pair + 1) * LANES)
        pair_dy = low_dy[:, columns]
        pair_in = low_inputs[:, columns]
        total = grad_inputs[:, columns]
        for side in range(2):
            h = 2 * pair + side
            chosen = left if side == 0 else ~left
            own_dy = jnp.where(chosen, pair_dy, jnp.zeros_like(pair_dy))
            decay = jnp.exp(log_rows[h : h + 1] - log_decay[:, h : h + 1] + closed)
            total = total + dot((scores * decay).astype(BF16), own_dy)
            grad_decay = dot(pair_in, own_dy, NT) * decay
            if h == 0:
                dcb[...] = grad_decay
            else:
                dcb[...] += grad_decay
        parts.append(total)
    grad_inputs = jnp.concatenate(parts, axis=1)
    grad_scores = dcb[...]
    grad_in = dot(grad_scores.astype(BF16), out_state) + dot(
        (inputs * tail_wide).astype(BF16), later[0]
    )
    grad_out = dot(grad_scores.T.astype(BF16), in_state) + dot(
        (wide_dy * entry_wide).astype(BF16), hin[0]
    )
    entry_last = jnp.broadcast_to(entry[length - 1 :], (8, LANES))
    later_wide = later[0].astype(F32)
    lane_ones = jnp.ones((8, nstate), BF16)
    through = head_sums(
        sum(dot(lane_ones, piece, NT) for piece in split2(later_wide * hin[0].astype(F32))), spread
    )
    born = head_sums(
        sum(dot(lane_ones, piece, NT) for piece in split2(later_wide * state[0].astype(F32))), spread
    )
    ending = (born + entry_last * through)[:1]
    grad_log = head_sums(wide_dy * full[0], spread) - head_sums(
        low_inputs.astype(F32) * grad_inputs, spread
    )
    grad_rate_step = running_sum(ones_upper, grad_log) + ending
    rate = prm[RATE : RATE + 1, :LANES]
    grad_step = head_sums(values * grad_inputs, spread) + rate * grad_rate_step
    gpre = grad_step * sigmoid(step_pre)
    lane = lax.broadcasted_iota(jnp.int32, (length, LANES), 1)
    gpre = jnp.where(lane < inner // size, gpre, 0.0)
    gpre_o[0] = gpre
    grad_values = step_wide * grad_inputs + prm[SKIP : SKIP + 1, :inner] * wide_dy
    px = pre[0, :, :inner]
    sig = sigmoid(px)
    gcx = grad_values * (sig * (1.0 + px * (1.0 - sig)))
    gcx_o[0] = gcx
    edge_o[0] = gcx[:EDGE]
    is_first = core == 0
    own_o[0] = jnp.where(is_first, grad_in, grad_out)
    send_o[0] = jnp.where(is_first, grad_out, grad_in).astype(BF16)
    ps = pre[0, :EDGE, pl.ds(pl.multiple_of(inner + core * nstate, LANES), nstate)]
    sig = sigmoid(ps)
    slope_o[0] = sig * (1.0 + ps * (1.0 - sig))
    rows = jnp.concatenate(
        [
            jnp.sum(gpre, axis=0, keepdims=True),
            rate * jnp.sum(step * grad_rate_step, axis=0, keepdims=True),
            jnp.zeros((6, LANES), F32),
        ],
        axis=0,
    )

    @pl.when(at == 0)
    def _():
        small_o[...] = rows

    @pl.when(at > 0)
    def _():
        small_o[...] += rows


def conv_kernel(
    sizes, gcx, own, recv, edge, edge_state, pre, xs, gpre, ggate, normed, prm, w,
    part_o, dx_o, small_o, acc, ext, gext,
):
    length, inner, nstate, size, taps = sizes
    at = pl.program_id(0)
    core = lax.axis_index("head")
    last = lax.axis_index("seq") == lax.axis_size("seq") - 1
    mine = pl.ds(pl.multiple_of(inner + core * nstate, LANES), nstate)
    channels = inner + nstate
    ps = pre[0, :, mine]
    sig = sigmoid(ps)
    gst = (own[0] + recv[0].astype(F32)) * (sig * (1.0 + ps * (1.0 - sig)))
    gext[:length, :inner] = gcx[0]
    gext[:length, inner:] = gst
    gext[length:, :inner] = jnp.where(last, 0.0, edge[0])
    gext[length:, inner:] = jnp.where(last, 0.0, edge_state[0])
    ext[:, :inner] = xs[0, :, :inner].astype(F32)
    ext[:, inner:] = xs[0, :, mine].astype(F32)
    grad_conv = gext[:length]
    grad_in = None
    rows = []
    for k in range(taps):
        row = jnp.concatenate(
            [prm[TAPS + k : TAPS + k + 1, :inner], prm[TAPS + k : TAPS + k + 1, mine]], axis=1
        )
        term = row * gext[taps - 1 - k : taps - 1 - k + length]
        grad_in = term if grad_in is None else grad_in + term
        start = HALO - taps + 1 + k
        rows.append(jnp.sum(ext[start : start + length] * grad_conv, axis=0, keepdims=True))
    rows.append(jnp.sum(grad_conv, axis=0, keepdims=True))
    rows.append(jnp.zeros((8 - taps - 1, channels), F32))
    rows = jnp.concatenate(rows, axis=0)
    low = grad_in.astype(BF16)
    low_pre = gpre[0].astype(BF16)
    part = dot(ggate[0], w[:, :inner], NT)
    part = part + dot(low[:, :inner], w[:, inner : 2 * inner], NT)
    wst = w[:, pl.ds(pl.multiple_of(2 * inner + core * nstate, LANES), nstate)]
    part = part + dot(low[:, inner:], wst, NT)
    part = part + dot(low_pre, w[:, 2 * inner + 2 * nstate :], NT)
    part_o[0] = part.astype(BF16)
    stacked = jnp.concatenate([low, low_pre], axis=1)
    term = dot(normed[0], stacked, TN)

    @pl.when(at == 0)
    def _():
        small_o[...] = rows
        acc[...] = term

    @pl.when(at > 0)
    def _():
        small_o[...] += rows
        acc[...] += term

    @pl.when(at == pl.num_programs(0) - 1)
    def _():
        dx_o[...] = acc[...].astype(BF16)


def tokens_kernel(sizes, tok, part, recv, g, prm, out_o, small_o, wide):
    at = pl.program_id(0)
    core = lax.axis_index("head")
    x = tok[0].astype(F32)
    model = x.shape[1]
    scale = lax.rsqrt(jnp.mean(x * x, axis=-1, keepdims=True) + EPSILON)
    unit = x * scale
    grad_normed = part[0].astype(F32) + recv[0].astype(F32)
    r = grad_normed * prm[GAIN : GAIN + 1, :model]
    wide[...] = scale * (r - unit * jnp.mean(r * unit, axis=-1, keepdims=True))
    half = model // 2
    out_o[0] = g[0].astype(F32) + wide[:, pl.ds(pl.multiple_of(core * half, LANES), half)]
    rows = jnp.concatenate(
        [jnp.sum(grad_normed * unit, axis=0, keepdims=True), jnp.zeros((7, model), F32)], axis=0
    )

    @pl.when(at == 0)
    def _():
        small_o[...] = rows

    @pl.when(at > 0)
    def _():
        small_o[...] += rows


def swap_heads(v):
    return lax.ppermute(v, "head", [(0, 1), (1, 0)])


def shift(v, distance):
    devices = range(lax.axis_size("seq"))
    return lax.ppermute(
        v, "seq", [(i - distance, i) for i in devices if i - distance in devices]
    )


def plain_gather(w_in, w_out, tokens, grads, tails):
    return (
        lax.all_gather(w_in, "seq", axis=0, tiled=True),
        lax.all_gather(w_out, "seq", axis=0, tiled=True),
        lax.all_gather(tokens, "head", axis=2, tiled=True),
        lax.all_gather(grads, "head", axis=2, tiled=True),
        lax.all_gather(shift(tails, 1), "head", axis=2, tiled=True),
    )


def plain_scan(state, decay, size, backward):
    count, place = lax.axis_size("seq"), lax.axis_index("seq")
    heads = state.shape[1] // size
    wide = jnp.repeat(decay[:, :heads, 0], size, axis=1)[..., None]
    states = lax.all_gather(state, "seq")
    decays = lax.all_gather(wide, "seq")

    def one(k, carried):
        at = count - 1 - k if backward else k
        reached = at > place if backward else at < place
        return jnp.where(reached, decays[at] * carried + states[at].astype(F32), carried)

    return lax.fori_loop(0, count, one, jnp.zeros(state.shape, F32)).astype(BF16)


def plain_states(send, own, slope, edge):
    recv = swap_heads(send)
    mine = (own[:, :EDGE] + recv[:, :EDGE].astype(F32)) * slope
    return recv, shift(edge, -1), shift(mine, -1)


def plain_sum(pieces, small, shared):
    totals = [
        lax.psum_scatter(p.astype(F32), "seq", scatter_dimension=0, tiled=True) for p in pieces
    ]
    shared = lax.psum(shared, ("seq", "head"))
    return totals, lax.psum(small, "seq"), shared


def plain_both(v):
    return lax.all_gather(v, "head", axis=1, tiled=True)


PLANE = 4
LINE = 4
OFFSETS = (0, -1, 1, -2, 2, -3, 3)


def place():
    s, c = lax.axis_index("seq"), lax.axis_index("head")
    return s, c, s // PLANE, (s // 2) % 2, s % 2


def remote(src, dst, send_sem, recv_sem, device):
    return pltpu.make_async_remote_copy(
        src_ref=src,
        dst_ref=dst,
        send_sem=send_sem,
        recv_sem=recv_sem,
        device_id=device,
        device_id_type=MESH,
    )


def greet(relations):
    barrier = pltpu.get_barrier_semaphore()
    total = 0
    for exists, device in relations:
        if exists is True:
            pl.semaphore_signal(barrier, inc=1, device_id=device, device_id_type=MESH)
            total = total + 1
        else:
            pl.when(exists)(
                functools.partial(
                    pl.semaphore_signal, barrier, inc=1, device_id=device, device_id_type=MESH
                )
            )
            total = total + jnp.where(exists, 1, 0)
    pl.semaphore_wait(barrier, total)


def comm_call(kernel, ins, outs, scratch, collective, name, anywhere=False):
    space = pl.ANY if anywhere else pltpu.VMEM
    return pl.pallas_call(
        kernel,
        in_specs=[pl.BlockSpec(memory_space=space) for _ in ins],
        out_specs=[pl.BlockSpec(memory_space=space) for _ in outs],
        out_shape=outs,
        scratch_shapes=list(scratch),
        compiler_params=pltpu.CompilerParams(
            collective_id=collective, has_side_effects=True, vmem_limit_bytes=VMEM_LIMIT
        ),
        name=name,
    )(*ins)


def dma(*dims):
    return pltpu.SemaphoreType.DMA(dims)


SUM_OFFSETS = (3, -3, 2, -2, 1, -1, 0)


class Refs:
    def __init__(self, names, refs):
        self.__dict__.update(zip(names, refs))


def fused_call(body, steps, ins, outs, scratch, collective, name):
    names = list(ins) + list(outs) + list(scratch)

    def kernel(*refs):
        body(Refs(names, refs))

    results = pl.pallas_call(
        kernel,
        grid=(steps,) if steps else (),
        in_specs=[spec for _, spec in ins.values()],
        out_specs=[spec for _, spec in outs.values()],
        out_shape=[shaped for shaped, _ in outs.values()],
        scratch_shapes=list(scratch.values()),
        compiler_params=pltpu.CompilerParams(
            collective_id=collective,
            has_side_effects=True,
            vmem_limit_bytes=VMEM_LIMIT,
            dimension_semantics=("arbitrary",) if steps else None,
        ),
        name=name,
    )(*[array for array, _ in ins.values()])
    return Refs(list(outs), results)


ANYWHERE = pl.BlockSpec(memory_space=pl.ANY)
INSIDE = pl.BlockSpec(memory_space=pltpu.VMEM)


def stepped(array, index):
    rank = len(array.shape)
    return pl.BlockSpec((1,) + tuple(array.shape[1:]), lambda k: (index(k),) + (0,) * (rank - 1))


def during(first, count=4):
    return lambda k: jnp.clip(k - first, 0, count - 1)


def cyclic(last, count=4):
    return lambda k: jnp.where(k < last, k % count, count - 1)


def either(core, own, other):
    low = jnp.where(core == 0, own, other)
    return jnp.concatenate([low, jnp.where(core == 0, other, own)], axis=1)


LINE_X, LINE_Y, PLANE_X, PLANE_Y = range(4)


class Gather:
    def __init__(self, pieces, rows, sems):
        self.pieces, self.rows = pieces, rows
        self.local, self.zs, self.zr, self.as_, self.ar, self.bs, self.br = sems
        self.s, self.c, self.z, self.y, self.x = place()
        s, c = self.s, self.c
        self.up, self.down = self.z < LINE - 1, self.z > 0
        self.to_x, self.to_y = (s + 1 - 2 * self.x, c), (s + 2 - 4 * self.y, c)
        self.to_up, self.to_down = (s + PLANE, c), (s - PLANE, c)
        kinds = [piece[4] for piece in pieces]
        self.span = range(len(pieces))
        self.lines = [p for p in self.span if kinds[p] in (LINE_X, LINE_Y)]
        self.planes = [p for p in self.span if kinds[p] in (PLANE_X, PLANE_Y)]
        self.x_first = [kind in (LINE_X, PLANE_X) for kind in kinds]

    @staticmethod
    def semaphores(n):
        return dict(
            g0=dma(n), g1=dma(n, 2, 4), g2=dma(n, 4), g3=dma(n, 4), g4=dma(n, 4), g5=dma(n, 4, 2),
            g6=dma(n, 4, 2),
        )

    def at(self, p, index, count=1):
        src, dst, start, width, order = self.pieces[p]
        begin = pl.multiple_of(index * self.rows, 16)
        return dst.at[pl.ds(begin, count * self.rows), pl.ds(start, width)]

    def own(self, p):
        src, dst, start, width, order = self.pieces[p]
        return src.at[:, pl.ds(start, width)]

    def local_copy(self, p):
        return pltpu.make_async_copy(self.own(p), self.at(p, self.s), self.local.at[p])

    def block(self, p, zz):
        if p in self.planes:
            return self.at(p, zz * PLANE, PLANE)
        return self.at(p, zz * PLANE + self.y * 2 + self.x)

    def z_copy(self, p, off):
        zz = self.z + off
        dst = self.block(p, zz)
        src = self.own(p) if off == 0 and p in self.lines else dst
        step = abs(off)
        moves = []
        if off <= 0:
            sems = self.zs.at[p, 0, step], self.zr.at[p, zz]
            moves.append((self.up, remote(src, dst, *sems, self.to_up)))
        if off >= 0:
            sems = self.zs.at[p, 1, step], self.zr.at[p, zz]
            moves.append((self.down, remote(src, dst, *sems, self.to_down)))
        return moves

    def first_copy(self, p, off):
        zz = self.z + off
        dst = self.at(p, zz * PLANE + self.y * 2 + self.x)
        src = self.own(p) if off == 0 else dst
        device = self.to_x if self.x_first[p] else self.to_y
        return remote(src, dst, self.as_.at[p, zz], self.ar.at[p, zz], device)

    def second_copies(self, p, off):
        zz = self.z + off
        if self.x_first[p]:
            pair = self.at(p, zz * PLANE + self.y * 2, 2)
            return [remote(pair, pair, self.bs.at[p, zz, 0], self.br.at[p, zz, 0], self.to_y)]
        copies = []
        for k in range(2):
            block = self.at(p, zz * PLANE + k * 2 + self.x)
            copies.append(
                remote(block, block, self.bs.at[p, zz, k], self.br.at[p, zz, k], self.to_x)
            )
        return copies

    def exists(self, off):
        zz = self.z + off
        return (zz >= 0) & (zz < LINE)

    def begin(self):
        for p in self.span:
            if p in self.lines:
                for there, copy in self.z_copy(p, 0):
                    pl.when(there)(copy.start)
            self.first_copy(p, 0).start()
            self.local_copy(p).start()

    def z_arrived(self, *offs):
        for off in offs:

            @pl.when(self.exists(off))
            def _():
                for p in self.lines:
                    for there, copy in self.z_copy(p, off):
                        copy.wait_recv()
                        pl.when(there)(copy.start)
                    self.first_copy(p, off).start()

    def first_arrived(self, *offs):
        for off in offs:

            @pl.when(self.exists(off))
            def _():
                for p in self.lines:
                    if off == 0:
                        self.local_copy(p).wait()
                    self.first_copy(p, off).wait_recv()
                    for copy in self.second_copies(p, off):
                        copy.start()

    def plane_first(self):
        for p in self.planes:
            self.local_copy(p).wait()
            self.first_copy(p, 0).wait_recv()
            for copy in self.second_copies(p, 0):
                copy.start()

    def plane_second(self):
        for p in self.planes:
            for copy in self.second_copies(p, 0):
                copy.wait_recv()
            for there, copy in self.z_copy(p, 0):
                pl.when(there)(copy.start)

    def plane_arrived(self, *offs):
        for off in offs:

            @pl.when(self.exists(off))
            def _():
                for p in self.planes:
                    for there, copy in self.z_copy(p, off):
                        copy.wait_recv()
                        pl.when(there)(copy.start)

    def received(self):
        for off in OFFSETS:

            @pl.when(self.exists(off))
            def _():
                for p in self.lines:
                    for copy in self.second_copies(p, off):
                        copy.wait_recv()

    def drain(self):
        for off in OFFSETS:

            @pl.when(self.exists(off))
            def _():
                for p in self.lines:
                    for copy in self.second_copies(p, off):
                        copy.wait_send()
                    self.first_copy(p, off).wait_send()
                for p in self.span:
                    for there, copy in self.z_copy(p, off):
                        pl.when(there)(copy.wait_send)

        for p in self.planes:
            self.first_copy(p, 0).wait_send()
            for copy in self.second_copies(p, 0):
                copy.wait_send()


class Scan:
    def __init__(self, backward, size, state, decay, out, refs):
        self.state, self.decay, self.out, self.size = state, decay, out, size
        (
            self.slots, self.rates, self.total, self.through, self.pair, self.pair_through,
            self.far, self.leaving, self.staged, self.s1, self.r1, self.s2, self.r2, self.zs,
            self.zr, self.s3, self.r3,
        ) = refs
        s, c, z, y, x = place()
        self.s, self.c, self.p = s, c, s % PLANE
        self.base = s - self.p
        self.order = tuple(range(PLANE - 1, -1, -1)) if backward else tuple(range(PLANE))
        self.rows = state.shape[1] // PLANE
        self.place = LINE - 1 - z if backward else z
        self.step = -PLANE if backward else PLANE

    @staticmethod
    def scratch(count, rows, nstate, heads):
        quarter = rows // PLANE
        return dict(
            slots=pltpu.VMEM((count, PLANE, quarter, nstate), BF16),
            rates=pltpu.VMEM((count, PLANE, heads, nstate), F32),
            total=pltpu.VMEM((count, quarter, nstate), F32),
            through=pltpu.VMEM((count, 8, nstate), F32),
            pair=pltpu.VMEM((count, quarter, nstate), BF16),
            pair_through=pltpu.VMEM((count, 8, nstate), F32),
            far=pltpu.VMEM((count, quarter, nstate), BF16),
            leaving=pltpu.VMEM((count, quarter, nstate), BF16),
            staged=pltpu.VMEM((count, PLANE, quarter, nstate), BF16),
            s1=dma(count, PLANE), r1=dma(count, PLANE),
            s2=dma(count, PLANE), r2=dma(count, PLANE),
            zs=dma(count, 3), zr=dma(count, 3),
            s3=dma(count, PLANE), r3=dma(count, PLANE),
        )

    def relations(self):
        plane = [(self.p != j, (self.base + j, self.c)) for j in range(PLANE)]
        s, c, at, step = self.s, self.c, self.place, self.step
        return plane + [
            (at > 0, (s - step, c)),
            (at < LINE - 1, (s + step, c)),
            (at == 1, (s + 2 * step, c)),
            (at == 3, (s - 2 * step, c)),
        ]

    def part(self, j):
        return pl.ds(pl.multiple_of(j * self.rows, 16), self.rows)

    def first(self, i, j, slot):
        device = (self.base + j, self.c)
        return [
            remote(
                self.state.at[i, self.part(j)], self.slots.at[i, slot],
                self.s1.at[i, j], self.r1.at[i, slot], device,
            ),
            remote(
                self.decay.at[i], self.rates.at[i, slot], self.s2.at[i, j], self.r2.at[i, slot],
                device,
            ),
        ]

    def to_pair(self, i):
        device = (self.s + self.step, self.c)
        return [
            remote(self.leaving.at[i], self.pair.at[i], self.zs.at[i, 0], self.zr.at[i, 0], device),
            remote(
                self.through.at[i], self.pair_through.at[i], self.zs.at[i, 1], self.zr.at[i, 1],
                device,
            ),
        ]

    def to_far(self, i, n):
        return remote(
            self.leaving.at[i], self.far.at[i], self.zs.at[i, 0 if n == 1 else 2],
            self.zr.at[i, 2], (self.s + n * self.step, self.c),
        )

    def last(self, i, j, quarter):
        return remote(
            self.staged.at[i, j], self.out.at[i, self.part(quarter)],
            self.s3.at[i, j], self.r3.at[i, quarter], (self.base + j, self.c),
        )

    def others(self, act):
        for j in range(PLANE):
            pl.when(self.p != j)(functools.partial(act, j))

    def start(self, i):
        def send(j):
            for copy in self.first(i, j, self.p):
                copy.start()

        self.others(send)
        self.slots[i, self.p] = self.state[i, self.part(self.p)]
        self.rates[i, self.p] = self.decay[i]

    def pieces(self):
        for n in range(self.rows // self.size):
            yield n, slice(n * self.size, (n + 1) * self.size)

    def rate(self, i, j, n):
        return self.rates[i, j, pl.ds(self.p * (self.rows // self.size) + n, 1)]

    def deliver(self, i, entering):
        for n, rows in self.pieces():
            held = entering(n, rows)
            for at, j in enumerate(self.order):
                self.staged[i, j, rows] = held.astype(BF16)
                if at < PLANE - 1:
                    held = self.rate(i, j, n) * held + self.slots[i, j, rows].astype(F32)
        self.others(lambda j: self.last(i, j, self.p).start())
        self.out[i, self.part(self.p)] = self.staged[i, self.p]

    def fold(self, i):
        def arrived(j):
            for copy in self.first(i, j, j):
                copy.wait_recv()

        self.others(arrived)
        for n, rows in self.pieces():
            held = self.slots[i, self.order[0], rows].astype(F32)
            rate = self.rate(i, self.order[0], n)
            for j in self.order[1:]:
                own = self.rate(i, j, n)
                held = own * held + self.slots[i, j, rows].astype(F32)
                rate = own * rate
            self.total[i, rows] = held
            self.through[i, n : n + 1] = rate

        @pl.when((self.place == 0) | (self.place == 2))
        def _():
            self.leaving[i] = self.total[i].astype(BF16)
            for copy in self.to_pair(i):
                copy.start()

        @pl.when(self.place == 0)
        def _():
            self.deliver(i, lambda n, rows: jnp.zeros((self.size, self.out.shape[2]), F32))

    def join(self, i):
        @pl.when(self.place == 1)
        def _():
            for copy in self.to_pair(i):
                copy.wait_recv()
            for n, rows in self.pieces():
                self.leaving[i, rows] = (
                    self.total[i, rows]
                    + self.through[i, n : n + 1] * self.pair[i, rows].astype(F32)
                ).astype(BF16)
            for n in (1, 2):
                self.to_far(i, n).start()
            self.deliver(i, lambda n, rows: self.pair[i, rows].astype(F32))

    def close(self, i):
        @pl.when(self.place == 2)
        def _():
            self.to_far(i, 1).wait_recv()
            self.deliver(i, lambda n, rows: self.far[i, rows].astype(F32))

        @pl.when(self.place == 3)
        def _():
            for copy in self.to_pair(i):
                copy.wait_recv()
            self.to_far(i, 1).wait_recv()
            self.deliver(
                i,
                lambda n, rows: self.pair[i, rows].astype(F32)
                + self.pair_through[i, n : n + 1] * self.far[i, rows].astype(F32),
            )

    def arrived(self, i):
        self.others(lambda j: self.last(i, j, j).wait_recv())

    def finish(self):
        @pl.loop(0, self.state.shape[0])
        def _(i):
            def close(j):
                for copy in self.first(i, j, self.p):
                    copy.wait_send()
                self.last(i, j, self.p).wait_send()

            self.others(close)

            @pl.when((self.place == 0) | (self.place == 2))
            def _():
                for copy in self.to_pair(i):
                    copy.wait_send()

            @pl.when(self.place == 1)
            def _():
                for n in (1, 2):
                    self.to_far(i, n).wait_send()


class Reduce:
    def __init__(self, pieces, rows, refs):
        self.pieces, self.rows = pieces, rows
        (
            self.near, self.mid, self.above, self.below, self.mid_send, self.kept,
            self.s1, self.r1, self.s2, self.r2, self.sz, self.rz,
        ) = refs
        self.s, self.c, self.z, self.y, self.x = place()
        s, c = self.s, self.c
        self.up, self.down = self.z < LINE - 1, self.z > 0
        self.to_x, self.to_y = (s + 1 - 2 * self.x, c), (s + 2 - 4 * self.y, c)
        self.to_up, self.to_down = (s + PLANE, c), (s - PLANE, c)
        self.span = range(len(pieces))

    @staticmethod
    def scratch(n, rows, wide):
        return dict(
            near=pltpu.VMEM((LINE, 2 * rows, wide), BF16),
            mid=pltpu.VMEM((LINE, rows, wide), BF16),
            above=pltpu.VMEM((LINE, rows, wide), BF16),
            below=pltpu.VMEM((LINE, rows, wide), BF16),
            mid_send=pltpu.VMEM((LINE, rows, wide), BF16),
            kept=pltpu.VMEM((LINE, rows, wide), F32),
            t1=dma(n, LINE, 2), u1=dma(n, LINE, 2), t2=dma(n, LINE),
            u2=dma(n, LINE), tz=dma(n, LINE), uz=dma(n, 2, LINE),
        )

    def columns(self, p):
        return pl.ds(self.pieces[p][6], self.pieces[p][2])

    def source(self, p, index, count=1):
        ref, start, width = self.pieces[p][:3]
        begin = pl.multiple_of(index * self.rows, 16)
        return ref.at[pl.ds(begin, count * self.rows), pl.ds(start, width)]

    def index(self, zz, yy, xx):
        return zz * PLANE + yy * 2 + xx

    def near_copies(self, p, zz):
        if self.pieces[p][3]:
            return [
                remote(
                    self.source(p, self.index(zz, 1 - self.y, 0), 2),
                    self.near.at[zz, :, self.columns(p)],
                    self.s1.at[p, zz, 0], self.r1.at[p, zz, 0], self.to_y,
                )
            ]
        return [
            remote(
                self.source(p, self.index(zz, k, 1 - self.x)),
                self.near.at[zz, pl.ds(k * self.rows, self.rows), self.columns(p)],
                self.s1.at[p, zz, k], self.r1.at[p, zz, k], self.to_x,
            )
            for k in range(2)
        ]

    def mid_copy(self, p, zz):
        at = self.columns(p)
        return remote(
            self.mid_send.at[zz, :, at], self.mid.at[zz, :, at],
            self.s2.at[p, zz], self.r2.at[p, zz], self.to_x if self.pieces[p][3] else self.to_y,
        )

    def line_copy(self, p, zz, upward):
        at = self.columns(p)
        target = self.above if upward else self.below
        return remote(
            self.mid_send.at[zz, :, at], target.at[zz, :, at],
            self.sz.at[p, zz], self.rz.at[p, 0 if upward else 1, zz],
            self.to_up if upward else self.to_down,
        )

    def exists(self, off):
        zz = self.z + off
        return (zz >= 0) & (zz < LINE)

    def rows_of(self, k):
        return pl.ds(pl.multiple_of(k * self.rows, 16), self.rows)

    def begin(self, *pieces):
        for off in SUM_OFFSETS:

            @pl.when(self.exists(off))
            def _():
                for p in pieces or self.span:
                    for copy in self.near_copies(p, self.z + off):
                        copy.start()

    def second(self, *offs):
        for off in offs:

            @pl.when(self.exists(off))
            def _():
                zz = self.z + off
                y, x = self.y, self.x
                for p in self.span:
                    for copy in self.near_copies(p, zz):
                        copy.wait_recv()
                    own = self.index(zz, y, x)
                    if self.pieces[p][3]:
                        other, mine = self.index(zz, y, 1 - x), x
                    else:
                        other, mine = self.index(zz, 1 - y, x), y
                    at = self.columns(p)
                    sent = self.source(p, other)[...].astype(F32) + self.near[
                        zz, self.rows_of(1 - mine), at
                    ].astype(F32)
                    self.mid_send[zz, :, at] = sent.astype(BF16)
                    self.mid_copy(p, zz).start()
                    self.kept[zz, :, at] = self.source(p, own)[...].astype(F32) + self.near[
                        zz, self.rows_of(mine), at
                    ].astype(F32)

    def third(self, *offs, only=None):
        for off in offs:

            @pl.when(self.exists(off))
            def _():
                zz = self.z + off
                for p in self.span if only is None else only:
                    at = self.columns(p)
                    self.mid_copy(p, zz).wait_recv()
                    self.kept[zz, :, at] = self.kept[zz, :, at] + self.mid[zz, :, at].astype(F32)
                    if off >= 0:

                        @pl.when(self.down)
                        def _():
                            self.line_copy(p, zz, True).wait_recv()
                            self.kept[zz, :, at] = self.kept[zz, :, at] + self.above[
                                zz, :, at
                            ].astype(F32)

                    if off <= 0:

                        @pl.when(self.up)
                        def _():
                            self.line_copy(p, zz, False).wait_recv()
                            self.kept[zz, :, at] = self.kept[zz, :, at] + self.below[
                                zz, :, at
                            ].astype(F32)

                    if off == 0:
                        _, _, width, _, out, start, _ = self.pieces[p]
                        out[:, start : start + width] = self.kept[zz, :, at]
                    else:
                        self.mid_copy(p, zz).wait_send()
                        self.mid_send[zz, :, at] = self.kept[zz, :, at].astype(BF16)
                        self.line_copy(p, zz, off > 0).start()

    def near_sent(self):
        for off in SUM_OFFSETS:

            @pl.when(self.exists(off))
            def _():
                for p in self.span:
                    for copy in self.near_copies(p, self.z + off):
                        copy.wait_send()

    def finish(self):
        for off in SUM_OFFSETS:

            @pl.when(self.exists(off))
            def _():
                zz = self.z + off
                for p in self.span:
                    if off == 0:
                        self.mid_copy(p, zz).wait_send()
                    else:
                        self.line_copy(p, zz, off > 0).wait_send()


def picked(r, names):
    return tuple(r.__dict__[n] for n in names)


GATHER_REFS = tuple(Gather.semaphores(1))
SCAN_REFS = tuple(Scan.scratch(1, PLANE, 1, 1))
REDUCE_REFS = tuple(Reduce.scratch(1, 16, 1))


def main_body(sizes, total_inner, r):
    length, inner, nstate, size, taps = sizes
    channels = inner + 2 * nstate
    heads = inner // size
    count = r.tok.shape[0]
    half = r.tok.shape[2]
    s, c, z, y, x = place()
    to_core, to_prv = (s, 1 - c), (s - 1, c)
    nxt, prv = s < LINE * PLANE - 1, s > 0
    first_gather = Gather(
        (
            (r.w1, r.w, 0, 512, LINE_X),
            (r.w1, r.w, 512, 384, LINE_Y),
            (r.w1, r.w, 896, 128, PLANE_X),
            (r.w1, r.w, 1024, 128, PLANE_Y),
        ),
        r.w1.shape[0],
        picked(r, GATHER_REFS),
    )
    second_gather = Gather(
        (
            (r.w2, r.w2_full, 0, 512, LINE_X),
            (r.w2, r.w2_full, 512, 512, LINE_Y),
            (r.w2, r.w2_full, 1024, 256, PLANE_X),
            (r.w2, r.w2_full, 1280, 256, PLANE_Y),
        ),
        r.w2.shape[0],
        picked(r, SECOND_REFS),
    )
    prefix = Scan(False, size, r.state, r.dec, r.hin, picked(r, SCAN_REFS))
    suffix = Scan(True, size, r.prior, r.dec, r.later, picked(r, SUFFIX_REFS))
    reduce_ = Reduce(
        ((r.dout, 0, inner, True, r.g_out, 0, 0), (r.dgate, 0, inner, False, r.g_gate, 0, inner)),
        r.g_out.shape[0],
        picked(r, REDUCE_REFS),
    )
    wide = inner + nstate + LANES
    late = Reduce(
        (
            (r.dout, 0, wide // 2, True, r.g_x, 0, 0),
            (r.dgate, 0, wide // 2, False, r.g_x, wide // 2, wide // 2),
        ),
        r.g_x.shape[0],
        picked(r, LATE_REFS),
    )
    spread = head_spread(inner, size)
    mine = pl.ds(pl.multiple_of(inner + c * nstate, LANES), nstate)
    side = pl.ds(pl.multiple_of(c * half, LANES), half)
    other_side = pl.ds(pl.multiple_of((1 - c) * half, LANES), half)
    log_at, step_at, pre_at, entry_at = (
        slice(n * LANES, (n + 1) * LANES) for n in range(4)
    )
    scores_at = slice(half, half + length)
    own_at, slope_at, gpre_at = (
        slice(half + n * nstate, half + (n + 1) * nstate) for n in range(3)
    )
    left = lax.broadcasted_iota(jnp.int32, (length, LANES), 1) < size

    def swap(n, source, target):
        return lambda i: remote(
            source.at[i], target.at[i], r.ss.at[n, i], r.rs.at[n, i], to_core
        )

    swap_tokens = swap(0, r.tok, r.tok_in)
    swap_grads = swap(1, r.g, r.g_in)
    swap_sums = swap(2, r.sums, r.sums_in)
    swap_out = swap(3, r.osend, r.out_in)
    swap_states = swap(4, r.bsend, r.brecv)
    swap_part = swap(6, r.normal, r.low)

    def send_edge(i):
        return remote(r.edge.at[i], r.edge_in.at[i], r.ss.at[5, i], r.rs.at[5, i], to_prv)

    def halo_copy(k):
        tails = r.tok.at[:, pl.ds(length - HALO, HALO), :]
        device = (s + 1, c if k == 0 else 1 - c)
        return remote(tails, r.halo.at[:, :, side], r.hs.at[k], r.hr.at[k], device)

    def store_grad(i):
        return pltpu.make_async_copy(
            r.full.at[i, :, pl.ds(0, half)], r.tokens_grad.at[i], r.store.at[0, i]
        )

    def store_mixed(i):
        return pltpu.make_async_copy(r.g_in.at[i], r.mixed.at[i], r.store.at[1, i])

    def conv(at):
        pre = r.prm[BIAS : BIAS + 1, at]
        for t in range(taps):
            start = HALO - taps + 1 + t
            pre = pre + r.prm[TAPS + t : TAPS + t + 1, at] * r.ext[start : start + length, at]
        return pre

    greet(
        prefix.relations()
        + [(z != j, (s + (j - z) * PLANE, c)) for j in range(LINE)]
        + [
            (True, to_core),
            (nxt, (s + 1, c)),
            (nxt, (s + 1, 1 - c)),
            (prv, (s - 1, c)),
            (prv, (s - 1, 1 - c)),
        ]
    )
    first_gather.begin()
    for k in range(2):
        pl.when(nxt)(halo_copy(k).start)
    for i in range(count):
        swap_tokens(i).start()
    r.small[...] = jnp.zeros_like(r.small)
    first_gather.z_arrived(-1, 1)
    first_gather.plane_first()
    first_gather.first_arrived(0)
    second_gather.begin()
    for i in range(count):
        swap_grads(i).start()

    @pl.loop(0, count)
    def _(i):
        swap_tokens(i).wait()
        own, other = r.tok[i].astype(F32), r.tok_in[i].astype(F32)
        scale = lax.rsqrt(
            jnp.mean(own * own + other * other, axis=-1, keepdims=True) * 0.5 + EPSILON
        )
        gain_own = r.prm[GAIN : GAIN + 1, side]
        gain_other = r.prm[GAIN : GAIN + 1, other_side]
        r.normed_s[i, HALO:, side] = (own * scale * gain_own).astype(BF16)
        r.normed_s[i, HALO:, other_side] = (other * scale * gain_other).astype(BF16)

    first_gather.z_arrived(-2, 2)
    first_gather.plane_second()
    first_gather.first_arrived(-1, 1)
    for k in range(2):
        pl.when(nxt)(halo_copy(k).wait_send)
        pl.when(prv)(halo_copy(k).wait_recv)

    @pl.when(prv)
    def _():
        for i in range(count):
            edge = r.halo[i].astype(F32)
            scale = lax.rsqrt(jnp.mean(edge * edge, axis=-1, keepdims=True) + EPSILON)
            r.normed_s[i, :HALO] = (
                edge * scale * r.prm[GAIN : GAIN + 1, : edge.shape[1]]
            ).astype(BF16)

    @pl.when(jnp.logical_not(prv))
    def _():
        for i in range(count):
            r.normed_s[i, :HALO] = jnp.zeros((HALO, 2 * half), BF16)

    first_gather.z_arrived(-3, 3)
    first_gather.plane_arrived(-1, 1)
    first_gather.first_arrived(-2, 2)
    second_gather.z_arrived(-1, 1)
    second_gather.plane_first()
    first_gather.plane_arrived(-2, 2)
    first_gather.first_arrived(-3, 3)
    second_gather.first_arrived(0)
    first_gather.plane_arrived(-3, 3)
    first_gather.received()
    kept, ones = triangle(length)

    chunk = 2 * LANES
    chunks = [slice(n, n + chunk) for n in range(0, inner, chunk)]

    def spread_of(pieces, at):
        return sum(dot(piece, spread[:, at]) for piece in pieces)

    def tail_of(log_decay, doc_col):
        return jnp.where(
            doc_col == doc_col[length - 1 :], jnp.exp(log_decay[length - 1 :] - log_decay), 0.0
        )

    def project_chunk(i, at):
        xs = dot(r.normed_s[i], r.w[:, at]).astype(BF16)
        r.xs_s[i, :, at] = xs
        r.ext[:, at] = xs.astype(F32)
        pre = conv(at)
        act = (pre * sigmoid(pre)).astype(BF16)
        r.act[i, :, at] = act
        return act

    def project(i):
        project_chunk(i, slice(inner, channels))
        step_pre = (
            dot(r.normed_s[i, HALO:], r.w[:, channels:])
            + r.prm[STEP_BIAS : STEP_BIAS + 1, :LANES]
        )
        step = softplus(step_pre)
        log_decay = running_sum(ones, step * r.prm[RATE : RATE + 1, :LANES])
        doc_col, doc_row = doc_numbers(r.doc[i], ones)
        r.aux[i, :, log_at] = log_decay
        r.aux[i, :, step_at] = step
        r.aux[i, :, pre_at] = step_pre
        r.aux[i, :, entry_at] = jnp.where(doc_col == 0.0, jnp.exp(log_decay), 0.0)
        log_rows = log_decay.T
        whole_decay = jnp.where(
            doc_row[:, length - 1 :] == 0.0, jnp.exp(log_rows[:HEAD_ROWS, length - 1 :]), 0.0
        )
        r.dec[i] = jnp.broadcast_to(whole_decay, (HEAD_ROWS, LANES))
        steps, tails = split2(step), split2(tail_of(log_decay, doc_col))
        for at in chunks:
            act = project_chunk(i, at)
            inputs = act.astype(F32) * spread_of(steps, at)
            r.low[i, :, at] = inputs.astype(BF16)
            r.state[i, at] = dot(
                (inputs * spread_of(tails, at)).astype(BF16),
                r.act[i, :, inner : inner + nstate],
                TN,
            ).astype(BF16)
        prefix.start(i)

    @pl.loop(0, count)
    def _(i):
        project(i)

        @pl.when(i == 0)
        def _():
            second_gather.z_arrived(-2, 2)
            second_gather.plane_second()
            second_gather.first_arrived(-1, 1)

        @pl.when(i == 1)
        def _():
            second_gather.z_arrived(-3, 3)
            second_gather.first_arrived(-2, 2)

        @pl.when(i == 2)
        def _():
            prefix.fold(0)
            second_gather.plane_arrived(-1, 1)
            second_gather.first_arrived(-3, 3)

        @pl.when(i == 3)
        def _():
            prefix.fold(1)
            second_gather.plane_arrived(-2, 2)

    middle = length // 2
    below = ((slice(0, middle), slice(0, middle)), (slice(middle, length), slice(0, length)))
    above = ((slice(0, middle), slice(0, length)), (slice(middle, length), slice(middle, length)))

    def inside(i):
        log_decay = r.aux[i, :, log_at]
        log_rows = log_decay.T
        doc_col, doc_row = doc_numbers(r.doc[i], ones)
        scores = dot(r.act[i, :, inner + nstate :], r.act[i, :, inner : inner + nstate], NT)
        scores = jnp.where(kept & (doc_col == doc_row), scores, 0.0)
        for pair in range(inner // LANES):
            columns = slice(pair * LANES, (pair + 1) * LANES)
            part = r.low[i, :, columns]
            sides = [jnp.where(chosen, part, jnp.zeros_like(part)) for chosen in (left, ~left)]
            for to, ahead in below:
                total = None
                for n in range(2):
                    h = 2 * pair + n
                    decay = jnp.exp(
                        jnp.minimum(log_decay[to, h : h + 1] - log_rows[h : h + 1, ahead], 0.0)
                    )
                    term = dot((scores[to, ahead] * decay).astype(BF16), sides[n][ahead])
                    total = term if total is None else total + term
                r.full[i, to, columns] = total

    @pl.loop(0, count)
    def _(i):
        inside(i)

        @pl.when(i == 0)
        def _():
            prefix.join(0)
            second_gather.plane_arrived(-3, 3)

        @pl.when(i == 1)
        def _():
            prefix.fold(2)
            prefix.join(1)

        @pl.when(i == 2)
        def _():
            prefix.fold(3)
            prefix.close(0)

        @pl.when(i == 3)
        def _():
            prefix.join(2)
            prefix.close(1)

    second_gather.received()
    for i in range(count):
        swap_grads(i).wait()

    def gates(i):
        r.gate[i] = dot(r.normed_s[i, HALO:], r.w2_full[:, :inner])
        r.gn[i] = dot(either(c, r.g[i], r.g_in[i]), r.w2_full[:, inner:])

    @pl.loop(0, count)
    def _(i):
        gates(i)

        @pl.when(i == 0)
        def _():
            prefix.join(3)

        @pl.when(i == 1)
        def _():
            prefix.close(2)

    def combine(i):
        prefix.arrived(i)
        entries = split2(r.aux[i, :, entry_at])
        squares, cross = jnp.zeros((length, chunk), F32), jnp.zeros((length, chunk), F32)
        for at in chunks:
            from_behind = dot(r.act[i, :, inner + nstate :], r.hin[i, at], NT)
            scanned = r.full[i, :, at] + from_behind * spread_of(entries, at)
            r.full[i, :, at] = scanned
            mixed = scanned + r.prm[SKIP : SKIP + 1, at] * r.act[i, :, at].astype(F32)
            gate = r.gate[i, :, at]
            gated = mixed * (gate * sigmoid(gate))
            squares += gated * gated
            cross += r.gn[i, :, at] * r.prm[INNER_GAIN : INNER_GAIN + 1, at] * gated
        squares = jnp.sum(squares, axis=-1, keepdims=True)
        cross = jnp.sum(cross, axis=-1, keepdims=True)
        lane = lax.broadcasted_iota(jnp.int32, (length, LANES), 1)
        r.sums[i] = jnp.where(lane == 0, squares, jnp.where(lane == 1, cross, 0.0)).T[:EDGE]
        swap_sums(i).start()

    def norm_back(i):
        swap_sums(i).wait_recv()
        both = jnp.concatenate(
            [r.sums[i] + r.sums_in[i], jnp.zeros((LANES - EDGE, length), F32)], axis=0
        ).T
        inner_scale = lax.rsqrt(both[:, 0:1] / total_inner + EPSILON)
        factor = inner_scale * inner_scale * (both[:, 1:2] / total_inner)
        entries = split2(r.aux[i, :, entry_at])
        per_head = None
        for at in chunks:
            values = r.act[i, :, at].astype(F32)
            mixed = r.full[i, :, at] + r.prm[SKIP : SKIP + 1, at] * values
            gate = r.gate[i, :, at]
            sig = sigmoid(gate)
            swish = gate * sig
            unit = mixed * swish * inner_scale
            gain = r.prm[INNER_GAIN : INNER_GAIN + 1, at]
            r.normal[i, :, at] = (unit * gain).astype(BF16)
            grad_norm = r.gn[i, :, at]
            r.small[0:1, at] += jnp.sum(grad_norm * unit, axis=0, keepdims=True)
            grad_gated = inner_scale * (grad_norm * gain) - unit * factor
            dy = grad_gated * swish
            r.dy[i, :, at] = dy.astype(BF16)
            r.ggate_s[i, :, at] = (
                grad_gated * mixed * (sig * (1.0 + gate * (1.0 - sig)))
            ).astype(BF16)
            r.prior[i, at] = dot(
                (dy * spread_of(entries, at)).astype(BF16), r.act[i, :, inner + nstate :], TN
            ).astype(BF16)
            term = head_sums(
                jnp.broadcast_to(jnp.sum(dy * values, axis=0, keepdims=True), (8, chunk)),
                spread[:, at],
            )
            per_head = term if per_head is None else per_head + term
        suffix.start(i)
        r.small[1:2, :LANES] += per_head[:1]

    combine(0)
    combine(1)
    prefix.close(3)
    norm_back(0)
    combine(2)
    norm_back(1)
    combine(3)
    prefix.finish()
    norm_back(2)
    suffix.fold(0)
    norm_back(3)
    suffix.fold(1)

    def outputs(i):
        r.ginputs[...] = dot(r.normal[i], r.w2_full[:, inner:], NT)
        r.gate[i, :, :half] = r.ginputs[:, side]
        r.osend[i] = r.ginputs[:, other_side].astype(BF16)
        swap_out(i).start()

    pl.loop(0, count)(outputs)
    suffix.join(0)

    def weights_gradient(source, target, values, start, rows, step):
        for n in range(0, rows, step):
            total = None
            for i in range(count):
                term = dot(source(i, n, step), values[i], TN)
                total = term if total is None else total + term
            target[pl.ds(pl.multiple_of(start + n, LANES), step), :] = total.astype(BF16)

    def normed_block(i, n, step):
        return r.normed_s[i, HALO:, n : n + step]

    weights_gradient(
        lambda i, n, step: r.g[i, :, n : n + step], r.dout, r.normal, c * half, half, LANES
    )
    suffix.fold(2)
    weights_gradient(
        lambda i, n, step: r.g_in[i, :, n : n + step], r.dout, r.normal, (1 - c) * half, half,
        LANES,
    )
    suffix.fold(3)
    suffix.join(1)
    suffix.close(0)
    weights_gradient(normed_block, r.dgate, r.ggate_s, 0, 2 * half, 256)
    suffix.join(2)

    upper, ones_upper = triangle(length, True)

    def back_inside(i):
        log_decay = r.aux[i, :, log_at]
        in_state = r.act[i, :, inner : inner + nstate]
        out_state = r.act[i, :, inner + nstate :]
        doc_col, doc_row = doc_numbers(r.doc[i], ones)
        scores = dot(in_state, out_state, NT)
        scores = jnp.where(upper & (doc_col == doc_row), scores, 0.0)
        log_rows = log_decay.T
        for pair in range(inner // LANES):
            columns = slice(pair * LANES, (pair + 1) * LANES)
            pair_dy = r.dy[i, :, columns]
            pair_in = r.low[i, :, columns]
            sides = [jnp.where(chosen, pair_dy, jnp.zeros_like(pair_dy)) for chosen in (left, ~left)]
            for to, after in above:
                total, grad = None, None
                for n in range(2):
                    h = 2 * pair + n
                    own_dy = sides[n][after]
                    decay = jnp.exp(
                        jnp.minimum(log_rows[h : h + 1, after] - log_decay[to, h : h + 1], 0.0)
                    )
                    term = dot((scores[to, after] * decay).astype(BF16), own_dy)
                    total = term if total is None else total + term
                    term = dot(pair_in[to], own_dy, NT) * decay
                    grad = term if grad is None else grad + term
                at = slice(half + after.start, half + after.stop)
                if pair == 0:
                    r.gate[i, to, at] = grad
                else:
                    r.gate[i, to, at] += grad
                r.gn[i, to, columns] = total

    @pl.loop(0, count)
    def _(i):
        back_inside(i)

        @pl.when(i == 0)
        def _():
            suffix.close(1)
            suffix.join(3)

        @pl.when(i == 1)
        def _():
            suffix.close(2)

        @pl.when(i == 2)
        def _():
            suffix.close(3)
            reduce_.begin(0, 1)

    def back_rest(i):
        suffix.arrived(i)
        doc_col, doc_row = doc_numbers(r.doc[i], ones)
        log_decay = r.aux[i, :, log_at]
        step = r.aux[i, :, step_at]
        in_state = r.act[i, :, inner : inner + nstate]
        out_state = r.act[i, :, inner + nstate :]
        steps, tails, entries = (
            split2(v) for v in (step, tail_of(log_decay, doc_col), r.aux[i, :, entry_at])
        )
        grad_scores = jnp.where(upper & (doc_col == doc_row), r.gate[i, :, scores_at], 0.0)
        grad_in = dot(grad_scores.astype(BF16), out_state)
        grad_out = dot(grad_scores.T.astype(BF16), in_state)
        grad_log = jnp.zeros((length, LANES), F32)
        grad_step = jnp.zeros((length, LANES), F32)
        state_rows = []
        for pair in range(inner // LANES):
            at = slice(pair * LANES, (pair + 1) * LANES)
            step_wide, tail_wide, entry_wide = (
                spread_of(v, at) for v in (steps, tails, entries)
            )
            values = r.act[i, :, at].astype(F32)
            dy = r.dy[i, :, at].astype(F32)
            later, hin = r.later[i, at], r.hin[i, at]
            grad_inputs = r.gn[i, :, at] + tail_wide * dot(in_state, later, NT)
            grad_in += dot((values * step_wide * tail_wide).astype(BF16), later)
            grad_out += dot((dy * entry_wide).astype(BF16), hin)
            grad_log += head_sums(
                dy * r.full[i, :, at] - r.low[i, :, at].astype(F32) * grad_inputs, spread[:, at]
            )
            grad_step += head_sums(values * grad_inputs, spread[:, at])
            grad_values = step_wide * grad_inputs + r.prm[SKIP : SKIP + 1, at] * dy
            r.ext[:, at] = r.xs_s[i, :, at].astype(F32)
            px = conv(at)
            sig = sigmoid(px)
            gcx = grad_values * (sig * (1.0 + px * (1.0 - sig)))
            r.gn[i, :, at] = gcx
            r.edge[i, :, at] = gcx[:EDGE]
            leaving = r.state[i, at].astype(F32)
            for n in range(LANES // size):
                rows = slice(n * size, (n + 1) * size)
                h = pair * (LANES // size) + n
                whole_state = leaving[rows] + r.dec[i, h : h + 1] * hin[rows].astype(F32)
                state_rows.append(
                    jnp.sum(later[rows].astype(F32) * whole_state, axis=0, keepdims=True)
                )
        is_first = c == 0
        r.gate[i, :, own_at] = jnp.where(is_first, grad_in, grad_out)
        r.bsend[i] = jnp.where(is_first, grad_out, grad_in).astype(BF16)
        swap_states(i).start()
        state_rows.append(jnp.zeros((LANES - heads, LANES), F32))
        pieces = split2(jnp.concatenate(state_rows, axis=0))
        ending = sum(dot(jnp.ones((8, LANES), BF16), piece, NT) for piece in pieces)[:1]
        grad_rate_step = running_sum(ones_upper, grad_log) + ending
        rate = r.prm[RATE : RATE + 1, :LANES]
        grad_step = grad_step + rate * grad_rate_step
        lane = lax.broadcasted_iota(jnp.int32, (length, LANES), 1)
        gpre = jnp.where(lane < heads, grad_step * sigmoid(r.aux[i, :, pre_at]), 0.0)
        r.gate[i, :, gpre_at] = gpre
        r.ext[:, mine] = r.xs_s[i, :, mine].astype(F32)
        ps = conv(mine)
        sig = sigmoid(ps)
        r.gate[i, :, slope_at] = sig * (1.0 + ps * (1.0 - sig))
        r.small[1:2, LANES : 2 * LANES] += jnp.sum(gpre, axis=0, keepdims=True)
        r.small[1:2, 2 * LANES : 3 * LANES] += rate * jnp.sum(
            step * grad_rate_step, axis=0, keepdims=True
        )

    def finish_states(n):
        swap_states(n).wait_recv()
        gst = (r.gate[n, :, own_at] + r.brecv[n].astype(F32)) * r.gate[n, :, slope_at]
        r.gate[n, :, own_at] = gst
        r.edge[n, :, inner:] = gst[:EDGE]
        pl.when(prv)(send_edge(n).start)

    @pl.loop(0, count)
    def _(i):
        back_rest(i)
        pl.when(i > 0)(lambda: finish_states(i - 1))

        @pl.when(i == 1)
        def _():
            reduce_.second(3, -3)

        @pl.when(i == 2)
        def _():
            reduce_.second(2, -2)

        @pl.when(i == 3)
        def _():
            reduce_.second(1, -1)

    r.conv_rows[...] = jnp.zeros_like(r.conv_rows)
    r.bc[...] = jnp.zeros_like(r.bc)

    def conv_back(i):
        pl.when(nxt)(send_edge(i).wait_recv)

        def channel_block(source, at, own):
            grad_conv = source[...]
            r.gext[:length, at] = grad_conv
            r.gext[length:, at] = jnp.where(nxt, r.edge_in[i, :, at], 0.0)
            r.ext[:, at] = r.xs_s[i, :, own].astype(F32)
            grad_in = None
            for t in range(taps):
                term = r.prm[TAPS + t : TAPS + t + 1, own] * r.gext[
                    taps - 1 - t : taps - 1 - t + length, at
                ]
                grad_in = term if grad_in is None else grad_in + term
                start = HALO - taps + 1 + t
                r.conv_rows[t : t + 1, at] += jnp.sum(
                    r.ext[start : start + length, at] * grad_conv, axis=0, keepdims=True
                )
            r.conv_rows[taps : taps + 1, at] += jnp.sum(grad_conv, axis=0, keepdims=True)
            return grad_in.astype(BF16)

        for n in range(0, inner, LANES):
            at = slice(n, n + LANES)
            r.dy[i, :, at] = channel_block(r.gn.at[i, :, at], at, at)
        r.gtail[i, :, :nstate] = channel_block(
            r.gate.at[i, :, own_at], slice(inner, inner + nstate), mine
        )
        r.gtail[i, :, nstate:] = r.gate[i, :, gpre_at].astype(BF16)

    @pl.loop(0, count)
    def _(i):
        conv_back(i)

        @pl.when(i == 0)
        def _():
            finish_states(count - 1)
            reduce_.second(0)

        @pl.when(i == 1)
        def _():
            reduce_.third(3, -3)

        @pl.when(i == 2)
        def _():
            reduce_.third(2, -2)

        @pl.when(i == 3)
        def _():
            reduce_.third(1, -1)

    def small_copy(source, target, at, device):
        return remote(source, target, r.qs.at[at], r.qr.at[at], device)

    core_copy = small_copy(r.bc, r.bc_in, 0, to_core)
    x_copy = small_copy(r.work.at[0], r.from_x, 1, late.to_x)
    y_copy = small_copy(r.work.at[1], r.from_y, 2, late.to_y)
    states_copy = small_copy(r.states_s.at[c], r.states_s.at[c], 7, to_core)

    def z_small(j, slot):
        return remote(
            r.work.at[2], r.from_z.at[slot], r.qs.at[3 + j], r.qr.at[3 + slot],
            (s + (j - z) * PLANE, c),
        )

    for t in range(taps + 1):
        begin = (t % 3) * 2 * nstate
        own = r.conv_rows[t : t + 1, inner:]
        row = 1 + t // 3
        r.bc[row : row + 1, begin : begin + nstate] = jnp.where(c == 0, own, 0.0)
        r.bc[row : row + 1, begin + nstate : begin + 2 * nstate] = jnp.where(c == 1, own, 0.0)

    half_wide = wide // 2

    def last_gradient(values, target):
        for n in range(0, 2 * half, 256):
            total = None
            for i in range(count):
                term = dot(normed_block(i, n, 256), values(i), TN)
                total = term if total is None else total + term
            target[n : n + 256, :half_wide] = total.astype(BF16)

    reduce_.near_sent()
    last_gradient(lambda i: r.dy[i, :, :half_wide], r.dout)
    late.begin(0)
    last_gradient(
        lambda i: jnp.concatenate([r.dy[i, :, half_wide:], r.gtail[i]], axis=1), r.dgate
    )
    late.begin(1)
    reduce_.third(0)
    reduce_.finish()

    def part_back(i):
        part = dot(r.ggate_s[i], r.w2_full[:, :inner], NT)
        part = part + dot(r.dy[i], r.w[:, :inner], NT)
        part = part + dot(r.gtail[i, :, :nstate], r.w[:, mine], NT)
        part = part + dot(r.gtail[i, :, nstate:], r.w[:, channels:], NT)
        low_part = part.astype(BF16)
        r.normal[i] = low_part
        swap_part(i).start()
        tok = either(c, r.tok[i].astype(F32), r.tok_in[i].astype(F32))
        unit = tok * lax.rsqrt(jnp.mean(tok * tok, axis=-1, keepdims=True) + EPSILON)
        r.bc[0:1, :inner] += jnp.sum(low_part.astype(F32) * unit, axis=0, keepdims=True)

    @pl.loop(0, count)
    def _(i):
        part_back(i)

        @pl.when(i == 1)
        def _():
            late.second(3, -3)

        @pl.when(i == 2)
        def _():
            late.second(2, -2)

    core_copy.start()

    def tokens_back(i):
        swap_part(i).wait_recv()
        swap_out(i).wait_recv()
        own_tok = r.tok[i].astype(F32)
        tok = either(c, own_tok, r.tok_in[i].astype(F32))
        scale = lax.rsqrt(jnp.mean(tok * tok, axis=-1, keepdims=True) + EPSILON)
        unit = tok * scale
        grad_normed = r.normal[i].astype(F32) + r.low[i].astype(F32)
        grad = grad_normed * r.prm[GAIN : GAIN + 1, : 2 * half]
        r.ginputs[...] = scale * (grad - unit * jnp.mean(grad * unit, axis=-1, keepdims=True))
        r.full[i, :, :half] = r.g[i].astype(F32) + r.ginputs[:, side]
        store_grad(i).start()
        r.g_in[i] = (own_tok + (r.gate[i, :, :half] + r.out_in[i].astype(F32))).astype(BF16)
        store_mixed(i).start()

    @pl.loop(0, count)
    def _(i):
        tokens_back(i)

        @pl.when(i == 0)
        def _():
            late.second(1, -1)
            core_copy.wait_recv()
            r.work[0, 0:2] = r.small[0:2]
            r.work[0, 2 : 3 + taps] = r.conv_rows[: taps + 1, :inner]
            r.work[0, 3 + taps : 8] = jnp.zeros((5 - taps, inner), F32)
            r.work[0, 8:16] = r.bc[...] + r.bc_in[...]
            x_copy.start()

        @pl.when(i == 1)
        def _():
            late.third(3, -3)

        @pl.when(i == 2)
        def _():
            late.second(0)

        @pl.when(i == 3)
        def _():
            late.third(2, -2)

    x_copy.wait_recv()
    r.work[1] = r.work[0] + r.from_x[...]
    y_copy.start()
    late.third(1, -1)
    y_copy.wait_recv()
    r.work[2] = r.work[1] + r.from_y[...]
    for j in range(LINE):
        pl.when(z != j)(z_small(j, z).start)
    r.from_z[z] = r.work[2]
    late.third(0, only=(1,))
    r.states_s[c] = r.g_x[:, inner : inner + nstate]
    states_copy.start()
    late.third(0, only=(0,))
    for j in range(LINE):
        pl.when(z != j)(z_small(j, j).wait_recv)
    r.sums_out[...] = (r.from_z[0] + r.from_z[1]) + (r.from_z[2] + r.from_z[3])
    states_copy.wait()
    r.states[...] = r.states_s[...]
    core_copy.wait_send()
    x_copy.wait_send()
    y_copy.wait_send()
    for j in range(LINE):
        pl.when(z != j)(z_small(j, z).wait_send)
    late.near_sent()
    late.finish()
    suffix.finish()
    for gather in (first_gather, second_gather):
        gather.drain()

    @pl.loop(0, count)
    def _(i):
        swap_sums(i).wait_send()
        swap_out(i).wait_send()
        swap_states(i).wait_send()
        pl.when(prv)(send_edge(i).wait_send)
        swap_part(i).wait_send()
        store_grad(i).wait()
        store_mixed(i).wait()


LOCAL_REFS = tuple(dict(kept=0, mid_send=0))
LATE_REFS = tuple(n if n in LOCAL_REFS else "l" + n for n in REDUCE_REFS)
SECOND_REFS = tuple("s" + n for n in GATHER_REFS)
SHARED_REFS = tuple(dict(total=0, leaving=0, staged=0))
SUFFIX_REFS = tuple(n if n in SHARED_REFS else "s" + n for n in SCAN_REFS)


def main_call(sizes, total_inner, tok, g, doc, prm, w1, w2):
    length, inner, nstate, size, taps = sizes
    count, _, half = tok.shape
    model = 2 * half
    channels = inner + 2 * nstate
    rows = w1.shape[0]
    wide = inner + nstate + LANES
    ins = dict(
        tok=(tok, INSIDE), g=(g, INSIDE), doc=(doc, INSIDE), prm=(prm, INSIDE),
        w1=(w1, ANYWHERE), w2=(w2, ANYWHERE),
    )
    outs = dict(
        mixed=(shape((count, length, half), BF16), ANYWHERE),
        tokens_grad=(shape((count, length, half), F32), ANYWHERE),
        g_out=(shape((rows, inner), F32), INSIDE),
        g_gate=(shape((rows, inner), F32), INSIDE),
        g_x=(shape((rows, wide), F32), INSIDE),
        states=(shape((2, rows, nstate), F32), INSIDE),
        sums_out=(shape((16, inner), F32), INSIDE),
    )

    def vmem(*dims, dtype=F32):
        return pltpu.VMEM(dims, dtype)

    def low(*dims):
        return pltpu.VMEM(dims, BF16)

    scratch = dict(
        g_in=low(count, length, half),
        tok_in=low(count, length, half),
        out_in=low(count, length, half),
        edge_in=vmem(count, EDGE, inner + nstate),
        small=vmem(8, inner),
        gtail=low(count, length, nstate + LANES),
        gext=vmem(length + EDGE, inner + nstate),
        conv_rows=vmem(8, inner + nstate),
        states_s=vmem(2, rows, nstate),
        bc=vmem(8, inner),
        bc_in=vmem(8, inner),
        work=vmem(3, 16, inner),
        from_x=vmem(16, inner),
        from_y=vmem(16, inner),
        from_z=vmem(LINE, 16, inner),
        qs=dma(8),
        qr=dma(8),
        halo=low(count, HALO, model),
        w=low(model, w1.shape[1]),
        w2_full=low(model, 2 * inner),
        normed_s=low(count, HALO + length, model),
        xs_s=low(count, HALO + length, channels),
        act=low(count, length, channels),
        aux=vmem(count, length, 4 * LANES),
        low=low(count, length, inner),
        dec=vmem(count, HEAD_ROWS, LANES),
        state=low(count, inner, nstate),
        hin=low(count, inner, nstate),
        prior=low(count, inner, nstate),
        later=low(count, inner, nstate),
        full=vmem(count, length, inner),
        gate=vmem(count, length, inner),
        gn=vmem(count, length, inner),
        sums=vmem(count, EDGE, length),
        sums_in=vmem(count, EDGE, length),
        normal=low(count, length, inner),
        dy=low(count, length, inner),
        ggate_s=low(count, length, inner),
        osend=low(count, length, half),
        dout=low(model, inner),
        dgate=low(model, inner),
        ext=vmem(HALO + length, channels),
        ginputs=vmem(length, inner),
        bsend=low(count, length, nstate),
        brecv=low(count, length, nstate),
        edge=vmem(count, EDGE, inner + nstate),
        ss=dma(7, count),
        rs=dma(7, count),
        hs=dma(2),
        hr=dma(2),
        store=dma(2, count),
    )
    scan = Scan.scratch(count, inner, nstate, HEAD_ROWS)
    gather = Gather.semaphores(4)
    scratch.update(zip(SUFFIX_REFS, scan.values()))
    scratch.update(scan)
    scratch.update(gather)
    scratch.update(zip(SECOND_REFS, gather.values()))
    scratch.update(zip(LATE_REFS, Reduce.scratch(2, rows, wide).values()))
    scratch.update(Reduce.scratch(2, rows, 2 * inner))
    return fused_call(
        functools.partial(main_body, sizes, total_inner), None, ins, outs, scratch, 1, "main"
    )


def local_call(body, ins, outs, name):
    names = list(ins) + list(outs)

    def kernel(*refs):
        body(Refs(names, refs))

    results = pl.pallas_call(
        kernel,
        in_specs=[INSIDE for _ in ins],
        out_specs=[INSIDE for _ in outs],
        out_shape=list(outs.values()),
        name=name,
    )(*ins.values())
    return Refs(list(outs), results)


def pack_body(sizes, r):
    length, inner, nstate, size, taps = sizes
    heads = inner // size
    channels = inner + 2 * nstate
    model = r.norm_gain.shape[0]

    def line(v):
        return v.reshape(1, v.shape[0])

    r.prm[...] = jnp.zeros_like(r.prm)
    r.prm[GAIN : GAIN + 1, :model] = line(r.norm_gain[...])
    r.prm[INNER_GAIN : INNER_GAIN + 1, :inner] = line(r.inner_gain[...])
    r.prm[BIAS : BIAS + 1, :inner] = line(r.conv_bias_x[...])
    r.prm[BIAS : BIAS + 1, inner:] = line(r.conv_bias_bc[...])
    r.prm[STEP_BIAS : STEP_BIAS + 1, :heads] = line(r.step_bias[...])
    r.prm[RATE : RATE + 1, :heads] = -jnp.exp(line(r.decay_log[...]))
    r.prm[TAPS : TAPS + taps, :inner] = r.conv_taps_x[...]
    r.prm[TAPS : TAPS + taps, inner:] = r.conv_taps_bc[...]
    r.prm[SKIP : SKIP + 1, :heads] = line(r.skip_gain[...])
    skip = jnp.broadcast_to(r.prm[SKIP : SKIP + 1, :LANES], (8, LANES))
    spread = head_spread(inner, size)
    r.prm[SKIP : SKIP + 1, :inner] = sum(dot(v, spread) for v in split3(skip))[:1]
    r.w2[:, :inner] = r.features[:, 0, :]
    same = lax.broadcasted_iota(jnp.int32, (heads, LANES), 0) == lax.broadcasted_iota(
        jnp.int32, (heads, LANES), 1
    )
    r.w2[:, inner:] = r.output_projection[...]
    r.w1[:, :inner] = r.features[:, 1, :]
    r.w1[:, inner:channels] = r.state_weight[...]
    r.w1[:, channels:] = dot(
        r.step_weight[...], jnp.where(same, 1.0, 0.0).astype(BF16), TN
    ).astype(BF16)
    seqs = r.starts.shape[1]
    for i in range(r.doc.shape[0]):
        flags = r.starts[i // seqs, i % seqs : i % seqs + 1].astype(F32)
        r.doc[i] = jnp.broadcast_to(flags, (8, length))


def results_body(sizes, r):
    length, inner, nstate, size, taps = sizes
    heads = inner // size
    r.norm_gain[...] = r.sums[8]
    r.gate_x[:, 0, :] = r.g_gate[...]
    r.gate_x[:, 1, :] = r.g_x[:, :inner]
    r.state_weight[:, :nstate] = r.states[0]
    r.state_weight[:, nstate:] = r.states[1]
    r.step_weight[...] = r.g_x[:, inner + nstate :].T[:heads]
    r.taps_x[...] = r.sums[2 : 2 + taps]
    r.bias_x[...] = r.sums[2 + taps]
    for t in range(taps + 1):
        begin = (t % 3) * 2 * nstate
        row = r.sums[9 + t // 3, begin : begin + 2 * nstate]
        if t < taps:
            r.taps_bc[t] = row
        else:
            r.bias_bc[...] = row
    r.step_bias[...] = r.sums[1, LANES : LANES + heads]
    r.decay_log[...] = r.sums[1, 2 * LANES : 2 * LANES + heads]
    r.out_weight[...] = r.g_out[...]
    r.mixed[...] = r.mixed_in[...]
    r.tokens_grad[...] = r.grad_in[...]
    r.skip_gain[...] = r.sums[1, :heads]
    r.inner_gain[...] = r.sums[0]


def fused_layer(
    sizes, total_inner, tok, g, starts, norm_gain, features, state_weight, step_weight, conv_taps_x,
    conv_bias_x, conv_taps_bc, conv_bias_bc, step_bias, decay_log, skip_gain, inner_gain,
    output_projection,
):
    length, inner, nstate, size, taps = sizes
    heads = inner // size
    count, _, half = tok.shape
    model = 2 * half
    rows = features.shape[0]
    channels = inner + 2 * nstate
    packed = local_call(
        functools.partial(pack_body, sizes),
        dict(
            norm_gain=norm_gain, inner_gain=inner_gain, conv_bias_x=conv_bias_x,
            conv_bias_bc=conv_bias_bc, step_bias=step_bias, decay_log=decay_log,
            conv_taps_x=conv_taps_x, conv_taps_bc=conv_taps_bc, skip_gain=skip_gain,
            features=features, state_weight=state_weight, step_weight=step_weight.T,
            output_projection=output_projection.T, starts=starts,
        ),
        dict(
            prm=shape((16, channels), F32),
            w1=shape((rows, channels + LANES), BF16),
            w2=shape((rows, 2 * inner), BF16),
            doc=shape((count, 8, length), F32),
        ),
        "pack",
    )
    m = main_call(sizes, total_inner, tok, g, packed.doc, packed.prm, packed.w1, packed.w2)
    o = local_call(
        functools.partial(results_body, sizes),
        dict(
            sums=m.sums_out, g_x=m.g_x, g_gate=m.g_gate, states=m.states, g_out=m.g_out,
            mixed_in=m.mixed, grad_in=m.tokens_grad,
        ),
        dict(
            mixed=shape((count, length, half), BF16),
            tokens_grad=shape((count, length, half), F32),
            norm_gain=shape((model,), F32),
            gate_x=shape((rows, 2, inner), F32),
            state_weight=shape((rows, 2 * nstate), F32),
            step_weight=shape((heads, rows), F32),
            taps_x=shape((taps, inner), F32),
            bias_x=shape((inner,), F32),
            taps_bc=shape((taps, 2 * nstate), F32),
            bias_bc=shape((2 * nstate,), F32),
            step_bias=shape((heads,), F32),
            decay_log=shape((heads,), F32),
            skip_gain=shape((heads,), F32),
            inner_gain=shape((inner,), F32),
            out_weight=shape((rows, inner), F32),
        ),
        "results",
    )
    o.step_weight, o.out_weight = o.step_weight.T, o.out_weight.T
    return tuple(o.__dict__.values())


def shards(
    tokens, doc_starts, norm_gain, input_gate_features, input_state_weight, input_step_weight,
    conv_taps_x, conv_bias_x, conv_taps_bc, conv_bias_bc, step_bias, decay_log, skip_gain,
    inner_gain, output_projection, out_grad,
):
    micro, seqs, length, half = tokens.shape
    count = micro * seqs
    model = 2 * half
    heads = step_bias.shape[0]
    inner = inner_gain.shape[0]
    size = inner // heads
    nstate = conv_taps_bc.shape[1] // 2
    taps = conv_taps_x.shape[0]
    channels = inner + 2 * nstate
    rows = input_gate_features.shape[0]
    total_inner = inner * lax.axis_size("head")
    sizes = (length, inner, nstate, size, taps)
    core = lax.axis_index("head")

    tok = tokens.reshape(count, length, half)
    g = out_grad.reshape(count, length, half)
    if lax.axis_size("seq") == PLANE * LINE and lax.axis_size("head") == 2:
        outputs = fused_layer(
            sizes, total_inner, tok, g, doc_starts, norm_gain, input_gate_features,
            input_state_weight, input_step_weight, conv_taps_x, conv_bias_x, conv_taps_bc,
            conv_bias_bc, step_bias, decay_log, skip_gain, inner_gain, output_projection,
        )
        return tuple(o.reshape(tokens.shape) if n < 2 else o for n, o in enumerate(outputs))

    doc = jnp.broadcast_to(
        doc_starts.reshape(count, 1, length).astype(F32), (count, 8, length)
    )

    def row(v):
        return jnp.pad(v, (0, channels - v.shape[0]))[None]

    prm = jnp.concatenate(
        [
            row(norm_gain),
            row(inner_gain),
            row(jnp.repeat(skip_gain, size)),
            row(jnp.concatenate([conv_bias_x, conv_bias_bc])),
            row(step_bias),
            row(-jnp.exp(decay_log)),
            jnp.concatenate([conv_taps_x, conv_taps_bc], axis=1),
        ],
        axis=0,
    )
    prm = jnp.pad(prm, ((0, 16 - prm.shape[0]), (0, 0)))
    w_own = jnp.concatenate(
        [
            input_gate_features.reshape(rows, 2 * inner),
            input_state_weight,
            jnp.pad(input_step_weight, ((0, 0), (0, LANES - heads))),
        ],
        axis=1,
    )
    w_out_own = output_projection.T

    w_in, w_out, tok_full, g_full, halo = plain_gather(
        w_own, w_out_own, tok, g, tok[:, length - HALO :]
    )
    grid = (count,)
    outs = [
        shape((count, length, model), BF16),
        shape((count, length, inner), F32),
        shape((count, HALO + length, channels), BF16),
        shape((count, length, channels), F32),
        shape((count, length, channels), BF16),
        shape((count, length, inner), F32),
        shape((count, inner, nstate), BF16),
        shape((count, length, 5 * LANES), F32),
        shape((count, HEAD_ROWS, LANES), F32),
    ]
    normed, gate, xs, pre, act, scan, state, aux, dec = call(
        functools.partial(forward_kernel, sizes),
        grid,
        [per_seq(tok_full), per_seq(halo), per_seq(doc), whole(prm), whole(w_in)],
        [per_seq(o) for o in outs],
        outs,
        [pltpu.VMEM((HALO + length, channels), F32)],
        name="forward",
    )(tok_full, halo, doc, prm, w_in)

    hin = plain_scan(state, dec, size, False)

    outs = [
        shape((count, length, inner), F32),
        shape((count, length, inner), F32),
        shape((count, length, LANES), F32),
    ]
    ins = (scan, act, aux, gate, hin, g_full)
    full, grad_norm, sums = call(
        functools.partial(gate_kernel, sizes),
        grid,
        [per_seq(a) for a in ins] + [whole(prm), whole(w_out)],
        [per_seq(o) for o in outs],
        outs,
        name="gate",
    )(*ins, prm, w_out)

    sums_in = swap_heads(sums)

    outs = [
        shape((count, length, half), F32),
        shape((count, length, half), BF16),
        shape((count, length, inner), BF16),
        shape((count, length, inner), BF16),
        shape((count, inner, nstate), BF16),
        shape((8, inner), F32),
        shape((model, inner), BF16),
        shape((model, inner), BF16),
    ]
    ins = (full, act, aux, gate, grad_norm, sums, sums_in, g_full, normed)
    keep, send, dy, ggate, prior, small_out, dout, dgate = call(
        functools.partial(output_kernel, sizes, total_inner),
        grid,
        [per_seq(a) for a in ins] + [whole(prm), whole(w_out)],
        [per_seq(o) for o in outs[:5]] + [whole(o) for o in outs[5:]],
        outs,
        [
            pltpu.VMEM((model, inner), F32),
            pltpu.VMEM((model, inner), F32),
            pltpu.VMEM((length, model), F32),
        ],
        name="output",
    )(*ins, prm, w_out)

    mixed = (tok.astype(F32) + (keep + swap_heads(send).astype(F32))).astype(BF16)
    later = plain_scan(prior, dec, size, True)

    outs = [
        shape((count, length, inner), F32),
        shape((count, length, nstate), F32),
        shape((count, length, nstate), BF16),
        shape((count, length, LANES), F32),
        shape((8, LANES), F32),
        shape((count, EDGE, inner), F32),
        shape((count, EDGE, nstate), F32),
    ]
    ins = (full, act, aux, dy, hin, later, state, doc, pre)
    gcx, own, other, gpre, small_scan, edge, slope = call(
        functools.partial(backward_kernel, sizes),
        grid,
        [per_seq(a) for a in ins] + [whole(prm)],
        [per_seq(o) if len(o.shape) == 3 else whole(o) for o in outs],
        outs,
        [pltpu.VMEM((length, length), F32)],
        name="backward",
    )(*ins, prm)

    recv, edge_in, edge_state = plain_states(other, own, slope, edge)

    outs = [
        shape((count, length, model), BF16),
        shape((model, inner + nstate + LANES), BF16),
        shape((8, inner + nstate), F32),
    ]
    ins = (gcx, own, recv, edge_in, edge_state, pre, xs, gpre, ggate, normed)
    part, dx, small_conv = call(
        functools.partial(conv_kernel, sizes),
        grid,
        [per_seq(a) for a in ins] + [whole(prm), whole(w_in)],
        [per_seq(outs[0]), whole(outs[1]), whole(outs[2])],
        outs,
        [
            pltpu.VMEM((model, inner + nstate + LANES), F32),
            pltpu.VMEM((HALO + length, inner + nstate), F32),
            pltpu.VMEM((length + EDGE, inner + nstate), F32),
        ],
        name="conv",
    )(*ins, prm, w_in)

    part_in = swap_heads(part)

    outs = [shape((count, length, half), F32), shape((8, model), F32)]
    ins = (tok_full, part, part_in, g)
    tokens_grad, small_norm = call(
        functools.partial(tokens_kernel, sizes),
        grid,
        [per_seq(a) for a in ins] + [whole(prm)],
        [per_seq(outs[0]), whole(outs[1])],
        outs,
        [pltpu.VMEM((length, model), F32)],
        name="tokens",
    )(*ins, prm)

    small = jnp.concatenate(
        [
            row(small_norm[0]),
            row(small_out[0]),
            row(small_out[1]),
            row(jnp.concatenate([small_scan[0], small_scan[1]])),
            jnp.pad(small_conv[: taps + 1, :inner], ((0, 0), (0, channels - inner))),
            jnp.zeros((16 - 5 - taps, channels), F32),
        ],
        axis=0,
    )
    own_states = small_conv[:, inner:]
    shared = jnp.concatenate(
        [jnp.where(core == 0, own_states, 0.0), jnp.where(core == 1, own_states, 0.0)], axis=1
    )
    (g_out, g_gate, g_x), small, shared = plain_sum((dout, dgate, dx), small, shared)
    g_states = plain_both(g_x[:, inner : inner + nstate])
    return (
        mixed.reshape(tokens.shape),
        tokens_grad.reshape(tokens.shape),
        small[0, :model],
        jnp.stack([g_gate, g_x[:, :inner]], axis=1),
        g_states,
        g_x[:, inner + nstate : inner + nstate + heads],
        small[4 : 4 + taps, :inner],
        small[4 + taps, :inner],
        shared[:taps],
        shared[taps],
        small[3, :heads],
        small[3, LANES : LANES + heads],
        small[2, :inner].reshape(heads, size).sum(axis=1),
        small[1, :inner],
        g_out.T,
    )


def solution(mesh):
    placed = (
        P(None, None, "seq", "head"),
        P(None, None, "seq"),
        P(),
        P("seq", None, "head"),
        P("seq", None),
        P("seq", "head"),
        P(None, "head"),
        P("head"),
        P(),
        P(),
        P("head"),
        P("head"),
        P("head"),
        P("head"),
        P("head", "seq"),
        P(None, None, "seq", "head"),
    )
    return jax.shard_map(
        shards,
        mesh=mesh,
        in_specs=placed,
        out_specs=(
            P(None, None, "seq", "head"),
            P(None, None, "seq", "head"),
            P(),
            P("seq", None, "head"),
            P("seq", None),
            P("seq", "head"),
            P(None, "head"),
            P("head"),
            P(),
            P(),
            P("head"),
            P("head"),
            P("head"),
            P("head"),
            P("head", "seq"),
        ),
        check_vma=False,
    )
```
